32 devices in a mesh: srow: 4 (over z), scol: 4 (over x, core), trow: 2 (over y).
Axes of the slice: x: 2, y: 2, z: 4, core: 2. Of those that a mesh axis runs over, the one named last changes fastest.
Arguments:
- volume: bfloat16 [8, 8, 16, 128, 128], P(None, 'srow', 'scol', 'trow'), may hold values from -6 to 6
- src_weight: bfloat16 [2, 9, 8, 8], replicated, may hold values from -0.75 to 0.75
- tgt_weight: bfloat16 [2, 9, 8, 8], replicated, may hold values from -0.75 to 0.75
- bias: float32 [2, 8], replicated, may hold values from -3 to 3
Outputs:
- refined: bfloat16 [8, 8, 16, 128, 128], P(None, 'srow', 'scol', 'trow')
The draws below stay inside these ranges and needn't reach their ends.
All inputs are finite; a program needn't handle non-finite values.
Results may differ from the reference program's by a relative error of at most 0.0036.
Values may be sent and summed in bfloat16 or wider, within the bound.
No kernel may reach another device: no remote copies, remote signals or barrier semaphores. Data moves between devices by JAX's collectives and lax.ppermute only.
A program may use at most 64 MiB of HBM per device.

```python
import jax
import jax.numpy as jnp
from jax import lax

C = 8
TC = 128
LAYERS = 2
NI = 8
NJ = 16
NK = 128


def levels(own_key, extent, cuts, smallest, top_value):
    gain, own = 1.0, jax.random.fold_in(own_key, 6)
    for dim, shards_of in cuts:
        steps = jnp.exp(jax.random.uniform(jax.random.fold_in(own, dim), (shards_of,), jnp.float32, smallest / len(cuts), top_value / len(cuts)))
        gain = gain * jnp.repeat(steps, extent[dim] // shards_of).reshape([-1 if axis == dim else 1 for axis in range(len(extent))])
    return gain


def centred(stream_key, extent, deviation, reach, cuts=(), held_as=jnp.bfloat16):
    array = deviation * jax.random.normal(stream_key, extent, jnp.float32)
    if cuts:
        array = array * levels(stream_key, extent, cuts, -0.22, 0.18)
    return jnp.clip(array, -reach, reach).astype(held_as)


def setup_inputs(seed: int = 0) -> dict:
    key_of = jax.random.split(jax.random.key(seed), 5)
    volume = centred(key_of[0], (C, NI, NJ, NK, TC), 1.0, 6.0, ((1, 4), (2, 4), (3, 2)))
    src_weight = centred(key_of[1], (LAYERS, 9, C, C), (9 * C) ** -0.5, 0.75)
    tgt_weight = centred(key_of[2], (LAYERS, 9, C, C), (9 * C) ** -0.5, 0.75)
    bias = centred(key_of[3], (LAYERS, C), 0.5, 3.0, (), jnp.float32)
    return dict(volume=volume, src_weight=src_weight, tgt_weight=tgt_weight, bias=bias)


def apply_layer(src_pad, tgt_pad, w_src, w_tgt, bias_row):
    source = src_pad.astype(jnp.float32)
    target = tgt_pad.astype(jnp.float32)
    channels, rows_two, cols_two, depth, width = source.shape
    row_count = rows_two - 2
    col_count = cols_two - 2
    widened = jnp.pad(target, ((0, 0), (0, 0), (0, 0), (0, 0), (1, 1)))
    total = jnp.zeros((channels, row_count, col_count, depth, width), jnp.float32)
    for first in range(3):
        for second in range(3):
            piece = source[:, first:first + row_count, second:second + col_count]
            kernel = w_src[3 * first + second].astype(jnp.float32)
            total = total + jnp.einsum("oc,cijkl->oijkl", kernel, piece, precision=lax.Precision.HIGHEST)
    for first in range(3):
        for second in range(3):
            piece = widened[:, :, :, first:first + depth, second:second + width]
            kernel = w_tgt[3 * first + second].astype(jnp.float32)
            total = total + jnp.einsum("oc,cijkl->oijkl", kernel, piece, precision=lax.Precision.HIGHEST)
    center = target[:, :, :, 1:1 + depth]
    return center + jnp.maximum(total + bias_row[:, None, None, None, None], 0.0)


def reference(volume, src_weight, tgt_weight, bias):
    state = volume
    for layer_id in range(LAYERS):
        src_pad = jnp.pad(state, ((0, 0), (1, 1), (1, 1), (0, 0), (0, 0)))
        tgt_pad = jnp.pad(state, ((0, 0), (0, 0), (0, 0), (1, 1), (0, 0)))
        state = apply_layer(src_pad, tgt_pad, src_weight[layer_id], tgt_weight[layer_id], bias[layer_id]).astype(jnp.bfloat16)
    return state
```

```python
import functools

import jax
import jax.numpy as jnp
from jax import lax
from jax.experimental import pallas as pl
from jax.experimental.pallas import tpu as pltpu
from jax.sharding import PartitionSpec as P

BAND = 32
EDGE = 16
VMEM_LIMIT = 56 * 1024 * 1024
F32 = jnp.float32
BF16 = jnp.bfloat16


def in_vmem(count):
    return [pl.BlockSpec(memory_space=pltpu.VMEM)] * count


def call(body, outs, scratch=(), flops=0, moved=0):
    def run(*args):
        return pl.pallas_call(
            body,
            out_shape=outs,
            in_specs=in_vmem(len(args)),
            out_specs=tuple(in_vmem(len(outs))),
            scratch_shapes=list(scratch),
            compiler_params=pltpu.CompilerParams(vmem_limit_bytes=VMEM_LIMIT),
            cost_estimate=pl.CostEstimate(flops=flops, bytes_accessed=moved, transcendentals=0),
        )(*args)

    return run


def dot(a, b):
    return jnp.dot(a, b, preferred_element_type=F32)


def build_body(taps, channels, table_ref, src_ref, tgt_ref, low_ref, high_ref):
    span = channels * BAND
    small = channels * EDGE
    row = lax.broadcasted_iota(jnp.int32, (span, span), 0)
    col = lax.broadcasted_iota(jnp.int32, (span, span), 1)
    shift = (row % BAND) - (col % BAND)
    row_s = lax.broadcasted_iota(jnp.int32, (span, small), 0) % BAND
    col_s = lax.broadcasted_iota(jnp.int32, (span, small), 1) % EDGE
    at_low = (row_s == 0) & (col_s == EDGE - 1)
    at_high = (row_s == BAND - 1) & (col_s == 0)
    pick_r = lax.broadcasted_iota(jnp.int32, (span, channels), 0) // BAND
    pick_c = lax.broadcasted_iota(jnp.int32, (span, channels), 1)
    spread = (pick_r == pick_c).astype(BF16)
    layers = table_ref.shape[0]
    width = taps * channels
    gate_r = lax.broadcasted_iota(jnp.int32, (width, span), 0)
    gate_c = lax.broadcasted_iota(jnp.int32, (width, span), 1) // BAND
    gate_rs = lax.broadcasted_iota(jnp.int32, (width, small), 0)
    gate_cs = lax.broadcasted_iota(jnp.int32, (width, small), 1) // EDGE
    for layer in range(layers):
        tall = dot(spread, table_ref[layer]).astype(BF16)

        def full(tap):
            return dot(tall, (gate_r == gate_c + tap * channels).astype(BF16))

        def part(tap):
            return dot(tall, (gate_rs == gate_cs + tap * channels).astype(BF16))

        for tap in range(9):
            first, second = divmod(tap, 3)
            src_ref[layer, first, :, second * span : (second + 1) * span] = jnp.where(
                shift == 0, full(tap), 0.0
            ).astype(BF16)
        for second in range(3):
            band = jnp.where(shift == 1, full(9 + second), 0.0)
            band = jnp.where(shift == 0, full(12 + second), band)
            band = jnp.where(shift == -1, full(15 + second), band)
            tgt_ref[layer, :, second * span : (second + 1) * span] = band.astype(BF16)
            cut = slice(second * small, (second + 1) * small)
            low_ref[layer, :, cut] = jnp.where(at_low, part(9 + second), 0.0).astype(BF16)
            high_ref[layer, :, cut] = jnp.where(at_high, part(15 + second), 0.0).astype(BF16)


def build(src_weight, tgt_weight):
    layers, _, outs, ins = src_weight.shape
    both = jnp.concatenate([src_weight, tgt_weight], axis=1)
    taps = both.shape[1]
    table = jnp.transpose(both, (0, 2, 1, 3)).reshape(layers, outs, taps * ins)
    span, small = ins * BAND, ins * EDGE
    shape = jax.ShapeDtypeStruct
    return call(
        functools.partial(build_body, taps, ins),
        (
            shape((layers, 3, span, 3 * span), BF16),
            shape((layers, span, 3 * span), BF16),
            shape((layers, span, 3 * small), BF16),
            shape((layers, span, 3 * small), BF16),
        ),
        flops=2 * layers * taps * span * span * taps * ins,
        moved=layers * 14 * span * span * 2,
    )(table)


def source_rows(x_ref, left_ref, right_ref, i, start, size):
    cols = x_ref.shape[2]
    channels = x_ref.shape[0]
    tiles = [left_ref[:, i, start : start + size, :]]
    tiles += [x_ref[:, i, j, start : start + size, :] for j in range(cols)]
    tiles += [right_ref[:, i, start : start + size, :]]
    return [t.reshape(channels * size, t.shape[-1]) for t in tiles]


def src_operand(tiles, cols):
    return jnp.concatenate([jnp.concatenate(tiles[b : b + cols], axis=1) for b in range(3)], axis=0)


def edge_body(layer, x_ref, left_ref, right_ref, src_ref, down_ref, up_ref):
    channels, rows, cols, depth, width = x_ref.shape
    for start in range(0, depth, BAND):
        for i, first, out_ref in ((rows - 1, 0, down_ref), (0, 2, up_ref)):
            tiles = source_rows(x_ref, left_ref, right_ref, i, start, BAND)
            got = dot(src_ref[layer, first], src_operand(tiles, cols)).astype(BF16)
            for j in range(cols):
                out_ref[:, j, start : start + BAND, :] = got[:, j * width : (j + 1) * width].reshape(
                    channels, BAND, width
                )


def shifted(tile, step):
    lane = lax.broadcasted_iota(jnp.int32, tile.shape, 1)
    width = tile.shape[1]
    rolled = pltpu.roll(tile.astype(F32), step % width, 1)
    gone = 0 if step == 1 else width - 1
    return jnp.where(lane == gone, 0.0, rolled).astype(BF16)


def main_body(
    layer, x_ref, left_ref, right_ref, lowy_ref, highy_ref, src_ref, tgt_ref, lo_ref, hi_ref, bias_ref, acc_ref, side_ref
):
    channels, rows, cols, depth, width = x_ref.shape
    span = channels * BAND
    bands = depth // BAND
    out_channel = lax.broadcasted_iota(jnp.int32, (span, 1), 0) // BAND
    bias = jnp.zeros((span, 1), F32)
    for o in range(channels):
        bias = jnp.where(out_channel == o, bias_ref[layer, o], bias)

    def three(read, size):
        lanes = []
        for step in (1, 0, -1):
            tiles = [read(j).reshape(channels * size, width) for j in range(cols)]
            if step:
                tiles = [shifted(t, step) for t in tiles]
            lanes.append(jnp.concatenate(tiles, axis=1))
        return lanes

    for i in range(rows):
        for q in range(bands):
            for n, value in enumerate(three(lambda j: x_ref[:, i, j, q * BAND : (q + 1) * BAND, :], BAND)):
                side_ref[q, n] = value
        low_y = jnp.concatenate(three(lambda j: lowy_ref[:, i, j], EDGE), axis=0)
        high_y = jnp.concatenate(three(lambda j: highy_ref[:, i, j], EDGE), axis=0)
        for q in range(bands):
            total = jnp.broadcast_to(bias, (span, cols * width))
            for a in range(3):
                if 0 <= i + a - 1 < rows:
                    tiles = source_rows(x_ref, left_ref, right_ref, i + a - 1, q * BAND, BAND)
                    total = total + dot(src_ref[layer, a], src_operand(tiles, cols))
            total = total + dot(tgt_ref[layer], side_ref[q].reshape(3 * span, cols * width))

            def near(band, start):
                parts = [
                    side_ref[band, n].reshape(channels, BAND, cols * width)[:, start : start + EDGE].reshape(
                        channels * EDGE, cols * width
                    )
                    for n in range(3)
                ]
                return jnp.concatenate(parts, axis=0)

            total = total + dot(lo_ref[layer], low_y if q == 0 else near(q - 1, BAND - EDGE))
            total = total + dot(hi_ref[layer], high_y if q == bands - 1 else near(q + 1, 0))
            for j in range(cols):
                acc_ref[:, i, j, q * BAND : (q + 1) * BAND, :] = total[:, j * width : (j + 1) * width].reshape(
                    channels, BAND, width
                )


def finish_body(last, x_ref, acc_ref, fromlow_ref, fromhigh_ref, out_ref, *more):
    channels, rows, cols, depth, width = x_ref.shape
    for i in range(rows):
        for j in range(cols):
            total = acc_ref[:, i, j]
            if i == 0:
                total = total + fromlow_ref[:, j].astype(F32)
            if i == rows - 1:
                total = total + fromhigh_ref[:, j].astype(F32)
            value = (x_ref[:, i, j].astype(F32) + jnp.maximum(total, 0.0)).astype(BF16)
            out_ref[:, i, j] = value
            if not last:
                first_ref, final_ref, top_ref, bottom_ref = more
                if j == 0:
                    first_ref[:, i] = value
                if j == cols - 1:
                    final_ref[:, i] = value
                top_ref[:, i, j] = value[:, :EDGE]
                bottom_ref[:, i, j] = value[:, depth - EDGE :]


def beside(block_up, block_down, axis):
    count = lax.axis_size(axis)
    forward = [(i, i + 1) for i in range(count - 1)]
    backward = [(i + 1, i) for i in range(count - 1)]
    return lax.ppermute(block_up, axis, forward), lax.ppermute(block_down, axis, backward)


def target_halo(top, bottom):
    axis = "trow"
    count = lax.axis_size(axis)
    if count != 2:
        return beside(bottom, top, axis)
    me = lax.axis_index(axis)
    both = lax.all_gather(jnp.where(me == 0, bottom, top), axis)
    zero = jnp.zeros_like(top)
    return jnp.where(me == 0, zero, both[0]), jnp.where(me == 0, both[1], zero)


def shards(volume, src_weight, tgt_weight, bias):
    layers = src_weight.shape[0]
    channels, rows, cols, depth, width = volume.shape
    shape = jax.ShapeDtypeStruct
    state = volume
    edges = (volume[:, :, 0], volume[:, :, cols - 1], volume[:, :, :, :EDGE], volume[:, :, :, depth - EDGE :])
    src, tgt, low, high = build(src_weight, tgt_weight)
    size = channels * rows * cols * depth * width
    for layer in range(layers):
        first, final, top, bottom = edges
        left, right = beside(final, first, "scol")
        low_y, high_y = target_halo(top, bottom)
        row = shape((channels, cols, depth, width), BF16)
        down, up = call(
            functools.partial(edge_body, layer), (row, row), flops=2 * size // rows * 2 * 3 * channels * BAND, moved=size * 2
        )(state, left, right, src)
        from_low, from_high = beside(down, up, "srow")
        (acc,) = call(
            functools.partial(main_body, layer),
            (shape(volume.shape, F32),),
            scratch=[pltpu.VMEM((depth // BAND, 3, channels * BAND, cols * width), BF16)],
            flops=2 * size * 12 * channels * BAND,
            moved=size * 8,
        )(state, left, right, low_y, high_y, src, tgt, low, high, bias)
        last = layer == layers - 1
        outs = (shape(volume.shape, BF16),)
        if not last:
            outs += tuple(shape(e.shape, BF16) for e in edges)
        state, *edges = call(functools.partial(finish_body, last), outs, flops=size, moved=size * 10)(
            state, acc, from_low, from_high
        )
    return state


def solution(mesh):
    return jax.shard_map(
        shards,
        mesh=mesh,
        in_specs=(P(None, "srow", "scol", "trow", None), P(), P(), P()),
        out_specs=P(None, "srow", "scol", "trow", None),
        check_vma=False,
    )
```

```python
import functools

import jax
import jax.numpy as jnp
from jax import lax
from jax.experimental import pallas as pl
from jax.experimental.pallas import tpu as pltpu
from jax.sharding import PartitionSpec as P

BAND = 32
EDGE = 16
SCOPED = 24 * 1024 * 1024
F32 = jnp.float32
BF16 = jnp.bfloat16
VMEM, SMEM = pltpu.VMEM, pltpu.SMEM


def call(body, outs, args, places=None, scratch=(), flops=0, moved=0):
    places = places or {}
    specs = [pl.BlockSpec(memory_space=places.get(n, VMEM)) for n in range(len(args))]
    held = [
        pltpu.with_memory_space_constraint(a, VMEM) if places.get(n, VMEM) is VMEM else a for n, a in enumerate(args)
    ]
    return pl.pallas_call(
        body,
        out_shape=tuple(outs),
        in_specs=specs,
        out_specs=tuple(pl.BlockSpec(memory_space=VMEM) for _ in outs),
        scratch_shapes=list(scratch),
        compiler_params=pltpu.CompilerParams(vmem_limit_bytes=SCOPED),
        cost_estimate=pl.CostEstimate(flops=flops, bytes_accessed=moved, transcendentals=0),
    )(*held)


def dot(a, b):
    return jnp.dot(a, b, preferred_element_type=F32)


def operators(parts, src_w_ref, tgt_w_ref, after_ref, *out_refs):
    channels = src_w_ref.shape[1]
    span, small = channels * BAND, channels * EDGE

    def columns(size):
        pick_c = lax.broadcasted_iota(jnp.int32, (channels, channels * size), 1) // size
        pick_r = lax.broadcasted_iota(jnp.int32, (channels, channels * size), 0)
        return (pick_c == pick_r).astype(BF16)

    wide, narrow = columns(BAND), columns(EDGE)
    row = lax.broadcasted_iota(jnp.int32, (BAND, span), 0)
    shift = row - lax.broadcasted_iota(jnp.int32, (BAND, span), 1) % BAND
    row_s = lax.broadcasted_iota(jnp.int32, (BAND, small), 0)
    col_s = lax.broadcasted_iota(jnp.int32, (BAND, small), 1) % EDGE
    at_low = (row_s == 0) & (col_s == EDGE - 1)
    at_high = (row_s == BAND - 1) & (col_s == 0)
    spread = {}

    def taps(ref, layer, o, pick, key):
        key = (key, layer, o)
        if key not in spread:
            spread[key] = lax.dot_general(ref[layer, o], pick, (((0,), (0,)), ((), ())), preferred_element_type=F32)
        return spread[key]

    for (kind, layer, first), out_ref in zip(parts, out_refs):
        for o in range(channels):
            rows = slice(o * BAND, (o + 1) * BAND)
            for b in range(3):
                if kind == "src":
                    got = taps(src_w_ref, layer, o, wide, "s")
                    value = jnp.where(shift == 0, got[3 * first + b][None, :], 0.0)
                elif kind == "tgt":
                    got = taps(tgt_w_ref, layer, o, wide, "t")
                    value = jnp.where(shift == 1, got[b][None, :], 0.0)
                    value = jnp.where(shift == 0, got[3 + b][None, :], value)
                    value = jnp.where(shift == -1, got[6 + b][None, :], value)
                else:
                    got = taps(tgt_w_ref, layer, o, narrow, "n")
                    value = jnp.where(at_low if first == 0 else at_high, got[3 * first + b][None, :], 0.0)
                size = value.shape[1]
                out_ref[rows, b * size : (b + 1) * size] = value.astype(BF16)


def build(parts, src_w, tgt_w, after):
    channels = src_w.shape[1]
    span, small = channels * BAND, channels * EDGE
    outs = [VMEM((span, 3 * (small if kind == "near" else span)), BF16) for kind, _, _ in parts]
    got = call(
        functools.partial(operators, parts), outs, (src_w, tgt_w, after), {2: pl.ANY}, flops=len(parts) * 10**7, moved=10**6
    )
    return dict(zip(parts, got))


def source_rows(x_ref, left_ref, right_ref, i, start, size):
    cols = x_ref.shape[2]
    channels = x_ref.shape[0]
    tiles = [left_ref[:, i, start : start + size, :]]
    tiles += [x_ref[:, i, j, start : start + size, :] for j in range(cols)]
    tiles += [right_ref[:, i, start : start + size, :]]
    return [t.reshape(channels * size, t.shape[-1]) for t in tiles]


def src_operand(tiles, cols):
    return jnp.concatenate([jnp.concatenate(tiles[b : b + cols], axis=1) for b in range(3)], axis=0)


def edge_body(x_ref, left_ref, right_ref, first_ref, last_ref, down_ref, up_ref):
    channels, rows, cols, depth, width = x_ref.shape
    for i, w_ref, out_ref in ((rows - 1, first_ref, down_ref), (0, last_ref, up_ref)):
        for start in range(0, depth, BAND):
            tiles = source_rows(x_ref, left_ref, right_ref, i, start, BAND)
            got = dot(w_ref[...], src_operand(tiles, cols)).astype(BF16)
            for j in range(cols):
                out_ref[:, j, start : start + BAND, :] = got[:, j * width : (j + 1) * width].reshape(
                    channels, BAND, width
                )


def shifted(tile, step):
    lane = lax.broadcasted_iota(jnp.int32, tile.shape, 1)
    width = tile.shape[1]
    rolled = pltpu.roll(tile.astype(F32), step % width, 1)
    gone = 0 if step == 1 else width - 1
    return jnp.where(lane == gone, 0.0, rolled).astype(BF16)


def main_body(
    layer, x_ref, left_ref, right_ref, lowy_ref, highy_ref, s0_ref, s1_ref, s2_ref, tgt_ref, lo_ref, hi_ref, bias_ref, me_ref, acc_ref, side_ref
):
    channels, rows, cols, depth, width = x_ref.shape
    span = channels * BAND
    bands = depth // BAND
    out_channel = lax.broadcasted_iota(jnp.int32, (span, 1), 0) // BAND
    bias = jnp.zeros((span, 1), F32)
    for o in range(channels):
        bias = jnp.where(out_channel == o, bias_ref[layer, o], bias)
    src_refs = (s0_ref, s1_ref, s2_ref)

    def three(read, size):
        lanes = []
        for step in (1, 0, -1):
            tiles = [read(j).reshape(channels * size, width) for j in range(cols)]
            if step:
                tiles = [shifted(t, step) for t in tiles]
            lanes.append(jnp.concatenate(tiles, axis=1))
        return lanes

    def halo(ref, flag, i):
        value = jnp.concatenate(three(lambda j: ref[:, i, j], EDGE), axis=0)
        return jnp.where(flag != 0, value, jnp.zeros_like(value))

    for i in range(rows):
        for q in range(bands):
            for n, value in enumerate(three(lambda j: x_ref[:, i, j, q * BAND : (q + 1) * BAND, :], BAND)):
                side_ref[q, n] = value
        low_y = halo(lowy_ref, me_ref[0], i)
        high_y = halo(highy_ref, me_ref[1], i)
        for q in range(bands):
            total = jnp.broadcast_to(bias, (span, cols * width))
            for a in range(3):
                if 0 <= i + a - 1 < rows:
                    tiles = source_rows(x_ref, left_ref, right_ref, i + a - 1, q * BAND, BAND)
                    total = total + dot(src_refs[a][...], src_operand(tiles, cols))
            total = total + dot(tgt_ref[...], side_ref[q].reshape(3 * span, cols * width))

            def near(band, start):
                parts = [
                    side_ref[band, n].reshape(channels, BAND, cols * width)[:, start : start + EDGE].reshape(
                        channels * EDGE, cols * width
                    )
                    for n in range(3)
                ]
                return jnp.concatenate(parts, axis=0)

            total = total + dot(lo_ref[...], low_y if q == 0 else near(q - 1, BAND - EDGE))
            total = total + dot(hi_ref[...], high_y if q == bands - 1 else near(q + 1, 0))
            for j in range(cols):
                acc_ref[:, i, j, q * BAND : (q + 1) * BAND, :] = total[:, j * width : (j + 1) * width].reshape(
                    channels, BAND, width
                )


def finish_body(last, x_ref, acc_ref, fromlow_ref, fromhigh_ref, out_ref, *more):
    channels, rows, cols, depth, width = x_ref.shape
    for i in range(rows):
        for j in range(cols):
            total = acc_ref[:, i, j]
            if i == 0:
                total = total + fromlow_ref[:, j].astype(F32)
            if i == rows - 1:
                total = total + fromhigh_ref[:, j].astype(F32)
            value = (x_ref[:, i, j].astype(F32) + jnp.maximum(total, 0.0)).astype(BF16)
            out_ref[:, i, j] = value
            if not last:
                first_ref, final_ref, top_ref, bottom_ref = more
                if j == 0:
                    first_ref[:, i] = value
                if j == cols - 1:
                    final_ref[:, i] = value
                top_ref[:, i, j] = value[:, :EDGE]
                bottom_ref[:, i, j] = value[:, depth - EDGE :]


def open_body(x_ref, *refs):
    out_ref, first_ref, final_ref, top_ref, bottom_ref, sems = refs
    cols, depth = x_ref.shape[2:4]
    pairs = (
        (x_ref.at[:, :, 0], first_ref),
        (x_ref.at[:, :, cols - 1], final_ref),
        (x_ref.at[:, :, :, :EDGE], top_ref),
        (x_ref.at[:, :, :, depth - EDGE :], bottom_ref),
        (x_ref, out_ref),
    )
    copies = [pltpu.make_async_copy(a, b, sems.at[n]) for n, (a, b) in enumerate(pairs)]
    for copy in copies:
        copy.start()
    for copy in copies:
        copy.wait()


def beside(block_up, block_down, axis):
    count = lax.axis_size(axis)
    forward = [(i, i + 1) for i in range(count - 1)]
    backward = [(i + 1, i) for i in range(count - 1)]
    return lax.ppermute(block_up, axis, forward), lax.ppermute(block_down, axis, backward)


def target_halo(top, bottom, me):
    axis = "trow"
    if lax.axis_size(axis) != 2:
        return beside(bottom, top, axis)
    got = lax.ppermute(jnp.where(me == 0, bottom, top), axis, [(0, 1), (1, 0)])
    return got, got


def shards(volume, src_weight, tgt_weight, bias):
    layers = src_weight.shape[0]
    channels, rows, cols, depth, width = volume.shape
    me = lax.axis_index("trow")
    flags = jnp.stack([me > 0, me < lax.axis_size("trow") - 1]).astype(jnp.int32)
    src_w = jnp.transpose(src_weight, (0, 2, 3, 1))
    tgt_w = jnp.transpose(tgt_weight, (0, 2, 3, 1))
    full = VMEM(volume.shape, BF16)
    sides = [VMEM((channels, rows, depth, width), BF16)] * 2 + [VMEM((channels, rows, cols, EDGE, width), BF16)] * 2
    row = VMEM((channels, cols, depth, width), BF16)
    size = channels * rows * cols * depth * width
    state, *edges = call(open_body, [full] + sides, (volume,), {0: pl.ANY}, scratch=[pltpu.SemaphoreType.DMA((5,))], moved=size * 4)
    made = build([("src", 0, 0), ("src", 0, 2)], src_w, tgt_w, state)
    for layer in range(layers):
        first, final, top, bottom = edges
        left, right = beside(final, first, "scol")
        low_y, high_y = target_halo(top, bottom, me)
        down, up = call(
            edge_body,
            [row, row],
            (state, left, right, made["src", layer, 0], made["src", layer, 2]),
            flops=2 * size // rows * 2 * 3 * channels * BAND,
            moved=size * 2,
        )
        from_low, from_high = beside(down, up, "srow")
        if layer == 0:
            rest = [("src", 0, 1), ("tgt", 0, 0), ("near", 0, 0), ("near", 0, 2)]
            for n in range(1, layers):
                rest += [("src", n, 0), ("src", n, 2), ("src", n, 1), ("tgt", n, 0), ("near", n, 0), ("near", n, 2)]
            made |= build(rest, src_w, tgt_w, up)
        ops = [made["src", layer, a] for a in range(3)]
        ops += [made["tgt", layer, 0], made["near", layer, 0], made["near", layer, 2]]
        (acc,) = call(
            functools.partial(main_body, layer),
            [VMEM(volume.shape, F32)],
            (state, left, right, low_y, high_y, *ops, bias, flags),
            {11: SMEM, 12: SMEM},
            scratch=[VMEM((depth // BAND, 3, channels * BAND, cols * width), BF16)],
            flops=2 * size * 12 * channels * BAND,
            moved=size * 8,
        )
        last = layer == layers - 1
        outs = [jax.ShapeDtypeStruct(volume.shape, BF16)] if last else [full] + sides
        state, *edges = call(
            functools.partial(finish_body, last), outs, (state, acc, from_low, from_high), flops=size, moved=size * 10
        )
    return state


def solution(mesh):
    return jax.shard_map(
        shards,
        mesh=mesh,
        in_specs=(P(None, "srow", "scol", "trow", None), P(), P(), P()),
        out_specs=P(None, "srow", "scol", "trow", None),
        check_vma=False,
    )
```

```python
import functools

import jax
import jax.numpy as jnp
from jax import lax
from jax.experimental import pallas as pl
from jax.experimental.pallas import tpu as pltpu
from jax.sharding import PartitionSpec as P

BAND = 32
EDGE = 16
SCOPED = 16 * 1024 * 1024
F32 = jnp.float32
BF16 = jnp.bfloat16
VMEM, SMEM, HBM = pltpu.VMEM, pltpu.SMEM, pltpu.HBM
ROW_ODD, COL_ODD, DEEP_ODD, HAS_LOW, HAS_HIGH = range(5)


def call(body, outs, args, places=None, out_place=VMEM, scratch=(), flops=0, moved=0):
    places = places or {}
    spaces = [places.get(n, VMEM) for n in range(len(args))]
    held = [pltpu.with_memory_space_constraint(a, m) if m in (VMEM, HBM) else a for a, m in zip(args, spaces)]
    return pl.pallas_call(
        body,
        out_shape=tuple(outs),
        in_specs=[pl.BlockSpec(memory_space=m) for m in spaces],
        out_specs=tuple(pl.BlockSpec(memory_space=out_place) for _ in outs),
        scratch_shapes=list(scratch),
        compiler_params=pltpu.CompilerParams(vmem_limit_bytes=SCOPED),
        cost_estimate=pl.CostEstimate(flops=flops, bytes_accessed=moved, transcendentals=0),
    )(*held)


def dot(a, b):
    return jnp.dot(a, b, preferred_element_type=F32)


def operators(parts, src_w_ref, tgt_w_ref, out_refs):
    channels = src_w_ref.shape[1]
    span, small = channels * BAND, channels * EDGE

    def columns(size):
        pick_c = lax.broadcasted_iota(jnp.int32, (channels, channels * size), 1) // size
        pick_r = lax.broadcasted_iota(jnp.int32, (channels, channels * size), 0)
        return (pick_c == pick_r).astype(BF16)

    wide, narrow = columns(BAND), columns(EDGE)
    row = lax.broadcasted_iota(jnp.int32, (BAND, span), 0)
    shift = row - lax.broadcasted_iota(jnp.int32, (BAND, span), 1) % BAND
    row_s = lax.broadcasted_iota(jnp.int32, (BAND, small), 0)
    col_s = lax.broadcasted_iota(jnp.int32, (BAND, small), 1) % EDGE
    at_low = (row_s == 0) & (col_s == EDGE - 1)
    at_high = (row_s == BAND - 1) & (col_s == 0)
    spread = {}

    def taps(ref, layer, o, pick, key):
        key = (key, layer, o)
        if key not in spread:
            spread[key] = lax.dot_general(ref[layer, o], pick, (((0,), (0,)), ((), ())), preferred_element_type=F32)
        return spread[key]

    for (kind, layer, first), out_ref in zip(parts, out_refs):
        for o in range(channels):
            rows = slice(o * BAND, (o + 1) * BAND)
            for b in range(3):
                if kind == "src":
                    got = taps(src_w_ref, layer, o, wide, "s")
                    value = jnp.where(shift == 0, got[3 * first + b][None, :], 0.0)
                elif kind == "tgt":
                    got = taps(tgt_w_ref, layer, o, wide, "t")
                    value = jnp.where(shift == 1, got[b][None, :], 0.0)
                    value = jnp.where(shift == 0, got[3 + b][None, :], value)
                    value = jnp.where(shift == -1, got[6 + b][None, :], value)
                else:
                    got = taps(tgt_w_ref, layer, o, narrow, "n")
                    value = jnp.where(at_low if first == 0 else at_high, got[3 * first + b][None, :], 0.0)
                size = value.shape[1]
                out_ref[rows, b * size : (b + 1) * size] = value.astype(BF16)


def operator_shapes(parts, channels):
    span, small = channels * BAND, channels * EDGE
    return [VMEM((span, 3 * (small if kind == "near" else span)), BF16) for kind, _, _ in parts]


def build_body(parts, src_w_ref, tgt_w_ref, after_ref, *out_refs):
    operators(parts, src_w_ref, tgt_w_ref, out_refs)


def build(parts, src_w, tgt_w, after):
    got = call(
        functools.partial(build_body, parts),
        operator_shapes(parts, src_w.shape[1]),
        (src_w, tgt_w, after),
        {2: pl.ANY},
        flops=len(parts) * 10**7,
        moved=10**6,
    )
    return dict(zip(parts, got))


def band(tile):
    channels, size, width = tile.shape
    return tile.reshape(channels * size, width)


def unband(tile, channels):
    return tile.reshape(channels, tile.shape[0] // channels, tile.shape[1])


def src_operand(tiles, cols):
    return jnp.concatenate([jnp.concatenate(tiles[b : b + cols], axis=1) for b in range(3)], axis=0)


def sides(odd, a, b):
    return jnp.where(odd, a, b), jnp.where(odd, b, a)


def inner_sums(x_ref, odd, first_ref, last_ref, a_ref, b_ref):
    channels, rows, cols, depth, width = x_ref.shape
    for start in range(0, depth, BAND):
        cut = slice(start, start + BAND)
        down, up = (
            dot(w_ref[...], src_operand([band(x_ref[:, i, j, cut]) for j in range(cols)], cols - 2)).astype(BF16)
            for i, w_ref in ((rows - 1, first_ref), (0, last_ref))
        )
        for out_ref, got in ((a_ref, jnp.where(odd, up, down)), (b_ref, jnp.where(odd, down, up))):
            for j in range(cols - 2):
                out_ref[:, j, cut] = unband(got[:, j * width : (j + 1) * width], channels)


def edge_body(x_ref, cola_ref, colb_ref, first_ref, last_ref, flag_ref, a_ref, b_ref):
    channels, rows, cols, depth, width = x_ref.shape
    odd, odd_col = flag_ref[ROW_ODD] != 0, flag_ref[COL_ODD] != 0
    for start in range(0, depth, BAND):
        cut = slice(start, start + BAND)
        sums = []
        for i, w_ref in ((rows - 1, first_ref), (0, last_ref)):
            left, right = sides(odd_col, band(cola_ref[:, i, cut]), band(colb_ref[:, i, cut]))
            near = [left] + [band(x_ref[:, i, j, cut]) for j in range(2)]
            far = [band(x_ref[:, i, j, cut]) for j in range(cols - 2, cols)] + [right]
            operand = jnp.concatenate([jnp.concatenate(pair, axis=1) for pair in zip(near, far)], axis=0)
            sums.append(dot(w_ref[...], operand).astype(BF16))
        down, up = sums
        for out_ref, got in ((a_ref, jnp.where(odd, up, down)), (b_ref, jnp.where(odd, down, up))):
            for n in range(2):
                out_ref[:, n, cut] = unband(got[:, n * width : (n + 1) * width], channels)


def shifted(tile, step):
    lane = lax.broadcasted_iota(jnp.int32, tile.shape, 1)
    width = tile.shape[1]
    rolled = pltpu.roll(tile.astype(F32), step % width, 1)
    gone = 0 if step == 1 else width - 1
    return jnp.where(lane == gone, 0.0, rolled).astype(BF16)


def main_body(
    layer, x_ref, cola_ref, colb_ref, deepa_ref, deepb_ref, s0_ref, s1_ref, s2_ref, tgt_ref, lo_ref, hi_ref, bias_ref, flag_ref, acc_ref, side_ref
):
    channels, rows, cols, depth, width = x_ref.shape
    span = channels * BAND
    bands = depth // BAND
    out_channel = lax.broadcasted_iota(jnp.int32, (span, 1), 0) // BAND
    bias = jnp.zeros((span, 1), F32)
    for o in range(channels):
        bias = jnp.where(out_channel == o, bias_ref[layer, o], bias)
    src_refs = (s0_ref, s1_ref, s2_ref)
    odd_col, odd_deep = flag_ref[COL_ODD] != 0, flag_ref[DEEP_ODD] != 0

    def three(tiles):
        lanes = []
        for step in (1, 0, -1):
            lanes.append(jnp.concatenate([shifted(t, step) if step else t for t in tiles], axis=1))
        return lanes

    def halo(tiles, flag):
        value = jnp.concatenate(three(tiles), axis=0)
        return jnp.where(flag_ref[flag] != 0, value, jnp.zeros_like(value))

    for i in range(rows):
        for q in range(bands):
            cut = slice(q * BAND, (q + 1) * BAND)
            for n, value in enumerate(three([band(x_ref[:, i, j, cut]) for j in range(cols)])):
                side_ref[q, n] = value
        both = [sides(odd_deep, band(deepa_ref[:, i, j]), band(deepb_ref[:, i, j])) for j in range(cols)]
        low_y = halo([b[0] for b in both], HAS_LOW)
        high_y = halo([b[1] for b in both], HAS_HIGH)
        for q in range(bands):
            cut = slice(q * BAND, (q + 1) * BAND)
            total = jnp.broadcast_to(bias, (span, cols * width))
            for a in range(3):
                r = i + a - 1
                if 0 <= r < rows:
                    left, right = sides(odd_col, band(cola_ref[:, r, cut]), band(colb_ref[:, r, cut]))
                    tiles = [left] + [band(x_ref[:, r, j, cut]) for j in range(cols)] + [right]
                    total = total + dot(src_refs[a][...], src_operand(tiles, cols))
            total = total + dot(tgt_ref[...], side_ref[q].reshape(3 * span, cols * width))

            def near(other, start):
                parts = [unband(side_ref[other, n], channels)[:, start : start + EDGE] for n in range(3)]
                return jnp.concatenate([band(p) for p in parts], axis=0)

            total = total + dot(lo_ref[...], low_y if q == 0 else near(q - 1, BAND - EDGE))
            total = total + dot(hi_ref[...], high_y if q == bands - 1 else near(q + 1, 0))
            for j in range(cols):
                acc_ref[:, i, j, cut] = unband(total[:, j * width : (j + 1) * width], channels)


def row_values(x_ref, acc_ref, odd, inner, outer, i, j):
    rows, cols = x_ref.shape[1:3]
    if j in (0, cols - 1):
        (a_ref, b_ref), n = outer, 0 if j == 0 else 1
    else:
        (a_ref, b_ref), n = inner, j - 1
    total = acc_ref[:, i, j]
    low, high = sides(odd, a_ref[:, n], b_ref[:, n])
    if i == 0:
        total = total + low.astype(F32)
    if i == rows - 1:
        total = total + high.astype(F32)
    return (x_ref[:, i, j].astype(F32) + jnp.maximum(total, 0.0)).astype(BF16)


def next_body(
    x_ref, acc_ref, ina_ref, inb_ref, outa_ref, outb_ref, first_ref, last_ref, flag_ref, out_ref, cola_ref, colb_ref, deepa_ref, deepb_ref, a_ref, b_ref
):
    channels, rows, cols, depth, width = x_ref.shape
    odd, odd_col, odd_deep = (flag_ref[n] != 0 for n in (ROW_ODD, COL_ODD, DEEP_ODD))
    for i in range(rows):
        kept = {}
        for j in range(cols):
            value = row_values(x_ref, acc_ref, odd, (ina_ref, inb_ref), (outa_ref, outb_ref), i, j)
            out_ref[:, i, j] = value
            if j in (0, cols - 1):
                kept[j] = value
            top, bottom = value[:, :EDGE], value[:, depth - EDGE :]
            deepa_ref[:, i, j] = jnp.where(odd_deep, top, bottom)
            deepb_ref[:, i, j] = jnp.where(odd_deep, bottom, top)
        cola_ref[:, i] = jnp.where(odd_col, kept[0], kept[cols - 1])
        colb_ref[:, i] = jnp.where(odd_col, kept[cols - 1], kept[0])
    inner_sums(out_ref, odd, first_ref, last_ref, a_ref, b_ref)


def last_body(x_ref, acc_ref, ina_ref, inb_ref, outa_ref, outb_ref, flag_ref, out_ref, hold_ref, sems):
    rows, cols = x_ref.shape[1:3]
    odd = flag_ref[ROW_ODD] != 0
    copies = []
    for i in range(rows):
        for j in range(cols):
            hold_ref[:, i, j] = row_values(x_ref, acc_ref, odd, (ina_ref, inb_ref), (outa_ref, outb_ref), i, j)
            copies.append(pltpu.make_async_copy(hold_ref.at[:, i, j], out_ref.at[:, i, j], sems.at[i, j]))
            copies[-1].start()
    for copy in copies:
        copy.wait()


def open_body(
    parts, x_ref, src_w_ref, tgt_w_ref, flag_ref, out_ref, cola_ref, colb_ref, deepa_ref, deepb_ref, a_ref, b_ref, *rest
):
    *op_refs, src_ref, tgt_ref, sems = rest
    cols, depth = x_ref.shape[2:4]
    odd, odd_col, odd_deep = (flag_ref[n] for n in (ROW_ODD, COL_ODD, DEEP_ODD))
    edge_a, edge_b = (cols - 1) * (1 - odd_col), (cols - 1) * odd_col
    deep_a = pl.multiple_of((depth - EDGE) * (1 - odd_deep), EDGE)
    deep_b = pl.multiple_of((depth - EDGE) * odd_deep, EDGE)
    pairs = (
        (src_w_ref, src_ref),
        (x_ref, out_ref),
        (x_ref.at[:, :, edge_a], cola_ref),
        (x_ref.at[:, :, edge_b], colb_ref),
        (x_ref.at[:, :, :, pl.ds(deep_a, EDGE)], deepa_ref),
        (x_ref.at[:, :, :, pl.ds(deep_b, EDGE)], deepb_ref),
    )
    copies = [pltpu.make_async_copy(a, b, sems.at[n]) for n, (a, b) in enumerate(pairs)]
    for copy in copies:
        copy.start()
    copies[0].wait()
    operators(parts, src_ref, tgt_ref, op_refs)
    copies[1].wait()
    inner_sums(out_ref, odd != 0, op_refs[0], op_refs[1], a_ref, b_ref)
    for copy in copies[2:]:
        copy.wait()


def swaps(a, b, axis):
    count = lax.axis_size(axis)
    pairs = [[(n, n + 1), (n + 1, n)] for n in range(count - 1)]
    got_a = lax.ppermute(a, axis, sum(pairs[0::2], []))
    got_b = lax.ppermute(b, axis, sum(pairs[1::2], [])) if count > 2 else jnp.zeros_like(b)
    return got_a, got_b


def shards(volume, src_weight, tgt_weight, bias):
    layers = src_weight.shape[0]
    channels, rows, cols, depth, width = volume.shape
    row, col, deep = (lax.axis_index(n) for n in ("srow", "scol", "trow"))
    deep_count = lax.axis_size("trow")
    flags = jnp.stack([row % 2, col % 2, deep % 2, deep > 0, deep < deep_count - 1]).astype(jnp.int32)
    src_w = jnp.transpose(src_weight, (0, 2, 3, 1))
    tgt_w = jnp.transpose(tgt_weight, (0, 2, 3, 1))
    full = VMEM(volume.shape, BF16)
    sent = [VMEM((channels, rows, depth, width), BF16)] * 2 + [VMEM((channels, rows, cols, EDGE, width), BF16)] * 2
    sent += [VMEM((channels, cols - 2, depth, width), BF16)] * 2
    size = channels * rows * cols * depth * width
    inner_flops = 2 * size // rows * 3 * channels * BAND
    early = [("src", 0, 0), ("src", 0, 2)]
    state, *edges, op_a, op_b = call(
        functools.partial(open_body, early),
        [full] + sent + operator_shapes(early, channels),
        (volume, src_w, tgt_w, flags),
        {0: HBM, 1: HBM, 2: HBM, 3: SMEM},
        scratch=[VMEM(src_w.shape, BF16), VMEM(tgt_w.shape, BF16), pltpu.SemaphoreType.DMA((6,))],
        flops=inner_flops,
        moved=size * 4,
    )
    made = dict(zip(early, (op_a, op_b)))
    for layer in range(layers):
        col_a, col_b, deep_a, deep_b, sum_a, sum_b = edges
        inner = swaps(sum_a, sum_b, "srow")
        beside = swaps(col_a, col_b, "scol")
        if deep_count == 2:
            deeper = (lax.ppermute(deep_a, "trow", [(0, 1), (1, 0)]),) * 2
        else:
            deeper = swaps(deep_a, deep_b, "trow")
        pair = VMEM((channels, 2, depth, width), BF16)
        owed = call(
            edge_body,
            [pair, pair],
            (state, *beside, made["src", layer, 0], made["src", layer, 2], flags),
            {5: SMEM},
            flops=inner_flops,
            moved=size * 2,
        )
        outer = swaps(*owed, "srow")
        if layer == 0:
            rest = [("src", 0, 1), ("tgt", 0, 0), ("near", 0, 0), ("near", 0, 2)]
            for n in range(1, layers):
                rest += [("src", n, 0), ("src", n, 2), ("src", n, 1), ("tgt", n, 0), ("near", n, 0), ("near", n, 2)]
            made |= build(rest, src_w, tgt_w, owed[0])
        ops = [made["src", layer, a] for a in range(3)]
        ops += [made["tgt", layer, 0], made["near", layer, 0], made["near", layer, 2]]
        (acc,) = call(
            functools.partial(main_body, layer),
            [VMEM(volume.shape, F32)],
            (state, *beside, *deeper, *ops, bias, flags),
            {11: SMEM, 12: SMEM},
            scratch=[VMEM((depth // BAND, 3, channels * BAND, cols * width), BF16)],
            flops=2 * size * 12 * channels * BAND,
            moved=size * 8,
        )
        if layer < layers - 1:
            state, *edges = call(
                next_body,
                [full] + sent,
                (state, acc, *inner, *outer, made["src", layer + 1, 0], made["src", layer + 1, 2], flags),
                {8: SMEM},
                flops=inner_flops,
                moved=size * 10,
            )
        else:
            (state,) = call(
                last_body,
                [jax.ShapeDtypeStruct(volume.shape, BF16)],
                (state, acc, *inner, *outer, flags),
                {6: SMEM},
                out_place=HBM,
                scratch=[VMEM(volume.shape, BF16), pltpu.SemaphoreType.DMA((rows, cols))],
                flops=size,
                moved=size * 10,
            )
    return state


def solution(mesh):
    return jax.shard_map(
        shards,
        mesh=mesh,
        in_specs=(P(None, "srow", "scol", "trow", None), P(), P(), P()),
        out_specs=P(None, "srow", "scol", "trow", None),
        check_vma=False,
    )
```

```python
import functools

import jax
import jax.numpy as jnp
from jax import lax
from jax.experimental import pallas as pl
from jax.experimental.pallas import tpu as pltpu
from jax.sharding import PartitionSpec as P

BAND = 32
EDGE = 16
SCOPED = 16 * 1024 * 1024
F32 = jnp.float32
BF16 = jnp.bfloat16
VMEM, SMEM, HBM = pltpu.VMEM, pltpu.SMEM, pltpu.HBM
ROW_ODD, COL_ODD, DEEP_ODD, ROW_PAIRED, COL_PAIRED, HAS_LOW, HAS_HIGH = range(7)


def call(body, outs, args, places=None, out_place=VMEM, scratch=(), flops=0, moved=0):
    places = places or {}
    spaces = [places.get(n, VMEM) for n in range(len(args))]
    held = [pltpu.with_memory_space_constraint(a, m) if m in (VMEM, HBM) else a for a, m in zip(args, spaces)]
    return pl.pallas_call(
        body,
        out_shape=tuple(outs),
        in_specs=[pl.BlockSpec(memory_space=m) for m in spaces],
        out_specs=tuple(pl.BlockSpec(memory_space=out_place) for _ in outs),
        scratch_shapes=list(scratch),
        compiler_params=pltpu.CompilerParams(vmem_limit_bytes=SCOPED),
        cost_estimate=pl.CostEstimate(flops=flops, bytes_accessed=moved, transcendentals=0),
    )(*held)


def dot(a, b):
    return jnp.dot(a, b, preferred_element_type=F32)


def operators(parts, src_w_ref, tgt_w_ref, out_refs):
    channels = src_w_ref.shape[1]
    span, small = channels * BAND, channels * EDGE

    def columns(size):
        pick_c = lax.broadcasted_iota(jnp.int32, (channels, channels * size), 1) // size
        pick_r = lax.broadcasted_iota(jnp.int32, (channels, channels * size), 0)
        return (pick_c == pick_r).astype(BF16)

    wide, narrow = columns(BAND), columns(EDGE)
    row = lax.broadcasted_iota(jnp.int32, (BAND, span), 0)
    shift = row - lax.broadcasted_iota(jnp.int32, (BAND, span), 1) % BAND
    row_s = lax.broadcasted_iota(jnp.int32, (BAND, small), 0)
    col_s = lax.broadcasted_iota(jnp.int32, (BAND, small), 1) % EDGE
    at_low = (row_s == 0) & (col_s == EDGE - 1)
    at_high = (row_s == BAND - 1) & (col_s == 0)
    spread = {}

    def taps(ref, layer, o, pick, key):
        key = (key, layer, o)
        if key not in spread:
            spread[key] = lax.dot_general(ref[layer, o], pick, (((0,), (0,)), ((), ())), preferred_element_type=F32)
        return spread[key]

    for (kind, layer, first), out_ref in zip(parts, out_refs):
        for o in range(channels):
            rows = slice(o * BAND, (o + 1) * BAND)
            for b in range(3):
                if kind == "src":
                    got = taps(src_w_ref, layer, o, wide, "s")
                    value = jnp.where(shift == 0, got[3 * first + b][None, :], 0.0)
                elif kind == "tgt":
                    got = taps(tgt_w_ref, layer, o, wide, "t")
                    value = jnp.where(shift == 1, got[b][None, :], 0.0)
                    value = jnp.where(shift == 0, got[3 + b][None, :], value)
                    value = jnp.where(shift == -1, got[6 + b][None, :], value)
                else:
                    got = taps(tgt_w_ref, layer, o, narrow, "n")
                    value = jnp.where(at_low if first == 0 else at_high, got[3 * first + b][None, :], 0.0)
                size = value.shape[1]
                out_ref[rows, b * size : (b + 1) * size] = value.astype(BF16)


def operator_shapes(parts, channels):
    span, small = channels * BAND, channels * EDGE
    return [VMEM((span, 3 * (small if kind == "near" else span)), BF16) for kind, _, _ in parts]


def build_body(parts, src_w_ref, tgt_w_ref, after_ref, *out_refs):
    operators(parts, src_w_ref, tgt_w_ref, out_refs)


def build(parts, src_w, tgt_w, after):
    got = call(
        functools.partial(build_body, parts),
        operator_shapes(parts, src_w.shape[1]),
        (src_w, tgt_w, after),
        {2: pl.ANY},
        flops=len(parts) * 10**7,
        moved=10**6,
    )
    return dict(zip(parts, got))


def band(tile):
    channels, size, width = tile.shape
    return tile.reshape(channels * size, width)


def unband(tile, channels):
    return tile.reshape(channels, tile.shape[0] // channels, tile.shape[1])


def src_operand(tiles, cols):
    return jnp.concatenate([jnp.concatenate(tiles[b : b + cols], axis=1) for b in range(3)], axis=0)


def sides(odd, paired, a, b):
    if paired is not True:
        b = jnp.where(paired, b, jnp.zeros_like(b))
    return jnp.where(odd, a, b), jnp.where(odd, b, a)


def inner_sums(x_ref, odd, first_ref, last_ref, a_ref, b_ref):
    channels, rows, cols, depth, width = x_ref.shape
    for start in range(0, depth, BAND):
        cut = slice(start, start + BAND)
        down, up = (
            dot(w_ref[...], src_operand([band(x_ref[:, i, j, cut]) for j in range(cols)], cols - 2)).astype(BF16)
            for i, w_ref in ((rows - 1, first_ref), (0, last_ref))
        )
        for out_ref, got in ((a_ref, jnp.where(odd, up, down)), (b_ref, jnp.where(odd, down, up))):
            for j in range(cols - 2):
                out_ref[:, j, cut] = unband(got[:, j * width : (j + 1) * width], channels)


def edge_body(x_ref, cola_ref, colb_ref, first_ref, last_ref, flag_ref, a_ref, b_ref):
    channels, rows, cols, depth, width = x_ref.shape
    odd, *col = (flag_ref[n] != 0 for n in (ROW_ODD, COL_ODD, COL_PAIRED))
    for start in range(0, depth, BAND):
        cut = slice(start, start + BAND)
        sums = []
        for i, w_ref in ((rows - 1, first_ref), (0, last_ref)):
            left, right = sides(*col, band(cola_ref[:, i, cut]), band(colb_ref[:, i, cut]))
            near = [left] + [band(x_ref[:, i, j, cut]) for j in range(2)]
            far = [band(x_ref[:, i, j, cut]) for j in range(cols - 2, cols)] + [right]
            operand = jnp.concatenate([jnp.concatenate(pair, axis=1) for pair in zip(near, far)], axis=0)
            sums.append(dot(w_ref[...], operand).astype(BF16))
        down, up = sums
        for out_ref, got in ((a_ref, jnp.where(odd, up, down)), (b_ref, jnp.where(odd, down, up))):
            for n in range(2):
                out_ref[:, n, cut] = unband(got[:, n * width : (n + 1) * width], channels)


def shifted(tile, step):
    lane = lax.broadcasted_iota(jnp.int32, tile.shape, 1)
    width = tile.shape[1]
    rolled = pltpu.roll(tile.astype(F32), step % width, 1)
    gone = 0 if step == 1 else width - 1
    return jnp.where(lane == gone, 0.0, rolled).astype(BF16)


def main_body(
    layer, x_ref, cola_ref, colb_ref, deepa_ref, deepb_ref, s0_ref, s1_ref, s2_ref, tgt_ref, lo_ref, hi_ref, bias_ref, flag_ref, acc_ref, side_ref
):
    channels, rows, cols, depth, width = x_ref.shape
    span = channels * BAND
    bands = depth // BAND
    out_channel = lax.broadcasted_iota(jnp.int32, (span, 1), 0) // BAND
    bias = jnp.zeros((span, 1), F32)
    for o in range(channels):
        bias = jnp.where(out_channel == o, bias_ref[layer, o], bias)
    src_refs = (s0_ref, s1_ref, s2_ref)
    odd_deep, *col = (flag_ref[n] != 0 for n in (DEEP_ODD, COL_ODD, COL_PAIRED))

    def three(tiles):
        lanes = []
        for step in (1, 0, -1):
            lanes.append(jnp.concatenate([shifted(t, step) if step else t for t in tiles], axis=1))
        return lanes

    def halo(tiles, flag):
        value = jnp.concatenate(three(tiles), axis=0)
        return jnp.where(flag_ref[flag] != 0, value, jnp.zeros_like(value))

    for i in range(rows):
        for q in range(bands):
            cut = slice(q * BAND, (q + 1) * BAND)
            for n, value in enumerate(three([band(x_ref[:, i, j, cut]) for j in range(cols)])):
                side_ref[q, n] = value
        both = [sides(odd_deep, True, band(deepa_ref[:, i, j]), band(deepb_ref[:, i, j])) for j in range(cols)]
        low_y = halo([b[0] for b in both], HAS_LOW)
        high_y = halo([b[1] for b in both], HAS_HIGH)
        for q in range(bands):
            cut = slice(q * BAND, (q + 1) * BAND)
            total = jnp.broadcast_to(bias, (span, cols * width))
            for a in range(3):
                r = i + a - 1
                if 0 <= r < rows:
                    left, right = sides(*col, band(cola_ref[:, r, cut]), band(colb_ref[:, r, cut]))
                    tiles = [left] + [band(x_ref[:, r, j, cut]) for j in range(cols)] + [right]
                    total = total + dot(src_refs[a][...], src_operand(tiles, cols))
            total = total + dot(tgt_ref[...], side_ref[q].reshape(3 * span, cols * width))

            def near(other, start):
                parts = [unband(side_ref[other, n], channels)[:, start : start + EDGE] for n in range(3)]
                return jnp.concatenate([band(p) for p in parts], axis=0)

            total = total + dot(lo_ref[...], low_y if q == 0 else near(q - 1, BAND - EDGE))
            total = total + dot(hi_ref[...], high_y if q == bands - 1 else near(q + 1, 0))
            for j in range(cols):
                acc_ref[:, i, j, cut] = unband(total[:, j * width : (j + 1) * width], channels)


def row_values(x_ref, acc_ref, row, inner, outer, i, j):
    rows, cols = x_ref.shape[1:3]
    if j in (0, cols - 1):
        (a_ref, b_ref), n = outer, 0 if j == 0 else 1
    else:
        (a_ref, b_ref), n = inner, j - 1
    total = acc_ref[:, i, j]
    low, high = sides(*row, a_ref[:, n], b_ref[:, n])
    if i == 0:
        total = total + low.astype(F32)
    if i == rows - 1:
        total = total + high.astype(F32)
    return (x_ref[:, i, j].astype(F32) + jnp.maximum(total, 0.0)).astype(BF16)


def next_body(
    x_ref, acc_ref, ina_ref, inb_ref, outa_ref, outb_ref, first_ref, last_ref, flag_ref, out_ref, cola_ref, colb_ref, deepa_ref, deepb_ref, a_ref, b_ref
):
    channels, rows, cols, depth, width = x_ref.shape
    odd, paired, odd_col, odd_deep = (flag_ref[n] != 0 for n in (ROW_ODD, ROW_PAIRED, COL_ODD, DEEP_ODD))
    for i in range(rows):
        kept = {}
        for j in range(cols):
            value = row_values(x_ref, acc_ref, (odd, paired), (ina_ref, inb_ref), (outa_ref, outb_ref), i, j)
            out_ref[:, i, j] = value
            if j in (0, cols - 1):
                kept[j] = value
            top, bottom = value[:, :EDGE], value[:, depth - EDGE :]
            deepa_ref[:, i, j] = jnp.where(odd_deep, top, bottom)
            deepb_ref[:, i, j] = jnp.where(odd_deep, bottom, top)
        cola_ref[:, i] = jnp.where(odd_col, kept[0], kept[cols - 1])
        colb_ref[:, i] = jnp.where(odd_col, kept[cols - 1], kept[0])
    inner_sums(out_ref, odd, first_ref, last_ref, a_ref, b_ref)


def last_body(x_ref, acc_ref, ina_ref, inb_ref, outa_ref, outb_ref, flag_ref, out_ref, hold_ref, sems):
    rows, cols = x_ref.shape[1:3]
    row = [flag_ref[n] != 0 for n in (ROW_ODD, ROW_PAIRED)]
    copies = []
    for i in range(rows):
        for j in range(cols):
            hold_ref[:, i, j] = row_values(x_ref, acc_ref, row, (ina_ref, inb_ref), (outa_ref, outb_ref), i, j)
            copies.append(pltpu.make_async_copy(hold_ref.at[:, i, j], out_ref.at[:, i, j], sems.at[i, j]))
            copies[-1].start()
    for copy in copies:
        copy.wait()


def open_body(
    parts, x_ref, src_w_ref, tgt_w_ref, flag_ref, out_ref, cola_ref, colb_ref, deepa_ref, deepb_ref, a_ref, b_ref, *rest
):
    *op_refs, src_ref, tgt_ref, sems = rest
    cols, depth = x_ref.shape[2:4]
    odd, odd_col, odd_deep = (flag_ref[n] for n in (ROW_ODD, COL_ODD, DEEP_ODD))
    edge_a, edge_b = (cols - 1) * (1 - odd_col), (cols - 1) * odd_col
    deep_a = pl.multiple_of((depth - EDGE) * (1 - odd_deep), EDGE)
    deep_b = pl.multiple_of((depth - EDGE) * odd_deep, EDGE)
    pairs = (
        (src_w_ref, src_ref),
        (x_ref, out_ref),
        (x_ref.at[:, :, edge_a], cola_ref),
        (x_ref.at[:, :, edge_b], colb_ref),
        (x_ref.at[:, :, :, pl.ds(deep_a, EDGE)], deepa_ref),
        (x_ref.at[:, :, :, pl.ds(deep_b, EDGE)], deepb_ref),
    )
    copies = [pltpu.make_async_copy(a, b, sems.at[n]) for n, (a, b) in enumerate(pairs)]
    for copy in copies:
        copy.start()
    copies[0].wait()
    operators(parts, src_ref, tgt_ref, op_refs)
    copies[1].wait()
    inner_sums(out_ref, odd != 0, op_refs[0], op_refs[1], a_ref, b_ref)
    for copy in copies[2:]:
        copy.wait()


def swaps(a, b, axis):
    count = lax.axis_size(axis)

    def swap(value, first):
        pairs = {n: n for n in range(count)}
        for n in range(first, count - 1, 2):
            pairs[n], pairs[n + 1] = n + 1, n
        return lax.ppermute(value, axis, list(pairs.items()))

    return swap(a, 0), swap(b, 1)


def shards(volume, src_weight, tgt_weight, bias):
    layers = src_weight.shape[0]
    channels, rows, cols, depth, width = volume.shape
    row, col, deep = (lax.axis_index(n) for n in ("srow", "scol", "trow"))
    deep_count = lax.axis_size("trow")
    for axis in ("srow", "scol"):
        assert lax.axis_size(axis) % 2 == 0
    paired = [(n > 0) & (n < lax.axis_size(axis) - 1) for n, axis in ((row, "srow"), (col, "scol"))]
    flags = jnp.stack([row % 2, col % 2, deep % 2, *paired, deep > 0, deep < deep_count - 1]).astype(jnp.int32)
    src_w = jnp.transpose(src_weight, (0, 2, 3, 1))
    tgt_w = jnp.transpose(tgt_weight, (0, 2, 3, 1))
    full = VMEM(volume.shape, BF16)
    sent = [VMEM((channels, rows, depth, width), BF16)] * 2 + [VMEM((channels, rows, cols, EDGE, width), BF16)] * 2
    sent += [VMEM((channels, cols - 2, depth, width), BF16)] * 2
    size = channels * rows * cols * depth * width
    inner_flops = 2 * size // rows * 3 * channels * BAND
    early = [("src", 0, 0), ("src", 0, 2)]
    state, *edges, op_a, op_b = call(
        functools.partial(open_body, early),
        [full] + sent + operator_shapes(early, channels),
        (volume, src_w, tgt_w, flags),
        {0: HBM, 1: HBM, 2: HBM, 3: SMEM},
        scratch=[VMEM(src_w.shape, BF16), VMEM(tgt_w.shape, BF16), pltpu.SemaphoreType.DMA((6,))],
        flops=inner_flops,
        moved=size * 4,
    )
    made = dict(zip(early, (op_a, op_b)))
    for layer in range(layers):
        col_a, col_b, deep_a, deep_b, sum_a, sum_b = edges
        inner = swaps(sum_a, sum_b, "srow")
        beside = swaps(col_a, col_b, "scol")
        if deep_count == 2:
            deeper = (lax.ppermute(deep_a, "trow", [(0, 1), (1, 0)]),) * 2
        else:
            deeper = swaps(deep_a, deep_b, "trow")
        pair = VMEM((channels, 2, depth, width), BF16)
        owed = call(
            edge_body,
            [pair, pair],
            (state, *beside, made["src", layer, 0], made["src", layer, 2], flags),
            {5: SMEM},
            flops=inner_flops,
            moved=size * 2,
        )
        outer = swaps(*owed, "srow")
        if layer == 0:
            rest = [("src", 0, 1), ("tgt", 0, 0), ("near", 0, 0), ("near", 0, 2)]
            for n in range(1, layers):
                rest += [("src", n, 0), ("src", n, 2), ("src", n, 1), ("tgt", n, 0), ("near", n, 0), ("near", n, 2)]
            made |= build(rest, src_w, tgt_w, owed[0])
        ops = [made["src", layer, a] for a in range(3)]
        ops += [made["tgt", layer, 0], made["near", layer, 0], made["near", layer, 2]]
        (acc,) = call(
            functools.partial(main_body, layer),
            [VMEM(volume.shape, F32)],
            (state, *beside, *deeper, *ops, bias, flags),
            {11: SMEM, 12: SMEM},
            scratch=[VMEM((depth // BAND, 3, channels * BAND, cols * width), BF16)],
            flops=2 * size * 12 * channels * BAND,
            moved=size * 8,
        )
        if layer < layers - 1:
            state, *edges = call(
                next_body,
                [full] + sent,
                (state, acc, *inner, *outer, made["src", layer + 1, 0], made["src", layer + 1, 2], flags),
                {8: SMEM},
                flops=inner_flops,
                moved=size * 10,
            )
        else:
            (state,) = call(
                last_body,
                [jax.ShapeDtypeStruct(volume.shape, BF16)],
                (state, acc, *inner, *outer, flags),
                {6: SMEM},
                out_place=HBM,
                scratch=[VMEM(volume.shape, BF16), pltpu.SemaphoreType.DMA((rows, cols))],
                flops=size,
                moved=size * 10,
            )
    return state


def solution(mesh):
    return jax.shard_map(
        shards,
        mesh=mesh,
        in_specs=(P(None, "srow", "scol", "trow", None), P(), P(), P()),
        out_specs=P(None, "srow", "scol", "trow", None),
        check_vma=False,
    )
```

```python
import functools

import jax
import jax.numpy as jnp
from jax import lax
from jax.experimental import pallas as pl
from jax.experimental.pallas import tpu as pltpu
from jax.sharding import PartitionSpec as P

BAND = 32
EDGE = 16
SCOPED = 16 * 1024 * 1024
F32 = jnp.float32
BF16 = jnp.bfloat16
VMEM, SMEM, HBM = pltpu.VMEM, pltpu.SMEM, pltpu.HBM
ROW_ODD, COL_ODD, DEEP_ODD, ROW_PAIRED, COL_PAIRED, HAS_LOW, HAS_HIGH = range(7)


def call(body, outs, args, places=None, out_place=VMEM, scratch=(), flops=0, moved=0):
    places = places or {}
    spaces = [places.get(n, VMEM) for n in range(len(args))]
    held = [pltpu.with_memory_space_constraint(a, m) if m in (VMEM, HBM) else a for a, m in zip(args, spaces)]
    return pl.pallas_call(
        body,
        out_shape=tuple(outs),
        in_specs=[pl.BlockSpec(memory_space=m) for m in spaces],
        out_specs=tuple(pl.BlockSpec(memory_space=out_place) for _ in outs),
        scratch_shapes=list(scratch),
        compiler_params=pltpu.CompilerParams(vmem_limit_bytes=SCOPED),
        cost_estimate=pl.CostEstimate(flops=flops, bytes_accessed=moved, transcendentals=0),
    )(*held)


def dot(a, b):
    return jnp.dot(a, b, preferred_element_type=F32)


def operators(parts, src_w_ref, tgt_w_ref, out_refs):
    channels = src_w_ref.shape[1]
    span, small = channels * BAND, channels * EDGE

    def columns(size):
        pick_c = lax.broadcasted_iota(jnp.int32, (channels, channels * size), 1) // size
        pick_r = lax.broadcasted_iota(jnp.int32, (channels, channels * size), 0)
        return (pick_c == pick_r).astype(BF16)

    wide, narrow = columns(BAND), columns(EDGE)
    row = lax.broadcasted_iota(jnp.int32, (BAND, span), 0)
    shift = row - lax.broadcasted_iota(jnp.int32, (BAND, span), 1) % BAND
    row_s = lax.broadcasted_iota(jnp.int32, (BAND, small), 0)
    col_s = lax.broadcasted_iota(jnp.int32, (BAND, small), 1) % EDGE
    at_low = (row_s == 0) & (col_s == EDGE - 1)
    at_high = (row_s == BAND - 1) & (col_s == 0)
    spread = {}

    def taps(ref, layer, o, pick, key):
        key = (key, layer, o)
        if key not in spread:
            spread[key] = lax.dot_general(ref[layer, o], pick, (((0,), (0,)), ((), ())), preferred_element_type=F32)
        return spread[key]

    for (kind, layer, first), out_ref in zip(parts, out_refs):
        for o in range(channels):
            rows = slice(o * BAND, (o + 1) * BAND)
            for b in range(3):
                if kind == "src":
                    got = taps(src_w_ref, layer, o, wide, "s")
                    value = jnp.where(shift == 0, got[3 * first + b][None, :], 0.0)
                elif kind == "tgt":
                    got = taps(tgt_w_ref, layer, o, wide, "t")
                    value = jnp.where(shift == 1, got[b][None, :], 0.0)
                    value = jnp.where(shift == 0, got[3 + b][None, :], value)
                    value = jnp.where(shift == -1, got[6 + b][None, :], value)
                else:
                    got = taps(tgt_w_ref, layer, o, narrow, "n")
                    value = jnp.where(at_low if first == 0 else at_high, got[3 * first + b][None, :], 0.0)
                size = value.shape[1]
                out_ref[rows, b * size : (b + 1) * size] = value.astype(BF16)


def operator_shapes(parts, channels):
    span, small = channels * BAND, channels * EDGE
    return [VMEM((span, 3 * (small if kind == "near" else span)), BF16) for kind, _, _ in parts]


def build_body(parts, src_w_ref, tgt_w_ref, after_ref, *out_refs):
    operators(parts, src_w_ref, tgt_w_ref, out_refs)


def build(parts, src_w, tgt_w, after):
    got = call(
        functools.partial(build_body, parts),
        operator_shapes(parts, src_w.shape[1]),
        (src_w, tgt_w, after),
        {2: pl.ANY},
        flops=len(parts) * 10**7,
        moved=10**6,
    )
    return dict(zip(parts, got))


def band(tile):
    channels, size, width = tile.shape
    return tile.reshape(channels * size, width)


def unband(tile, channels):
    return tile.reshape(channels, tile.shape[0] // channels, tile.shape[1])


def src_operand(tiles, cols):
    return jnp.concatenate([jnp.concatenate(tiles[b : b + cols], axis=1) for b in range(3)], axis=0)


def sides(odd, paired, a, b):
    if paired is not True:
        b = jnp.where(paired, b, jnp.zeros_like(b))
    return jnp.where(odd, a, b), jnp.where(odd, b, a)


def inner_sums(x_ref, odd, first_ref, last_ref, a_ref, b_ref):
    channels, rows, cols, depth, width = x_ref.shape
    for start in range(0, depth, BAND):
        cut = slice(start, start + BAND)
        down, up = (
            dot(w_ref[...], src_operand([band(x_ref[:, i, j, cut]) for j in range(cols)], cols - 2)).astype(BF16)
            for i, w_ref in ((rows - 1, first_ref), (0, last_ref))
        )
        for out_ref, got in ((a_ref, jnp.where(odd, up, down)), (b_ref, jnp.where(odd, down, up))):
            for j in range(cols - 2):
                out_ref[:, j, cut] = unband(got[:, j * width : (j + 1) * width], channels)


def edge_body(x_ref, cola_ref, colb_ref, first_ref, last_ref, flag_ref, a_ref, b_ref):
    channels, rows, cols, depth, width = x_ref.shape
    odd, *col = (flag_ref[n] != 0 for n in (ROW_ODD, COL_ODD, COL_PAIRED))
    for start in range(0, depth, BAND):
        cut = slice(start, start + BAND)
        sums = []
        for i, w_ref in ((rows - 1, first_ref), (0, last_ref)):
            left, right = sides(*col, band(cola_ref[:, i, cut]), band(colb_ref[:, i, cut]))
            near = [left] + [band(x_ref[:, i, j, cut]) for j in range(2)]
            far = [band(x_ref[:, i, j, cut]) for j in range(cols - 2, cols)] + [right]
            operand = jnp.concatenate([jnp.concatenate(pair, axis=1) for pair in zip(near, far)], axis=0)
            sums.append(dot(w_ref[...], operand).astype(BF16))
        down, up = sums
        for out_ref, got in ((a_ref, jnp.where(odd, up, down)), (b_ref, jnp.where(odd, down, up))):
            for n in range(2):
                out_ref[:, n, cut] = unband(got[:, n * width : (n + 1) * width], channels)


def shifted(tile, step):
    lane = lax.broadcasted_iota(jnp.int32, tile.shape, 1)
    width = tile.shape[1]
    rolled = pltpu.roll(tile.astype(F32), step % width, 1)
    gone = 0 if step == 1 else width - 1
    return jnp.where(lane == gone, 0.0, rolled).astype(BF16)


def main_body(
    layer, x_ref, cola_ref, colb_ref, deepa_ref, deepb_ref, s0_ref, s1_ref, s2_ref, tgt_ref, lo_ref, hi_ref, bias_ref, flag_ref, acc_ref, side_ref
):
    channels, rows, cols, depth, width = x_ref.shape
    span = channels * BAND
    bands = depth // BAND
    out_channel = lax.broadcasted_iota(jnp.int32, (span, 1), 0) // BAND
    bias = jnp.zeros((span, 1), F32)
    for o in range(channels):
        bias = jnp.where(out_channel == o, bias_ref[layer, o], bias)
    src_refs = (s0_ref, s1_ref, s2_ref)
    odd_deep, *col = (flag_ref[n] != 0 for n in (DEEP_ODD, COL_ODD, COL_PAIRED))

    def three(tiles):
        lanes = []
        for step in (1, 0, -1):
            lanes.append(jnp.concatenate([shifted(t, step) if step else t for t in tiles], axis=1))
        return lanes

    def halo(tiles, flag):
        value = jnp.concatenate(three(tiles), axis=0)
        return jnp.where(flag_ref[flag] != 0, value, jnp.zeros_like(value))

    for i in range(rows):
        for q in range(bands):
            cut = slice(q * BAND, (q + 1) * BAND)
            for n, value in enumerate(three([band(x_ref[:, i, j, cut]) for j in range(cols)])):
                side_ref[q, n] = value
        both = [sides(odd_deep, True, band(deepa_ref[:, i, j]), band(deepb_ref[:, i, j])) for j in range(cols)]
        low_y = halo([b[0] for b in both], HAS_LOW)
        high_y = halo([b[1] for b in both], HAS_HIGH)
        for q in range(bands):
            cut = slice(q * BAND, (q + 1) * BAND)
            total = jnp.broadcast_to(bias, (span, cols * width))
            for a in range(3):
                r = i + a - 1
                if 0 <= r < rows:
                    left, right = sides(*col, band(cola_ref[:, r, cut]), band(colb_ref[:, r, cut]))
                    tiles = [left] + [band(x_ref[:, r, j, cut]) for j in range(cols)] + [right]
                    total = total + dot(src_refs[a][...], src_operand(tiles, cols))
            total = total + dot(tgt_ref[...], side_ref[q].reshape(3 * span, cols * width))

            def near(other, start):
                parts = [unband(side_ref[other, n], channels)[:, start : start + EDGE] for n in range(3)]
                return jnp.concatenate([band(p) for p in parts], axis=0)

            total = total + dot(lo_ref[...], low_y if q == 0 else near(q - 1, BAND - EDGE))
            total = total + dot(hi_ref[...], high_y if q == bands - 1 else near(q + 1, 0))
            for j in range(cols):
                acc_ref[:, i, j, cut] = unband(total[:, j * width : (j + 1) * width], channels)


def row_values(x_ref, acc_ref, row, inner, outer, i, j):
    rows, cols = x_ref.shape[1:3]
    if j in (0, cols - 1):
        (a_ref, b_ref), n = outer, 0 if j == 0 else 1
    else:
        (a_ref, b_ref), n = inner, j - 1
    total = acc_ref[:, i, j]
    low, high = sides(*row, a_ref[:, n], b_ref[:, n])
    if i == 0:
        total = total + low.astype(F32)
    if i == rows - 1:
        total = total + high.astype(F32)
    return (x_ref[:, i, j].astype(F32) + jnp.maximum(total, 0.0)).astype(BF16)


def next_body(
    x_ref, acc_ref, ina_ref, inb_ref, outa_ref, outb_ref, first_ref, last_ref, flag_ref, out_ref, cola_ref, colb_ref, deepa_ref, deepb_ref, a_ref, b_ref
):
    channels, rows, cols, depth, width = x_ref.shape
    odd, paired, odd_col, odd_deep = (flag_ref[n] != 0 for n in (ROW_ODD, ROW_PAIRED, COL_ODD, DEEP_ODD))
    for i in range(rows):
        kept = {}
        for j in range(cols):
            value = row_values(x_ref, acc_ref, (odd, paired), (ina_ref, inb_ref), (outa_ref, outb_ref), i, j)
            out_ref[:, i, j] = value
            if j in (0, cols - 1):
                kept[j] = value
            top, bottom = value[:, :EDGE], value[:, depth - EDGE :]
            deepa_ref[:, i, j] = jnp.where(odd_deep, top, bottom)
            deepb_ref[:, i, j] = jnp.where(odd_deep, bottom, top)
        cola_ref[:, i] = jnp.where(odd_col, kept[0], kept[cols - 1])
        colb_ref[:, i] = jnp.where(odd_col, kept[cols - 1], kept[0])
    inner_sums(out_ref, odd, first_ref, last_ref, a_ref, b_ref)


def last_body(x_ref, acc_ref, ina_ref, inb_ref, outa_ref, outb_ref, flag_ref, out_ref, hold_ref, sems):
    rows, cols = x_ref.shape[1:3]
    row = [flag_ref[n] != 0 for n in (ROW_ODD, ROW_PAIRED)]
    copies = []
    for i in range(rows):
        for j in range(cols):
            hold_ref[:, i, j] = row_values(x_ref, acc_ref, row, (ina_ref, inb_ref), (outa_ref, outb_ref), i, j)
            copies.append(pltpu.make_async_copy(hold_ref.at[:, i, j], out_ref.at[:, i, j], sems.at[i, j]))
            copies[-1].start()
    for copy in copies:
        copy.wait()


def open_body(
    parts, x_ref, src_w_ref, tgt_w_ref, flag_ref, out_ref, cola_ref, colb_ref, deepa_ref, deepb_ref, a_ref, b_ref, *rest
):
    *op_refs, src_ref, tgt_ref, sems = rest
    cols, depth = x_ref.shape[2:4]
    odd, odd_col, odd_deep = (flag_ref[n] for n in (ROW_ODD, COL_ODD, DEEP_ODD))
    edge_a, edge_b = (cols - 1) * (1 - odd_col), (cols - 1) * odd_col
    deep_a = pl.multiple_of((depth - EDGE) * (1 - odd_deep), EDGE)
    deep_b = pl.multiple_of((depth - EDGE) * odd_deep, EDGE)
    pairs = (
        (src_w_ref, src_ref),
        (x_ref, out_ref),
        (x_ref.at[:, :, edge_a], cola_ref),
        (x_ref.at[:, :, edge_b], colb_ref),
        (x_ref.at[:, :, :, pl.ds(deep_a, EDGE)], deepa_ref),
        (x_ref.at[:, :, :, pl.ds(deep_b, EDGE)], deepb_ref),
    )
    copies = [pltpu.make_async_copy(a, b, sems.at[n]) for n, (a, b) in enumerate(pairs)]
    for copy in copies:
        copy.start()
    copies[0].wait()
    operators(parts, src_ref, tgt_ref, op_refs)
    copies[1].wait()
    inner_sums(out_ref, odd != 0, op_refs[0], op_refs[1], a_ref, b_ref)
    for copy in copies[2:]:
        copy.wait()


def swaps(a, b, axis, other):
    count, across = lax.axis_size(axis), lax.axis_size(other)
    pairs = []
    for n in range(count):
        for m in range(across):
            if 0 < n < count - 1:
                target = (n + 1 if n % 2 else n - 1, m)
            else:
                target = (n, m ^ 1)
            pairs.append((n * across + m, target[0] * across + target[1]))
    got_a = lax.ppermute(a, axis, [(n, n ^ 1) for n in range(count)])
    return got_a, lax.ppermute(b, (axis, other), pairs)


def shards(volume, src_weight, tgt_weight, bias):
    layers = src_weight.shape[0]
    channels, rows, cols, depth, width = volume.shape
    row, col, deep = (lax.axis_index(n) for n in ("srow", "scol", "trow"))
    deep_count = lax.axis_size("trow")
    for axis in ("srow", "scol", "trow"):
        assert lax.axis_size(axis) % 2 == 0
    paired = [(n > 0) & (n < lax.axis_size(axis) - 1) for n, axis in ((row, "srow"), (col, "scol"))]
    flags = jnp.stack([row % 2, col % 2, deep % 2, *paired, deep > 0, deep < deep_count - 1]).astype(jnp.int32)
    src_w = jnp.transpose(src_weight, (0, 2, 3, 1))
    tgt_w = jnp.transpose(tgt_weight, (0, 2, 3, 1))
    full = VMEM(volume.shape, BF16)
    sent = [VMEM((channels, rows, depth, width), BF16)] * 2 + [VMEM((channels, rows, cols, EDGE, width), BF16)] * 2
    sent += [VMEM((channels, cols - 2, depth, width), BF16)] * 2
    size = channels * rows * cols * depth * width
    inner_flops = 2 * size // rows * 3 * channels * BAND
    early = [("src", 0, 0), ("src", 0, 2)]
    state, *edges, op_a, op_b = call(
        functools.partial(open_body, early),
        [full] + sent + operator_shapes(early, channels),
        (volume, src_w, tgt_w, flags),
        {0: HBM, 1: HBM, 2: HBM, 3: SMEM},
        scratch=[VMEM(src_w.shape, BF16), VMEM(tgt_w.shape, BF16), pltpu.SemaphoreType.DMA((6,))],
        flops=inner_flops,
        moved=size * 4,
    )
    made = dict(zip(early, (op_a, op_b)))
    for layer in range(layers):
        col_a, col_b, deep_a, deep_b, sum_a, sum_b = edges
        inner = swaps(sum_a, sum_b, "srow", "scol")
        beside = swaps(col_a, col_b, "scol", "trow")
        if deep_count == 2:
            deeper = (lax.ppermute(deep_a, "trow", [(0, 1), (1, 0)]),) * 2
        else:
            deeper = swaps(deep_a, deep_b, "trow", "scol")
        pair = VMEM((channels, 2, depth, width), BF16)
        owed = call(
            edge_body,
            [pair, pair],
            (state, *beside, made["src", layer, 0], made["src", layer, 2], flags),
            {5: SMEM},
            flops=inner_flops,
            moved=size * 2,
        )
        outer = swaps(*owed, "srow", "scol")
        if layer == 0:
            rest = [("src", 0, 1), ("tgt", 0, 0), ("near", 0, 0), ("near", 0, 2)]
            for n in range(1, layers):
                rest += [("src", n, 0), ("src", n, 2), ("src", n, 1), ("tgt", n, 0), ("near", n, 0), ("near", n, 2)]
            made |= build(rest, src_w, tgt_w, owed[0])
        ops = [made["src", layer, a] for a in range(3)]
        ops += [made["tgt", layer, 0], made["near", layer, 0], made["near", layer, 2]]
        (acc,) = call(
            functools.partial(main_body, layer),
            [VMEM(volume.shape, F32)],
            (state, *beside, *deeper, *ops, bias, flags),
            {11: SMEM, 12: SMEM},
            scratch=[VMEM((depth // BAND, 3, channels * BAND, cols * width), BF16)],
            flops=2 * size * 12 * channels * BAND,
            moved=size * 8,
        )
        if layer < layers - 1:
            state, *edges = call(
                next_body,
                [full] + sent,
                (state, acc, *inner, *outer, made["src", layer + 1, 0], made["src", layer + 1, 2], flags),
                {8: SMEM},
                flops=inner_flops,
                moved=size * 10,
            )
        else:
            (state,) = call(
                last_body,
                [jax.ShapeDtypeStruct(volume.shape, BF16)],
                (state, acc, *inner, *outer, flags),
                {6: SMEM},
                out_place=HBM,
                scratch=[VMEM(volume.shape, BF16), pltpu.SemaphoreType.DMA((rows, cols))],
                flops=size,
                moved=size * 10,
            )
    return state


def solution(mesh):
    return jax.shard_map(
        shards,
        mesh=mesh,
        in_specs=(P(None, "srow", "scol", "trow", None), P(), P(), P()),
        out_specs=P(None, "srow", "scol", "trow", None),
        check_vma=False,
    )
```

```python
import functools

import jax
import jax.numpy as jnp
from jax import lax
from jax.experimental import pallas as pl
from jax.experimental.pallas import tpu as pltpu
from jax.sharding import PartitionSpec as P

BAND = 32
EDGE = 16
SCOPED = 16 * 1024 * 1024
F32 = jnp.float32
BF16 = jnp.bfloat16
VMEM, SMEM, HBM = pltpu.VMEM, pltpu.SMEM, pltpu.HBM
ROW_ODD, COL_ODD, DEEP_ODD, ROW_PAIRED, COL_PAIRED, DEEP_PAIRED = range(6)


def call(body, outs, args, places=None, out_place=VMEM, scratch=(), flops=0, moved=0):
    places = places or {}
    spaces = [places.get(n, VMEM) for n in range(len(args))]
    held = [pltpu.with_memory_space_constraint(a, m) if m in (VMEM, HBM) else a for a, m in zip(args, spaces)]
    return pl.pallas_call(
        body,
        out_shape=tuple(outs),
        in_specs=[pl.BlockSpec(memory_space=m) for m in spaces],
        out_specs=tuple(pl.BlockSpec(memory_space=out_place) for _ in outs),
        scratch_shapes=list(scratch),
        compiler_params=pltpu.CompilerParams(vmem_limit_bytes=SCOPED),
        cost_estimate=pl.CostEstimate(flops=flops, bytes_accessed=moved, transcendentals=0),
    )(*held)


def dot(a, b):
    return jnp.dot(a, b, preferred_element_type=F32)


def operators(parts, src_w_ref, tgt_w_ref, out_refs):
    channels = src_w_ref.shape[1]
    span, small = channels * BAND, channels * EDGE

    def columns(size):
        pick_c = lax.broadcasted_iota(jnp.int32, (channels, channels * size), 1) // size
        pick_r = lax.broadcasted_iota(jnp.int32, (channels, channels * size), 0)
        return (pick_c == pick_r).astype(BF16)

    wide, narrow, single = columns(BAND), columns(EDGE), columns(1)
    row = lax.broadcasted_iota(jnp.int32, (BAND, span), 0)
    shift = row - lax.broadcasted_iota(jnp.int32, (BAND, span), 1) % BAND
    row_s = lax.broadcasted_iota(jnp.int32, (BAND, small), 0)
    col_s = lax.broadcasted_iota(jnp.int32, (BAND, small), 1) % EDGE
    near = ((row_s == 0) & (col_s == EDGE - 1), (row_s == BAND - 1) & (col_s == 0))
    row_1 = lax.broadcasted_iota(jnp.int32, (BAND, channels), 0)
    deep = (row_1 == 0, row_1 == BAND - 1)
    spread = {}

    def taps(ref, layer, o, pick, key):
        key = (key, layer, o)
        if key not in spread:
            spread[key] = lax.dot_general(ref[layer, o], pick, (((0,), (0,)), ((), ())), preferred_element_type=F32)
        return spread[key]

    for (kind, layer), out_ref in zip(parts, out_refs):
        for o in range(channels):
            rows = slice(o * BAND, (o + 1) * BAND)
            for b in range(3):
                if kind == "middle":
                    got = taps(src_w_ref, layer, o, wide, "s")
                    values = {(): jnp.where(shift == 0, got[3 + b][None, :], 0.0)}
                elif kind == "beside":
                    got = taps(src_w_ref, layer, o, wide, "s")
                    values = {(n,): jnp.where(shift == 0, got[6 * n + b][None, :], 0.0) for n in range(2)}
                elif kind == "target":
                    got = taps(tgt_w_ref, layer, o, wide, "t")
                    value = jnp.where(shift == 1, got[b][None, :], 0.0)
                    value = jnp.where(shift == 0, got[3 + b][None, :], value)
                    values = {(): jnp.where(shift == -1, got[6 + b][None, :], value)}
                else:
                    pick, at = (narrow, near) if kind == "near" else (single, deep)
                    got = taps(tgt_w_ref, layer, o, pick, kind)
                    values = {(n,): jnp.where(at[n], got[6 * n + b][None, :], 0.0) for n in range(2)}
                for index, value in values.items():
                    size = value.shape[1]
                    out_ref[(*index, rows, slice(b * size, (b + 1) * size))] = value.astype(BF16)


def operator_shapes(parts, channels):
    span = channels * BAND
    widths = dict(middle=span, beside=span, target=span, near=channels * EDGE, deep=channels)
    lead = dict(middle=(), beside=(2,), target=(), near=(2,), deep=(2,))
    return [VMEM((*lead[kind], span, 3 * widths[kind]), BF16) for kind, _ in parts]


def build_body(parts, src_w_ref, tgt_w_ref, after_ref, *out_refs):
    operators(parts, src_w_ref, tgt_w_ref, out_refs)


def build(parts, src_w, tgt_w, after):
    got = call(
        functools.partial(build_body, parts),
        operator_shapes(parts, src_w.shape[1]),
        (src_w, tgt_w, after),
        {2: pl.ANY},
        flops=len(parts) * 10**7,
        moved=10**6,
    )
    return dict(zip(parts, got))


def band(tile):
    channels, size, width = tile.shape
    return tile.reshape(channels * size, width)


def unband(tile, channels):
    return tile.reshape(channels, tile.shape[0] // channels, tile.shape[1])


def src_operand(tiles, cols):
    return jnp.concatenate([jnp.concatenate(tiles[b : b + cols], axis=1) for b in range(3)], axis=0)


def sent_rows(flag_ref, rows):
    odd = flag_ref[ROW_ODD]
    return ((rows - 1) * (1 - odd), odd), ((rows - 1) * odd, 1 - odd)


def inner_sums(x_ref, flag_ref, beside_ref, out_refs):
    channels, rows, cols, depth, width = x_ref.shape
    for (i, side), out_ref in zip(sent_rows(flag_ref, rows), out_refs):
        for start in range(0, depth, BAND):
            cut = slice(start, start + BAND)
            operand = src_operand([band(x_ref[:, i, j, cut]) for j in range(cols)], cols - 2)
            got = dot(beside_ref[side], operand).astype(BF16)
            for j in range(cols - 2):
                out_ref[:, j, cut] = unband(got[:, j * width : (j + 1) * width], channels)


def edge_body(x_ref, cola_ref, colb_ref, beside_ref, flag_ref, a_ref, b_ref, side_ref):
    channels, rows, cols, depth, width = x_ref.shape
    odd = flag_ref[COL_ODD]
    side_ref[1 - odd] = cola_ref[...]

    @pl.when(flag_ref[COL_PAIRED] != 0)
    def _():
        side_ref[odd] = colb_ref[...]

    @pl.when(flag_ref[COL_PAIRED] == 0)
    def _():
        side_ref[odd] = jnp.zeros_like(colb_ref)

    for (i, side), out_ref in zip(sent_rows(flag_ref, rows), (a_ref, b_ref)):
        for start in range(0, depth, BAND):
            cut = slice(start, start + BAND)
            near = [band(side_ref[0, :, i, cut])] + [band(x_ref[:, i, j, cut]) for j in range(2)]
            far = [band(x_ref[:, i, j, cut]) for j in range(cols - 2, cols)] + [band(side_ref[1, :, i, cut])]
            operand = jnp.concatenate([jnp.concatenate(pair, axis=1) for pair in zip(near, far)], axis=0)
            got = dot(beside_ref[side], operand).astype(BF16)
            for n in range(2):
                out_ref[:, n, cut] = unband(got[:, n * width : (n + 1) * width], channels)


def shifted(tile, step):
    lane = lax.broadcasted_iota(jnp.int32, tile.shape, 1)
    width = tile.shape[1]
    rolled = pltpu.roll(tile.astype(F32), step % width, 1)
    gone = 0 if step == 1 else width - 1
    return jnp.where(lane == gone, 0.0, rolled)


def three(tiles):
    return [jnp.concatenate([shifted(t, step) if step else t.astype(F32) for t in tiles], axis=1) for step in (1, 0, -1)]


def main_body(
    layer, x_ref, side_ref, middle_ref, beside_ref, target_ref, near_ref, deep_ref, bias_ref, flag_ref, *rest
):
    *deep_halos, acc_ref, lane_ref = rest
    channels, rows, cols, depth, width = x_ref.shape
    span = channels * BAND
    bands = depth // BAND
    out_channel = lax.broadcasted_iota(jnp.int32, (span, 1), 0) // BAND
    bias = jnp.zeros((span, 1), F32)
    for o in range(channels):
        bias = jnp.where(out_channel == o, bias_ref[layer, o], bias)

    for i in range(rows):
        for q in range(bands):
            cut = slice(q * BAND, (q + 1) * BAND)
            tiles = [band(x_ref[:, i, j, cut]) for j in range(cols)]
            lane_ref[q, 1] = jnp.concatenate(tiles, axis=1)
            for n, step in ((0, 1), (2, -1)):
                lane_ref[q, n] = jnp.concatenate([shifted(t, step).astype(BF16) for t in tiles], axis=1)
        for q in range(bands):
            cut = slice(q * BAND, (q + 1) * BAND)
            total = jnp.broadcast_to(bias, (span, cols * width))
            for a in range(3):
                r = i + a - 1
                if 0 <= r < rows:
                    tiles = [band(side_ref[0, :, r, cut])] + [band(x_ref[:, r, j, cut]) for j in range(cols)]
                    tiles += [band(side_ref[1, :, r, cut])]
                    operator = middle_ref[...] if a == 1 else beside_ref[a // 2]
                    total = total + dot(operator, src_operand(tiles, cols))
            total = total + dot(target_ref[...], lane_ref[q].reshape(3 * span, cols * width))
            for side, other, start in ((0, q - 1, BAND - EDGE), (1, q + 1, 0)):
                if 0 <= other < bands:
                    parts = [unband(lane_ref[other, n], channels)[:, start : start + EDGE] for n in range(3)]
                    total = total + dot(near_ref[side], jnp.concatenate([band(p) for p in parts], axis=0))
            for j in range(cols):
                acc_ref[:, i, j, cut] = unband(total[:, j * width : (j + 1) * width], channels)
        odd = flag_ref[DEEP_ODD]
        for n, halo_ref in enumerate(deep_halos):
            side = (1 - odd) if n == 0 else odd
            cut = pl.ds(pl.multiple_of(side * (depth - BAND), BAND), BAND)
            halo = three([halo_ref[i, :, j * width : (j + 1) * width] for j in range(cols)])
            halo = jnp.concatenate(halo, axis=0)
            if n == 1:
                halo = halo * flag_ref[DEEP_PAIRED].astype(F32)
            got = dot(deep_ref[side], halo.astype(BF16))
            for j in range(cols):
                acc_ref[:, i, j, cut] += unband(got[:, j * width : (j + 1) * width], channels)


def finished(x_ref, acc_ref, flag_ref, inner, outer, store):
    rows, cols = x_ref.shape[1:3]
    odd = flag_ref[ROW_ODD]
    paired = flag_ref[ROW_PAIRED].astype(F32)
    for n, i in enumerate([(rows - 1) * (1 - odd), (rows - 1) * odd, *range(1, rows - 1)]):
        for j in range(cols):
            total = acc_ref[:, i, j]
            if n < 2:
                ref, at = (outer[n], 0 if j == 0 else 1) if j in (0, cols - 1) else (inner[n], j - 1)
                owed = ref[:, at].astype(F32)
                total = total + (owed if n == 0 else owed * paired)
            store(i, j, (x_ref[:, i, j].astype(F32) + jnp.maximum(total, 0.0)).astype(BF16))


def sent_columns(x_ref, flag_ref, col_refs):
    cols = x_ref.shape[2]
    odd = flag_ref[COL_ODD]
    for j, ref in zip(((cols - 1) * (1 - odd), (cols - 1) * odd), col_refs):
        ref[...] = x_ref[:, :, j]


def sent_depths(x_ref, flag_ref, deep_refs):
    channels, rows, cols, depth, _ = x_ref.shape
    odd = flag_ref[DEEP_ODD]
    shape = (channels, channels * BAND)
    first = lax.broadcasted_iota(jnp.int32, shape, 0) * BAND
    for n, ref in enumerate(deep_refs):
        end = (1 - odd) if n == 0 else odd
        cut = pl.ds(pl.multiple_of(end * (depth - BAND), BAND), BAND)
        pick = (lax.broadcasted_iota(jnp.int32, shape, 1) == first + end * (BAND - 1)).astype(BF16)
        for i in range(rows):
            tiles = [band(x_ref[:, i, j, cut]) for j in range(cols)]
            ref[i] = dot(pick, jnp.concatenate(tiles, axis=1)).astype(BF16)


def next_body(
    x_ref, acc_ref, ina_ref, inb_ref, outa_ref, outb_ref, beside_ref, flag_ref, out_ref, cola_ref, colb_ref, a_ref, b_ref, *deep_refs
):
    def store(i, j, value):
        out_ref[:, i, j] = value

    finished(x_ref, acc_ref, flag_ref, (ina_ref, inb_ref), (outa_ref, outb_ref), store)
    inner_sums(out_ref, flag_ref, beside_ref, (a_ref, b_ref))
    sent_columns(out_ref, flag_ref, (cola_ref, colb_ref))
    sent_depths(out_ref, flag_ref, deep_refs)


def last_body(x_ref, acc_ref, ina_ref, inb_ref, outa_ref, outb_ref, flag_ref, out_ref, hold_ref, sems):
    cols = x_ref.shape[2]
    copies = []

    def store(i, j, value):
        hold_ref[:, i, j] = value
        if j % 2 == 1 or j == cols - 1:
            cut = slice(j - j % 2, j + 1)
            copy = pltpu.make_async_copy(hold_ref.at[:, i, cut], out_ref.at[:, i, cut], sems.at[len(copies)])
            copy.start()
            copies.append(copy)

    finished(x_ref, acc_ref, flag_ref, (ina_ref, inb_ref), (outa_ref, outb_ref), store)
    for copy in copies:
        copy.wait()


def open_body(parts, x_ref, src_w_ref, tgt_w_ref, flag_ref, *rest):
    beside_ref, out_ref, cola_ref, colb_ref, a_ref, b_ref, *deep_refs, src_ref, sems = rest
    copies = [pltpu.make_async_copy(src_w_ref, src_ref, sems.at[0]), pltpu.make_async_copy(x_ref, out_ref, sems.at[1])]
    for copy in copies:
        copy.start()
    copies[0].wait()
    operators(parts, src_ref, None, (beside_ref,))
    copies[1].wait()
    inner_sums(out_ref, flag_ref, beside_ref, (a_ref, b_ref))
    sent_columns(out_ref, flag_ref, (cola_ref, colb_ref))
    sent_depths(out_ref, flag_ref, deep_refs)


def swaps(a, b, axis, other):
    count, across = lax.axis_size(axis), lax.axis_size(other)
    pairs = []
    for n in range(count):
        for m in range(across):
            if 0 < n < count - 1:
                target = (n + 1 if n % 2 else n - 1, m)
            else:
                target = (n, m ^ 1)
            pairs.append((n * across + m, target[0] * across + target[1]))
    got_a = lax.ppermute(a, axis, [(n, n ^ 1) for n in range(count)])
    return got_a, lax.ppermute(b, (axis, other), pairs)


def shards(volume, src_weight, tgt_weight, bias):
    layers = src_weight.shape[0]
    channels, rows, cols, depth, width = volume.shape
    axes = ("srow", "scol", "trow")
    at, counts = [lax.axis_index(n) for n in axes], [lax.axis_size(n) for n in axes]
    assert all(count % 2 == 0 for count in counts) and rows > 1 and cols > 2
    paired = [(n > 0) & (n < count - 1) for n, count in zip(at, counts)]
    flags = jnp.stack([n % 2 for n in at] + paired).astype(jnp.int32)
    src_w = jnp.transpose(src_weight, (0, 2, 3, 1))
    tgt_w = jnp.transpose(tgt_weight, (0, 2, 3, 1))
    full = VMEM(volume.shape, BF16)
    deep_swaps = 1 if counts[2] == 2 else 2
    sent = [full] + [VMEM((channels, rows, depth, width), BF16)] * 2 + [VMEM((channels, cols - 2, depth, width), BF16)] * 2
    sent += [VMEM((rows, channels, cols * width), BF16)] * deep_swaps
    size = channels * rows * cols * depth * width
    inner_flops = 2 * size // rows * 3 * channels * BAND
    early = [("beside", 0)]
    made = {}
    made[early[0]], state, col_a, col_b, sum_a, sum_b, *deep = call(
        functools.partial(open_body, early),
        operator_shapes(early, channels) + sent,
        (volume, src_w, tgt_w, flags),
        {0: HBM, 1: HBM, 2: HBM, 3: SMEM},
        scratch=[VMEM(src_w.shape, BF16), pltpu.SemaphoreType.DMA((2,))],
        flops=inner_flops,
        moved=size * 4,
    )
    rest = [(kind, n) for n in range(layers) for kind in ("middle", "beside", "target", "near", "deep")]
    made |= build([part for part in rest if part not in early], src_w, tgt_w, sum_a)
    for layer in range(layers):
        inner = swaps(sum_a, sum_b, "srow", "scol")
        beside = swaps(col_a, col_b, "scol", "trow")
        if deep_swaps == 1:
            deeper = [lax.ppermute(deep[0], "trow", [(0, 1), (1, 0)])]
        else:
            deeper = swaps(*deep, "trow", "scol")
        pair = VMEM((channels, 2, depth, width), BF16)
        *owed, side = call(
            edge_body,
            [pair, pair, VMEM((2, channels, rows, depth, width), BF16)],
            (state, *beside, made["beside", layer], flags),
            {4: SMEM},
            flops=inner_flops,
            moved=size * 2,
        )
        outer = swaps(*owed, "srow", "scol")
        ops = [made[kind, layer] for kind in ("middle", "beside", "target", "near", "deep")]
        (acc,) = call(
            functools.partial(main_body, layer),
            [VMEM(volume.shape, F32)],
            (state, side, *ops, bias, flags, *deeper),
            {7: SMEM, 8: SMEM},
            scratch=[VMEM((depth // BAND, 3, channels * BAND, cols * width), BF16)],
            flops=2 * size * 12 * channels * BAND,
            moved=size * 8,
        )
        if layer < layers - 1:
            state, col_a, col_b, sum_a, sum_b, *deep = call(
                next_body,
                sent,
                (state, acc, *inner, *outer, made["beside", layer + 1], flags),
                {7: SMEM},
                flops=inner_flops,
                moved=size * 10,
            )
        else:
            (state,) = call(
                last_body,
                [jax.ShapeDtypeStruct(volume.shape, BF16)],
                (state, acc, *inner, *outer, flags),
                {6: SMEM},
                out_place=HBM,
                scratch=[VMEM(volume.shape, BF16), pltpu.SemaphoreType.DMA((rows * cols,))],
                flops=size,
                moved=size * 10,
            )
    return state


def solution(mesh):
    return jax.shard_map(
        shards,
        mesh=mesh,
        in_specs=(P(None, "srow", "scol", "trow", None), P(), P(), P()),
        out_specs=P(None, "srow", "scol", "trow", None),
        check_vma=False,
    )
```

```python
import functools

import jax
import jax.numpy as jnp
from jax import lax
from jax.experimental import pallas as pl
from jax.experimental.pallas import tpu as pltpu
from jax.sharding import PartitionSpec as P

BAND = 32
EDGE = 16
SCOPED = 16 * 1024 * 1024
F32 = jnp.float32
BF16 = jnp.bfloat16
VMEM, SMEM, HBM = pltpu.VMEM, pltpu.SMEM, pltpu.HBM
ROW_ODD, COL_ODD, DEEP_ODD, ROW_PAIRED, COL_PAIRED, DEEP_PAIRED = range(6)


def call(body, outs, args, places=None, out_place=VMEM, scratch=(), flops=0, moved=0, aliases=None):
    places = places or {}
    spaces = [places.get(n, VMEM) for n in range(len(args))]
    held = [pltpu.with_memory_space_constraint(a, m) if m in (VMEM, HBM) else a for a, m in zip(args, spaces)]
    return pl.pallas_call(
        body,
        out_shape=tuple(outs),
        in_specs=[pl.BlockSpec(memory_space=m) for m in spaces],
        out_specs=tuple(pl.BlockSpec(memory_space=out_place) for _ in outs),
        scratch_shapes=list(scratch),
        input_output_aliases=aliases or {},
        compiler_params=pltpu.CompilerParams(vmem_limit_bytes=SCOPED),
        cost_estimate=pl.CostEstimate(flops=flops // 1000, bytes_accessed=moved // 1000, transcendentals=0),
    )(*held)


def dot(a, b):
    return jnp.dot(a, b, preferred_element_type=F32)


def operators(parts, src_w_ref, tgt_w_ref, out_refs):
    channels = src_w_ref.shape[1]
    span, small = channels * BAND, channels * EDGE

    def columns(size):
        pick_c = lax.broadcasted_iota(jnp.int32, (channels, channels * size), 1) // size
        pick_r = lax.broadcasted_iota(jnp.int32, (channels, channels * size), 0)
        return (pick_c == pick_r).astype(BF16)

    wide, narrow, single = columns(BAND), columns(EDGE), columns(1)
    row = lax.broadcasted_iota(jnp.int32, (BAND, span), 0)
    shift = row - lax.broadcasted_iota(jnp.int32, (BAND, span), 1) % BAND
    row_s = lax.broadcasted_iota(jnp.int32, (BAND, small), 0)
    col_s = lax.broadcasted_iota(jnp.int32, (BAND, small), 1) % EDGE
    near = ((row_s == 0) & (col_s == EDGE - 1), (row_s == BAND - 1) & (col_s == 0))
    row_1 = lax.broadcasted_iota(jnp.int32, (BAND, channels), 0)
    deep = (row_1 == 0, row_1 == BAND - 1)
    spread = {}

    def taps(ref, layer, o, pick, key):
        key = (key, layer, o)
        if key not in spread:
            spread[key] = lax.dot_general(ref[layer, o], pick, (((0,), (0,)), ((), ())), preferred_element_type=F32)
        return spread[key]

    for (kind, layer), out_ref in zip(parts, out_refs):
        for o in range(channels):
            rows = slice(o * BAND, (o + 1) * BAND)
            for b in range(3):
                if kind == "middle":
                    got = taps(src_w_ref, layer, o, wide, "s")
                    values = {(): jnp.where(shift == 0, got[3 + b][None, :], 0.0)}
                elif kind == "beside":
                    got = taps(src_w_ref, layer, o, wide, "s")
                    values = {(n,): jnp.where(shift == 0, got[6 * n + b][None, :], 0.0) for n in range(2)}
                elif kind == "target":
                    got = taps(tgt_w_ref, layer, o, wide, "t")
                    value = jnp.where(shift == 1, got[b][None, :], 0.0)
                    value = jnp.where(shift == 0, got[3 + b][None, :], value)
                    values = {(): jnp.where(shift == -1, got[6 + b][None, :], value)}
                else:
                    pick, at = (narrow, near) if kind == "near" else (single, deep)
                    got = taps(tgt_w_ref, layer, o, pick, kind)
                    values = {(n,): jnp.where(at[n], got[6 * n + b][None, :], 0.0) for n in range(2)}
                for index, value in values.items():
                    size = value.shape[1]
                    out_ref[(*index, rows, slice(b * size, (b + 1) * size))] = value.astype(BF16)


def operator_shapes(parts, channels):
    span = channels * BAND
    widths = dict(middle=span, beside=span, target=span, near=channels * EDGE, deep=channels)
    lead = dict(middle=(), beside=(2,), target=(), near=(2,), deep=(2,))
    return [VMEM((*lead[kind], span, 3 * widths[kind]), BF16) for kind, _ in parts]


def build_body(parts, src_w_ref, tgt_w_ref, after_ref, *out_refs):
    operators(parts, src_w_ref, tgt_w_ref, out_refs)


def build(parts, src_w, tgt_w, after):
    got = call(
        functools.partial(build_body, parts),
        operator_shapes(parts, src_w.shape[1]),
        (src_w, tgt_w, after),
        {2: pl.ANY},
        flops=len(parts) * 10**7,
        moved=10**6,
    )
    return dict(zip(parts, got))


def band(tile):
    channels, size, width = tile.shape
    return tile.reshape(channels * size, width)


def unband(tile, channels):
    return tile.reshape(channels, tile.shape[0] // channels, tile.shape[1])


def src_operand(tiles, cols):
    return jnp.concatenate([jnp.concatenate(tiles[b : b + cols], axis=1) for b in range(3)], axis=0)


def sent_rows(flag_ref, rows):
    odd = flag_ref[ROW_ODD]
    return ((rows - 1) * (1 - odd), odd), ((rows - 1) * odd, 1 - odd)


def column(mid_ref, rim_ref, i, j, cut):
    last = mid_ref.shape[2] + 1
    return band(rim_ref[:, i, j // last, cut] if j in (0, last) else mid_ref[:, i, j - 1, cut])


def bands_of(depth):
    return [slice(start, start + BAND) for start in range(0, depth, BAND)]


def owed_sums(operator, tiles, out_ref):
    channels, cols, depth, width = out_ref.shape
    cuts = bands_of(depth)
    operand = jnp.concatenate([jnp.concatenate([t for cut in cuts for t in tiles(cut, b)], axis=1) for b in range(3)], axis=0)
    got = dot(operator, operand).astype(BF16)
    for q, cut in enumerate(cuts):
        for j in range(cols):
            at = (q * cols + j) * width
            out_ref[:, j, cut] = unband(got[:, at : at + width], channels)


def inner_sums(mid_ref, rim_ref, flag_ref, beside_ref, out_refs):
    rows, cols = mid_ref.shape[1:3]
    for (i, side), out_ref in zip(sent_rows(flag_ref, rows), out_refs):
        owed_sums(
            beside_ref[side], lambda cut, b: [column(mid_ref, rim_ref, i, j + b, cut) for j in range(cols)], out_ref
        )


def edge_body(mid_ref, rim_ref, cola_ref, colb_ref, beside_ref, flag_ref, a_ref, b_ref, side_ref, *deep_refs):
    rows, cols = mid_ref.shape[1], mid_ref.shape[2] + 2
    odd = flag_ref[COL_ODD]
    side_ref[1 - odd] = cola_ref[...]

    @pl.when(flag_ref[COL_PAIRED] != 0)
    def _():
        side_ref[odd] = colb_ref[...]

    @pl.when(flag_ref[COL_PAIRED] == 0)
    def _():
        side_ref[odd] = jnp.zeros_like(colb_ref)

    def around(i, j, cut):
        if j in (-1, cols):
            return band(side_ref[0 if j < 0 else 1, :, i, cut])
        return column(mid_ref, rim_ref, i, j, cut)

    for (i, side), out_ref in zip(sent_rows(flag_ref, rows), (a_ref, b_ref)):
        owed_sums(beside_ref[side], lambda cut, b: [around(i, j + b - 1, cut) for j in (0, cols - 1)], out_ref)
    sent_depths(mid_ref, rim_ref, flag_ref, deep_refs)


def shifted(tile, step):
    lane = lax.broadcasted_iota(jnp.int32, tile.shape, 1)
    width = tile.shape[1]
    rolled = pltpu.roll(tile.astype(F32), step % width, 1)
    gone = 0 if step == 1 else width - 1
    return jnp.where(lane == gone, 0.0, rolled)


def three(tiles):
    return [jnp.concatenate([shifted(t, step) if step else t.astype(F32) for t in tiles], axis=1) for step in (1, 0, -1)]


def main_body(
    layer, mid_ref, rim_ref, side_ref, middle_ref, beside_ref, target_ref, near_ref, deep_ref, bias_ref, flag_ref, *rest
):
    *deep_halos, accmid_ref, accrim_ref, lane_ref = rest
    channels, rows, mids, depth, width = mid_ref.shape
    cols = mids + 2
    span = channels * BAND
    cuts = bands_of(depth)
    bands = len(cuts)
    out_channel = lax.broadcasted_iota(jnp.int32, (span, 1), 0) // BAND
    bias = jnp.zeros((span, 1), F32)
    for o in range(channels):
        bias = jnp.where(out_channel == o, bias_ref[layer, o], bias)

    def place(j):
        return (accrim_ref, j // (cols - 1)) if j in (0, cols - 1) else (accmid_ref, j - 1)

    for i in range(rows):
        for q, cut in enumerate(cuts):
            tiles = [column(mid_ref, rim_ref, i, j, cut) for j in range(cols)]
            lane_ref[q, 1] = jnp.concatenate(tiles, axis=1)
            for n, step in ((0, 1), (2, -1)):
                lane_ref[q, n] = jnp.concatenate([shifted(t, step).astype(BF16) for t in tiles], axis=1)
        for q, cut in enumerate(cuts):
            total = jnp.broadcast_to(bias, (span, cols * width))
            for a in range(3):
                r = i + a - 1
                if 0 <= r < rows:
                    tiles = [band(side_ref[0, :, r, cut])] + [column(mid_ref, rim_ref, r, j, cut) for j in range(cols)]
                    tiles += [band(side_ref[1, :, r, cut])]
                    operator = middle_ref[...] if a == 1 else beside_ref[a // 2]
                    total = total + dot(operator, src_operand(tiles, cols))
            total = total + dot(target_ref[...], lane_ref[q].reshape(3 * span, cols * width))
            for side, other, start in ((0, q - 1, BAND - EDGE), (1, q + 1, 0)):
                if 0 <= other < bands:
                    parts = [unband(lane_ref[other, n], channels)[:, start : start + EDGE] for n in range(3)]
                    total = total + dot(near_ref[side], jnp.concatenate([band(p) for p in parts], axis=0))
            for j in range(cols):
                acc_ref, at = place(j)
                acc_ref[:, i, at, cut] = unband(total[:, j * width : (j + 1) * width], channels)
        odd = flag_ref[DEEP_ODD]
        for n, halo_ref in enumerate(deep_halos):
            side = (1 - odd) if n == 0 else odd
            cut = pl.ds(pl.multiple_of(side * (depth - BAND), BAND), BAND)
            halo = three([halo_ref[i, :, j * width : (j + 1) * width] for j in range(cols)])
            halo = jnp.concatenate(halo, axis=0)
            if n == 1:
                halo = halo * flag_ref[DEEP_PAIRED].astype(F32)
            got = dot(deep_ref[side], halo.astype(BF16))
            for j in range(cols):
                acc_ref, at = place(j)
                acc_ref[:, i, at, cut] += unband(got[:, j * width : (j + 1) * width], channels)


def finished(x_ref, acc_ref, flag_ref, owed_refs, store):
    rows, cols = x_ref.shape[1:3]
    odd = flag_ref[ROW_ODD]
    paired = flag_ref[ROW_PAIRED].astype(F32)
    for n, i in enumerate([(rows - 1) * (1 - odd), (rows - 1) * odd, *range(1, rows - 1)]):
        for j in range(cols):
            total = acc_ref[:, i, j]
            if n < 2:
                owed = owed_refs[n][:, j].astype(F32)
                total = total + (owed if n == 0 else owed * paired)
            store(i, j, (x_ref[:, i, j].astype(F32) + jnp.maximum(total, 0.0)).astype(BF16))


def sent_columns(rim_ref, flag_ref, col_refs):
    odd = flag_ref[COL_ODD]
    for n, ref in zip((1 - odd, odd), col_refs):
        ref[...] = rim_ref[:, :, n]


def sent_depths(mid_ref, rim_ref, flag_ref, deep_refs):
    channels, rows, mids, depth, _ = mid_ref.shape
    odd = flag_ref[DEEP_ODD]
    shape = (channels, channels * BAND)
    first = lax.broadcasted_iota(jnp.int32, shape, 0) * BAND
    for n, ref in enumerate(deep_refs):
        end = (1 - odd) if n == 0 else odd
        cut = pl.ds(pl.multiple_of(end * (depth - BAND), BAND), BAND)
        pick = (lax.broadcasted_iota(jnp.int32, shape, 1) == first + end * (BAND - 1)).astype(BF16)
        for i in range(rows):
            tiles = [column(mid_ref, rim_ref, i, j, cut) for j in range(mids + 2)]
            ref[i] = dot(pick, jnp.concatenate(tiles, axis=1)).astype(BF16)


def mid_body(x_ref, acc_ref, a_ref, b_ref, flag_ref, out_ref):
    def store(i, j, value):
        out_ref[:, i, j] = value

    finished(x_ref, acc_ref, flag_ref, (a_ref, b_ref), store)


def next_body(mid_ref, rim_ref, acc_ref, outa_ref, outb_ref, beside_ref, flag_ref, out_ref, cola_ref, colb_ref, a_ref, b_ref):
    mid_body(rim_ref, acc_ref, outa_ref, outb_ref, flag_ref, out_ref)
    sent_columns(out_ref, flag_ref, (cola_ref, colb_ref))
    inner_sums(mid_ref, out_ref, flag_ref, beside_ref, (a_ref, b_ref))


def write_mid_body(x_ref, acc_ref, a_ref, b_ref, flag_ref, out_ref, hold_ref, sems):
    rows, mids = x_ref.shape[1:3]
    copies = []

    def store(i, j, value):
        hold_ref[:, i, j] = value
        if j == mids - 1:
            copies.append(pltpu.make_async_copy(hold_ref.at[:, i], out_ref.at[:, i, 1 : mids + 1], sems.at[len(copies)]))
            copies[-1].start()

    finished(x_ref, acc_ref, flag_ref, (a_ref, b_ref), store)
    for copy in copies:
        copy.wait()


def write_rim_body(x_ref, acc_ref, a_ref, b_ref, flag_ref, begun_ref, out_ref, hold_ref, sems):
    last = out_ref.shape[2] - 1
    copies = []

    def store(i, j, value):
        hold_ref[:, i, j] = value
        copies.append(pltpu.make_async_copy(hold_ref.at[:, i, j], out_ref.at[:, i, j * last], sems.at[len(copies)]))
        copies[-1].start()

    finished(x_ref, acc_ref, flag_ref, (a_ref, b_ref), store)
    for copy in copies:
        copy.wait()


def open_body(parts, x_ref, src_w_ref, flag_ref, *rest):
    beside_ref, mid_ref, rim_ref, cola_ref, colb_ref, a_ref, b_ref, src_ref, sems = rest
    last = x_ref.shape[2] - 1
    pairs = (
        (src_w_ref, src_ref),
        (x_ref.at[:, :, 0], rim_ref.at[:, :, 0]),
        (x_ref.at[:, :, last], rim_ref.at[:, :, 1]),
        (x_ref.at[:, :, 1:last], mid_ref),
    )
    copies = [pltpu.make_async_copy(a, b, sems.at[n]) for n, (a, b) in enumerate(pairs)]
    for copy in copies:
        copy.start()
    copies[0].wait()
    operators(parts, src_ref, None, (beside_ref,))
    for copy in copies[1:]:
        copy.wait()
    sent_columns(rim_ref, flag_ref, (cola_ref, colb_ref))
    inner_sums(mid_ref, rim_ref, flag_ref, beside_ref, (a_ref, b_ref))


def swaps(a, b, axis, other):
    count, across = lax.axis_size(axis), lax.axis_size(other)
    pairs = []
    for n in range(count):
        for m in range(across):
            if 0 < n < count - 1:
                target = (n + 1 if n % 2 else n - 1, m)
            else:
                target = (n, m ^ 1)
            pairs.append((n * across + m, target[0] * across + target[1]))
    got_a = lax.ppermute(a, axis, [(n, n ^ 1) for n in range(count)])
    return got_a, lax.ppermute(b, (axis, other), pairs)


def shards(volume, src_weight, tgt_weight, bias):
    layers = src_weight.shape[0]
    channels, rows, cols, depth, width = volume.shape
    axes = ("srow", "scol", "trow")
    at, counts = [lax.axis_index(n) for n in axes], [lax.axis_size(n) for n in axes]
    assert all(count % 2 == 0 for count in counts) and rows > 1 and cols > 2
    paired = [(n > 0) & (n < count - 1) for n, count in zip(at, counts)]
    flags = jnp.stack([n % 2 for n in at] + paired).astype(jnp.int32)
    src_w = jnp.transpose(src_weight, (0, 2, 3, 1))
    tgt_w = jnp.transpose(tgt_weight, (0, 2, 3, 1))
    deep_swaps = 1 if counts[2] == 2 else 2
    mid_shape, rim_shape = ((channels, rows, n, depth, width) for n in (cols - 2, 2))
    line = VMEM((channels, rows, depth, width), BF16)
    owed_mid, owed_rim = (VMEM((channels, n, depth, width), BF16) for n in (cols - 2, 2))
    size = channels * rows * cols * depth * width
    inner_flops = 2 * size // rows * 3 * channels * BAND
    early = [("beside", 0)]
    made = {}
    made[early[0]], mid, rim, col_a, col_b, sum_a, sum_b = call(
        functools.partial(open_body, early),
        operator_shapes(early, channels) + [VMEM(mid_shape, BF16), VMEM(rim_shape, BF16), line, line, owed_mid, owed_mid],
        (volume, src_w, flags),
        {0: HBM, 1: HBM, 2: SMEM},
        scratch=[VMEM(src_w.shape, BF16), pltpu.SemaphoreType.DMA((4,))],
        flops=inner_flops,
        moved=size * 4,
    )
    for layer in range(layers):
        inner = swaps(sum_a, sum_b, "srow", "scol")
        beside = swaps(col_a, col_b, "scol", "trow")
        a, b, side, *deep = call(
            edge_body,
            [owed_rim, owed_rim, VMEM((2, *line.shape), BF16)] + [VMEM((rows, channels, cols * width), BF16)] * deep_swaps,
            (mid, rim, *beside, made["beside", layer], flags),
            {5: SMEM},
            flops=inner_flops,
            moved=size * 2,
        )
        outer = swaps(a, b, "srow", "scol")
        if deep_swaps == 1:
            deeper = [lax.ppermute(deep[0], "trow", [(0, 1), (1, 0)])]
        else:
            deeper = swaps(*deep, "trow", "scol")
        if layer == 0:
            rest = [(kind, n) for n in range(layers) for kind in ("middle", "beside", "target", "near", "deep")]
            made |= build([part for part in rest if part not in early], src_w, tgt_w, a)
        ops = [made[kind, layer] for kind in ("middle", "beside", "target", "near", "deep")]
        acc_mid, acc_rim = call(
            functools.partial(main_body, layer),
            [VMEM(mid_shape, F32), VMEM(rim_shape, F32)],
            (mid, rim, side, *ops, bias, flags, *deeper),
            {8: SMEM, 9: SMEM},
            scratch=[VMEM((depth // BAND, 3, channels * BAND, cols * width), BF16)],
            flops=2 * size * 12 * channels * BAND,
            moved=size * 8,
        )
        mid_args, rim_args = (mid, acc_mid, *inner, flags), (rim, acc_rim, *outer, flags)
        if layer < layers - 1:
            (mid,) = call(mid_body, [VMEM(mid_shape, BF16)], mid_args, {4: SMEM}, flops=size, moved=size * 5)
            rim, col_a, col_b, sum_a, sum_b = call(
                next_body,
                [VMEM(rim_shape, BF16), line, line, owed_mid, owed_mid],
                (mid, *rim_args[:-1], made["beside", layer + 1], flags),
                {6: SMEM},
                flops=inner_flops,
                moved=size * 10,
            )
        else:
            whole = jax.ShapeDtypeStruct(volume.shape, BF16)
            (state,) = call(
                write_mid_body,
                [whole],
                mid_args,
                {4: SMEM},
                out_place=HBM,
                scratch=[VMEM(mid_shape, BF16), pltpu.SemaphoreType.DMA((rows,))],
                flops=size,
                moved=size * 5,
            )
            (state,) = call(
                write_rim_body,
                [whole],
                (*rim_args, state),
                {4: SMEM, 5: HBM},
                out_place=HBM,
                scratch=[VMEM(rim_shape, BF16), pltpu.SemaphoreType.DMA((rows * 2,))],
                flops=size,
                moved=size * 5,
                aliases={5: 0},
            )
    return state


def solution(mesh):
    return jax.shard_map(
        shards,
        mesh=mesh,
        in_specs=(P(None, "srow", "scol", "trow", None), P(), P(), P()),
        out_specs=P(None, "srow", "scol", "trow", None),
        check_vma=False,
    )
```

```python
import functools

import jax
import jax.numpy as jnp
from jax import lax
from jax.experimental import pallas as pl
from jax.experimental.pallas import tpu as pltpu
from jax.sharding import PartitionSpec as P

BAND = 32
EDGE = 16
SCOPED = 16 * 1024 * 1024
F32 = jnp.float32
BF16 = jnp.bfloat16
VMEM, HBM = pltpu.VMEM, pltpu.HBM
def parity(axis):
    return lax.axis_index(axis) % 2


def has_second(axis):
    at = lax.axis_index(axis)
    return (at > 0) & (at < lax.axis_size(axis) - 1)


def call(body, outs, args, places=None, out_place=VMEM, scratch=(), aliases=None):
    places = places or {}
    spaces = [places.get(n, VMEM) for n in range(len(args))]
    held = [pltpu.with_memory_space_constraint(a, m) if m in (VMEM, HBM) else a for a, m in zip(args, spaces)]
    return pl.pallas_call(
        body,
        out_shape=tuple(outs),
        in_specs=[pl.BlockSpec(memory_space=m) for m in spaces],
        out_specs=tuple(pl.BlockSpec(memory_space=out_place) for _ in outs),
        scratch_shapes=list(scratch),
        input_output_aliases=aliases or {},
        compiler_params=pltpu.CompilerParams(vmem_limit_bytes=SCOPED),
        cost_estimate=pl.CostEstimate(flops=10**6, bytes_accessed=10**4, transcendentals=0),
    )(*held)


def dot(a, b):
    return jnp.dot(a, b, preferred_element_type=F32)


def operators(parts, src_w_ref, tgt_w_ref, out_refs):
    channels = src_w_ref.shape[1]
    span, small = channels * BAND, channels * EDGE

    def columns(size):
        pick_c = lax.broadcasted_iota(jnp.int32, (channels, channels * size), 1) // size
        pick_r = lax.broadcasted_iota(jnp.int32, (channels, channels * size), 0)
        return (pick_c == pick_r).astype(BF16)

    wide, narrow, single = columns(BAND), columns(EDGE), columns(1)
    row = lax.broadcasted_iota(jnp.int32, (BAND, span), 0)
    shift = row - lax.broadcasted_iota(jnp.int32, (BAND, span), 1) % BAND
    row_s = lax.broadcasted_iota(jnp.int32, (BAND, small), 0)
    col_s = lax.broadcasted_iota(jnp.int32, (BAND, small), 1) % EDGE
    near = ((row_s == 0) & (col_s == EDGE - 1), (row_s == BAND - 1) & (col_s == 0))
    row_1 = lax.broadcasted_iota(jnp.int32, (BAND, channels), 0)
    deep = (row_1 == 0, row_1 == BAND - 1)
    spread = {}

    def taps(ref, layer, o, pick, key):
        key = (key, layer, o)
        if key not in spread:
            spread[key] = lax.dot_general(ref[layer, o], pick, (((0,), (0,)), ((), ())), preferred_element_type=F32)
        return spread[key]

    for (kind, layer), out_ref in zip(parts, out_refs):
        for o in range(channels):
            rows = slice(o * BAND, (o + 1) * BAND)
            for b in range(3):
                if kind == "middle":
                    got = taps(src_w_ref, layer, o, wide, "s")
                    values = {(): jnp.where(shift == 0, got[3 + b][None, :], 0.0)}
                elif kind == "beside":
                    got = taps(src_w_ref, layer, o, wide, "s")
                    values = {(n,): jnp.where(shift == 0, got[6 * n + b][None, :], 0.0) for n in range(2)}
                elif kind == "target":
                    got = taps(tgt_w_ref, layer, o, wide, "t")
                    value = jnp.where(shift == 1, got[b][None, :], 0.0)
                    value = jnp.where(shift == 0, got[3 + b][None, :], value)
                    values = {(): jnp.where(shift == -1, got[6 + b][None, :], value)}
                else:
                    pick, at = (narrow, near) if kind == "near" else (single, deep)
                    got = taps(tgt_w_ref, layer, o, pick, kind)
                    values = {(n,): jnp.where(at[n], got[6 * n + b][None, :], 0.0) for n in range(2)}
                for index, value in values.items():
                    size = value.shape[1]
                    out_ref[(*index, rows, slice(b * size, (b + 1) * size))] = value.astype(BF16)


def operator_shapes(parts, channels):
    span = channels * BAND
    widths = dict(middle=span, beside=span, target=span, near=channels * EDGE, deep=channels)
    lead = dict(middle=(), beside=(2,), target=(), near=(2,), deep=(2,))
    return [VMEM((*lead[kind], span, 3 * widths[kind]), BF16) for kind, _ in parts]


def build_body(parts, src_w_ref, tgt_w_ref, after_ref, *out_refs):
    operators(parts, src_w_ref, tgt_w_ref, out_refs)


def build(parts, src_w, tgt_w, after):
    got = call(
        functools.partial(build_body, parts),
        operator_shapes(parts, src_w.shape[1]),
        (src_w, tgt_w, after),
        {2: pl.ANY},
    )
    return dict(zip(parts, got))


def band(tile):
    channels, size, width = tile.shape
    return tile.reshape(channels * size, width)


def unband(tile, channels):
    return tile.reshape(channels, tile.shape[0] // channels, tile.shape[1])


def src_operand(tiles, cols):
    return jnp.concatenate([jnp.concatenate(tiles[b : b + cols], axis=1) for b in range(3)], axis=0)


def sent_rows(rows):
    odd = parity("srow")
    return ((rows - 1) * (1 - odd), odd), ((rows - 1) * odd, 1 - odd)


def column(mid_ref, rim_ref, i, j, cut):
    last = mid_ref.shape[2] + 1
    return band(rim_ref[:, i, j // last, cut] if j in (0, last) else mid_ref[:, i, j - 1, cut])


def bands_of(depth):
    return [slice(start, start + BAND) for start in range(0, depth, BAND)]


def owed_sums(operator, tiles, out_ref):
    channels, cols, depth, width = out_ref.shape
    cuts = bands_of(depth)
    operand = jnp.concatenate([jnp.concatenate([t for cut in cuts for t in tiles(cut, b)], axis=1) for b in range(3)], axis=0)
    got = dot(operator, operand).astype(BF16)
    for q, cut in enumerate(cuts):
        for j in range(cols):
            at = (q * cols + j) * width
            out_ref[:, j, cut] = unband(got[:, at : at + width], channels)


def inner_sums(mid_ref, rim_ref, beside_ref, out_refs):
    rows, cols = mid_ref.shape[1:3]
    for (i, side), out_ref in zip(sent_rows(rows), out_refs):
        owed_sums(
            beside_ref[side], lambda cut, b: [column(mid_ref, rim_ref, i, j + b, cut) for j in range(cols)], out_ref
        )


def edge_body(mid_ref, rim_ref, cola_ref, colb_ref, beside_ref, after_ref, a_ref, b_ref, side_ref):
    rows, cols = mid_ref.shape[1], mid_ref.shape[2] + 2
    odd, paired = parity("scol"), has_second("scol")
    side_ref[1 - odd] = cola_ref[...]

    @pl.when(paired)
    def _():
        side_ref[odd] = colb_ref[...]

    @pl.when(jnp.logical_not(paired))
    def _():
        side_ref[odd] = jnp.zeros_like(colb_ref)

    def around(i, j, cut):
        if j in (-1, cols):
            return band(side_ref[0 if j < 0 else 1, :, i, cut])
        return column(mid_ref, rim_ref, i, j, cut)

    for (i, side), out_ref in zip(sent_rows(rows), (a_ref, b_ref)):
        owed_sums(beside_ref[side], lambda cut, b: [around(i, j + b - 1, cut) for j in (0, cols - 1)], out_ref)


def shifted(tile, step):
    lane = lax.broadcasted_iota(jnp.int32, tile.shape, 1)
    width = tile.shape[1]
    rolled = pltpu.roll(tile.astype(F32), step % width, 1)
    gone = 0 if step == 1 else width - 1
    return jnp.where(lane == gone, 0.0, rolled)


def three(tiles):
    return [jnp.concatenate([shifted(t, step) if step else t.astype(F32) for t in tiles], axis=1) for step in (1, 0, -1)]


def own_body(
    layer, mid_ref, rim_ref, middle_ref, beside_ref, target_ref, near_ref, bias_ref, after_ref, accmid_ref, accrim_ref, lane_ref
):
    channels, rows, mids, depth, width = mid_ref.shape
    cols = mids + 2
    cuts = bands_of(depth)
    shape = (BAND, cols * width)
    bias = [jnp.broadcast_to(bias_ref[layer : layer + 1, o : o + 1], shape) for o in range(channels)]
    bias = jnp.concatenate(bias, axis=0)
    for i in range(rows):
        for q, cut in enumerate(cuts):
            tiles = [column(mid_ref, rim_ref, i, j, cut) for j in range(cols)]
            lane_ref[q, 1] = jnp.concatenate(tiles, axis=1)
            for n, step in ((0, 1), (2, -1)):
                lane_ref[q, n] = jnp.concatenate([shifted(t, step).astype(BF16) for t in tiles], axis=1)
        for q, cut in enumerate(cuts):
            total = bias + dot(target_ref[...], lane_ref[q].reshape(3 * channels * BAND, cols * width))
            for side, other, start in ((0, q - 1, BAND - EDGE), (1, q + 1, 0)):
                if 0 <= other < len(cuts):
                    parts = [unband(lane_ref[other, n], channels)[:, start : start + EDGE] for n in range(3)]
                    total = total + dot(near_ref[side], jnp.concatenate([band(p) for p in parts], axis=0))
            for n, j in enumerate((0, cols - 1)):
                accrim_ref[:, i, n, cut] = unband(total[:, j * width : (j + 1) * width], channels)
            for j in range(1, cols - 1):
                accmid_ref[:, i, j - 1, cut] = unband(total[:, j * width : (j + 1) * width], channels)
        for a in range(3):
            r = i + a - 1
            if 0 <= r < rows:
                operator = middle_ref[...] if a == 1 else beside_ref[a // 2]
                add_sums(operator, lambda cut, b: [column(mid_ref, rim_ref, r, j + b, cut) for j in range(mids)], accmid_ref, i)


def add_sums(operator, tiles, acc_ref, i):
    channels, _, cols, depth, width = acc_ref.shape
    cuts = bands_of(depth)
    operand = jnp.concatenate([jnp.concatenate([t for cut in cuts for t in tiles(cut, b)], axis=1) for b in range(3)], axis=0)
    got = dot(operator, operand)
    for q, cut in enumerate(cuts):
        for j in range(cols):
            at = (q * cols + j) * width
            acc_ref[:, i, j, cut] += unband(got[:, at : at + width], channels)


def rest_body(
    mid_ref, rim_ref, side_ref, middle_ref, beside_ref, deep_ref, accmid_ref, accrim_ref, *rest
):
    *deep_halos, outmid_ref, outrim_ref = rest
    channels, rows, mids, depth, width = mid_ref.shape
    cols = mids + 2

    def around(r, j, cut):
        if j in (-1, cols):
            return band(side_ref[0 if j < 0 else 1, :, r, cut])
        return column(mid_ref, rim_ref, r, j, cut)

    for i in range(rows):
        for a in range(3):
            r = i + a - 1
            if 0 <= r < rows:
                operator = middle_ref[...] if a == 1 else beside_ref[a // 2]
                add_sums(operator, lambda cut, b: [around(r, j + b - 1, cut) for j in (0, cols - 1)], outrim_ref, i)
        odd = parity("trow")
        for n, halo_ref in enumerate(deep_halos):
            side = (1 - odd) if n == 0 else odd
            cut = pl.ds(pl.multiple_of(side * (depth - BAND), BAND), BAND)
            halo = three([halo_ref[i, :, j * width : (j + 1) * width] for j in range(cols)])
            halo = jnp.concatenate(halo, axis=0)
            if n == 1:
                halo = halo * has_second("trow").astype(F32)
            got = dot(deep_ref[side], halo.astype(BF16))
            for j in range(cols):
                acc_ref, at = (outrim_ref, j // (cols - 1)) if j in (0, cols - 1) else (outmid_ref, j - 1)
                acc_ref[:, i, at, cut] += unband(got[:, j * width : (j + 1) * width], channels)


def finished(x_ref, acc_ref, owed_refs, store):
    rows, cols = x_ref.shape[1:3]
    odd = parity("srow")
    paired = has_second("srow").astype(F32)
    for n, i in enumerate([(rows - 1) * (1 - odd), (rows - 1) * odd, *range(1, rows - 1)]):
        for j in range(cols):
            total = acc_ref[:, i, j]
            if n < 2:
                owed = owed_refs[n][:, j].astype(F32)
                total = total + (owed if n == 0 else owed * paired)
            store(i, j, (x_ref[:, i, j].astype(F32) + jnp.maximum(total, 0.0)).astype(BF16))


def sent_columns(rim_ref, col_refs):
    odd = parity("scol")
    for n, ref in zip((1 - odd, odd), col_refs):
        ref[...] = rim_ref[:, :, n]


def sent_depths(mid_ref, rim_ref, deep_refs):
    channels, rows, mids, depth, _ = mid_ref.shape
    odd = parity("trow")
    shape = (channels, channels * BAND)
    first = lax.broadcasted_iota(jnp.int32, shape, 0) * BAND
    for n, ref in enumerate(deep_refs):
        end = (1 - odd) if n == 0 else odd
        cut = pl.ds(pl.multiple_of(end * (depth - BAND), BAND), BAND)
        pick = (lax.broadcasted_iota(jnp.int32, shape, 1) == first + end * (BAND - 1)).astype(BF16)
        for i in range(rows):
            tiles = [column(mid_ref, rim_ref, i, j, cut) for j in range(mids + 2)]
            ref[i] = dot(pick, jnp.concatenate(tiles, axis=1)).astype(BF16)


def mid_body(x_ref, acc_ref, a_ref, b_ref, out_ref):
    def store(i, j, value):
        out_ref[:, i, j] = value

    finished(x_ref, acc_ref, (a_ref, b_ref), store)


def next_body(mid_ref, rim_ref, acc_ref, outa_ref, outb_ref, beside_ref, out_ref, cola_ref, colb_ref, a_ref, b_ref, *deep_refs):
    mid_body(rim_ref, acc_ref, outa_ref, outb_ref, out_ref)
    sent_columns(out_ref, (cola_ref, colb_ref))
    inner_sums(mid_ref, out_ref, beside_ref, (a_ref, b_ref))
    sent_depths(mid_ref, out_ref, deep_refs)


def last_body(mid_ref, rim_ref, acc_ref, a_ref, b_ref, out_ref, hold_ref, sems):
    rows, mids = mid_ref.shape[1:3]
    copies = [pltpu.make_async_copy(mid_ref, out_ref.at[:, :, 1 : mids + 1], sems.at[0])]
    copies[0].start()

    def store(i, j, value):
        hold_ref[:, i, j] = value
        copy = pltpu.make_async_copy(hold_ref.at[:, i, j], out_ref.at[:, i, j * (mids + 1)], sems.at[len(copies)])
        copy.start()
        copies.append(copy)

    finished(rim_ref, acc_ref, (a_ref, b_ref), store)
    for copy in copies:
        copy.wait()


def open_body(parts, x_ref, src_w_ref, tgt_w_ref, bias_ref, *rest):
    src_ref, tgt_ref, held_ref, beside_ref, mid_ref, rim_ref, cola_ref, colb_ref, a_ref, b_ref, *deep_refs, sems = rest
    last = x_ref.shape[2] - 1
    pairs = (
        (src_w_ref, src_ref),
        (x_ref.at[:, :, 0], rim_ref.at[:, :, 0]),
        (x_ref.at[:, :, last], rim_ref.at[:, :, 1]),
        (x_ref.at[:, :, 1:last], mid_ref),
        (tgt_w_ref, tgt_ref),
        (bias_ref, held_ref),
    )
    copies = [pltpu.make_async_copy(a, b, sems.at[n]) for n, (a, b) in enumerate(pairs)]
    for copy in copies:
        copy.start()
    copies[0].wait()
    operators(parts, src_ref, None, (beside_ref,))
    for copy in copies[1:]:
        copy.wait()
    sent_columns(rim_ref, (cola_ref, colb_ref))
    inner_sums(mid_ref, rim_ref, beside_ref, (a_ref, b_ref))
    sent_depths(mid_ref, rim_ref, deep_refs)


def swaps(a, b, axis, other):
    count, across = lax.axis_size(axis), lax.axis_size(other)
    pairs = []
    for n in range(count):
        for m in range(across):
            if 0 < n < count - 1:
                target = (n + 1 if n % 2 else n - 1, m)
            else:
                target = (n, m ^ 1)
            pairs.append((n * across + m, target[0] * across + target[1]))
    got_a = lax.ppermute(a, axis, [(n, n ^ 1) for n in range(count)])
    return got_a, lax.ppermute(b, (axis, other), pairs)


def shards(volume, src_weight, tgt_weight, bias):
    layers = src_weight.shape[0]
    channels, rows, cols, depth, width = volume.shape
    axes = ("srow", "scol", "trow")
    counts = [lax.axis_size(n) for n in axes]
    assert all(count % 2 == 0 for count in counts) and rows > 1 and cols > 2
    src_w = jnp.transpose(src_weight, (0, 2, 3, 1))
    tgt_w = jnp.transpose(tgt_weight, (0, 2, 3, 1))
    deep_swaps = 1 if counts[2] == 2 else 2
    mid_shape, rim_shape = ((channels, rows, n, depth, width) for n in (cols - 2, 2))
    line = VMEM((channels, rows, depth, width), BF16)
    owed_mid, owed_rim = (VMEM((channels, n, depth, width), BF16) for n in (cols - 2, 2))
    sent = [VMEM(rim_shape, BF16), line, line, owed_mid, owed_mid]
    sent += [VMEM((rows, channels, cols * width), BF16)] * deep_swaps
    early = [("beside", 0)]
    src_w, tgt_w, bias, made_early, mid, rim, col_a, col_b, sum_a, sum_b, *deep = call(
        functools.partial(open_body, early),
        [VMEM(src_w.shape, BF16), VMEM(tgt_w.shape, BF16), VMEM(bias.shape, F32)]
        + operator_shapes(early, channels)
        + [VMEM(mid_shape, BF16)]
        + sent,
        (volume, src_w, tgt_w, bias),
        {n: HBM for n in range(4)},
        scratch=[pltpu.SemaphoreType.DMA((6,))],
    )
    made = {early[0]: made_early}
    made |= build([(kind, 0) for kind in ("middle", "target", "near", "deep")], src_w, tgt_w, sum_a)
    for layer in range(layers):
        inner = swaps(sum_a, sum_b, "srow", "scol")
        beside = swaps(col_a, col_b, "scol", "trow")
        if deep_swaps == 1:
            deeper = [lax.ppermute(deep[0], "trow", [(0, 1), (1, 0)])]
        else:
            deeper = swaps(*deep, "trow", "scol")
        operator = {kind: made[kind, layer] for kind in ("middle", "beside", "target", "near", "deep")}

        def own(after):
            return call(
                functools.partial(own_body, layer),
                [VMEM(mid_shape, F32), VMEM(rim_shape, F32)],
                (mid, rim, *(operator[kind] for kind in ("middle", "beside", "target", "near")), bias, after),
                {7: pl.ANY},
                scratch=[VMEM((depth // BAND, 3, channels * BAND, cols * width), BF16)],
            )

        accs = own(sum_a) if layer else None
        a, b, side = call(
            edge_body,
            [owed_rim, owed_rim, VMEM((2, *line.shape), BF16)],
            (mid, rim, *beside, operator["beside"], accs[0] if layer else operator["middle"]),
            {5: pl.ANY},
        )
        outer = swaps(a, b, "srow", "scol")
        accs = accs or own(a)
        acc_mid, acc_rim = call(
            rest_body,
            [VMEM(mid_shape, F32), VMEM(rim_shape, F32)],
            (mid, rim, side, *(operator[kind] for kind in ("middle", "beside", "deep")), *accs, *deeper),
            aliases={6: 0, 7: 1},
        )
        (mid,) = call(mid_body, [VMEM(mid_shape, BF16)], (mid, acc_mid, *inner))
        if layer < layers - 1:
            later = [(kind, layer + 1) for kind in operator]
            made |= build(later, src_w, tgt_w, mid)
            rim, col_a, col_b, sum_a, sum_b, *deep = call(
                next_body, sent, (mid, rim, acc_rim, *outer, made["beside", layer + 1])
            )
        else:
            (state,) = call(
                last_body,
                [jax.ShapeDtypeStruct(volume.shape, BF16)],
                (mid, rim, acc_rim, *outer),
                out_place=HBM,
                scratch=[VMEM(rim_shape, BF16), pltpu.SemaphoreType.DMA((1 + rows * 2,))],
            )
    return state


def solution(mesh):
    return jax.shard_map(
        shards,
        mesh=mesh,
        in_specs=(P(None, "srow", "scol", "trow", None), P(), P(), P()),
        out_specs=P(None, "srow", "scol", "trow", None),
        check_vma=False,
    )
```

```python
import functools

import jax
import jax.numpy as jnp
from jax import lax
from jax.experimental import pallas as pl
from jax.experimental.pallas import tpu as pltpu
from jax.sharding import PartitionSpec as P

BAND = 32
EDGE = 16
SCOPED = 16 * 1024 * 1024
F32 = jnp.float32
BF16 = jnp.bfloat16
VMEM, HBM = pltpu.VMEM, pltpu.HBM
def parity(axis):
    return lax.axis_index(axis) % 2


def has_second(axis):
    at = lax.axis_index(axis)
    return (at > 0) & (at < lax.axis_size(axis) - 1)


def call(body, outs, args, places=None, out_place=VMEM, scratch=(), aliases=None):
    places = places or {}
    spaces = [places.get(n, VMEM) for n in range(len(args))]
    held = [pltpu.with_memory_space_constraint(a, m) if m in (VMEM, HBM) else a for a, m in zip(args, spaces)]
    return pl.pallas_call(
        body,
        out_shape=tuple(outs),
        in_specs=[pl.BlockSpec(memory_space=m) for m in spaces],
        out_specs=tuple(pl.BlockSpec(memory_space=out_place) for _ in outs),
        scratch_shapes=list(scratch),
        input_output_aliases=aliases or {},
        compiler_params=pltpu.CompilerParams(vmem_limit_bytes=SCOPED),
        cost_estimate=pl.CostEstimate(flops=10**6, bytes_accessed=10**4, transcendentals=0),
    )(*held)


def dot(a, b):
    return jnp.dot(a, b, preferred_element_type=F32)


def operators(parts, src_w_ref, tgt_w_ref, out_refs):
    channels = src_w_ref.shape[1]
    span, small = channels * BAND, channels * EDGE

    def columns(size):
        pick_c = lax.broadcasted_iota(jnp.int32, (channels, channels * size), 1) // size
        pick_r = lax.broadcasted_iota(jnp.int32, (channels, channels * size), 0)
        return (pick_c == pick_r).astype(BF16)

    wide, narrow, single = columns(BAND), columns(EDGE), columns(1)
    row = lax.broadcasted_iota(jnp.int32, (BAND, span), 0)
    shift = row - lax.broadcasted_iota(jnp.int32, (BAND, span), 1) % BAND
    row_s = lax.broadcasted_iota(jnp.int32, (BAND, small), 0)
    col_s = lax.broadcasted_iota(jnp.int32, (BAND, small), 1) % EDGE
    near = ((row_s == 0) & (col_s == EDGE - 1), (row_s == BAND - 1) & (col_s == 0))
    row_1 = lax.broadcasted_iota(jnp.int32, (BAND, channels), 0)
    deep = (row_1 == 0, row_1 == BAND - 1)
    spread = {}

    def taps(ref, layer, o, pick, key):
        key = (key, layer, o)
        if key not in spread:
            spread[key] = lax.dot_general(ref[layer, o], pick, (((0,), (0,)), ((), ())), preferred_element_type=F32)
        return spread[key]

    for (kind, layer), out_ref in zip(parts, out_refs):
        for o in range(channels):
            rows = slice(o * BAND, (o + 1) * BAND)
            for b in range(3):
                if kind == "middle":
                    got = taps(src_w_ref, layer, o, wide, "s")
                    values = {(): jnp.where(shift == 0, got[3 + b][None, :], 0.0)}
                elif kind == "beside":
                    got = taps(src_w_ref, layer, o, wide, "s")
                    values = {(n,): jnp.where(shift == 0, got[6 * n + b][None, :], 0.0) for n in range(2)}
                elif kind == "target":
                    got = taps(tgt_w_ref, layer, o, wide, "t")
                    value = jnp.where(shift == 1, got[b][None, :], 0.0)
                    value = jnp.where(shift == 0, got[3 + b][None, :], value)
                    values = {(): jnp.where(shift == -1, got[6 + b][None, :], value)}
                else:
                    pick, at = (narrow, near) if kind == "near" else (single, deep)
                    got = taps(tgt_w_ref, layer, o, pick, kind)
                    values = {(n,): jnp.where(at[n], got[6 * n + b][None, :], 0.0) for n in range(2)}
                for index, value in values.items():
                    size = value.shape[1]
                    out_ref[(*index, rows, slice(b * size, (b + 1) * size))] = value.astype(BF16)


def operator_shapes(parts, channels):
    span = channels * BAND
    widths = dict(middle=span, beside=span, target=span, near=channels * EDGE, deep=channels)
    lead = dict(middle=(), beside=(2,), target=(), near=(2,), deep=(2,))
    return [VMEM((*lead[kind], span, 3 * widths[kind]), BF16) for kind, _ in parts]


def build_body(parts, src_w_ref, tgt_w_ref, after_ref, *out_refs):
    operators(parts, src_w_ref, tgt_w_ref, out_refs)


def build(parts, src_w, tgt_w, after):
    got = call(
        functools.partial(build_body, parts),
        operator_shapes(parts, src_w.shape[1]),
        (src_w, tgt_w, after),
        {2: pl.ANY},
    )
    return dict(zip(parts, got))


def band(tile):
    channels, size, width = tile.shape
    return tile.reshape(channels * size, width)


def unband(tile, channels):
    return tile.reshape(channels, tile.shape[0] // channels, tile.shape[1])


def src_operand(tiles, cols):
    return jnp.concatenate([jnp.concatenate(tiles[b : b + cols], axis=1) for b in range(3)], axis=0)


def sent_rows(rows):
    odd = parity("srow")
    return ((rows - 1) * (1 - odd), odd), ((rows - 1) * odd, 1 - odd)


def column(mid_ref, rim_ref, i, j, cut):
    last = mid_ref.shape[2] + 1
    return band(rim_ref[:, i, j // last, cut] if j in (0, last) else mid_ref[:, i, j - 1, cut])


def bands_of(depth):
    return [slice(start, start + BAND) for start in range(0, depth, BAND)]


def owed_sums(operator, tiles, out_ref):
    channels, cols, depth, width = out_ref.shape
    cuts = bands_of(depth)
    operand = jnp.concatenate([jnp.concatenate([t for cut in cuts for t in tiles(cut, b)], axis=1) for b in range(3)], axis=0)
    got = dot(operator, operand).astype(BF16)
    for q, cut in enumerate(cuts):
        for j in range(cols):
            at = (q * cols + j) * width
            out_ref[:, j, cut] = unband(got[:, at : at + width], channels)


def inner_sums(mid_ref, rim_ref, beside_ref, out_refs):
    rows, cols = mid_ref.shape[1:3]
    for (i, side), out_ref in zip(sent_rows(rows), out_refs):
        owed_sums(
            beside_ref[side], lambda cut, b: [column(mid_ref, rim_ref, i, j + b, cut) for j in range(cols)], out_ref
        )


def edge_body(mid_ref, rim_ref, cola_ref, colb_ref, beside_ref, after_ref, a_ref, b_ref, side_ref, *deep_refs):
    rows, cols = mid_ref.shape[1], mid_ref.shape[2] + 2
    odd, paired = parity("scol"), has_second("scol")
    side_ref[1 - odd] = cola_ref[...]

    @pl.when(paired)
    def _():
        side_ref[odd] = colb_ref[...]

    @pl.when(jnp.logical_not(paired))
    def _():
        side_ref[odd] = jnp.zeros_like(colb_ref)

    def around(i, j, cut):
        if j in (-1, cols):
            return band(side_ref[0 if j < 0 else 1, :, i, cut])
        return column(mid_ref, rim_ref, i, j, cut)

    for (i, side), out_ref in zip(sent_rows(rows), (a_ref, b_ref)):
        owed_sums(beside_ref[side], lambda cut, b: [around(i, j + b - 1, cut) for j in (0, cols - 1)], out_ref)
    sent_depths(mid_ref, rim_ref, deep_refs)


def shifted(tile, step):
    lane = lax.broadcasted_iota(jnp.int32, tile.shape, 1)
    width = tile.shape[1]
    rolled = pltpu.roll(tile.astype(F32), step % width, 1)
    gone = 0 if step == 1 else width - 1
    return jnp.where(lane == gone, 0.0, rolled)


def three(tiles):
    return [jnp.concatenate([shifted(t, step) if step else t.astype(F32) for t in tiles], axis=1) for step in (1, 0, -1)]


def own_body(
    layer, mid_ref, rim_ref, middle_ref, beside_ref, target_ref, near_ref, bias_ref, accmid_ref, accrim_ref, lane_ref
):
    channels, rows, mids, depth, width = mid_ref.shape
    cols = mids + 2
    cuts = bands_of(depth)
    shape = (BAND, cols * width)
    bias = [jnp.broadcast_to(bias_ref[layer : layer + 1, o : o + 1], shape) for o in range(channels)]
    bias = jnp.concatenate(bias, axis=0)
    for i in range(rows):
        for q, cut in enumerate(cuts):
            tiles = [column(mid_ref, rim_ref, i, j, cut) for j in range(cols)]
            lane_ref[q, 1] = jnp.concatenate(tiles, axis=1)
            for n, step in ((0, 1), (2, -1)):
                lane_ref[q, n] = jnp.concatenate([shifted(t, step).astype(BF16) for t in tiles], axis=1)
        for q, cut in enumerate(cuts):
            total = bias + dot(target_ref[...], lane_ref[q].reshape(3 * channels * BAND, cols * width))
            for side, other, start in ((0, q - 1, BAND - EDGE), (1, q + 1, 0)):
                if 0 <= other < len(cuts):
                    parts = [unband(lane_ref[other, n], channels)[:, start : start + EDGE] for n in range(3)]
                    total = total + dot(near_ref[side], jnp.concatenate([band(p) for p in parts], axis=0))
            for n, j in enumerate((0, cols - 1)):
                accrim_ref[:, i, n, cut] = unband(total[:, j * width : (j + 1) * width], channels)
            for j in range(1, cols - 1):
                accmid_ref[:, i, j - 1, cut] = unband(total[:, j * width : (j + 1) * width], channels)
        for a in range(3):
            r = i + a - 1
            if 0 <= r < rows:
                operator = middle_ref[...] if a == 1 else beside_ref[a // 2]
                add_sums(operator, lambda cut, b: [column(mid_ref, rim_ref, r, j + b, cut) for j in range(mids)], accmid_ref, i)


def add_sums(operator, tiles, acc_ref, i):
    channels, _, cols, depth, width = acc_ref.shape
    cuts = bands_of(depth)
    operand = jnp.concatenate([jnp.concatenate([t for cut in cuts for t in tiles(cut, b)], axis=1) for b in range(3)], axis=0)
    got = dot(operator, operand)
    for q, cut in enumerate(cuts):
        for j in range(cols):
            at = (q * cols + j) * width
            acc_ref[:, i, j, cut] += unband(got[:, at : at + width], channels)


def rest_body(
    mid_ref, rim_ref, side_ref, middle_ref, beside_ref, deep_ref, accmid_ref, accrim_ref, *rest
):
    *deep_halos, outmid_ref, outrim_ref = rest
    channels, rows, mids, depth, width = mid_ref.shape
    cols = mids + 2

    def around(r, j, cut):
        if j in (-1, cols):
            return band(side_ref[0 if j < 0 else 1, :, r, cut])
        return column(mid_ref, rim_ref, r, j, cut)

    for i in range(rows):
        for a in range(3):
            r = i + a - 1
            if 0 <= r < rows:
                operator = middle_ref[...] if a == 1 else beside_ref[a // 2]
                add_sums(operator, lambda cut, b: [around(r, j + b - 1, cut) for j in (0, cols - 1)], outrim_ref, i)
        odd = parity("trow")
        for n, halo_ref in enumerate(deep_halos):
            side = (1 - odd) if n == 0 else odd
            cut = pl.ds(pl.multiple_of(side * (depth - BAND), BAND), BAND)
            halo = three([halo_ref[i, :, j * width : (j + 1) * width] for j in range(cols)])
            halo = jnp.concatenate(halo, axis=0)
            if n == 1:
                halo = halo * has_second("trow").astype(F32)
            got = dot(deep_ref[side], halo.astype(BF16))
            for j in range(cols):
                acc_ref, at = (outrim_ref, j // (cols - 1)) if j in (0, cols - 1) else (outmid_ref, j - 1)
                acc_ref[:, i, at, cut] += unband(got[:, j * width : (j + 1) * width], channels)


def finished(x_ref, acc_ref, owed_refs, store):
    rows, cols = x_ref.shape[1:3]
    odd = parity("srow")
    paired = has_second("srow").astype(F32)
    for n, i in enumerate([(rows - 1) * (1 - odd), (rows - 1) * odd, *range(1, rows - 1)]):
        for j in range(cols):
            total = acc_ref[:, i, j]
            if n < 2:
                owed = owed_refs[n][:, j].astype(F32)
                total = total + (owed if n == 0 else owed * paired)
            store(i, j, (x_ref[:, i, j].astype(F32) + jnp.maximum(total, 0.0)).astype(BF16))


def sent_columns(rim_ref, col_refs):
    odd = parity("scol")
    for n, ref in zip((1 - odd, odd), col_refs):
        ref[...] = rim_ref[:, :, n]


def sent_depths(mid_ref, rim_ref, deep_refs):
    channels, rows, mids, depth, _ = mid_ref.shape
    odd = parity("trow")
    shape = (channels, channels * BAND)
    first = lax.broadcasted_iota(jnp.int32, shape, 0) * BAND
    for n, ref in enumerate(deep_refs):
        end = (1 - odd) if n == 0 else odd
        cut = pl.ds(pl.multiple_of(end * (depth - BAND), BAND), BAND)
        pick = (lax.broadcasted_iota(jnp.int32, shape, 1) == first + end * (BAND - 1)).astype(BF16)
        for i in range(rows):
            tiles = [column(mid_ref, rim_ref, i, j, cut) for j in range(mids + 2)]
            ref[i] = dot(pick, jnp.concatenate(tiles, axis=1)).astype(BF16)


def mid_body(x_ref, acc_ref, a_ref, b_ref, out_ref):
    def store(i, j, value):
        out_ref[:, i, j] = value

    finished(x_ref, acc_ref, (a_ref, b_ref), store)


def next_body(mid_ref, rim_ref, acc_ref, outa_ref, outb_ref, beside_ref, out_ref, cola_ref, colb_ref, a_ref, b_ref):
    mid_body(rim_ref, acc_ref, outa_ref, outb_ref, out_ref)
    sent_columns(out_ref, (cola_ref, colb_ref))
    inner_sums(mid_ref, out_ref, beside_ref, (a_ref, b_ref))


def last_body(mid_ref, rim_ref, acc_ref, a_ref, b_ref, out_ref, hold_ref, sems):
    rows, mids = mid_ref.shape[1:3]
    copies = [pltpu.make_async_copy(mid_ref, out_ref.at[:, :, 1 : mids + 1], sems.at[0])]
    copies[0].start()

    def store(i, j, value):
        hold_ref[:, i, j] = value
        copy = pltpu.make_async_copy(hold_ref.at[:, i, j], out_ref.at[:, i, j * (mids + 1)], sems.at[len(copies)])
        copy.start()
        copies.append(copy)

    finished(rim_ref, acc_ref, (a_ref, b_ref), store)
    for copy in copies:
        copy.wait()


def open_body(parts, x_ref, src_w_ref, tgt_w_ref, bias_ref, *rest):
    src_ref, tgt_ref, held_ref, beside_ref, mid_ref, rim_ref, cola_ref, colb_ref, a_ref, b_ref, sems = rest
    last = x_ref.shape[2] - 1
    pairs = (
        (src_w_ref, src_ref),
        (x_ref.at[:, :, 0], rim_ref.at[:, :, 0]),
        (x_ref.at[:, :, last], rim_ref.at[:, :, 1]),
        (x_ref.at[:, :, 1:last], mid_ref),
        (tgt_w_ref, tgt_ref),
        (bias_ref, held_ref),
    )
    copies = [pltpu.make_async_copy(a, b, sems.at[n]) for n, (a, b) in enumerate(pairs)]
    for copy in copies:
        copy.start()
    copies[0].wait()
    operators(parts, src_ref, None, (beside_ref,))
    for copy in copies[1:]:
        copy.wait()
    sent_columns(rim_ref, (cola_ref, colb_ref))
    inner_sums(mid_ref, rim_ref, beside_ref, (a_ref, b_ref))


def swaps(a, b, axis, other):
    count, across = lax.axis_size(axis), lax.axis_size(other)
    pairs = []
    for n in range(count):
        for m in range(across):
            if 0 < n < count - 1:
                target = (n + 1 if n % 2 else n - 1, m)
            else:
                target = (n, m ^ 1)
            pairs.append((n * across + m, target[0] * across + target[1]))
    got_a = lax.ppermute(a, axis, [(n, n ^ 1) for n in range(count)])
    return got_a, lax.ppermute(b, (axis, other), pairs)


def shards(volume, src_weight, tgt_weight, bias):
    layers = src_weight.shape[0]
    channels, rows, cols, depth, width = volume.shape
    axes = ("srow", "scol", "trow")
    counts = [lax.axis_size(n) for n in axes]
    assert all(count % 2 == 0 for count in counts) and rows > 1 and cols > 2
    src_w = jnp.transpose(src_weight, (0, 2, 3, 1))
    tgt_w = jnp.transpose(tgt_weight, (0, 2, 3, 1))
    deep_swaps = 1 if counts[2] == 2 else 2
    mid_shape, rim_shape = ((channels, rows, n, depth, width) for n in (cols - 2, 2))
    line = VMEM((channels, rows, depth, width), BF16)
    owed_mid, owed_rim = (VMEM((channels, n, depth, width), BF16) for n in (cols - 2, 2))
    sent = [VMEM(rim_shape, BF16), line, line, owed_mid, owed_mid]
    early = [("beside", 0)]
    src_w, tgt_w, bias, made_early, mid, rim, col_a, col_b, sum_a, sum_b = call(
        functools.partial(open_body, early),
        [VMEM(src_w.shape, BF16), VMEM(tgt_w.shape, BF16), VMEM(bias.shape, F32)]
        + operator_shapes(early, channels)
        + [VMEM(mid_shape, BF16)]
        + sent,
        (volume, src_w, tgt_w, bias),
        {n: HBM for n in range(4)},
        scratch=[pltpu.SemaphoreType.DMA((6,))],
    )
    made = {early[0]: made_early}
    made |= build([(kind, 0) for kind in ("middle", "target", "near", "deep")], src_w, tgt_w, col_b)
    for layer in range(layers):
        inner = swaps(sum_a, sum_b, "srow", "scol")
        beside = swaps(col_a, col_b, "scol", "trow")
        operator = {kind: made[kind, layer] for kind in ("middle", "beside", "target", "near", "deep")}
        accs = call(
            functools.partial(own_body, layer),
            [VMEM(mid_shape, F32), VMEM(rim_shape, F32)],
            (mid, rim, *(operator[kind] for kind in ("middle", "beside", "target", "near")), bias),
            scratch=[VMEM((depth // BAND, 3, channels * BAND, cols * width), BF16)],
        )
        a, b, side, *deep = call(
            edge_body,
            [owed_rim, owed_rim, VMEM((2, *line.shape), BF16)] + [VMEM((rows, channels, cols * width), BF16)] * deep_swaps,
            (mid, rim, *beside, operator["beside"], accs[0]),
            {5: pl.ANY},
        )
        outer = swaps(a, b, "srow", "scol")
        if deep_swaps == 1:
            deeper = [lax.ppermute(deep[0], "trow", [(0, 1), (1, 0)])]
        else:
            deeper = swaps(*deep, "trow", "scol")
        acc_mid, acc_rim = call(
            rest_body,
            [VMEM(mid_shape, F32), VMEM(rim_shape, F32)],
            (mid, rim, side, *(operator[kind] for kind in ("middle", "beside", "deep")), *accs, *deeper),
            aliases={6: 0, 7: 1},
        )
        (mid,) = call(mid_body, [VMEM(mid_shape, BF16)], (mid, acc_mid, *inner))
        if layer < layers - 1:
            later = [(kind, layer + 1) for kind in operator]
            made |= build(later, src_w, tgt_w, mid)
            rim, col_a, col_b, sum_a, sum_b = call(
                next_body, sent, (mid, rim, acc_rim, *outer, made["beside", layer + 1])
            )
        else:
            (state,) = call(
                last_body,
                [jax.ShapeDtypeStruct(volume.shape, BF16)],
                (mid, rim, acc_rim, *outer),
                out_place=HBM,
                scratch=[VMEM(rim_shape, BF16), pltpu.SemaphoreType.DMA((1 + rows * 2,))],
            )
    return state


def solution(mesh):
    return jax.shard_map(
        shards,
        mesh=mesh,
        in_specs=(P(None, "srow", "scol", "trow", None), P(), P(), P()),
        out_specs=P(None, "srow", "scol", "trow", None),
        check_vma=False,
    )
```

```python
import functools

import jax
import jax.numpy as jnp
from jax import lax
from jax.experimental import pallas as pl
from jax.experimental.pallas import tpu as pltpu
from jax.sharding import PartitionSpec as P

BAND = 32
EDGE = 16
SCOPED = 16 * 1024 * 1024
F32 = jnp.float32
BF16 = jnp.bfloat16
VMEM, HBM = pltpu.VMEM, pltpu.HBM
def parity(axis):
    return lax.axis_index(axis) % 2


def has_second(axis):
    at = lax.axis_index(axis)
    return (at > 0) & (at < lax.axis_size(axis) - 1)


def call(body, outs, args, places=None, out_place=VMEM, scratch=(), aliases=None):
    places = places or {}
    spaces = [places.get(n, VMEM) for n in range(len(args))]
    held = [pltpu.with_memory_space_constraint(a, m) if m in (VMEM, HBM) else a for a, m in zip(args, spaces)]
    return pl.pallas_call(
        body,
        out_shape=tuple(outs),
        in_specs=[pl.BlockSpec(memory_space=m) for m in spaces],
        out_specs=tuple(pl.BlockSpec(memory_space=out_place) for _ in outs),
        scratch_shapes=list(scratch),
        input_output_aliases=aliases or {},
        compiler_params=pltpu.CompilerParams(vmem_limit_bytes=SCOPED),
        cost_estimate=pl.CostEstimate(flops=10**6, bytes_accessed=10**4, transcendentals=0),
    )(*held)


def dot(a, b):
    return jnp.dot(a, b, preferred_element_type=F32)


def operators(parts, src_w_ref, tgt_w_ref, out_refs):
    channels = src_w_ref.shape[1]
    span, small = channels * BAND, channels * EDGE

    def columns(size):
        pick_c = lax.broadcasted_iota(jnp.int32, (channels, channels * size), 1) // size
        pick_r = lax.broadcasted_iota(jnp.int32, (channels, channels * size), 0)
        return (pick_c == pick_r).astype(BF16)

    wide, narrow, single = columns(BAND), columns(EDGE), columns(1)
    row = lax.broadcasted_iota(jnp.int32, (BAND, span), 0)
    shift = row - lax.broadcasted_iota(jnp.int32, (BAND, span), 1) % BAND
    row_s = lax.broadcasted_iota(jnp.int32, (BAND, small), 0)
    col_s = lax.broadcasted_iota(jnp.int32, (BAND, small), 1) % EDGE
    near = ((row_s == 0) & (col_s == EDGE - 1), (row_s == BAND - 1) & (col_s == 0))
    row_1 = lax.broadcasted_iota(jnp.int32, (BAND, channels), 0)
    deep = (row_1 == 0, row_1 == BAND - 1)
    spread = {}

    def taps(ref, layer, o, pick, key):
        key = (key, layer, o)
        if key not in spread:
            spread[key] = lax.dot_general(ref[layer, o], pick, (((0,), (0,)), ((), ())), preferred_element_type=F32)
        return spread[key]

    for (kind, layer), out_ref in zip(parts, out_refs):
        for o in range(channels):
            rows = slice(o * BAND, (o + 1) * BAND)
            for b in range(3):
                if kind == "middle":
                    got = taps(src_w_ref, layer, o, wide, "s")
                    values = {(): jnp.where(shift == 0, got[3 + b][None, :], 0.0)}
                elif kind == "beside":
                    got = taps(src_w_ref, layer, o, wide, "s")
                    values = {(n,): jnp.where(shift == 0, got[6 * n + b][None, :], 0.0) for n in range(2)}
                elif kind == "target":
                    got = taps(tgt_w_ref, layer, o, wide, "t")
                    value = jnp.where(shift == 1, got[b][None, :], 0.0)
                    value = jnp.where(shift == 0, got[3 + b][None, :], value)
                    values = {(): jnp.where(shift == -1, got[6 + b][None, :], value)}
                else:
                    pick, at = (narrow, near) if kind == "near" else (single, deep)
                    got = taps(tgt_w_ref, layer, o, pick, kind)
                    values = {(n,): jnp.where(at[n], got[6 * n + b][None, :], 0.0) for n in range(2)}
                for index, value in values.items():
                    size = value.shape[1]
                    out_ref[(*index, rows, slice(b * size, (b + 1) * size))] = value.astype(BF16)


def operator_shapes(parts, channels):
    span = channels * BAND
    widths = dict(middle=span, beside=span, target=span, near=channels * EDGE, deep=channels)
    lead = dict(middle=(), beside=(2,), target=(), near=(2,), deep=(2,))
    return [VMEM((*lead[kind], span, 3 * widths[kind]), BF16) for kind, _ in parts]


def build_body(parts, src_w_ref, tgt_w_ref, after_ref, *out_refs):
    operators(parts, src_w_ref, tgt_w_ref, out_refs)


def build(parts, src_w, tgt_w, after):
    got = call(
        functools.partial(build_body, parts),
        operator_shapes(parts, src_w.shape[1]),
        (src_w, tgt_w, after),
        {2: pl.ANY},
    )
    return dict(zip(parts, got))


def band(tile):
    channels, size, width = tile.shape
    return tile.reshape(channels * size, width)


def unband(tile, channels):
    return tile.reshape(channels, tile.shape[0] // channels, tile.shape[1])


def src_operand(tiles, cols):
    return jnp.concatenate([jnp.concatenate(tiles[b : b + cols], axis=1) for b in range(3)], axis=0)


def sent_rows(rows):
    odd = parity("srow")
    return ((rows - 1) * (1 - odd), odd), ((rows - 1) * odd, 1 - odd)


def column(mid_ref, rim_ref, i, j, cut):
    last = mid_ref.shape[2] + 1
    return band(rim_ref[:, i, j // last, cut] if j in (0, last) else mid_ref[:, i, j - 1, cut])


def bands_of(depth):
    return [slice(start, start + BAND) for start in range(0, depth, BAND)]


def owed_sums(operator, tiles, out_ref):
    channels, cols, depth, width = out_ref.shape
    cuts = bands_of(depth)
    operand = jnp.concatenate([jnp.concatenate([t for cut in cuts for t in tiles(cut, b)], axis=1) for b in range(3)], axis=0)
    got = dot(operator, operand).astype(BF16)
    for q, cut in enumerate(cuts):
        for j in range(cols):
            at = (q * cols + j) * width
            out_ref[:, j, cut] = unband(got[:, at : at + width], channels)


def inner_body(mid_ref, rim_ref, beside_ref, *out_refs):
    rows, cols = mid_ref.shape[1:3]
    for (i, side), out_ref in zip(sent_rows(rows), out_refs):
        owed_sums(
            beside_ref[side], lambda cut, b: [column(mid_ref, rim_ref, i, j + b, cut) for j in range(cols)], out_ref
        )


def edge_body(mid_ref, rim_ref, cola_ref, colb_ref, beside_ref, after_ref, a_ref, b_ref, side_ref):
    rows, cols = mid_ref.shape[1], mid_ref.shape[2] + 2
    odd, paired = parity("scol"), has_second("scol")
    side_ref[1 - odd] = cola_ref[...]

    @pl.when(paired)
    def _():
        side_ref[odd] = colb_ref[...]

    @pl.when(jnp.logical_not(paired))
    def _():
        side_ref[odd] = jnp.zeros_like(colb_ref)

    def around(i, j, cut):
        if j in (-1, cols):
            return band(side_ref[0 if j < 0 else 1, :, i, cut])
        return column(mid_ref, rim_ref, i, j, cut)

    for (i, side), out_ref in zip(sent_rows(rows), (a_ref, b_ref)):
        owed_sums(beside_ref[side], lambda cut, b: [around(i, j + b - 1, cut) for j in (0, cols - 1)], out_ref)


def shifted(tile, step):
    lane = lax.broadcasted_iota(jnp.int32, tile.shape, 1)
    width = tile.shape[1]
    rolled = pltpu.roll(tile.astype(F32), step % width, 1)
    gone = 0 if step == 1 else width - 1
    return jnp.where(lane == gone, 0.0, rolled)


def three(tiles):
    return [jnp.concatenate([shifted(t, step) if step else t.astype(F32) for t in tiles], axis=1) for step in (1, 0, -1)]


def own_body(
    layer, mid_ref, rim_ref, middle_ref, beside_ref, target_ref, near_ref, bias_ref, after_ref, accmid_ref, accrim_ref, lane_ref
):
    channels, rows, mids, depth, width = mid_ref.shape
    cols = mids + 2
    cuts = bands_of(depth)
    shape = (BAND, cols * width)
    bias = [jnp.broadcast_to(bias_ref[layer : layer + 1, o : o + 1], shape) for o in range(channels)]
    bias = jnp.concatenate(bias, axis=0)
    for i in range(rows):
        for q, cut in enumerate(cuts):
            tiles = [column(mid_ref, rim_ref, i, j, cut) for j in range(cols)]
            lane_ref[q, 1] = jnp.concatenate(tiles, axis=1)
            for n, step in ((0, 1), (2, -1)):
                lane_ref[q, n] = jnp.concatenate([shifted(t, step).astype(BF16) for t in tiles], axis=1)
        for q, cut in enumerate(cuts):
            total = bias + dot(target_ref[...], lane_ref[q].reshape(3 * channels * BAND, cols * width))
            for side, other, start in ((0, q - 1, BAND - EDGE), (1, q + 1, 0)):
                if 0 <= other < len(cuts):
                    parts = [unband(lane_ref[other, n], channels)[:, start : start + EDGE] for n in range(3)]
                    total = total + dot(near_ref[side], jnp.concatenate([band(p) for p in parts], axis=0))
            for n, j in enumerate((0, cols - 1)):
                accrim_ref[:, i, n, cut] = unband(total[:, j * width : (j + 1) * width], channels)
            for j in range(1, cols - 1):
                accmid_ref[:, i, j - 1, cut] = unband(total[:, j * width : (j + 1) * width], channels)
        for a in range(3):
            r = i + a - 1
            if 0 <= r < rows:
                operator = middle_ref[...] if a == 1 else beside_ref[a // 2]
                add_sums(operator, lambda cut, b: [column(mid_ref, rim_ref, r, j + b, cut) for j in range(mids)], accmid_ref, i)


def add_sums(operator, tiles, acc_ref, i):
    channels, _, cols, depth, width = acc_ref.shape
    cuts = bands_of(depth)
    operand = jnp.concatenate([jnp.concatenate([t for cut in cuts for t in tiles(cut, b)], axis=1) for b in range(3)], axis=0)
    got = dot(operator, operand)
    for q, cut in enumerate(cuts):
        for j in range(cols):
            at = (q * cols + j) * width
            acc_ref[:, i, j, cut] += unband(got[:, at : at + width], channels)


def rest_body(
    mid_ref, rim_ref, side_ref, middle_ref, beside_ref, deep_ref, accmid_ref, accrim_ref, *rest
):
    *deep_halos, outmid_ref, outrim_ref = rest
    channels, rows, mids, depth, width = mid_ref.shape
    cols = mids + 2

    def around(r, j, cut):
        if j in (-1, cols):
            return band(side_ref[0 if j < 0 else 1, :, r, cut])
        return column(mid_ref, rim_ref, r, j, cut)

    for i in range(rows):
        for a in range(3):
            r = i + a - 1
            if 0 <= r < rows:
                operator = middle_ref[...] if a == 1 else beside_ref[a // 2]
                add_sums(operator, lambda cut, b: [around(r, j + b - 1, cut) for j in (0, cols - 1)], outrim_ref, i)
        odd = parity("trow")
        for n, halo_ref in enumerate(deep_halos):
            side = (1 - odd) if n == 0 else odd
            cut = pl.ds(pl.multiple_of(side * (depth - BAND), BAND), BAND)
            halo = three([halo_ref[i, :, j * width : (j + 1) * width] for j in range(cols)])
            halo = jnp.concatenate(halo, axis=0)
            if n == 1:
                halo = halo * has_second("trow").astype(F32)
            got = dot(deep_ref[side], halo.astype(BF16))
            for j in range(cols):
                acc_ref, at = (outrim_ref, j // (cols - 1)) if j in (0, cols - 1) else (outmid_ref, j - 1)
                acc_ref[:, i, at, cut] += unband(got[:, j * width : (j + 1) * width], channels)


def finished(x_ref, acc_ref, owed_refs, store):
    rows, cols = x_ref.shape[1:3]
    odd = parity("srow")
    paired = has_second("srow").astype(F32)
    for n, i in enumerate([(rows - 1) * (1 - odd), (rows - 1) * odd, *range(1, rows - 1)]):
        for j in range(cols):
            total = acc_ref[:, i, j]
            if n < 2:
                owed = owed_refs[n][:, j].astype(F32)
                total = total + (owed if n == 0 else owed * paired)
            store(i, j, (x_ref[:, i, j].astype(F32) + jnp.maximum(total, 0.0)).astype(BF16))


def sent_columns(rim_ref, col_refs):
    odd = parity("scol")
    for n, ref in zip((1 - odd, odd), col_refs):
        ref[...] = rim_ref[:, :, n]


def depth_body(mid_ref, rim_ref, after_ref, *deep_refs):
    channels, rows, mids, depth, _ = mid_ref.shape
    odd = parity("trow")
    shape = (channels, channels * BAND)
    first = lax.broadcasted_iota(jnp.int32, shape, 0) * BAND
    for n, ref in enumerate(deep_refs):
        end = (1 - odd) if n == 0 else odd
        cut = pl.ds(pl.multiple_of(end * (depth - BAND), BAND), BAND)
        pick = (lax.broadcasted_iota(jnp.int32, shape, 1) == first + end * (BAND - 1)).astype(BF16)
        for i in range(rows):
            tiles = [column(mid_ref, rim_ref, i, j, cut) for j in range(mids + 2)]
            ref[i] = dot(pick, jnp.concatenate(tiles, axis=1)).astype(BF16)


def mid_body(x_ref, acc_ref, a_ref, b_ref, out_ref):
    def store(i, j, value):
        out_ref[:, i, j] = value

    finished(x_ref, acc_ref, (a_ref, b_ref), store)


def next_body(x_ref, acc_ref, a_ref, b_ref, after_ref, out_ref, cola_ref, colb_ref):
    mid_body(x_ref, acc_ref, a_ref, b_ref, out_ref)
    sent_columns(out_ref, (cola_ref, colb_ref))


def last_body(mid_ref, rim_ref, acc_ref, a_ref, b_ref, out_ref, hold_ref, sems):
    rows, mids = mid_ref.shape[1:3]
    copies = []
    for i in range(rows):
        for j in range(mids):
            copy = pltpu.make_async_copy(mid_ref.at[:, i, j], out_ref.at[:, i, j + 1], sems.at[len(copies)])
            copy.start()
            copies.append(copy)

    def store(i, j, value):
        hold_ref[:, i, j] = value
        copy = pltpu.make_async_copy(hold_ref.at[:, i, j], out_ref.at[:, i, j * (mids + 1)], sems.at[len(copies)])
        copy.start()
        copies.append(copy)

    finished(rim_ref, acc_ref, (a_ref, b_ref), store)
    for copy in copies:
        copy.wait()


def open_body(parts, x_ref, src_w_ref, tgt_w_ref, bias_ref, *rest):
    src_ref, tgt_ref, held_ref, beside_ref, mid_ref, rim_ref, cola_ref, colb_ref, sems = rest
    rows, last = x_ref.shape[1], x_ref.shape[2] - 1
    pairs = [(src_w_ref, src_ref)]
    pairs += [(x_ref.at[:, i, n * last], rim_ref.at[:, i, n]) for i in range(rows) for n in range(2)]
    pairs += [(x_ref.at[:, i, j], mid_ref.at[:, i, j - 1]) for i in range(rows) for j in range(1, last)]
    pairs += [(tgt_w_ref, tgt_ref), (bias_ref, held_ref)]
    copies = [pltpu.make_async_copy(a, b, sems.at[n]) for n, (a, b) in enumerate(pairs)]
    for copy in copies:
        copy.start()
    copies[0].wait()
    operators(parts, src_ref, None, (beside_ref,))
    for copy in copies[1 : 1 + 2 * rows]:
        copy.wait()
    sent_columns(rim_ref, (cola_ref, colb_ref))
    for copy in copies[1 + 2 * rows :]:
        copy.wait()


def swaps(a, b, axis, other):
    count, across = lax.axis_size(axis), lax.axis_size(other)
    pairs = []
    for n in range(count):
        for m in range(across):
            if 0 < n < count - 1:
                target = (n + 1 if n % 2 else n - 1, m)
            else:
                target = (n, m ^ 1)
            pairs.append((n * across + m, target[0] * across + target[1]))
    got_a = lax.ppermute(a, axis, [(n, n ^ 1) for n in range(count)])
    return got_a, lax.ppermute(b, (axis, other), pairs)


def shards(volume, src_weight, tgt_weight, bias):
    layers = src_weight.shape[0]
    channels, rows, cols, depth, width = volume.shape
    axes = ("srow", "scol", "trow")
    counts = [lax.axis_size(n) for n in axes]
    assert all(count % 2 == 0 for count in counts) and rows > 1 and cols > 2
    src_w = jnp.transpose(src_weight, (0, 2, 3, 1))
    tgt_w = jnp.transpose(tgt_weight, (0, 2, 3, 1))
    deep_swaps = 1 if counts[2] == 2 else 2
    mid_shape, rim_shape = ((channels, rows, n, depth, width) for n in (cols - 2, 2))
    line = VMEM((channels, rows, depth, width), BF16)
    owed_mid, owed_rim = (VMEM((channels, n, depth, width), BF16) for n in (cols - 2, 2))
    sent = [VMEM(rim_shape, BF16), line, line]
    early = [("beside", 0)]
    src_w, tgt_w, bias, beside_0, mid, rim, col_a, col_b = call(
        functools.partial(open_body, early),
        [VMEM(src_w.shape, BF16), VMEM(tgt_w.shape, BF16), VMEM(bias.shape, F32)]
        + operator_shapes(early, channels)
        + [VMEM(mid_shape, BF16)]
        + sent,
        (volume, src_w, tgt_w, bias),
        {n: HBM for n in range(4)},
        scratch=[pltpu.SemaphoreType.DMA((3 + rows * cols,))],
    )
    made = {early[0]: beside_0}
    kinds = ("middle", "beside", "target", "near", "deep")
    for layer in range(layers):
        beside = swaps(col_a, col_b, "scol", "trow")
        sum_a, sum_b = call(inner_body, [owed_mid, owed_mid], (mid, rim, made["beside", layer]))
        inner = swaps(sum_a, sum_b, "srow", "scol")
        if layer == 0:
            late = [(kind, n) for n in range(layers) for kind in kinds]
            made |= build([part for part in late if part not in early], src_w, tgt_w, sum_b)
        operator = {kind: made[kind, layer] for kind in kinds}

        def own(after):
            return call(
                functools.partial(own_body, layer),
                [VMEM(mid_shape, F32), VMEM(rim_shape, F32)],
                (mid, rim, *(operator[kind] for kind in ("middle", "beside", "target", "near")), bias, after),
                {7: pl.ANY},
                scratch=[VMEM((depth // BAND, 3, channels * BAND, cols * width), BF16)],
            )

        accs = own(sum_b) if layer else None
        a, b, side = call(
            edge_body,
            [owed_rim, owed_rim, VMEM((2, *line.shape), BF16)],
            (mid, rim, *beside, operator["beside"], accs[0] if layer else operator["middle"]),
            {5: pl.ANY},
        )
        outer = swaps(a, b, "srow", "scol")
        deep = call(
            depth_body, [VMEM((rows, channels, cols * width), BF16)] * deep_swaps, (mid, rim, b), {2: pl.ANY}
        )
        if deep_swaps == 1:
            deeper = [lax.ppermute(deep[0], "trow", [(0, 1), (1, 0)])]
        else:
            deeper = swaps(*deep, "trow", "scol")
        accs = accs or own(b)
        acc_mid, acc_rim = call(
            rest_body,
            [VMEM(mid_shape, F32), VMEM(rim_shape, F32)],
            (mid, rim, side, *(operator[kind] for kind in ("middle", "beside", "deep")), *accs, *deeper),
            aliases={6: 0, 7: 1},
        )
        (mid,) = call(mid_body, [VMEM(mid_shape, BF16)], (mid, acc_mid, *inner))
        if layer < layers - 1:
            rim, col_a, col_b = call(next_body, sent, (rim, acc_rim, *outer, mid), {4: pl.ANY})
        else:
            (state,) = call(
                last_body,
                [jax.ShapeDtypeStruct(volume.shape, BF16)],
                (mid, rim, acc_rim, *outer),
                out_place=HBM,
                scratch=[VMEM(rim_shape, BF16), pltpu.SemaphoreType.DMA((rows * cols,))],
            )
    return state


def solution(mesh):
    return jax.shard_map(
        shards,
        mesh=mesh,
        in_specs=(P(None, "srow", "scol", "trow", None), P(), P(), P()),
        out_specs=P(None, "srow", "scol", "trow", None),
        check_vma=False,
    )
```

```python
import functools

import jax
import jax.numpy as jnp
from jax import lax
from jax.experimental import pallas as pl
from jax.experimental.pallas import tpu as pltpu
from jax.sharding import PartitionSpec as P

BAND = 32
EDGE = 16
SCOPED = 16 * 1024 * 1024
F32 = jnp.float32
BF16 = jnp.bfloat16
VMEM, HBM = pltpu.VMEM, pltpu.HBM
def parity(axis):
    return lax.axis_index(axis) % 2


def has_second(axis):
    at = lax.axis_index(axis)
    return (at > 0) & (at < lax.axis_size(axis) - 1)


def call(body, outs, args, places=None, out_place=VMEM, scratch=(), aliases=None):
    places = places or {}
    spaces = [places.get(n, VMEM) for n in range(len(args))]
    held = [pltpu.with_memory_space_constraint(a, m) if m in (VMEM, HBM) else a for a, m in zip(args, spaces)]
    return pl.pallas_call(
        body,
        out_shape=tuple(outs),
        in_specs=[pl.BlockSpec(memory_space=m) for m in spaces],
        out_specs=tuple(pl.BlockSpec(memory_space=out_place) for _ in outs),
        scratch_shapes=list(scratch),
        input_output_aliases=aliases or {},
        compiler_params=pltpu.CompilerParams(vmem_limit_bytes=SCOPED),
        cost_estimate=pl.CostEstimate(flops=10**6, bytes_accessed=10**4, transcendentals=0),
    )(*held)


def dot(a, b):
    return jnp.dot(a, b, preferred_element_type=F32)


def operators(parts, src_w_ref, tgt_w_ref, out_refs):
    channels = src_w_ref.shape[1]
    span, small = channels * BAND, channels * EDGE

    def columns(size):
        pick_c = lax.broadcasted_iota(jnp.int32, (channels, channels * size), 1) // size
        pick_r = lax.broadcasted_iota(jnp.int32, (channels, channels * size), 0)
        return (pick_c == pick_r).astype(BF16)

    wide, narrow, single = columns(BAND), columns(EDGE), columns(1)
    row = lax.broadcasted_iota(jnp.int32, (BAND, span), 0)
    shift = row - lax.broadcasted_iota(jnp.int32, (BAND, span), 1) % BAND
    row_s = lax.broadcasted_iota(jnp.int32, (BAND, small), 0)
    col_s = lax.broadcasted_iota(jnp.int32, (BAND, small), 1) % EDGE
    near = ((row_s == 0) & (col_s == EDGE - 1), (row_s == BAND - 1) & (col_s == 0))
    row_1 = lax.broadcasted_iota(jnp.int32, (BAND, channels), 0)
    deep = (row_1 == 0, row_1 == BAND - 1)
    spread = {}

    def taps(ref, layer, o, pick, key):
        key = (key, layer, o)
        if key not in spread:
            spread[key] = lax.dot_general(ref[layer, o], pick, (((0,), (0,)), ((), ())), preferred_element_type=F32)
        return spread[key]

    for (kind, layer), out_ref in zip(parts, out_refs):
        for o in range(channels):
            rows = slice(o * BAND, (o + 1) * BAND)
            for b in range(3):
                if kind == "middle":
                    got = taps(src_w_ref, layer, o, wide, "s")
                    values = {(): jnp.where(shift == 0, got[3 + b][None, :], 0.0)}
                elif kind == "beside":
                    got = taps(src_w_ref, layer, o, wide, "s")
                    values = {(n,): jnp.where(shift == 0, got[6 * n + b][None, :], 0.0) for n in range(2)}
                elif kind == "target":
                    got = taps(tgt_w_ref, layer, o, wide, "t")
                    value = jnp.where(shift == 1, got[b][None, :], 0.0)
                    value = jnp.where(shift == 0, got[3 + b][None, :], value)
                    values = {(): jnp.where(shift == -1, got[6 + b][None, :], value)}
                else:
                    pick, at = (narrow, near) if kind == "near" else (single, deep)
                    got = taps(tgt_w_ref, layer, o, pick, kind)
                    values = {(n,): jnp.where(at[n], got[6 * n + b][None, :], 0.0) for n in range(2)}
                for index, value in values.items():
                    size = value.shape[1]
                    out_ref[(*index, rows, slice(b * size, (b + 1) * size))] = value.astype(BF16)


def operator_shapes(parts, channels):
    span = channels * BAND
    widths = dict(middle=span, beside=span, target=span, near=channels * EDGE, deep=channels)
    lead = dict(middle=(), beside=(2,), target=(), near=(2,), deep=(2,))
    return [VMEM((*lead[kind], span, 3 * widths[kind]), BF16) for kind, _ in parts]


def build_body(parts, src_w_ref, tgt_w_ref, after_ref, *out_refs):
    operators(parts, src_w_ref, tgt_w_ref, out_refs)


def build(parts, src_w, tgt_w, after):
    got = call(
        functools.partial(build_body, parts),
        operator_shapes(parts, src_w.shape[1]),
        (src_w, tgt_w, after),
        {2: pl.ANY},
    )
    return dict(zip(parts, got))


def band(tile):
    channels, size, width = tile.shape
    return tile.reshape(channels * size, width)


def unband(tile, channels):
    return tile.reshape(channels, tile.shape[0] // channels, tile.shape[1])


def src_operand(tiles, cols):
    return jnp.concatenate([jnp.concatenate(tiles[b : b + cols], axis=1) for b in range(3)], axis=0)


def sent_rows(rows):
    odd = parity("srow")
    return ((rows - 1) * (1 - odd), odd), ((rows - 1) * odd, 1 - odd)


def column(mid_ref, rim_ref, i, j, cut):
    last = mid_ref.shape[2] + 1
    return band(rim_ref[:, i, j // last, cut] if j in (0, last) else mid_ref[:, i, j - 1, cut])


def bands_of(depth):
    return [slice(start, start + BAND) for start in range(0, depth, BAND)]


def owed_sums(operator, tiles, out_ref):
    channels, cols, depth, width = out_ref.shape
    cuts = bands_of(depth)
    operand = jnp.concatenate([jnp.concatenate([t for cut in cuts for t in tiles(cut, b)], axis=1) for b in range(3)], axis=0)
    got = dot(operator, operand).astype(BF16)
    for q, cut in enumerate(cuts):
        for j in range(cols):
            at = (q * cols + j) * width
            out_ref[:, j, cut] = unband(got[:, at : at + width], channels)


def inner_body(mid_ref, rim_ref, beside_ref, *out_refs):
    rows, cols = mid_ref.shape[1:3]
    for (i, side), out_ref in zip(sent_rows(rows), out_refs):
        owed_sums(
            beside_ref[side], lambda cut, b: [column(mid_ref, rim_ref, i, j + b, cut) for j in range(cols)], out_ref
        )


def edge_body(mid_ref, rim_ref, cola_ref, colb_ref, beside_ref, after_ref, a_ref, b_ref, side_ref):
    rows, cols = mid_ref.shape[1], mid_ref.shape[2] + 2
    odd, paired = parity("scol"), has_second("scol")
    side_ref[1 - odd] = cola_ref[...]

    @pl.when(paired)
    def _():
        side_ref[odd] = colb_ref[...]

    @pl.when(jnp.logical_not(paired))
    def _():
        side_ref[odd] = jnp.zeros_like(colb_ref)

    def around(i, j, cut):
        if j in (-1, cols):
            return band(side_ref[0 if j < 0 else 1, :, i, cut])
        return column(mid_ref, rim_ref, i, j, cut)

    for (i, side), out_ref in zip(sent_rows(rows), (a_ref, b_ref)):
        owed_sums(beside_ref[side], lambda cut, b: [around(i, j + b - 1, cut) for j in (0, cols - 1)], out_ref)


def shifted(tile, step):
    lane = lax.broadcasted_iota(jnp.int32, tile.shape, 1)
    width = tile.shape[1]
    rolled = pltpu.roll(tile.astype(F32), step % width, 1)
    gone = 0 if step == 1 else width - 1
    return jnp.where(lane == gone, 0.0, rolled)


def three(tiles):
    return [jnp.concatenate([shifted(t, step) if step else t.astype(F32) for t in tiles], axis=1) for step in (1, 0, -1)]


def own_body(
    layer, mid_ref, rim_ref, middle_ref, beside_ref, target_ref, near_ref, bias_ref, after_ref, accmid_ref, accrim_ref, lane_ref
):
    channels, rows, mids, depth, width = mid_ref.shape
    cols = mids + 2
    cuts = bands_of(depth)
    shape = (BAND, cols * width)
    bias = [jnp.broadcast_to(bias_ref[layer : layer + 1, o : o + 1], shape) for o in range(channels)]
    bias = jnp.concatenate(bias, axis=0)
    for i in range(rows):
        for q, cut in enumerate(cuts):
            tiles = [column(mid_ref, rim_ref, i, j, cut) for j in range(cols)]
            lane_ref[q, 1] = jnp.concatenate(tiles, axis=1)
            for n, step in ((0, 1), (2, -1)):
                lane_ref[q, n] = jnp.concatenate([shifted(t, step).astype(BF16) for t in tiles], axis=1)
        for q, cut in enumerate(cuts):
            total = bias + dot(target_ref[...], lane_ref[q].reshape(3 * channels * BAND, cols * width))
            for side, other, start in ((0, q - 1, BAND - EDGE), (1, q + 1, 0)):
                if 0 <= other < len(cuts):
                    parts = [unband(lane_ref[other, n], channels)[:, start : start + EDGE] for n in range(3)]
                    total = total + dot(near_ref[side], jnp.concatenate([band(p) for p in parts], axis=0))
            for n, j in enumerate((0, cols - 1)):
                accrim_ref[:, i, n, cut] = unband(total[:, j * width : (j + 1) * width], channels)
            for j in range(1, cols - 1):
                accmid_ref[:, i, j - 1, cut] = unband(total[:, j * width : (j + 1) * width], channels)
        for a in range(3):
            r = i + a - 1
            if 0 <= r < rows:
                operator = middle_ref[...] if a == 1 else beside_ref[a // 2]
                add_sums(operator, lambda cut, b: [column(mid_ref, rim_ref, r, j + b, cut) for j in range(mids)], accmid_ref, i)


def add_sums(operator, tiles, acc_ref, i):
    channels, _, cols, depth, width = acc_ref.shape
    cuts = bands_of(depth)
    operand = jnp.concatenate([jnp.concatenate([t for cut in cuts for t in tiles(cut, b)], axis=1) for b in range(3)], axis=0)
    got = dot(operator, operand)
    for q, cut in enumerate(cuts):
        for j in range(cols):
            at = (q * cols + j) * width
            acc_ref[:, i, j, cut] += unband(got[:, at : at + width], channels)


def rest_body(
    mid_ref, rim_ref, side_ref, middle_ref, beside_ref, deep_ref, accmid_ref, accrim_ref, *rest
):
    *deep_halos, outmid_ref, outrim_ref = rest
    channels, rows, mids, depth, width = mid_ref.shape
    cols = mids + 2

    def around(r, j, cut):
        if j in (-1, cols):
            return band(side_ref[0 if j < 0 else 1, :, r, cut])
        return column(mid_ref, rim_ref, r, j, cut)

    for i in range(rows):
        for a in range(3):
            r = i + a - 1
            if 0 <= r < rows:
                operator = middle_ref[...] if a == 1 else beside_ref[a // 2]
                add_sums(operator, lambda cut, b: [around(r, j + b - 1, cut) for j in (0, cols - 1)], outrim_ref, i)
        odd = parity("trow")
        for n, halo_ref in enumerate(deep_halos):
            side = (1 - odd) if n == 0 else odd
            cut = pl.ds(pl.multiple_of(side * (depth - BAND), BAND), BAND)
            halo = three([halo_ref[i, :, j * width : (j + 1) * width] for j in range(cols)])
            halo = jnp.concatenate(halo, axis=0)
            if n == 1:
                halo = halo * has_second("trow").astype(F32)
            got = dot(deep_ref[side], halo.astype(BF16))
            for j in range(cols):
                acc_ref, at = (outrim_ref, j // (cols - 1)) if j in (0, cols - 1) else (outmid_ref, j - 1)
                acc_ref[:, i, at, cut] += unband(got[:, j * width : (j + 1) * width], channels)


def finished(x_ref, acc_ref, owed_refs, store):
    rows, cols = x_ref.shape[1:3]
    odd = parity("srow")
    paired = has_second("srow").astype(F32)
    for n, i in enumerate([(rows - 1) * (1 - odd), (rows - 1) * odd, *range(1, rows - 1)]):
        for j in range(cols):
            total = acc_ref[:, i, j]
            if n < 2:
                owed = owed_refs[n][:, j].astype(F32)
                total = total + (owed if n == 0 else owed * paired)
            store(i, j, (x_ref[:, i, j].astype(F32) + jnp.maximum(total, 0.0)).astype(BF16))


def sent_columns(rim_ref, col_refs):
    odd = parity("scol")
    for n, ref in zip((1 - odd, odd), col_refs):
        ref[...] = rim_ref[:, :, n]


def depth_body(mid_ref, rim_ref, after_ref, *deep_refs):
    channels, rows, mids, depth, _ = mid_ref.shape
    odd = parity("trow")
    shape = (channels, channels * BAND)
    first = lax.broadcasted_iota(jnp.int32, shape, 0) * BAND
    for n, ref in enumerate(deep_refs):
        end = (1 - odd) if n == 0 else odd
        cut = pl.ds(pl.multiple_of(end * (depth - BAND), BAND), BAND)
        pick = (lax.broadcasted_iota(jnp.int32, shape, 1) == first + end * (BAND - 1)).astype(BF16)
        for i in range(rows):
            tiles = [column(mid_ref, rim_ref, i, j, cut) for j in range(mids + 2)]
            ref[i] = dot(pick, jnp.concatenate(tiles, axis=1)).astype(BF16)


def mid_body(x_ref, acc_ref, a_ref, b_ref, out_ref):
    def store(i, j, value):
        out_ref[:, i, j] = value

    finished(x_ref, acc_ref, (a_ref, b_ref), store)


def next_body(x_ref, acc_ref, a_ref, b_ref, after_ref, out_ref, cola_ref, colb_ref):
    mid_body(x_ref, acc_ref, a_ref, b_ref, out_ref)
    sent_columns(out_ref, (cola_ref, colb_ref))


def last_body(mid_ref, rim_ref, acc_ref, a_ref, b_ref, out_ref, hold_ref, sems):
    rows, mids = mid_ref.shape[1:3]
    copies = []
    for i in range(rows):
        for j in range(mids):
            copy = pltpu.make_async_copy(mid_ref.at[:, i, j], out_ref.at[:, i, j + 1], sems.at[len(copies)])
            copy.start()
            copies.append(copy)

    def store(i, j, value):
        hold_ref[:, i, j] = value
        copy = pltpu.make_async_copy(hold_ref.at[:, i, j], out_ref.at[:, i, j * (mids + 1)], sems.at[len(copies)])
        copy.start()
        copies.append(copy)

    finished(rim_ref, acc_ref, (a_ref, b_ref), store)
    for copy in copies:
        copy.wait()


def open_body(parts, x_ref, src_w_ref, tgt_w_ref, bias_ref, *rest):
    src_ref, tgt_ref, held_ref, beside_ref, mid_ref, rim_ref, cola_ref, colb_ref, sems = rest
    rows, last = x_ref.shape[1], x_ref.shape[2] - 1
    pairs = [(src_w_ref, src_ref)]
    pairs += [(x_ref.at[:, i, n * last], rim_ref.at[:, i, n]) for i in range(rows) for n in range(2)]
    pairs += [(x_ref.at[:, i, j], mid_ref.at[:, i, j - 1]) for i in range(rows) for j in range(1, last)]
    pairs += [(tgt_w_ref, tgt_ref), (bias_ref, held_ref)]
    copies = [pltpu.make_async_copy(a, b, sems.at[n]) for n, (a, b) in enumerate(pairs)]
    for copy in copies:
        copy.start()
    copies[0].wait()
    operators(parts, src_ref, None, (beside_ref,))
    for copy in copies[1 : 1 + 2 * rows]:
        copy.wait()
    sent_columns(rim_ref, (cola_ref, colb_ref))
    for copy in copies[1 + 2 * rows :]:
        copy.wait()


def swaps(a, b, axis, other):
    count, across = lax.axis_size(axis), lax.axis_size(other)
    pairs = []
    for n in range(count):
        for m in range(across):
            if 0 < n < count - 1:
                target = (n + 1 if n % 2 else n - 1, m)
            else:
                target = (n, m ^ 1)
            pairs.append((n * across + m, target[0] * across + target[1]))
    got_a = lax.ppermute(a, axis, [(n, n ^ 1) for n in range(count)])
    return got_a, lax.ppermute(b, (axis, other), pairs)


def shards(volume, src_weight, tgt_weight, bias):
    layers = src_weight.shape[0]
    channels, rows, cols, depth, width = volume.shape
    axes = ("srow", "scol", "trow")
    counts = [lax.axis_size(n) for n in axes]
    assert all(count % 2 == 0 for count in counts) and rows > 1 and cols > 2
    src_w = jnp.transpose(src_weight, (0, 2, 3, 1))
    tgt_w = jnp.transpose(tgt_weight, (0, 2, 3, 1))
    deep_swaps = 1 if counts[2] == 2 else 2
    mid_shape, rim_shape = ((channels, rows, n, depth, width) for n in (cols - 2, 2))
    line = VMEM((channels, rows, depth, width), BF16)
    owed_mid, owed_rim = (VMEM((channels, n, depth, width), BF16) for n in (cols - 2, 2))
    sent = [VMEM(rim_shape, BF16), line, line]
    early = [("beside", 0)]
    src_w, tgt_w, bias, beside_0, mid, rim, col_a, col_b = call(
        functools.partial(open_body, early),
        [VMEM(src_w.shape, BF16), VMEM(tgt_w.shape, BF16), VMEM(bias.shape, F32)]
        + operator_shapes(early, channels)
        + [VMEM(mid_shape, BF16)]
        + sent,
        (volume, src_w, tgt_w, bias),
        {n: HBM for n in range(4)},
        scratch=[pltpu.SemaphoreType.DMA((3 + rows * cols,))],
    )
    made = {early[0]: beside_0}
    kinds = ("middle", "beside", "target", "near", "deep")
    for layer in range(layers):
        beside = swaps(col_a, col_b, "scol", "trow")
        sum_a, sum_b = call(inner_body, [owed_mid, owed_mid], (mid, rim, made["beside", layer]))
        inner = swaps(sum_a, sum_b, "srow", "scol")
        if layer == 0:
            late = [(kind, n) for n in range(layers) for kind in kinds]
            made |= build([part for part in late if part not in early], src_w, tgt_w, sum_a)
        operator = {kind: made[kind, layer] for kind in kinds}

        def own(after):
            return call(
                functools.partial(own_body, layer),
                [VMEM(mid_shape, F32), VMEM(rim_shape, F32)],
                (mid, rim, *(operator[kind] for kind in ("middle", "beside", "target", "near")), bias, after),
                {7: pl.ANY},
                scratch=[VMEM((depth // BAND, 3, channels * BAND, cols * width), BF16)],
            )

        accs = own(sum_a) if layer else None
        a, b, side = call(
            edge_body,
            [owed_rim, owed_rim, VMEM((2, *line.shape), BF16)],
            (mid, rim, *beside, operator["beside"], accs[0] if layer else operator["middle"]),
            {5: pl.ANY},
        )
        outer = swaps(a, b, "srow", "scol")
        deep = call(
            depth_body, [VMEM((rows, channels, cols * width), BF16)] * deep_swaps, (mid, rim, a), {2: pl.ANY}
        )
        if deep_swaps == 1:
            deeper = [lax.ppermute(deep[0], "trow", [(0, 1), (1, 0)])]
        else:
            deeper = swaps(*deep, "trow", "scol")
        accs = accs or own(a)
        acc_mid, acc_rim = call(
            rest_body,
            [VMEM(mid_shape, F32), VMEM(rim_shape, F32)],
            (mid, rim, side, *(operator[kind] for kind in ("middle", "beside", "deep")), *accs, *deeper),
            aliases={6: 0, 7: 1},
        )
        (mid,) = call(mid_body, [VMEM(mid_shape, BF16)], (mid, acc_mid, *inner))
        if layer < layers - 1:
            rim, col_a, col_b = call(next_body, sent, (rim, acc_rim, *outer, mid), {4: pl.ANY})
        else:
            (state,) = call(
                last_body,
                [jax.ShapeDtypeStruct(volume.shape, BF16)],
                (mid, rim, acc_rim, *outer),
                out_place=HBM,
                scratch=[VMEM(rim_shape, BF16), pltpu.SemaphoreType.DMA((rows * cols,))],
            )
    return state


def solution(mesh):
    return jax.shard_map(
        shards,
        mesh=mesh,
        in_specs=(P(None, "srow", "scol", "trow", None), P(), P(), P()),
        out_specs=P(None, "srow", "scol", "trow", None),
        check_vma=False,
    )
```

```python
import functools

import jax
import jax.numpy as jnp
from jax import lax
from jax.experimental import pallas as pl
from jax.experimental.pallas import tpu as pltpu
from jax.sharding import PartitionSpec as P

BAND = 32
EDGE = 16
SCOPED = 16 * 1024 * 1024
F32 = jnp.float32
BF16 = jnp.bfloat16
VMEM, HBM = pltpu.VMEM, pltpu.HBM
def parity(axis):
    return lax.axis_index(axis) % 2


def has_second(axis):
    at = lax.axis_index(axis)
    return (at > 0) & (at < lax.axis_size(axis) - 1)


def call(body, outs, args, places=None, out_place=VMEM, scratch=(), aliases=None):
    places = places or {}
    spaces = [places.get(n, VMEM) for n in range(len(args))]
    held = [pltpu.with_memory_space_constraint(a, m) if m in (VMEM, HBM) else a for a, m in zip(args, spaces)]
    return pl.pallas_call(
        body,
        out_shape=tuple(outs),
        in_specs=[pl.BlockSpec(memory_space=m) for m in spaces],
        out_specs=tuple(pl.BlockSpec(memory_space=out_place) for _ in outs),
        scratch_shapes=list(scratch),
        input_output_aliases=aliases or {},
        compiler_params=pltpu.CompilerParams(vmem_limit_bytes=SCOPED),
        cost_estimate=pl.CostEstimate(flops=10**6, bytes_accessed=10**4, transcendentals=0),
    )(*held)


def dot(a, b):
    return jnp.dot(a, b, preferred_element_type=F32)


def operators(parts, src_w_ref, tgt_w_ref, out_refs):
    channels = src_w_ref.shape[1]
    span, small = channels * BAND, channels * EDGE

    def columns(size):
        pick_c = lax.broadcasted_iota(jnp.int32, (channels, channels * size), 1) // size
        pick_r = lax.broadcasted_iota(jnp.int32, (channels, channels * size), 0)
        return (pick_c == pick_r).astype(BF16)

    wide, narrow, single = columns(BAND), columns(EDGE), columns(1)
    row = lax.broadcasted_iota(jnp.int32, (BAND, span), 0)
    shift = row - lax.broadcasted_iota(jnp.int32, (BAND, span), 1) % BAND
    row_s = lax.broadcasted_iota(jnp.int32, (BAND, small), 0)
    col_s = lax.broadcasted_iota(jnp.int32, (BAND, small), 1) % EDGE
    near = ((row_s == 0) & (col_s == EDGE - 1), (row_s == BAND - 1) & (col_s == 0))
    row_1 = lax.broadcasted_iota(jnp.int32, (BAND, channels), 0)
    deep = (row_1 == 0, row_1 == BAND - 1)
    spread = {}

    def taps(ref, layer, o, pick, key):
        key = (key, layer, o)
        if key not in spread:
            spread[key] = lax.dot_general(ref[layer, o], pick, (((0,), (0,)), ((), ())), preferred_element_type=F32)
        return spread[key]

    for (kind, layer), out_ref in zip(parts, out_refs):
        for o in range(channels):
            rows = slice(o * BAND, (o + 1) * BAND)
            for b in range(3):
                if kind == "middle":
                    got = taps(src_w_ref, layer, o, wide, "s")
                    values = {(): jnp.where(shift == 0, got[3 + b][None, :], 0.0)}
                elif kind == "beside":
                    got = taps(src_w_ref, layer, o, wide, "s")
                    values = {(n,): jnp.where(shift == 0, got[6 * n + b][None, :], 0.0) for n in range(2)}
                elif kind == "target":
                    got = taps(tgt_w_ref, layer, o, wide, "t")
                    value = jnp.where(shift == 1, got[b][None, :], 0.0)
                    value = jnp.where(shift == 0, got[3 + b][None, :], value)
                    values = {(): jnp.where(shift == -1, got[6 + b][None, :], value)}
                else:
                    pick, at = (narrow, near) if kind == "near" else (single, deep)
                    got = taps(tgt_w_ref, layer, o, pick, kind)
                    values = {(n,): jnp.where(at[n], got[6 * n + b][None, :], 0.0) for n in range(2)}
                for index, value in values.items():
                    size = value.shape[1]
                    out_ref[(*index, rows, slice(b * size, (b + 1) * size))] = value.astype(BF16)


def operator_shapes(parts, channels):
    span = channels * BAND
    widths = dict(middle=span, beside=span, target=span, near=channels * EDGE, deep=channels)
    lead = dict(middle=(), beside=(2,), target=(), near=(2,), deep=(2,))
    return [VMEM((*lead[kind], span, 3 * widths[kind]), BF16) for kind, _ in parts]


def build_body(parts, src_w_ref, tgt_w_ref, after_ref, *out_refs):
    operators(parts, src_w_ref, tgt_w_ref, out_refs)


def build(parts, src_w, tgt_w, after):
    got = call(
        functools.partial(build_body, parts),
        operator_shapes(parts, src_w.shape[1]),
        (src_w, tgt_w, after),
        {2: pl.ANY},
    )
    return dict(zip(parts, got))


def band(tile):
    channels, size, width = tile.shape
    return tile.reshape(channels * size, width)


def unband(tile, channels):
    return tile.reshape(channels, tile.shape[0] // channels, tile.shape[1])


def src_operand(tiles, cols):
    return jnp.concatenate([jnp.concatenate(tiles[b : b + cols], axis=1) for b in range(3)], axis=0)


def sent_rows(rows):
    odd = parity("srow")
    return ((rows - 1) * (1 - odd), odd), ((rows - 1) * odd, 1 - odd)


def column(mid_ref, rim_ref, i, j, cut):
    last = mid_ref.shape[2] + 1
    return band(rim_ref[:, i, j // last, cut] if j in (0, last) else mid_ref[:, i, j - 1, cut])


def bands_of(depth):
    return [slice(start, start + BAND) for start in range(0, depth, BAND)]


def owed_sums(operator, tiles, out_ref):
    channels, cols, depth, width = out_ref.shape
    cuts = bands_of(depth)
    operand = jnp.concatenate([jnp.concatenate([t for cut in cuts for t in tiles(cut, b)], axis=1) for b in range(3)], axis=0)
    got = dot(operator, operand).astype(BF16)
    for q, cut in enumerate(cuts):
        for j in range(cols):
            at = (q * cols + j) * width
            out_ref[:, j, cut] = unband(got[:, at : at + width], channels)


def inner_body(which, mid_ref, rim_ref, beside_ref, *out_refs):
    rows, cols = mid_ref.shape[1:3]
    for n, out_ref in zip(which, out_refs):
        i, side = sent_rows(rows)[n]
        owed_sums(
            beside_ref[side], lambda cut, b: [column(mid_ref, rim_ref, i, j + b, cut) for j in range(cols)], out_ref
        )


def part_body(mid_ref, rim_ref, beside_ref, after_ref, *part_refs):
    rows, cols = mid_ref.shape[1], mid_ref.shape[2] + 2
    cuts = bands_of(mid_ref.shape[3])
    for (i, side), part_ref in zip(sent_rows(rows), part_refs):
        span = part_ref.shape[1]
        for n, (first, j) in enumerate(((1, 0), (0, cols - 2))):
            tiles = [jnp.concatenate([column(mid_ref, rim_ref, i, j + b, cut) for cut in cuts], axis=1) for b in range(2)]
            operator = beside_ref[side, :, first * span : (first + 2) * span]
            part_ref[n] = dot(operator, jnp.concatenate(tiles, axis=0))


def edge_body(cola_ref, colb_ref, beside_ref, parta_ref, partb_ref, after_ref, a_ref, b_ref, side_ref):
    channels, rows, depth, width = cola_ref.shape
    odd, paired = parity("scol"), has_second("scol")
    side_ref[1 - odd] = cola_ref[...]

    @pl.when(paired)
    def _():
        side_ref[odd] = colb_ref[...]

    @pl.when(jnp.logical_not(paired))
    def _():
        side_ref[odd] = jnp.zeros_like(colb_ref)

    cuts = bands_of(depth)
    for (i, side), part_ref, out_ref in zip(sent_rows(rows), (parta_ref, partb_ref), (a_ref, b_ref)):
        span = part_ref.shape[1]
        for n, tap in enumerate((0, 2)):
            halo = jnp.concatenate([band(side_ref[n, :, i, cut]) for cut in cuts], axis=1)
            got = (part_ref[n] + dot(beside_ref[side, :, tap * span : (tap + 1) * span], halo)).astype(BF16)
            for q, cut in enumerate(cuts):
                out_ref[:, n, cut] = unband(got[:, q * width : (q + 1) * width], channels)


def shifted(tile, step):
    lane = lax.broadcasted_iota(jnp.int32, tile.shape, 1)
    width = tile.shape[1]
    rolled = pltpu.roll(tile.astype(F32), step % width, 1)
    gone = 0 if step == 1 else width - 1
    return jnp.where(lane == gone, 0.0, rolled)


def three(tiles):
    return [jnp.concatenate([shifted(t, step) if step else t.astype(F32) for t in tiles], axis=1) for step in (1, 0, -1)]


def own_body(
    layer, mid_ref, rim_ref, middle_ref, beside_ref, target_ref, near_ref, bias_ref, after_ref, accmid_ref, accrim_ref, lane_ref
):
    channels, rows, mids, depth, width = mid_ref.shape
    cols = mids + 2
    cuts = bands_of(depth)
    shape = (BAND, cols * width)
    bias = [jnp.broadcast_to(bias_ref[layer : layer + 1, o : o + 1], shape) for o in range(channels)]
    bias = jnp.concatenate(bias, axis=0)
    for i in range(rows):
        for q, cut in enumerate(cuts):
            tiles = [column(mid_ref, rim_ref, i, j, cut) for j in range(cols)]
            lane_ref[q, 1] = jnp.concatenate(tiles, axis=1)
            for n, step in ((0, 1), (2, -1)):
                lane_ref[q, n] = jnp.concatenate([shifted(t, step).astype(BF16) for t in tiles], axis=1)
        for q, cut in enumerate(cuts):
            total = bias + dot(target_ref[...], lane_ref[q].reshape(3 * channels * BAND, cols * width))
            for side, other, start in ((0, q - 1, BAND - EDGE), (1, q + 1, 0)):
                if 0 <= other < len(cuts):
                    parts = [unband(lane_ref[other, n], channels)[:, start : start + EDGE] for n in range(3)]
                    total = total + dot(near_ref[side], jnp.concatenate([band(p) for p in parts], axis=0))
            for n, j in enumerate((0, cols - 1)):
                accrim_ref[:, i, n, cut] = unband(total[:, j * width : (j + 1) * width], channels)
            for j in range(1, cols - 1):
                accmid_ref[:, i, j - 1, cut] = unband(total[:, j * width : (j + 1) * width], channels)
        for a in range(3):
            r = i + a - 1
            if 0 <= r < rows:
                operator = middle_ref[...] if a == 1 else beside_ref[a // 2]
                add_sums(operator, lambda cut, b: [column(mid_ref, rim_ref, r, j + b, cut) for j in range(mids)], accmid_ref, i)


def add_sums(operator, tiles, acc_ref, i):
    channels, _, cols, depth, width = acc_ref.shape
    cuts = bands_of(depth)
    operand = jnp.concatenate([jnp.concatenate([t for cut in cuts for t in tiles(cut, b)], axis=1) for b in range(3)], axis=0)
    got = dot(operator, operand)
    for q, cut in enumerate(cuts):
        for j in range(cols):
            at = (q * cols + j) * width
            acc_ref[:, i, j, cut] += unband(got[:, at : at + width], channels)


def rest_body(
    mid_ref, rim_ref, side_ref, middle_ref, beside_ref, deep_ref, accmid_ref, accrim_ref, *rest
):
    *deep_halos, outmid_ref, outrim_ref = rest
    channels, rows, mids, depth, width = mid_ref.shape
    cols = mids + 2

    def around(r, j, cut):
        if j in (-1, cols):
            return band(side_ref[0 if j < 0 else 1, :, r, cut])
        return column(mid_ref, rim_ref, r, j, cut)

    for i in range(rows):
        for a in range(3):
            r = i + a - 1
            if 0 <= r < rows:
                operator = middle_ref[...] if a == 1 else beside_ref[a // 2]
                add_sums(operator, lambda cut, b: [around(r, j + b - 1, cut) for j in (0, cols - 1)], outrim_ref, i)
        odd = parity("trow")
        for n, halo_ref in enumerate(deep_halos):
            side = (1 - odd) if n == 0 else odd
            cut = pl.ds(pl.multiple_of(side * (depth - BAND), BAND), BAND)
            halo = three([halo_ref[i, :, j * width : (j + 1) * width] for j in range(cols)])
            halo = jnp.concatenate(halo, axis=0)
            if n == 1:
                halo = halo * has_second("trow").astype(F32)
            got = dot(deep_ref[side], halo.astype(BF16))
            for j in range(cols):
                acc_ref, at = (outrim_ref, j // (cols - 1)) if j in (0, cols - 1) else (outmid_ref, j - 1)
                acc_ref[:, i, at, cut] += unband(got[:, j * width : (j + 1) * width], channels)


def finished(x_ref, acc_ref, owed_refs, store):
    rows, cols = x_ref.shape[1:3]
    odd = parity("srow")
    paired = has_second("srow").astype(F32)
    for n, i in enumerate([(rows - 1) * (1 - odd), (rows - 1) * odd, *range(1, rows - 1)]):
        if n < 2 and owed_refs[n] is None:
            continue
        for j in range(cols):
            total = acc_ref[:, i, j]
            if n < 2:
                owed = owed_refs[n][:, j].astype(F32)
                total = total + (owed if n == 0 else owed * paired)
            store(i, j, (x_ref[:, i, j].astype(F32) + jnp.maximum(total, 0.0)).astype(BF16))


def sent_columns(rim_ref, col_refs):
    odd = parity("scol")
    for n, ref in zip((1 - odd, odd), col_refs):
        ref[...] = rim_ref[:, :, n]


def depth_body(mid_ref, rim_ref, after_ref, *deep_refs):
    channels, rows, mids, depth, _ = mid_ref.shape
    odd = parity("trow")
    shape = (channels, channels * BAND)
    first = lax.broadcasted_iota(jnp.int32, shape, 0) * BAND
    for n, ref in enumerate(deep_refs):
        end = (1 - odd) if n == 0 else odd
        cut = pl.ds(pl.multiple_of(end * (depth - BAND), BAND), BAND)
        pick = (lax.broadcasted_iota(jnp.int32, shape, 1) == first + end * (BAND - 1)).astype(BF16)
        for i in range(rows):
            tiles = [column(mid_ref, rim_ref, i, j, cut) for j in range(mids + 2)]
            ref[i] = dot(pick, jnp.concatenate(tiles, axis=1)).astype(BF16)


def mid_body(x_ref, acc_ref, a_ref, b_ref, out_ref):
    def store(i, j, value):
        out_ref[:, i, j] = value

    finished(x_ref, acc_ref, (a_ref, b_ref), store)


def begin_body(x_ref, acc_ref, a_ref, after_ref, out_ref):
    mid_body(x_ref, acc_ref, a_ref, None, out_ref)


def next_body(x_ref, acc_ref, b_ref, begun_ref, after_ref, out_ref, cola_ref, colb_ref):
    mid_body(x_ref, acc_ref, None, b_ref, out_ref)
    sent_columns(out_ref, (cola_ref, colb_ref))


def last_body(mid_ref, rim_ref, acc_ref, a_ref, b_ref, out_ref, hold_ref, sems):
    rows, mids = mid_ref.shape[1:3]
    copies = []
    for i in range(rows):
        for j in range(mids):
            copy = pltpu.make_async_copy(mid_ref.at[:, i, j], out_ref.at[:, i, j + 1], sems.at[len(copies)])
            copy.start()
            copies.append(copy)

    def store(i, j, value):
        hold_ref[:, i, j] = value
        copy = pltpu.make_async_copy(hold_ref.at[:, i, j], out_ref.at[:, i, j * (mids + 1)], sems.at[len(copies)])
        copy.start()
        copies.append(copy)

    finished(rim_ref, acc_ref, (a_ref, b_ref), store)
    for copy in copies:
        copy.wait()


def open_body(parts, x_ref, src_w_ref, tgt_w_ref, bias_ref, *rest):
    src_ref, tgt_ref, held_ref, beside_ref, mid_ref, rim_ref, cola_ref, colb_ref, sems = rest
    rows, last = x_ref.shape[1], x_ref.shape[2] - 1
    pairs = [(src_w_ref, src_ref)]
    pairs += [(x_ref.at[:, i, n * last], rim_ref.at[:, i, n]) for i in range(rows) for n in range(2)]
    pairs += [(x_ref.at[:, i, j], mid_ref.at[:, i, j - 1]) for i in range(rows) for j in range(1, last)]
    pairs += [(tgt_w_ref, tgt_ref), (bias_ref, held_ref)]
    copies = [pltpu.make_async_copy(a, b, sems.at[n]) for n, (a, b) in enumerate(pairs)]
    for copy in copies:
        copy.start()
    copies[0].wait()
    operators(parts, src_ref, None, (beside_ref,))
    for copy in copies[1 : 1 + 2 * rows]:
        copy.wait()
    sent_columns(rim_ref, (cola_ref, colb_ref))
    for copy in copies[1 + 2 * rows :]:
        copy.wait()


def swap_first(value, axis):
    return lax.ppermute(value, axis, [(n, n ^ 1) for n in range(lax.axis_size(axis))])


def swap_second(value, axis, other):
    count, across = lax.axis_size(axis), lax.axis_size(other)
    pairs = []
    for n in range(count):
        for m in range(across):
            if 0 < n < count - 1:
                target = (n + 1 if n % 2 else n - 1, m)
            else:
                target = (n, m ^ 1)
            pairs.append((n * across + m, target[0] * across + target[1]))
    return lax.ppermute(value, (axis, other), pairs)


def shards(volume, src_weight, tgt_weight, bias):
    layers = src_weight.shape[0]
    channels, rows, cols, depth, width = volume.shape
    axes = ("srow", "scol", "trow")
    counts = [lax.axis_size(n) for n in axes]
    assert all(count % 2 == 0 for count in counts) and rows > 1 and cols > 2
    src_w = jnp.transpose(src_weight, (0, 2, 3, 1))
    tgt_w = jnp.transpose(tgt_weight, (0, 2, 3, 1))
    deep_swaps = 1 if counts[2] == 2 else 2
    mid_shape, rim_shape = ((channels, rows, n, depth, width) for n in (cols - 2, 2))
    line = VMEM((channels, rows, depth, width), BF16)
    owed_rim = VMEM((channels, 2, depth, width), BF16)
    sent = [VMEM(rim_shape, BF16), line, line]
    early = [("beside", 0)]
    src_w, tgt_w, bias, beside_0, mid, rim, col_a, col_b = call(
        functools.partial(open_body, early),
        [VMEM(src_w.shape, BF16), VMEM(tgt_w.shape, BF16), VMEM(bias.shape, F32)]
        + operator_shapes(early, channels)
        + [VMEM(mid_shape, BF16)]
        + sent,
        (volume, src_w, tgt_w, bias),
        {n: HBM for n in range(4)},
        scratch=[pltpu.SemaphoreType.DMA((3 + rows * cols,))],
    )
    made = {early[0]: beside_0}
    kinds = ("middle", "beside", "target", "near", "deep")
    owed_inner = [VMEM((channels, cols - 2, depth, width), BF16)]
    sum_a = None
    for layer in range(layers):
        beside = swap_first(col_a, "scol"), swap_second(col_b, "scol", "trow")
        which = (0, 1) if sum_a is None else (1,)
        sums = call(functools.partial(inner_body, which), owed_inner * len(which), (mid, rim, made["beside", layer]))
        sum_b = sums[-1]
        inner = swap_first(sums[0], "srow") if sum_a is None else got_a, swap_second(sum_b, "srow", "scol")
        if layer == 0:
            late = [(kind, n) for n in range(layers) for kind in kinds]
            made |= build([part for part in late if part not in early], src_w, tgt_w, sum_b)
        operator = {kind: made[kind, layer] for kind in kinds}

        def own(after):
            return call(
                functools.partial(own_body, layer),
                [VMEM(mid_shape, F32), VMEM(rim_shape, F32)],
                (mid, rim, *(operator[kind] for kind in ("middle", "beside", "target", "near")), bias, after),
                {7: pl.ANY},
                scratch=[VMEM((depth // BAND, 3, channels * BAND, cols * width), BF16)],
            )

        parts = call(
            part_body,
            [VMEM((2, channels * BAND, depth // BAND * width), F32)] * 2,
            (mid, rim, operator["beside"], sum_b),
            {3: pl.ANY},
        )
        accs = own(sum_b) if layer else None
        a, b, side = call(
            edge_body,
            [owed_rim, owed_rim, VMEM((2, *line.shape), BF16)],
            (*beside, operator["beside"], *parts, accs[0] if layer else operator["middle"]),
            {5: pl.ANY},
        )
        outer = swap_first(a, "srow"), swap_second(b, "srow", "scol")
        deep = call(
            depth_body, [VMEM((rows, channels, cols * width), BF16)] * deep_swaps, (mid, rim, b), {2: pl.ANY}
        )
        deeper = [swap_first(deep[0], "trow")]
        if deep_swaps == 2:
            deeper.append(swap_second(deep[1], "trow", "scol"))
        accs = accs or own(b)
        acc_mid, acc_rim = call(
            rest_body,
            [VMEM(mid_shape, F32), VMEM(rim_shape, F32)],
            (mid, rim, side, *(operator[kind] for kind in ("middle", "beside", "deep")), *accs, *deeper),
            aliases={6: 0, 7: 1},
        )
        (mid,) = call(mid_body, [VMEM(mid_shape, BF16)], (mid, acc_mid, *inner))
        if layer < layers - 1:
            begun, *_ = call(begin_body, sent[:1], (rim, acc_rim, outer[0], mid), {3: pl.ANY})
            (sum_a,) = call(functools.partial(inner_body, (0,)), owed_inner, (mid, begun, made["beside", layer + 1]))
            got_a = swap_first(sum_a, "srow")
            rim, col_a, col_b = call(
                next_body, sent, (rim, acc_rim, outer[1], begun, sum_a), {4: pl.ANY}, aliases={3: 0}
            )
        else:
            (state,) = call(
                last_body,
                [jax.ShapeDtypeStruct(volume.shape, BF16)],
                (mid, rim, acc_rim, *outer),
                out_place=HBM,
                scratch=[VMEM(rim_shape, BF16), pltpu.SemaphoreType.DMA((rows * cols,))],
            )
    return state


def solution(mesh):
    return jax.shard_map(
        shards,
        mesh=mesh,
        in_specs=(P(None, "srow", "scol", "trow", None), P(), P(), P()),
        out_specs=P(None, "srow", "scol", "trow", None),
        check_vma=False,
    )
```

```python
import functools

import jax
import jax.numpy as jnp
from jax import lax
from jax.experimental import pallas as pl
from jax.experimental.pallas import tpu as pltpu
from jax.sharding import PartitionSpec as P

BAND = 32
EDGE = 16
SCOPED = 16 * 1024 * 1024
F32 = jnp.float32
BF16 = jnp.bfloat16
VMEM, HBM = pltpu.VMEM, pltpu.HBM
def parity(axis):
    return lax.axis_index(axis) % 2


def has_second(axis):
    at = lax.axis_index(axis)
    return (at > 0) & (at < lax.axis_size(axis) - 1)


def call(body, outs, args, places=None, out_place=VMEM, scratch=(), aliases=None):
    places = places or {}
    spaces = [places.get(n, VMEM) for n in range(len(args))]
    held = [pltpu.with_memory_space_constraint(a, m) if m in (VMEM, HBM) else a for a, m in zip(args, spaces)]
    return pl.pallas_call(
        body,
        out_shape=tuple(outs),
        in_specs=[pl.BlockSpec(memory_space=m) for m in spaces],
        out_specs=tuple(pl.BlockSpec(memory_space=out_place) for _ in outs),
        scratch_shapes=list(scratch),
        input_output_aliases=aliases or {},
        compiler_params=pltpu.CompilerParams(vmem_limit_bytes=SCOPED),
        cost_estimate=pl.CostEstimate(flops=10**6, bytes_accessed=10**4, transcendentals=0),
    )(*held)


def dot(a, b):
    return jnp.dot(a, b, preferred_element_type=F32)


def operators(parts, src_w_ref, tgt_w_ref, out_refs):
    channels = src_w_ref.shape[1]
    span, small = channels * BAND, channels * EDGE

    def columns(size):
        pick_c = lax.broadcasted_iota(jnp.int32, (channels, channels * size), 1) // size
        pick_r = lax.broadcasted_iota(jnp.int32, (channels, channels * size), 0)
        return (pick_c == pick_r).astype(BF16)

    wide, narrow, single = columns(BAND), columns(EDGE), columns(1)
    row = lax.broadcasted_iota(jnp.int32, (BAND, span), 0)
    shift = row - lax.broadcasted_iota(jnp.int32, (BAND, span), 1) % BAND
    row_s = lax.broadcasted_iota(jnp.int32, (BAND, small), 0)
    col_s = lax.broadcasted_iota(jnp.int32, (BAND, small), 1) % EDGE
    near = ((row_s == 0) & (col_s == EDGE - 1), (row_s == BAND - 1) & (col_s == 0))
    row_1 = lax.broadcasted_iota(jnp.int32, (BAND, channels), 0)
    deep = (row_1 == 0, row_1 == BAND - 1)
    spread = {}

    def taps(ref, layer, o, pick, key):
        key = (key, layer, o)
        if key not in spread:
            spread[key] = lax.dot_general(ref[layer, o], pick, (((0,), (0,)), ((), ())), preferred_element_type=F32)
        return spread[key]

    for (kind, layer), out_ref in zip(parts, out_refs):
        for o in range(channels):
            rows = slice(o * BAND, (o + 1) * BAND)
            for b in range(3):
                if kind == "middle":
                    got = taps(src_w_ref, layer, o, wide, "s")
                    values = {(): jnp.where(shift == 0, got[3 + b][None, :], 0.0)}
                elif kind == "beside":
                    got = taps(src_w_ref, layer, o, wide, "s")
                    values = {(n,): jnp.where(shift == 0, got[6 * n + b][None, :], 0.0) for n in range(2)}
                elif kind == "target":
                    got = taps(tgt_w_ref, layer, o, wide, "t")
                    value = jnp.where(shift == 1, got[b][None, :], 0.0)
                    value = jnp.where(shift == 0, got[3 + b][None, :], value)
                    values = {(): jnp.where(shift == -1, got[6 + b][None, :], value)}
                else:
                    pick, at = (narrow, near) if kind == "near" else (single, deep)
                    got = taps(tgt_w_ref, layer, o, pick, kind)
                    values = {(n,): jnp.where(at[n], got[6 * n + b][None, :], 0.0) for n in range(2)}
                for index, value in values.items():
                    size = value.shape[1]
                    out_ref[(*index, rows, slice(b * size, (b + 1) * size))] = value.astype(BF16)


def operator_shapes(parts, channels):
    span = channels * BAND
    widths = dict(middle=span, beside=span, target=span, near=channels * EDGE, deep=channels)
    lead = dict(middle=(), beside=(2,), target=(), near=(2,), deep=(2,))
    return [VMEM((*lead[kind], span, 3 * widths[kind]), BF16) for kind, _ in parts]


def build_body(parts, src_w_ref, tgt_w_ref, after_ref, *out_refs):
    operators(parts, src_w_ref, tgt_w_ref, out_refs)


def build(parts, src_w, tgt_w, after):
    got = call(
        functools.partial(build_body, parts),
        operator_shapes(parts, src_w.shape[1]),
        (src_w, tgt_w, after),
        {2: pl.ANY},
    )
    return dict(zip(parts, got))


def band(tile):
    channels, size, width = tile.shape
    return tile.reshape(channels * size, width)


def unband(tile, channels):
    return tile.reshape(channels, tile.shape[0] // channels, tile.shape[1])


def src_operand(tiles, cols):
    return jnp.concatenate([jnp.concatenate(tiles[b : b + cols], axis=1) for b in range(3)], axis=0)


def sent_rows(rows):
    odd = parity("srow")
    return ((rows - 1) * (1 - odd), odd), ((rows - 1) * odd, 1 - odd)


def column(mid_ref, rim_ref, i, j, cut):
    last = mid_ref.shape[2] + 1
    return band(rim_ref[:, i, j // last, cut] if j in (0, last) else mid_ref[:, i, j - 1, cut])


def bands_of(depth):
    return [slice(start, start + BAND) for start in range(0, depth, BAND)]


def owed_sums(operator, tiles, out_ref):
    channels, cols, depth, width = out_ref.shape
    cuts = bands_of(depth)
    operand = jnp.concatenate([jnp.concatenate([t for cut in cuts for t in tiles(cut, b)], axis=1) for b in range(3)], axis=0)
    got = dot(operator, operand).astype(BF16)
    for q, cut in enumerate(cuts):
        for j in range(cols):
            at = (q * cols + j) * width
            out_ref[:, j, cut] = unband(got[:, at : at + width], channels)


def inner_body(which, mid_ref, rim_ref, beside_ref, *out_refs):
    rows, cols = mid_ref.shape[1:3]
    for n, out_ref in zip(which, out_refs):
        i, side = sent_rows(rows)[n]
        owed_sums(
            beside_ref[side], lambda cut, b: [column(mid_ref, rim_ref, i, j + b, cut) for j in range(cols)], out_ref
        )


def part_body(mid_ref, rim_ref, beside_ref, after_ref, *part_refs):
    rows, cols = mid_ref.shape[1], mid_ref.shape[2] + 2
    cuts = bands_of(mid_ref.shape[3])
    for (i, side), part_ref in zip(sent_rows(rows), part_refs):
        span = part_ref.shape[1]
        for n, (first, j) in enumerate(((1, 0), (0, cols - 2))):
            tiles = [jnp.concatenate([column(mid_ref, rim_ref, i, j + b, cut) for cut in cuts], axis=1) for b in range(2)]
            operator = beside_ref[side, :, first * span : (first + 2) * span]
            part_ref[n] = dot(operator, jnp.concatenate(tiles, axis=0))


def edge_body(cola_ref, colb_ref, beside_ref, parta_ref, partb_ref, after_ref, a_ref, b_ref, side_ref):
    channels, rows, depth, width = cola_ref.shape
    odd, paired = parity("scol"), has_second("scol")
    side_ref[1 - odd] = cola_ref[...]

    @pl.when(paired)
    def _():
        side_ref[odd] = colb_ref[...]

    @pl.when(jnp.logical_not(paired))
    def _():
        side_ref[odd] = jnp.zeros_like(colb_ref)

    cuts = bands_of(depth)
    for (i, side), part_ref, out_ref in zip(sent_rows(rows), (parta_ref, partb_ref), (a_ref, b_ref)):
        span = part_ref.shape[1]
        for n, tap in enumerate((0, 2)):
            halo = jnp.concatenate([band(side_ref[n, :, i, cut]) for cut in cuts], axis=1)
            got = (part_ref[n] + dot(beside_ref[side, :, tap * span : (tap + 1) * span], halo)).astype(BF16)
            for q, cut in enumerate(cuts):
                out_ref[:, n, cut] = unband(got[:, q * width : (q + 1) * width], channels)


def shifted(tile, step):
    lane = lax.broadcasted_iota(jnp.int32, tile.shape, 1)
    width = tile.shape[1]
    rolled = pltpu.roll(tile.astype(F32), step % width, 1)
    gone = 0 if step == 1 else width - 1
    return jnp.where(lane == gone, 0.0, rolled)


def three(tiles):
    return [jnp.concatenate([shifted(t, step) if step else t.astype(F32) for t in tiles], axis=1) for step in (1, 0, -1)]


def own_body(
    layer, mid_ref, rim_ref, middle_ref, beside_ref, target_ref, near_ref, bias_ref, after_ref, accmid_ref, accrim_ref, lane_ref
):
    channels, rows, mids, depth, width = mid_ref.shape
    cols = mids + 2
    cuts = bands_of(depth)
    shape = (BAND, cols * width)
    bias = [jnp.broadcast_to(bias_ref[layer : layer + 1, o : o + 1], shape) for o in range(channels)]
    bias = jnp.concatenate(bias, axis=0)
    for i in range(rows):
        for q, cut in enumerate(cuts):
            tiles = [column(mid_ref, rim_ref, i, j, cut) for j in range(cols)]
            lane_ref[q, 1] = jnp.concatenate(tiles, axis=1)
            for n, step in ((0, 1), (2, -1)):
                lane_ref[q, n] = jnp.concatenate([shifted(t, step).astype(BF16) for t in tiles], axis=1)
        for q, cut in enumerate(cuts):
            total = bias + dot(target_ref[...], lane_ref[q].reshape(3 * channels * BAND, cols * width))
            for side, other, start in ((0, q - 1, BAND - EDGE), (1, q + 1, 0)):
                if 0 <= other < len(cuts):
                    parts = [unband(lane_ref[other, n], channels)[:, start : start + EDGE] for n in range(3)]
                    total = total + dot(near_ref[side], jnp.concatenate([band(p) for p in parts], axis=0))
            for n, j in enumerate((0, cols - 1)):
                accrim_ref[:, i, n, cut] = unband(total[:, j * width : (j + 1) * width], channels)
            for j in range(1, cols - 1):
                accmid_ref[:, i, j - 1, cut] = unband(total[:, j * width : (j + 1) * width], channels)
        for a in range(3):
            r = i + a - 1
            if 0 <= r < rows:
                operator = middle_ref[...] if a == 1 else beside_ref[a // 2]
                add_sums(operator, lambda cut, b: [column(mid_ref, rim_ref, r, j + b, cut) for j in range(mids)], accmid_ref, i)


def add_sums(operator, tiles, acc_ref, i):
    channels, _, cols, depth, width = acc_ref.shape
    cuts = bands_of(depth)
    operand = jnp.concatenate([jnp.concatenate([t for cut in cuts for t in tiles(cut, b)], axis=1) for b in range(3)], axis=0)
    got = dot(operator, operand)
    for q, cut in enumerate(cuts):
        for j in range(cols):
            at = (q * cols + j) * width
            acc_ref[:, i, j, cut] += unband(got[:, at : at + width], channels)


def rest_body(
    mid_ref, rim_ref, side_ref, middle_ref, beside_ref, deep_ref, accmid_ref, accrim_ref, *rest
):
    *deep_halos, outmid_ref, outrim_ref = rest
    channels, rows, mids, depth, width = mid_ref.shape
    cols = mids + 2

    def around(r, j, cut):
        if j in (-1, cols):
            return band(side_ref[0 if j < 0 else 1, :, r, cut])
        return column(mid_ref, rim_ref, r, j, cut)

    for i in range(rows):
        for a in range(3):
            r = i + a - 1
            if 0 <= r < rows:
                operator = middle_ref[...] if a == 1 else beside_ref[a // 2]
                add_sums(operator, lambda cut, b: [around(r, j + b - 1, cut) for j in (0, cols - 1)], outrim_ref, i)
        odd = parity("trow")
        for n, halo_ref in enumerate(deep_halos):
            side = (1 - odd) if n == 0 else odd
            cut = pl.ds(pl.multiple_of(side * (depth - BAND), BAND), BAND)
            halo = three([halo_ref[i, :, j * width : (j + 1) * width] for j in range(cols)])
            halo = jnp.concatenate(halo, axis=0)
            if n == 1:
                halo = halo * has_second("trow").astype(F32)
            got = dot(deep_ref[side], halo.astype(BF16))
            for j in range(cols):
                acc_ref, at = (outrim_ref, j // (cols - 1)) if j in (0, cols - 1) else (outmid_ref, j - 1)
                acc_ref[:, i, at, cut] += unband(got[:, j * width : (j + 1) * width], channels)


def finished(x_ref, acc_ref, owed_refs, store):
    rows, cols = x_ref.shape[1:3]
    odd = parity("srow")
    paired = has_second("srow").astype(F32)
    for n, i in enumerate([(rows - 1) * (1 - odd), (rows - 1) * odd, *range(1, rows - 1)]):
        if n < 2 and owed_refs[n] is None:
            continue
        for j in range(cols):
            total = acc_ref[:, i, j]
            if n < 2:
                owed = owed_refs[n][:, j].astype(F32)
                total = total + (owed if n == 0 else owed * paired)
            store(i, j, (x_ref[:, i, j].astype(F32) + jnp.maximum(total, 0.0)).astype(BF16))


def sent_columns(rim_ref, col_refs):
    odd = parity("scol")
    for n, ref in zip((1 - odd, odd), col_refs):
        ref[...] = rim_ref[:, :, n]


def depth_body(mid_ref, rim_ref, after_ref, *deep_refs):
    channels, rows, mids, depth, _ = mid_ref.shape
    odd = parity("trow")
    shape = (channels, channels * BAND)
    first = lax.broadcasted_iota(jnp.int32, shape, 0) * BAND
    for n, ref in enumerate(deep_refs):
        end = (1 - odd) if n == 0 else odd
        cut = pl.ds(pl.multiple_of(end * (depth - BAND), BAND), BAND)
        pick = (lax.broadcasted_iota(jnp.int32, shape, 1) == first + end * (BAND - 1)).astype(BF16)
        for i in range(rows):
            tiles = [column(mid_ref, rim_ref, i, j, cut) for j in range(mids + 2)]
            ref[i] = dot(pick, jnp.concatenate(tiles, axis=1)).astype(BF16)


def mid_body(x_ref, acc_ref, a_ref, b_ref, out_ref):
    def store(i, j, value):
        out_ref[:, i, j] = value

    finished(x_ref, acc_ref, (a_ref, b_ref), store)


def begin_body(x_ref, acc_ref, a_ref, after_ref, out_ref):
    mid_body(x_ref, acc_ref, a_ref, None, out_ref)


def next_body(x_ref, acc_ref, b_ref, begun_ref, after_ref, out_ref, cola_ref, colb_ref):
    mid_body(x_ref, acc_ref, None, b_ref, out_ref)
    sent_columns(out_ref, (cola_ref, colb_ref))


def last_body(mid_ref, rim_ref, acc_ref, a_ref, b_ref, out_ref, hold_ref, sems):
    rows, mids = mid_ref.shape[1:3]
    copies = []
    for i in range(rows):
        for j in range(mids):
            copy = pltpu.make_async_copy(mid_ref.at[:, i, j], out_ref.at[:, i, j + 1], sems.at[len(copies)])
            copy.start()
            copies.append(copy)

    def store(i, j, value):
        hold_ref[:, i, j] = value
        copy = pltpu.make_async_copy(hold_ref.at[:, i, j], out_ref.at[:, i, j * (mids + 1)], sems.at[len(copies)])
        copy.start()
        copies.append(copy)

    finished(rim_ref, acc_ref, (a_ref, b_ref), store)
    for copy in copies:
        copy.wait()


def open_body(parts, x_ref, src_w_ref, tgt_w_ref, bias_ref, *rest):
    src_ref, tgt_ref, held_ref, beside_ref, mid_ref, rim_ref, cola_ref, colb_ref, sems = rest
    rows, last = x_ref.shape[1], x_ref.shape[2] - 1
    pairs = [(src_w_ref, src_ref)]
    pairs += [(x_ref.at[:, i, n * last], rim_ref.at[:, i, n]) for i in range(rows) for n in range(2)]
    pairs += [(x_ref.at[:, i, j], mid_ref.at[:, i, j - 1]) for i in range(rows) for j in range(1, last)]
    pairs += [(tgt_w_ref, tgt_ref), (bias_ref, held_ref)]
    copies = [pltpu.make_async_copy(a, b, sems.at[n]) for n, (a, b) in enumerate(pairs)]
    for copy in copies:
        copy.start()
    copies[0].wait()
    operators(parts, src_ref, None, (beside_ref,))
    for copy in copies[1 : 1 + 2 * rows]:
        copy.wait()
    sent_columns(rim_ref, (cola_ref, colb_ref))
    for copy in copies[1 + 2 * rows :]:
        copy.wait()


def swap_first(value, axis):
    return lax.ppermute(value, axis, [(n, n ^ 1) for n in range(lax.axis_size(axis))])


def swap_second(value, axis, other):
    count, across = lax.axis_size(axis), lax.axis_size(other)
    pairs = []
    for n in range(count):
        for m in range(across):
            if 0 < n < count - 1:
                target = (n + 1 if n % 2 else n - 1, m)
            else:
                target = (n, m ^ 1)
            pairs.append((n * across + m, target[0] * across + target[1]))
    return lax.ppermute(value, (axis, other), pairs)


def shards(volume, src_weight, tgt_weight, bias):
    layers = src_weight.shape[0]
    channels, rows, cols, depth, width = volume.shape
    axes = ("srow", "scol", "trow")
    counts = [lax.axis_size(n) for n in axes]
    assert all(count % 2 == 0 for count in counts) and rows > 1 and cols > 2
    src_w = jnp.transpose(src_weight, (0, 2, 3, 1))
    tgt_w = jnp.transpose(tgt_weight, (0, 2, 3, 1))
    deep_swaps = 1 if counts[2] == 2 else 2
    mid_shape, rim_shape = ((channels, rows, n, depth, width) for n in (cols - 2, 2))
    line = VMEM((channels, rows, depth, width), BF16)
    owed_rim = VMEM((channels, 2, depth, width), BF16)
    sent = [VMEM(rim_shape, BF16), line, line]
    early = [("beside", 0)]
    src_w, tgt_w, bias, beside_0, mid, rim, col_a, col_b = call(
        functools.partial(open_body, early),
        [VMEM(src_w.shape, BF16), VMEM(tgt_w.shape, BF16), VMEM(bias.shape, F32)]
        + operator_shapes(early, channels)
        + [VMEM(mid_shape, BF16)]
        + sent,
        (volume, src_w, tgt_w, bias),
        {n: HBM for n in range(4)},
        scratch=[pltpu.SemaphoreType.DMA((3 + rows * cols,))],
    )
    made = {early[0]: beside_0}
    kinds = ("middle", "beside", "target", "near", "deep")
    owed_inner = [VMEM((channels, cols - 2, depth, width), BF16)]
    sum_a = None
    for layer in range(layers):
        beside = swap_first(col_a, "scol"), swap_second(col_b, "scol", "trow")
        which = (0, 1) if sum_a is None else (1,)
        sums = call(functools.partial(inner_body, which), owed_inner * len(which), (mid, rim, made["beside", layer]))
        sum_b = sums[-1]
        inner = swap_first(sums[0], "srow") if sum_a is None else got_a, swap_second(sum_b, "srow", "scol")
        if layer == 0:
            late = [(kind, n) for n in range(layers) for kind in kinds]
            made |= build([part for part in late if part not in early], src_w, tgt_w, sum_b)
        operator = {kind: made[kind, layer] for kind in kinds}

        parts = call(
            part_body,
            [VMEM((2, channels * BAND, depth // BAND * width), F32)] * 2,
            (mid, rim, operator["beside"], sum_b),
            {3: pl.ANY},
        )
        a, b, side = call(
            edge_body,
            [owed_rim, owed_rim, VMEM((2, *line.shape), BF16)],
            (*beside, operator["beside"], *parts, operator["middle"]),
            {5: pl.ANY},
        )
        outer = swap_first(a, "srow"), swap_second(b, "srow", "scol")
        deep = call(
            depth_body, [VMEM((rows, channels, cols * width), BF16)] * deep_swaps, (mid, rim, b), {2: pl.ANY}
        )
        deeper = [swap_first(deep[0], "trow")]
        if deep_swaps == 2:
            deeper.append(swap_second(deep[1], "trow", "scol"))
        accs = call(
            functools.partial(own_body, layer),
            [VMEM(mid_shape, F32), VMEM(rim_shape, F32)],
            (mid, rim, *(operator[kind] for kind in ("middle", "beside", "target", "near")), bias, b),
            {7: pl.ANY},
            scratch=[VMEM((depth // BAND, 3, channels * BAND, cols * width), BF16)],
        )
        acc_mid, acc_rim = call(
            rest_body,
            [VMEM(mid_shape, F32), VMEM(rim_shape, F32)],
            (mid, rim, side, *(operator[kind] for kind in ("middle", "beside", "deep")), *accs, *deeper),
            aliases={6: 0, 7: 1},
        )
        (mid,) = call(mid_body, [VMEM(mid_shape, BF16)], (mid, acc_mid, *inner))
        if layer < layers - 1:
            begun, *_ = call(begin_body, sent[:1], (rim, acc_rim, outer[0], mid), {3: pl.ANY})
            (sum_a,) = call(functools.partial(inner_body, (0,)), owed_inner, (mid, begun, made["beside", layer + 1]))
            got_a = swap_first(sum_a, "srow")
            rim, col_a, col_b = call(
                next_body, sent, (rim, acc_rim, outer[1], begun, sum_a), {4: pl.ANY}, aliases={3: 0}
            )
        else:
            (state,) = call(
                last_body,
                [jax.ShapeDtypeStruct(volume.shape, BF16)],
                (mid, rim, acc_rim, *outer),
                out_place=HBM,
                scratch=[VMEM(rim_shape, BF16), pltpu.SemaphoreType.DMA((rows * cols,))],
            )
    return state


def solution(mesh):
    return jax.shard_map(
        shards,
        mesh=mesh,
        in_specs=(P(None, "srow", "scol", "trow", None), P(), P(), P()),
        out_specs=P(None, "srow", "scol", "trow", None),
        check_vma=False,
    )
```

```python
import functools

import jax
import jax.numpy as jnp
from jax import lax
from jax.experimental import pallas as pl
from jax.experimental.pallas import tpu as pltpu
from jax.sharding import PartitionSpec as P

BAND = 32
EDGE = 16
SCOPED = 16 * 1024 * 1024
F32 = jnp.float32
BF16 = jnp.bfloat16
VMEM, HBM = pltpu.VMEM, pltpu.HBM
def parity(axis):
    return lax.axis_index(axis) % 2


def has_second(axis):
    at = lax.axis_index(axis)
    return (at > 0) & (at < lax.axis_size(axis) - 1)


def call(body, outs, args, places=None, out_place=VMEM, scratch=(), aliases=None):
    places = places or {}
    spaces = [places.get(n, VMEM) for n in range(len(args))]
    held = [pltpu.with_memory_space_constraint(a, m) if m in (VMEM, HBM) else a for a, m in zip(args, spaces)]
    return pl.pallas_call(
        body,
        out_shape=tuple(outs),
        in_specs=[pl.BlockSpec(memory_space=m) for m in spaces],
        out_specs=tuple(pl.BlockSpec(memory_space=out_place) for _ in outs),
        scratch_shapes=list(scratch),
        input_output_aliases=aliases or {},
        compiler_params=pltpu.CompilerParams(vmem_limit_bytes=SCOPED),
        cost_estimate=pl.CostEstimate(flops=10**6, bytes_accessed=10**4, transcendentals=0),
    )(*held)


def dot(a, b):
    return jnp.dot(a, b, preferred_element_type=F32)


def operators(parts, src_w_ref, tgt_w_ref, out_refs):
    channels = src_w_ref.shape[1]
    span, small = channels * BAND, channels * EDGE

    def columns(size):
        pick_c = lax.broadcasted_iota(jnp.int32, (channels, channels * size), 1) // size
        pick_r = lax.broadcasted_iota(jnp.int32, (channels, channels * size), 0)
        return (pick_c == pick_r).astype(BF16)

    wide, narrow, single = columns(BAND), columns(EDGE), columns(1)
    row = lax.broadcasted_iota(jnp.int32, (BAND, span), 0)
    shift = row - lax.broadcasted_iota(jnp.int32, (BAND, span), 1) % BAND
    row_s = lax.broadcasted_iota(jnp.int32, (BAND, small), 0)
    col_s = lax.broadcasted_iota(jnp.int32, (BAND, small), 1) % EDGE
    near = ((row_s == 0) & (col_s == EDGE - 1), (row_s == BAND - 1) & (col_s == 0))
    row_1 = lax.broadcasted_iota(jnp.int32, (BAND, channels), 0)
    deep = (row_1 == 0, row_1 == BAND - 1)
    spread = {}

    def taps(ref, layer, o, pick, key):
        key = (key, layer, o)
        if key not in spread:
            spread[key] = lax.dot_general(ref[layer, o], pick, (((0,), (0,)), ((), ())), preferred_element_type=F32)
        return spread[key]

    for (kind, layer), out_ref in zip(parts, out_refs):
        for o in range(channels):
            rows = slice(o * BAND, (o + 1) * BAND)
            for b in range(3):
                if kind == "middle":
                    got = taps(src_w_ref, layer, o, wide, "s")
                    values = {(): jnp.where(shift == 0, got[3 + b][None, :], 0.0)}
                elif kind == "beside":
                    got = taps(src_w_ref, layer, o, wide, "s")
                    values = {(n,): jnp.where(shift == 0, got[6 * n + b][None, :], 0.0) for n in range(2)}
                elif kind == "target":
                    got = taps(tgt_w_ref, layer, o, wide, "t")
                    value = jnp.where(shift == 1, got[b][None, :], 0.0)
                    value = jnp.where(shift == 0, got[3 + b][None, :], value)
                    values = {(): jnp.where(shift == -1, got[6 + b][None, :], value)}
                else:
                    pick, at = (narrow, near) if kind == "near" else (single, deep)
                    got = taps(tgt_w_ref, layer, o, pick, kind)
                    values = {(n,): jnp.where(at[n], got[6 * n + b][None, :], 0.0) for n in range(2)}
                for index, value in values.items():
                    size = value.shape[1]
                    out_ref[(*index, rows, slice(b * size, (b + 1) * size))] = value.astype(BF16)


def operator_shapes(parts, channels):
    span = channels * BAND
    widths = dict(middle=span, beside=span, target=span, near=channels * EDGE, deep=channels)
    lead = dict(middle=(), beside=(2,), target=(), near=(2,), deep=(2,))
    return [VMEM((*lead[kind], span, 3 * widths[kind]), BF16) for kind, _ in parts]


def build_body(parts, src_w_ref, tgt_w_ref, after_ref, *out_refs):
    operators(parts, src_w_ref, tgt_w_ref, out_refs)


def build(parts, src_w, tgt_w, after):
    got = call(
        functools.partial(build_body, parts),
        operator_shapes(parts, src_w.shape[1]),
        (src_w, tgt_w, after),
        {2: pl.ANY},
    )
    return dict(zip(parts, got))


def band(tile):
    channels, size, width = tile.shape
    return tile.reshape(channels * size, width)


def unband(tile, channels):
    return tile.reshape(channels, tile.shape[0] // channels, tile.shape[1])


def src_operand(tiles, cols):
    return jnp.concatenate([jnp.concatenate(tiles[b : b + cols], axis=1) for b in range(3)], axis=0)


def sent_rows(rows):
    odd = parity("srow")
    return ((rows - 1) * (1 - odd), odd), ((rows - 1) * odd, 1 - odd)


def column(mid_ref, rim_ref, i, j, cut):
    last = mid_ref.shape[2] + 1
    return band(rim_ref[:, i, j // last, cut] if j in (0, last) else mid_ref[:, i, j - 1, cut])


def bands_of(depth):
    return [slice(start, start + BAND) for start in range(0, depth, BAND)]


def owed_sums(operator, tiles, out_ref):
    channels, cols, depth, width = out_ref.shape
    cuts = bands_of(depth)
    operand = jnp.concatenate([jnp.concatenate([t for cut in cuts for t in tiles(cut, b)], axis=1) for b in range(3)], axis=0)
    got = dot(operator, operand).astype(BF16)
    for q, cut in enumerate(cuts):
        for j in range(cols):
            at = (q * cols + j) * width
            out_ref[:, j, cut] = unband(got[:, at : at + width], channels)


def inner_body(which, mid_ref, rim_ref, beside_ref, *out_refs):
    rows, cols = mid_ref.shape[1:3]
    for n, out_ref in zip(which, out_refs):
        i, side = sent_rows(rows)[n]
        owed_sums(
            beside_ref[side], lambda cut, b: [column(mid_ref, rim_ref, i, j + b, cut) for j in range(cols)], out_ref
        )


def part_body(mid_ref, rim_ref, beside_ref, after_ref, *part_refs):
    rows, cols = mid_ref.shape[1], mid_ref.shape[2] + 2
    cuts = bands_of(mid_ref.shape[3])
    for (i, side), part_ref in zip(sent_rows(rows), part_refs):
        span = part_ref.shape[1]
        for n, (first, j) in enumerate(((1, 0), (0, cols - 2))):
            tiles = [jnp.concatenate([column(mid_ref, rim_ref, i, j + b, cut) for cut in cuts], axis=1) for b in range(2)]
            operator = beside_ref[side, :, first * span : (first + 2) * span]
            part_ref[n] = dot(operator, jnp.concatenate(tiles, axis=0))


def edge_body(cola_ref, colb_ref, beside_ref, parta_ref, partb_ref, after_ref, a_ref, b_ref, side_ref):
    channels, rows, depth, width = cola_ref.shape
    odd, paired = parity("scol"), has_second("scol")
    side_ref[1 - odd] = cola_ref[...]

    @pl.when(paired)
    def _():
        side_ref[odd] = colb_ref[...]

    @pl.when(jnp.logical_not(paired))
    def _():
        side_ref[odd] = jnp.zeros_like(colb_ref)

    cuts = bands_of(depth)
    for (i, side), part_ref, out_ref in zip(sent_rows(rows), (parta_ref, partb_ref), (a_ref, b_ref)):
        span = part_ref.shape[1]
        for n, tap in enumerate((0, 2)):
            halo = jnp.concatenate([band(side_ref[n, :, i, cut]) for cut in cuts], axis=1)
            got = (part_ref[n] + dot(beside_ref[side, :, tap * span : (tap + 1) * span], halo)).astype(BF16)
            for q, cut in enumerate(cuts):
                out_ref[:, n, cut] = unband(got[:, q * width : (q + 1) * width], channels)


def shifted(tile, step):
    lane = lax.broadcasted_iota(jnp.int32, tile.shape, 1)
    width = tile.shape[1]
    rolled = pltpu.roll(tile.astype(F32), step % width, 1)
    gone = 0 if step == 1 else width - 1
    return jnp.where(lane == gone, 0.0, rolled)


def three(tiles):
    return [jnp.concatenate([shifted(t, step) if step else t.astype(F32) for t in tiles], axis=1) for step in (1, 0, -1)]


def own_body(
    layer, mid_ref, rim_ref, middle_ref, beside_ref, target_ref, near_ref, bias_ref, after_ref, accmid_ref, accrim_ref, lane_ref
):
    channels, rows, mids, depth, width = mid_ref.shape
    cols = mids + 2
    cuts = bands_of(depth)
    shape = (BAND, cols * width)
    bias = [jnp.broadcast_to(bias_ref[layer : layer + 1, o : o + 1], shape) for o in range(channels)]
    bias = jnp.concatenate(bias, axis=0)
    for i in range(rows):
        for q, cut in enumerate(cuts):
            tiles = [column(mid_ref, rim_ref, i, j, cut) for j in range(cols)]
            lane_ref[q, 1] = jnp.concatenate(tiles, axis=1)
            for n, step in ((0, 1), (2, -1)):
                lane_ref[q, n] = jnp.concatenate([shifted(t, step).astype(BF16) for t in tiles], axis=1)
        for q, cut in enumerate(cuts):
            total = bias + dot(target_ref[...], lane_ref[q].reshape(3 * channels * BAND, cols * width))
            for side, other, start in ((0, q - 1, BAND - EDGE), (1, q + 1, 0)):
                if 0 <= other < len(cuts):
                    parts = [unband(lane_ref[other, n], channels)[:, start : start + EDGE] for n in range(3)]
                    total = total + dot(near_ref[side], jnp.concatenate([band(p) for p in parts], axis=0))
            for n, j in enumerate((0, cols - 1)):
                accrim_ref[:, i, n, cut] = unband(total[:, j * width : (j + 1) * width], channels)
            for j in range(1, cols - 1):
                accmid_ref[:, i, j - 1, cut] = unband(total[:, j * width : (j + 1) * width], channels)
        for a in range(3):
            r = i + a - 1
            if 0 <= r < rows:
                operator = middle_ref[...] if a == 1 else beside_ref[a // 2]
                add_sums(operator, lambda cut, b: [column(mid_ref, rim_ref, r, j + b, cut) for j in range(mids)], accmid_ref, i)


def add_sums(operator, tiles, acc_ref, i):
    channels, _, cols, depth, width = acc_ref.shape
    cuts = bands_of(depth)
    operand = jnp.concatenate([jnp.concatenate([t for cut in cuts for t in tiles(cut, b)], axis=1) for b in range(3)], axis=0)
    got = dot(operator, operand)
    for q, cut in enumerate(cuts):
        for j in range(cols):
            at = (q * cols + j) * width
            acc_ref[:, i, j, cut] += unband(got[:, at : at + width], channels)


def rest_body(
    mid_ref, rim_ref, side_ref, middle_ref, beside_ref, deep_ref, accmid_ref, accrim_ref, *rest
):
    *deep_halos, outmid_ref, outrim_ref = rest
    channels, rows, mids, depth, width = mid_ref.shape
    cols = mids + 2

    def around(r, j, cut):
        if j in (-1, cols):
            return band(side_ref[0 if j < 0 else 1, :, r, cut])
        return column(mid_ref, rim_ref, r, j, cut)

    for i in range(rows):
        for a in range(3):
            r = i + a - 1
            if 0 <= r < rows:
                operator = middle_ref[...] if a == 1 else beside_ref[a // 2]
                add_sums(operator, lambda cut, b: [around(r, j + b - 1, cut) for j in (0, cols - 1)], outrim_ref, i)
        odd = parity("trow")
        for n, halo_ref in enumerate(deep_halos):
            side = (1 - odd) if n == 0 else odd
            cut = pl.ds(pl.multiple_of(side * (depth - BAND), BAND), BAND)
            halo = three([halo_ref[i, :, j * width : (j + 1) * width] for j in range(cols)])
            halo = jnp.concatenate(halo, axis=0)
            if n == 1:
                halo = halo * has_second("trow").astype(F32)
            got = dot(deep_ref[side], halo.astype(BF16))
            for j in range(cols):
                acc_ref, at = (outrim_ref, j // (cols - 1)) if j in (0, cols - 1) else (outmid_ref, j - 1)
                acc_ref[:, i, at, cut] += unband(got[:, j * width : (j + 1) * width], channels)


def finished(x_ref, acc_ref, owed_refs, store):
    rows, cols = x_ref.shape[1:3]
    odd = parity("srow")
    paired = has_second("srow").astype(F32)
    for n, i in enumerate([(rows - 1) * (1 - odd), (rows - 1) * odd, *range(1, rows - 1)]):
        if n < 2 and owed_refs[n] is None:
            continue
        for j in range(cols):
            total = acc_ref[:, i, j]
            if n < 2:
                owed = owed_refs[n][:, j].astype(F32)
                total = total + (owed if n == 0 else owed * paired)
            store(i, j, (x_ref[:, i, j].astype(F32) + jnp.maximum(total, 0.0)).astype(BF16))


def sent_columns(rim_ref, col_refs):
    odd = parity("scol")
    for n, ref in zip((1 - odd, odd), col_refs):
        ref[...] = rim_ref[:, :, n]


def depth_body(mid_ref, rim_ref, after_ref, *deep_refs):
    channels, rows, mids, depth, _ = mid_ref.shape
    odd = parity("trow")
    shape = (channels, channels * BAND)
    first = lax.broadcasted_iota(jnp.int32, shape, 0) * BAND
    for n, ref in enumerate(deep_refs):
        end = (1 - odd) if n == 0 else odd
        cut = pl.ds(pl.multiple_of(end * (depth - BAND), BAND), BAND)
        pick = (lax.broadcasted_iota(jnp.int32, shape, 1) == first + end * (BAND - 1)).astype(BF16)
        for i in range(rows):
            tiles = [column(mid_ref, rim_ref, i, j, cut) for j in range(mids + 2)]
            ref[i] = dot(pick, jnp.concatenate(tiles, axis=1)).astype(BF16)


def mid_body(x_ref, acc_ref, a_ref, b_ref, out_ref):
    def store(i, j, value):
        out_ref[:, i, j] = value

    finished(x_ref, acc_ref, (a_ref, b_ref), store)


def begin_body(x_ref, acc_ref, a_ref, after_ref, out_ref):
    mid_body(x_ref, acc_ref, a_ref, None, out_ref)


def next_body(x_ref, acc_ref, b_ref, begun_ref, after_ref, out_ref, cola_ref, colb_ref):
    mid_body(x_ref, acc_ref, None, b_ref, out_ref)
    sent_columns(out_ref, (cola_ref, colb_ref))


def last_body(mid_ref, rim_ref, acc_ref, a_ref, b_ref, out_ref, hold_ref, sems):
    rows, mids = mid_ref.shape[1:3]
    copies = []
    for i in range(rows):
        for j in range(mids):
            copy = pltpu.make_async_copy(mid_ref.at[:, i, j], out_ref.at[:, i, j + 1], sems.at[len(copies)])
            copy.start()
            copies.append(copy)

    def store(i, j, value):
        hold_ref[:, i, j] = value
        copy = pltpu.make_async_copy(hold_ref.at[:, i, j], out_ref.at[:, i, j * (mids + 1)], sems.at[len(copies)])
        copy.start()
        copies.append(copy)

    finished(rim_ref, acc_ref, (a_ref, b_ref), store)
    for copy in copies:
        copy.wait()


def open_body(parts, x_ref, src_w_ref, tgt_w_ref, bias_ref, *rest):
    src_ref, tgt_ref, held_ref, beside_ref, mid_ref, rim_ref, cola_ref, colb_ref, sems = rest
    rows, last = x_ref.shape[1], x_ref.shape[2] - 1
    pairs = [(src_w_ref, src_ref)]
    pairs += [(x_ref.at[:, i, n * last], rim_ref.at[:, i, n]) for i in range(rows) for n in range(2)]
    pairs += [(x_ref.at[:, i, j], mid_ref.at[:, i, j - 1]) for i in range(rows) for j in range(1, last)]
    pairs += [(tgt_w_ref, tgt_ref), (bias_ref, held_ref)]
    copies = [pltpu.make_async_copy(a, b, sems.at[n]) for n, (a, b) in enumerate(pairs)]
    for copy in copies:
        copy.start()
    copies[0].wait()
    operators(parts, src_ref, None, (beside_ref,))
    for copy in copies[1 : 1 + 2 * rows]:
        copy.wait()
    sent_columns(rim_ref, (cola_ref, colb_ref))
    for copy in copies[1 + 2 * rows :]:
        copy.wait()


def swap_first(value, axis):
    return lax.ppermute(value, axis, [(n, n ^ 1) for n in range(lax.axis_size(axis))])


def swap_second(value, axis, other):
    count, across = lax.axis_size(axis), lax.axis_size(other)
    pairs = []
    for n in range(count):
        for m in range(across):
            if 0 < n < count - 1:
                target = (n + 1 if n % 2 else n - 1, m)
            else:
                target = (n, m ^ 1)
            pairs.append((n * across + m, target[0] * across + target[1]))
    return lax.ppermute(value, (axis, other), pairs)


def shards(volume, src_weight, tgt_weight, bias):
    layers = src_weight.shape[0]
    channels, rows, cols, depth, width = volume.shape
    axes = ("srow", "scol", "trow")
    counts = [lax.axis_size(n) for n in axes]
    assert all(count % 2 == 0 for count in counts) and rows > 1 and cols > 2
    src_w = jnp.transpose(src_weight, (0, 2, 3, 1))
    tgt_w = jnp.transpose(tgt_weight, (0, 2, 3, 1))
    deep_swaps = 1 if counts[2] == 2 else 2
    mid_shape, rim_shape = ((channels, rows, n, depth, width) for n in (cols - 2, 2))
    line = VMEM((channels, rows, depth, width), BF16)
    owed_rim = VMEM((channels, 2, depth, width), BF16)
    sent = [VMEM(rim_shape, BF16), line, line]
    early = [("beside", 0)]
    src_w, tgt_w, bias, beside_0, mid, rim, col_a, col_b = call(
        functools.partial(open_body, early),
        [VMEM(src_w.shape, BF16), VMEM(tgt_w.shape, BF16), VMEM(bias.shape, F32)]
        + operator_shapes(early, channels)
        + [VMEM(mid_shape, BF16)]
        + sent,
        (volume, src_w, tgt_w, bias),
        {n: HBM for n in range(4)},
        scratch=[pltpu.SemaphoreType.DMA((3 + rows * cols,))],
    )
    made = {early[0]: beside_0}
    kinds = ("middle", "beside", "target", "near", "deep")
    owed_inner = [VMEM((channels, cols - 2, depth, width), BF16)]
    sum_a = None
    for layer in range(layers):
        beside = swap_first(col_a, "scol"), swap_second(col_b, "scol", "trow")
        which = (0, 1) if sum_a is None else (1,)
        sums = call(functools.partial(inner_body, which), owed_inner * len(which), (mid, rim, made["beside", layer]))
        sum_b = sums[-1]
        inner = swap_first(sums[0], "srow") if sum_a is None else got_a, swap_second(sum_b, "srow", "scol")
        if layer == 0:
            late = [(kind, n) for n in range(layers) for kind in kinds]
            made |= build([part for part in late if part not in early], src_w, tgt_w, sum_b)
        operator = {kind: made[kind, layer] for kind in kinds}

        parts = call(
            part_body,
            [VMEM((2, channels * BAND, depth // BAND * width), F32)] * 2,
            (mid, rim, operator["beside"], inner[0] if layer else sum_b),
            {3: pl.ANY},
        )
        a, b, side = call(
            edge_body,
            [owed_rim, owed_rim, VMEM((2, *line.shape), BF16)],
            (*beside, operator["beside"], *parts, operator["middle"]),
            {5: pl.ANY},
        )
        outer = swap_first(a, "srow"), swap_second(b, "srow", "scol")
        deep = call(
            depth_body, [VMEM((rows, channels, cols * width), BF16)] * deep_swaps, (mid, rim, b), {2: pl.ANY}
        )
        deeper = [swap_first(deep[0], "trow")]
        if deep_swaps == 2:
            deeper.append(swap_second(deep[1], "trow", "scol"))
        accs = call(
            functools.partial(own_body, layer),
            [VMEM(mid_shape, F32), VMEM(rim_shape, F32)],
            (mid, rim, *(operator[kind] for kind in ("middle", "beside", "target", "near")), bias, b),
            {7: pl.ANY},
            scratch=[VMEM((depth // BAND, 3, channels * BAND, cols * width), BF16)],
        )
        acc_mid, acc_rim = call(
            rest_body,
            [VMEM(mid_shape, F32), VMEM(rim_shape, F32)],
            (mid, rim, side, *(operator[kind] for kind in ("middle", "beside", "deep")), *accs, *deeper),
            aliases={6: 0, 7: 1},
        )
        (mid,) = call(mid_body, [VMEM(mid_shape, BF16)], (mid, acc_mid, *inner))
        if layer < layers - 1:
            begun, *_ = call(begin_body, sent[:1], (rim, acc_rim, outer[0], mid), {3: pl.ANY})
            (sum_a,) = call(functools.partial(inner_body, (0,)), owed_inner, (mid, begun, made["beside", layer + 1]))
            got_a = swap_first(sum_a, "srow")
            rim, col_a, col_b = call(
                next_body, sent, (rim, acc_rim, outer[1], begun, sum_a), {4: pl.ANY}, aliases={3: 0}
            )
        else:
            (state,) = call(
                last_body,
                [jax.ShapeDtypeStruct(volume.shape, BF16)],
                (mid, rim, acc_rim, *outer),
                out_place=HBM,
                scratch=[VMEM(rim_shape, BF16), pltpu.SemaphoreType.DMA((rows * cols,))],
            )
    return state


def solution(mesh):
    return jax.shard_map(
        shards,
        mesh=mesh,
        in_specs=(P(None, "srow", "scol", "trow", None), P(), P(), P()),
        out_specs=P(None, "srow", "scol", "trow", None),
        check_vma=False,
    )
```

```python
import functools

import jax
import jax.numpy as jnp
from jax import lax
from jax.experimental import pallas as pl
from jax.experimental.pallas import tpu as pltpu
from jax.sharding import PartitionSpec as P

BAND = 32
EDGE = 16
SCOPED = 16 * 1024 * 1024
F32 = jnp.float32
BF16 = jnp.bfloat16
VMEM, HBM = pltpu.VMEM, pltpu.HBM
def parity(axis):
    return lax.axis_index(axis) % 2


def has_second(axis):
    at = lax.axis_index(axis)
    return (at > 0) & (at < lax.axis_size(axis) - 1)


def call(body, outs, args, places=None, out_place=VMEM, scratch=(), aliases=None):
    places = places or {}
    spaces = [places.get(n, VMEM) for n in range(len(args))]
    held = [pltpu.with_memory_space_constraint(a, m) if m in (VMEM, HBM) else a for a, m in zip(args, spaces)]
    return pl.pallas_call(
        body,
        out_shape=tuple(outs),
        in_specs=[pl.BlockSpec(memory_space=m) for m in spaces],
        out_specs=tuple(pl.BlockSpec(memory_space=out_place) for _ in outs),
        scratch_shapes=list(scratch),
        input_output_aliases=aliases or {},
        compiler_params=pltpu.CompilerParams(vmem_limit_bytes=SCOPED),
        cost_estimate=pl.CostEstimate(flops=10**6, bytes_accessed=10**4, transcendentals=0),
    )(*held)


def dot(a, b):
    return jnp.dot(a, b, preferred_element_type=F32)


def operators(parts, src_w_ref, tgt_w_ref, out_refs):
    channels = src_w_ref.shape[1]
    span, small = channels * BAND, channels * EDGE

    def columns(size):
        pick_c = lax.broadcasted_iota(jnp.int32, (channels, channels * size), 1) // size
        pick_r = lax.broadcasted_iota(jnp.int32, (channels, channels * size), 0)
        return (pick_c == pick_r).astype(BF16)

    wide, narrow, single = columns(BAND), columns(EDGE), columns(1)
    row = lax.broadcasted_iota(jnp.int32, (BAND, span), 0)
    shift = row - lax.broadcasted_iota(jnp.int32, (BAND, span), 1) % BAND
    row_s = lax.broadcasted_iota(jnp.int32, (BAND, small), 0)
    col_s = lax.broadcasted_iota(jnp.int32, (BAND, small), 1) % EDGE
    near = ((row_s == 0) & (col_s == EDGE - 1), (row_s == BAND - 1) & (col_s == 0))
    row_1 = lax.broadcasted_iota(jnp.int32, (BAND, channels), 0)
    deep = (row_1 == 0, row_1 == BAND - 1)
    spread = {}

    def taps(ref, layer, o, pick, key):
        key = (key, layer, o)
        if key not in spread:
            spread[key] = lax.dot_general(ref[layer, o], pick, (((0,), (0,)), ((), ())), preferred_element_type=F32)
        return spread[key]

    for (kind, layer), out_ref in zip(parts, out_refs):
        for o in range(channels):
            rows = slice(o * BAND, (o + 1) * BAND)
            for b in range(3):
                if kind == "middle":
                    got = taps(src_w_ref, layer, o, wide, "s")
                    values = {(): jnp.where(shift == 0, got[3 + b][None, :], 0.0)}
                elif kind == "beside":
                    got = taps(src_w_ref, layer, o, wide, "s")
                    values = {(n,): jnp.where(shift == 0, got[6 * n + b][None, :], 0.0) for n in range(2)}
                elif kind == "target":
                    got = taps(tgt_w_ref, layer, o, wide, "t")
                    value = jnp.where(shift == 1, got[b][None, :], 0.0)
                    value = jnp.where(shift == 0, got[3 + b][None, :], value)
                    values = {(): jnp.where(shift == -1, got[6 + b][None, :], value)}
                else:
                    pick, at = (narrow, near) if kind == "near" else (single, deep)
                    got = taps(tgt_w_ref, layer, o, pick, kind)
                    values = {(n,): jnp.where(at[n], got[6 * n + b][None, :], 0.0) for n in range(2)}
                for index, value in values.items():
                    size = value.shape[1]
                    out_ref[(*index, rows, slice(b * size, (b + 1) * size))] = value.astype(BF16)


def operator_shapes(parts, channels):
    span = channels * BAND
    widths = dict(middle=span, beside=span, target=span, near=channels * EDGE, deep=channels)
    lead = dict(middle=(), beside=(2,), target=(), near=(2,), deep=(2,))
    return [VMEM((*lead[kind], span, 3 * widths[kind]), BF16) for kind, _ in parts]


def build_body(parts, src_w_ref, tgt_w_ref, after_ref, *out_refs):
    operators(parts, src_w_ref, tgt_w_ref, out_refs)


def build(parts, src_w, tgt_w, after):
    got = call(
        functools.partial(build_body, parts),
        operator_shapes(parts, src_w.shape[1]),
        (src_w, tgt_w, after),
        {2: pl.ANY},
    )
    return dict(zip(parts, got))


class View:
    def __init__(self, ref, columns):
        self.ref, self.columns = ref, columns

    @property
    def shape(self):
        channels, rows, _, depth, width = self.ref.shape
        return channels, rows, len(self.columns), depth, width

    def __getitem__(self, index):
        first, i, j, *rest = index
        return self.ref[(first, i, self.columns[j], *rest)]


def middle(x_ref):
    return View(x_ref, tuple(range(1, x_ref.shape[2] - 1)))


def sides(x_ref):
    return View(x_ref, (0, x_ref.shape[2] - 1))


def whole(body, views, x_ref, *refs):
    body(*(view(x_ref) for view in views), *refs)


def band(tile):
    channels, size, width = tile.shape
    return tile.reshape(channels * size, width)


def unband(tile, channels):
    return tile.reshape(channels, tile.shape[0] // channels, tile.shape[1])


def src_operand(tiles, cols):
    return jnp.concatenate([jnp.concatenate(tiles[b : b + cols], axis=1) for b in range(3)], axis=0)


def sent_rows(rows):
    odd = parity("srow")
    return ((rows - 1) * (1 - odd), odd), ((rows - 1) * odd, 1 - odd)


def column(mid_ref, rim_ref, i, j, cut):
    last = mid_ref.shape[2] + 1
    return band(rim_ref[:, i, j // last, cut] if j in (0, last) else mid_ref[:, i, j - 1, cut])


def bands_of(depth):
    return [slice(start, start + BAND) for start in range(0, depth, BAND)]


def owed_sums(operator, tiles, out_ref):
    channels, cols, depth, width = out_ref.shape
    cuts = bands_of(depth)
    operand = jnp.concatenate([jnp.concatenate([t for cut in cuts for t in tiles(cut, b)], axis=1) for b in range(3)], axis=0)
    got = dot(operator, operand).astype(BF16)
    for q, cut in enumerate(cuts):
        for j in range(cols):
            at = (q * cols + j) * width
            out_ref[:, j, cut] = unband(got[:, at : at + width], channels)


def inner_body(which, mid_ref, rim_ref, beside_ref, *out_refs):
    rows, cols = mid_ref.shape[1:3]
    for n, out_ref in zip(which, out_refs):
        i, side = sent_rows(rows)[n]
        owed_sums(
            beside_ref[side], lambda cut, b: [column(mid_ref, rim_ref, i, j + b, cut) for j in range(cols)], out_ref
        )


def part_body(mid_ref, rim_ref, beside_ref, after_ref, *part_refs):
    rows, cols = mid_ref.shape[1], mid_ref.shape[2] + 2
    cuts = bands_of(mid_ref.shape[3])
    for (i, side), part_ref in zip(sent_rows(rows), part_refs):
        span = part_ref.shape[1]
        for n, (first, j) in enumerate(((1, 0), (0, cols - 2))):
            tiles = [jnp.concatenate([column(mid_ref, rim_ref, i, j + b, cut) for cut in cuts], axis=1) for b in range(2)]
            operator = beside_ref[side, :, first * span : (first + 2) * span]
            part_ref[n] = dot(operator, jnp.concatenate(tiles, axis=0))


def edge_body(cola_ref, colb_ref, beside_ref, parta_ref, partb_ref, after_ref, a_ref, b_ref, side_ref):
    channels, rows, depth, width = cola_ref.shape
    odd, paired = parity("scol"), has_second("scol")
    side_ref[1 - odd] = cola_ref[...]

    @pl.when(paired)
    def _():
        side_ref[odd] = colb_ref[...]

    @pl.when(jnp.logical_not(paired))
    def _():
        side_ref[odd] = jnp.zeros_like(colb_ref)

    cuts = bands_of(depth)
    for (i, side), part_ref, out_ref in zip(sent_rows(rows), (parta_ref, partb_ref), (a_ref, b_ref)):
        span = part_ref.shape[1]
        for n, tap in enumerate((0, 2)):
            halo = jnp.concatenate([band(side_ref[n, :, i, cut]) for cut in cuts], axis=1)
            got = (part_ref[n] + dot(beside_ref[side, :, tap * span : (tap + 1) * span], halo)).astype(BF16)
            for q, cut in enumerate(cuts):
                out_ref[:, n, cut] = unband(got[:, q * width : (q + 1) * width], channels)


def shifted(tile, step):
    lane = lax.broadcasted_iota(jnp.int32, tile.shape, 1)
    width = tile.shape[1]
    rolled = pltpu.roll(tile.astype(F32), step % width, 1)
    gone = 0 if step == 1 else width - 1
    return jnp.where(lane == gone, 0.0, rolled)


def three(tiles):
    return [jnp.concatenate([shifted(t, step) if step else t.astype(F32) for t in tiles], axis=1) for step in (1, 0, -1)]


def own_body(
    layer, mid_ref, rim_ref, middle_ref, beside_ref, target_ref, near_ref, bias_ref, after_ref, accmid_ref, accrim_ref, lane_ref
):
    channels, rows, mids, depth, width = mid_ref.shape
    cols = mids + 2
    cuts = bands_of(depth)
    shape = (BAND, cols * width)
    bias = [jnp.broadcast_to(bias_ref[layer : layer + 1, o : o + 1], shape) for o in range(channels)]
    bias = jnp.concatenate(bias, axis=0)
    for i in range(rows):
        for q, cut in enumerate(cuts):
            tiles = [column(mid_ref, rim_ref, i, j, cut) for j in range(cols)]
            lane_ref[q, 1] = jnp.concatenate(tiles, axis=1)
            for n, step in ((0, 1), (2, -1)):
                lane_ref[q, n] = jnp.concatenate([shifted(t, step).astype(BF16) for t in tiles], axis=1)
        for q, cut in enumerate(cuts):
            total = bias + dot(target_ref[...], lane_ref[q].reshape(3 * channels * BAND, cols * width))
            for side, other, start in ((0, q - 1, BAND - EDGE), (1, q + 1, 0)):
                if 0 <= other < len(cuts):
                    parts = [unband(lane_ref[other, n], channels)[:, start : start + EDGE] for n in range(3)]
                    total = total + dot(near_ref[side], jnp.concatenate([band(p) for p in parts], axis=0))
            for n, j in enumerate((0, cols - 1)):
                accrim_ref[:, i, n, cut] = unband(total[:, j * width : (j + 1) * width], channels)
            for j in range(1, cols - 1):
                accmid_ref[:, i, j - 1, cut] = unband(total[:, j * width : (j + 1) * width], channels)
        for a in range(3):
            r = i + a - 1
            if 0 <= r < rows:
                operator = middle_ref[...] if a == 1 else beside_ref[a // 2]
                add_sums(operator, lambda cut, b: [column(mid_ref, rim_ref, r, j + b, cut) for j in range(mids)], accmid_ref, i)


def add_sums(operator, tiles, acc_ref, i):
    channels, _, cols, depth, width = acc_ref.shape
    cuts = bands_of(depth)
    operand = jnp.concatenate([jnp.concatenate([t for cut in cuts for t in tiles(cut, b)], axis=1) for b in range(3)], axis=0)
    got = dot(operator, operand)
    for q, cut in enumerate(cuts):
        for j in range(cols):
            at = (q * cols + j) * width
            acc_ref[:, i, j, cut] += unband(got[:, at : at + width], channels)


def rest_body(
    mid_ref, rim_ref, side_ref, middle_ref, beside_ref, deep_ref, accmid_ref, accrim_ref, *rest
):
    *deep_halos, outmid_ref, outrim_ref = rest
    channels, rows, mids, depth, width = mid_ref.shape
    cols = mids + 2

    def around(r, j, cut):
        if j in (-1, cols):
            return band(side_ref[0 if j < 0 else 1, :, r, cut])
        return column(mid_ref, rim_ref, r, j, cut)

    for i in range(rows):
        for a in range(3):
            r = i + a - 1
            if 0 <= r < rows:
                operator = middle_ref[...] if a == 1 else beside_ref[a // 2]
                add_sums(operator, lambda cut, b: [around(r, j + b - 1, cut) for j in (0, cols - 1)], outrim_ref, i)
        odd = parity("trow")
        for n, halo_ref in enumerate(deep_halos):
            side = (1 - odd) if n == 0 else odd
            cut = pl.ds(pl.multiple_of(side * (depth - BAND), BAND), BAND)
            halo = three([halo_ref[i, :, j * width : (j + 1) * width] for j in range(cols)])
            halo = jnp.concatenate(halo, axis=0)
            if n == 1:
                halo = halo * has_second("trow").astype(F32)
            got = dot(deep_ref[side], halo.astype(BF16))
            for j in range(cols):
                acc_ref, at = (outrim_ref, j // (cols - 1)) if j in (0, cols - 1) else (outmid_ref, j - 1)
                acc_ref[:, i, at, cut] += unband(got[:, j * width : (j + 1) * width], channels)


def finished(x_ref, acc_ref, owed_refs, store):
    rows, cols = x_ref.shape[1:3]
    odd = parity("srow")
    paired = has_second("srow").astype(F32)
    for n, i in enumerate([(rows - 1) * (1 - odd), (rows - 1) * odd, *range(1, rows - 1)]):
        if n < 2 and owed_refs[n] is None:
            continue
        for j in range(cols):
            total = acc_ref[:, i, j]
            if n < 2:
                owed = owed_refs[n][:, j].astype(F32)
                total = total + (owed if n == 0 else owed * paired)
            store(i, j, (x_ref[:, i, j].astype(F32) + jnp.maximum(total, 0.0)).astype(BF16))


def sent_columns(rim_ref, col_refs):
    odd = parity("scol")
    for n, ref in zip((1 - odd, odd), col_refs):
        ref[...] = rim_ref[:, :, n]


def depth_body(mid_ref, rim_ref, after_ref, *deep_refs):
    channels, rows, mids, depth, _ = mid_ref.shape
    odd = parity("trow")
    shape = (channels, channels * BAND)
    first = lax.broadcasted_iota(jnp.int32, shape, 0) * BAND
    for n, ref in enumerate(deep_refs):
        end = (1 - odd) if n == 0 else odd
        cut = pl.ds(pl.multiple_of(end * (depth - BAND), BAND), BAND)
        pick = (lax.broadcasted_iota(jnp.int32, shape, 1) == first + end * (BAND - 1)).astype(BF16)
        for i in range(rows):
            tiles = [column(mid_ref, rim_ref, i, j, cut) for j in range(mids + 2)]
            ref[i] = dot(pick, jnp.concatenate(tiles, axis=1)).astype(BF16)


def mid_body(x_ref, acc_ref, a_ref, b_ref, out_ref):
    def store(i, j, value):
        out_ref[:, i, j] = value

    finished(x_ref, acc_ref, (a_ref, b_ref), store)


def begin_body(x_ref, acc_ref, a_ref, after_ref, out_ref):
    mid_body(x_ref, acc_ref, a_ref, None, out_ref)


def next_body(x_ref, acc_ref, b_ref, begun_ref, after_ref, out_ref, cola_ref, colb_ref):
    mid_body(x_ref, acc_ref, None, b_ref, out_ref)
    sent_columns(out_ref, (cola_ref, colb_ref))


def last_body(mid_ref, rim_ref, acc_ref, a_ref, b_ref, out_ref, hold_ref, sems):
    rows, mids = mid_ref.shape[1:3]
    copies = []
    for i in range(rows):
        for j in range(mids):
            copy = pltpu.make_async_copy(mid_ref.at[:, i, j], out_ref.at[:, i, j + 1], sems.at[len(copies)])
            copy.start()
            copies.append(copy)

    def store(i, j, value):
        hold_ref[:, i, j] = value
        copy = pltpu.make_async_copy(hold_ref.at[:, i, j], out_ref.at[:, i, j * (mids + 1)], sems.at[len(copies)])
        copy.start()
        copies.append(copy)

    finished(rim_ref, acc_ref, (a_ref, b_ref), store)
    for copy in copies:
        copy.wait()


def open_body(parts, x_ref, src_w_ref, tgt_w_ref, bias_ref, *rest):
    src_ref, tgt_ref, held_ref, beside_ref, cola_ref, colb_ref, sems = rest
    last = x_ref.shape[2] - 1
    odd = parity("scol")
    pairs = (
        (src_w_ref, src_ref),
        (x_ref.at[:, :, last * (1 - odd)], cola_ref),
        (x_ref.at[:, :, last * odd], colb_ref),
        (tgt_w_ref, tgt_ref),
        (bias_ref, held_ref),
    )
    copies = [pltpu.make_async_copy(a, b, sems.at[n]) for n, (a, b) in enumerate(pairs)]
    for copy in copies:
        copy.start()
    copies[0].wait()
    operators(parts, src_ref, None, (beside_ref,))
    for copy in copies[1:]:
        copy.wait()


def swap_first(value, axis):
    return lax.ppermute(value, axis, [(n, n ^ 1) for n in range(lax.axis_size(axis))])


def swap_second(value, axis, other):
    count, across = lax.axis_size(axis), lax.axis_size(other)
    pairs = []
    for n in range(count):
        for m in range(across):
            if 0 < n < count - 1:
                target = (n + 1 if n % 2 else n - 1, m)
            else:
                target = (n, m ^ 1)
            pairs.append((n * across + m, target[0] * across + target[1]))
    return lax.ppermute(value, (axis, other), pairs)


def shards(volume, src_weight, tgt_weight, bias):
    layers = src_weight.shape[0]
    channels, rows, cols, depth, width = volume.shape
    axes = ("srow", "scol", "trow")
    counts = [lax.axis_size(n) for n in axes]
    assert all(count % 2 == 0 for count in counts) and rows > 1 and cols > 2 and layers > 1
    src_w = jnp.transpose(src_weight, (0, 2, 3, 1))
    tgt_w = jnp.transpose(tgt_weight, (0, 2, 3, 1))
    deep_swaps = 1 if counts[2] == 2 else 2
    mid_shape, rim_shape = ((channels, rows, n, depth, width) for n in (cols - 2, 2))
    line = VMEM((channels, rows, depth, width), BF16)
    owed_rim = VMEM((channels, 2, depth, width), BF16)
    early = [("beside", 0)]
    src_w, tgt_w, bias, beside_0, col_a, col_b = call(
        functools.partial(open_body, early),
        [VMEM(src_w.shape, BF16), VMEM(tgt_w.shape, BF16), VMEM(bias.shape, F32)] + operator_shapes(early, channels) + [line, line],
        (volume, src_w, tgt_w, bias),
        {n: HBM for n in range(4)},
        scratch=[pltpu.SemaphoreType.DMA((5,))],
    )
    made = {early[0]: beside_0}
    kinds = ("middle", "beside", "target", "near", "deep")
    owed_inner = [VMEM((channels, cols - 2, depth, width), BF16)]
    block, sum_a = (volume,), None
    for layer in range(layers):

        def on(body, *views):
            return functools.partial(whole, body, views) if layer == 0 else body

        both, base = (middle, sides), len(block)
        mid, rim = block[0], block[-1]
        beside = swap_first(col_a, "scol"), swap_second(col_b, "scol", "trow")
        which = (0, 1) if sum_a is None else (1,)
        sums = call(on(functools.partial(inner_body, which), *both), owed_inner * len(which), (*block, made["beside", layer]))
        sum_b = sums[-1]
        inner = swap_first(sums[0], "srow") if sum_a is None else got_a, swap_second(sum_b, "srow", "scol")
        if layer == 0:
            late = [(kind, n) for n in range(layers) for kind in kinds]
            made |= build([part for part in late if part not in early], src_w, tgt_w, sum_b)
        operator = {kind: made[kind, layer] for kind in kinds}
        parts = call(
            on(part_body, *both),
            [VMEM((2, channels * BAND, depth // BAND * width), F32)] * 2,
            (*block, operator["beside"], sum_b),
            {base + 1: pl.ANY},
        )
        a, b, side = call(
            edge_body,
            [owed_rim, owed_rim, VMEM((2, *line.shape), BF16)],
            (*beside, operator["beside"], *parts, operator["middle"]),
            {5: pl.ANY},
        )
        outer = swap_first(a, "srow"), swap_second(b, "srow", "scol")
        deep = call(
            on(depth_body, *both),
            [VMEM((rows, channels, cols * width), BF16)] * deep_swaps,
            (*block, b),
            {base: pl.ANY},
        )
        deeper = [swap_first(deep[0], "trow")]
        if deep_swaps == 2:
            deeper.append(swap_second(deep[1], "trow", "scol"))
        accs = call(
            on(functools.partial(own_body, layer), *both),
            [VMEM(mid_shape, F32), VMEM(rim_shape, F32)],
            (*block, *(operator[kind] for kind in ("middle", "beside", "target", "near")), bias, b),
            {base + 5: pl.ANY},
            scratch=[VMEM((depth // BAND, 3, channels * BAND, cols * width), BF16)],
        )
        acc_mid, acc_rim = call(
            on(rest_body, *both),
            [VMEM(mid_shape, F32), VMEM(rim_shape, F32)],
            (*block, side, *(operator[kind] for kind in ("middle", "beside", "deep")), *accs, *deeper),
            aliases={base + 4: 0, base + 5: 1},
        )
        (mid,) = call(on(mid_body, middle), [VMEM(mid_shape, BF16)], (mid, acc_mid, *inner))
        if layer < layers - 1:
            whole_rim = [VMEM(rim_shape, BF16)]
            (begun,) = call(on(begin_body, sides), whole_rim, (rim, acc_rim, outer[0], mid), {3: pl.ANY})
            (sum_a,) = call(functools.partial(inner_body, (0,)), owed_inner, (mid, begun, made["beside", layer + 1]))
            got_a = swap_first(sum_a, "srow")
            rim, col_a, col_b = call(
                on(next_body, sides),
                whole_rim + [line, line],
                (rim, acc_rim, outer[1], begun, sum_a),
                {4: pl.ANY},
                aliases={3: 0},
            )
            block = (mid, rim)
        else:
            (state,) = call(
                last_body,
                [jax.ShapeDtypeStruct(volume.shape, BF16)],
                (mid, rim, acc_rim, *outer),
                out_place=HBM,
                scratch=[VMEM(rim_shape, BF16), pltpu.SemaphoreType.DMA((rows * cols,))],
            )
    return state


def solution(mesh):
    return jax.shard_map(
        shards,
        mesh=mesh,
        in_specs=(P(None, "srow", "scol", "trow", None), P(), P(), P()),
        out_specs=P(None, "srow", "scol", "trow", None),
        check_vma=False,
    )
```

```python
import functools

import jax
import jax.numpy as jnp
from jax import lax
from jax.experimental import pallas as pl
from jax.experimental.pallas import tpu as pltpu
from jax.sharding import PartitionSpec as P

BAND = 32
EDGE = 16
SCOPED = 16 * 1024 * 1024
F32 = jnp.float32
BF16 = jnp.bfloat16
VMEM, HBM = pltpu.VMEM, pltpu.HBM
def parity(axis):
    return lax.axis_index(axis) % 2


def has_second(axis):
    at = lax.axis_index(axis)
    return (at > 0) & (at < lax.axis_size(axis) - 1)


def call(body, outs, args, places=None, out_place=VMEM, scratch=(), aliases=None):
    places = places or {}
    spaces = [places.get(n, VMEM) for n in range(len(args))]
    held = [pltpu.with_memory_space_constraint(a, m) if m in (VMEM, HBM) else a for a, m in zip(args, spaces)]
    return pl.pallas_call(
        body,
        out_shape=tuple(outs),
        in_specs=[pl.BlockSpec(memory_space=m) for m in spaces],
        out_specs=tuple(pl.BlockSpec(memory_space=out_place) for _ in outs),
        scratch_shapes=list(scratch),
        input_output_aliases=aliases or {},
        compiler_params=pltpu.CompilerParams(vmem_limit_bytes=SCOPED),
        cost_estimate=pl.CostEstimate(flops=10**6, bytes_accessed=10**4, transcendentals=0),
    )(*held)


def dot(a, b):
    return jnp.dot(a, b, preferred_element_type=F32)


def operators(parts, src_w_ref, tgt_w_ref, out_refs):
    channels = src_w_ref.shape[1]
    span, small = channels * BAND, channels * EDGE

    def columns(size):
        pick_c = lax.broadcasted_iota(jnp.int32, (channels, channels * size), 1) // size
        pick_r = lax.broadcasted_iota(jnp.int32, (channels, channels * size), 0)
        return (pick_c == pick_r).astype(BF16)

    wide, narrow, single = columns(BAND), columns(EDGE), columns(1)
    row = lax.broadcasted_iota(jnp.int32, (BAND, span), 0)
    shift = row - lax.broadcasted_iota(jnp.int32, (BAND, span), 1) % BAND
    row_s = lax.broadcasted_iota(jnp.int32, (BAND, small), 0)
    col_s = lax.broadcasted_iota(jnp.int32, (BAND, small), 1) % EDGE
    near = ((row_s == 0) & (col_s == EDGE - 1), (row_s == BAND - 1) & (col_s == 0))
    row_1 = lax.broadcasted_iota(jnp.int32, (BAND, channels), 0)
    deep = (row_1 == 0, row_1 == BAND - 1)
    spread = {}

    def taps(ref, layer, o, pick, key):
        key = (key, layer, o)
        if key not in spread:
            spread[key] = lax.dot_general(ref[layer, o], pick, (((0,), (0,)), ((), ())), preferred_element_type=F32)
        return spread[key]

    for (kind, layer), out_ref in zip(parts, out_refs):
        for o in range(channels):
            rows = slice(o * BAND, (o + 1) * BAND)
            for b in range(3):
                if kind == "middle":
                    got = taps(src_w_ref, layer, o, wide, "s")
                    values = {(): jnp.where(shift == 0, got[3 + b][None, :], 0.0)}
                elif kind == "beside":
                    got = taps(src_w_ref, layer, o, wide, "s")
                    values = {(n,): jnp.where(shift == 0, got[6 * n + b][None, :], 0.0) for n in range(2)}
                elif kind == "target":
                    got = taps(tgt_w_ref, layer, o, wide, "t")
                    value = jnp.where(shift == 1, got[b][None, :], 0.0)
                    value = jnp.where(shift == 0, got[3 + b][None, :], value)
                    values = {(): jnp.where(shift == -1, got[6 + b][None, :], value)}
                else:
                    pick, at = (narrow, near) if kind == "near" else (single, deep)
                    got = taps(tgt_w_ref, layer, o, pick, kind)
                    values = {(n,): jnp.where(at[n], got[6 * n + b][None, :], 0.0) for n in range(2)}
                for index, value in values.items():
                    size = value.shape[1]
                    out_ref[(*index, rows, slice(b * size, (b + 1) * size))] = value.astype(BF16)


def operator_shapes(parts, channels):
    span = channels * BAND
    widths = dict(middle=span, beside=span, target=span, near=channels * EDGE, deep=channels)
    lead = dict(middle=(), beside=(2,), target=(), near=(2,), deep=(2,))
    return [VMEM((*lead[kind], span, 3 * widths[kind]), BF16) for kind, _ in parts]


def build_body(parts, src_w_ref, tgt_w_ref, after_ref, *out_refs):
    operators(parts, src_w_ref, tgt_w_ref, out_refs)


def build(parts, src_w, tgt_w, after):
    got = call(
        functools.partial(build_body, parts),
        operator_shapes(parts, src_w.shape[1]),
        (src_w, tgt_w, after),
        {2: pl.ANY},
    )
    return dict(zip(parts, got))


class View:
    def __init__(self, ref, columns):
        self.ref, self.columns = ref, columns

    @property
    def shape(self):
        channels, rows, _, depth, width = self.ref.shape
        return channels, rows, len(self.columns), depth, width

    def __getitem__(self, index):
        first, i, j, *rest = index
        return self.ref[(first, i, self.columns[j], *rest)]


def middle(x_ref):
    return View(x_ref, tuple(range(1, x_ref.shape[2] - 1)))


def sides(x_ref):
    return View(x_ref, (0, x_ref.shape[2] - 1))


def whole(body, views, x_ref, *refs):
    body(*(view(x_ref) for view in views), *refs)


def band(tile):
    channels, size, width = tile.shape
    return tile.reshape(channels * size, width)


def unband(tile, channels):
    return tile.reshape(channels, tile.shape[0] // channels, tile.shape[1])


def src_operand(tiles, cols):
    return jnp.concatenate([jnp.concatenate(tiles[b : b + cols], axis=1) for b in range(3)], axis=0)


def sent_rows(rows):
    odd = parity("srow")
    return ((rows - 1) * (1 - odd), odd), ((rows - 1) * odd, 1 - odd)


def column(mid_ref, rim_ref, i, j, cut):
    last = mid_ref.shape[2] + 1
    return band(rim_ref[:, i, j // last, cut] if j in (0, last) else mid_ref[:, i, j - 1, cut])


def bands_of(depth):
    return [slice(start, start + BAND) for start in range(0, depth, BAND)]


def owed_sums(operator, tiles, out_ref):
    channels, cols, depth, width = out_ref.shape
    cuts = bands_of(depth)
    operand = jnp.concatenate([jnp.concatenate([t for cut in cuts for t in tiles(cut, b)], axis=1) for b in range(3)], axis=0)
    got = dot(operator, operand).astype(BF16)
    for q, cut in enumerate(cuts):
        for j in range(cols):
            at = (q * cols + j) * width
            out_ref[:, j, cut] = unband(got[:, at : at + width], channels)


def inner_body(which, mid_ref, rim_ref, beside_ref, *out_refs):
    rows, cols = mid_ref.shape[1:3]
    for n, out_ref in zip(which, out_refs):
        i, side = sent_rows(rows)[n]
        owed_sums(
            beside_ref[side], lambda cut, b: [column(mid_ref, rim_ref, i, j + b, cut) for j in range(cols)], out_ref
        )


def part_body(mid_ref, rim_ref, beside_ref, after_ref, *part_refs):
    rows, cols = mid_ref.shape[1], mid_ref.shape[2] + 2
    cuts = bands_of(mid_ref.shape[3])
    for (i, side), part_ref in zip(sent_rows(rows), part_refs):
        span = part_ref.shape[1]
        for n, (first, j) in enumerate(((1, 0), (0, cols - 2))):
            tiles = [jnp.concatenate([column(mid_ref, rim_ref, i, j + b, cut) for cut in cuts], axis=1) for b in range(2)]
            operator = beside_ref[side, :, first * span : (first + 2) * span]
            part_ref[n] = dot(operator, jnp.concatenate(tiles, axis=0))


def edge_body(cola_ref, colb_ref, beside_ref, parta_ref, partb_ref, after_ref, a_ref, b_ref, side_ref):
    channels, rows, depth, width = cola_ref.shape
    odd, paired = parity("scol"), has_second("scol")
    side_ref[1 - odd] = cola_ref[...]

    @pl.when(paired)
    def _():
        side_ref[odd] = colb_ref[...]

    @pl.when(jnp.logical_not(paired))
    def _():
        side_ref[odd] = jnp.zeros_like(colb_ref)

    cuts = bands_of(depth)
    for (i, side), part_ref, out_ref in zip(sent_rows(rows), (parta_ref, partb_ref), (a_ref, b_ref)):
        span = part_ref.shape[1]
        for n, tap in enumerate((0, 2)):
            halo = jnp.concatenate([band(side_ref[n, :, i, cut]) for cut in cuts], axis=1)
            got = (part_ref[n] + dot(beside_ref[side, :, tap * span : (tap + 1) * span], halo)).astype(BF16)
            for q, cut in enumerate(cuts):
                out_ref[:, n, cut] = unband(got[:, q * width : (q + 1) * width], channels)


def shifted(tile, step):
    lane = lax.broadcasted_iota(jnp.int32, tile.shape, 1)
    width = tile.shape[1]
    rolled = pltpu.roll(tile.astype(F32), step % width, 1)
    gone = 0 if step == 1 else width - 1
    return jnp.where(lane == gone, 0.0, rolled)


def three(tiles):
    return [jnp.concatenate([shifted(t, step) if step else t.astype(F32) for t in tiles], axis=1) for step in (1, 0, -1)]


def own_body(
    layer, mid_ref, rim_ref, middle_ref, beside_ref, target_ref, near_ref, bias_ref, after_ref, accmid_ref, accrim_ref, lane_ref
):
    channels, rows, mids, depth, width = mid_ref.shape
    cols = mids + 2
    cuts = bands_of(depth)
    shape = (BAND, cols * width)
    bias = [jnp.broadcast_to(bias_ref[layer : layer + 1, o : o + 1], shape) for o in range(channels)]
    bias = jnp.concatenate(bias, axis=0)
    for i in range(rows):
        for q, cut in enumerate(cuts):
            tiles = [column(mid_ref, rim_ref, i, j, cut) for j in range(cols)]
            lane_ref[q, 1] = jnp.concatenate(tiles, axis=1)
            for n, step in ((0, 1), (2, -1)):
                lane_ref[q, n] = jnp.concatenate([shifted(t, step).astype(BF16) for t in tiles], axis=1)
        for q, cut in enumerate(cuts):
            total = bias + dot(target_ref[...], lane_ref[q].reshape(3 * channels * BAND, cols * width))
            for side, other, start in ((0, q - 1, BAND - EDGE), (1, q + 1, 0)):
                if 0 <= other < len(cuts):
                    parts = [unband(lane_ref[other, n], channels)[:, start : start + EDGE] for n in range(3)]
                    total = total + dot(near_ref[side], jnp.concatenate([band(p) for p in parts], axis=0))
            for n, j in enumerate((0, cols - 1)):
                accrim_ref[:, i, n, cut] = unband(total[:, j * width : (j + 1) * width], channels)
            for j in range(1, cols - 1):
                accmid_ref[:, i, j - 1, cut] = unband(total[:, j * width : (j + 1) * width], channels)
        for a in range(3):
            r = i + a - 1
            if 0 <= r < rows:
                operator = middle_ref[...] if a == 1 else beside_ref[a // 2]
                add_sums(operator, lambda cut, b: [column(mid_ref, rim_ref, r, j + b, cut) for j in range(mids)], accmid_ref, i)


def add_sums(operator, tiles, acc_ref, i):
    channels, _, cols, depth, width = acc_ref.shape
    cuts = bands_of(depth)
    operand = jnp.concatenate([jnp.concatenate([t for cut in cuts for t in tiles(cut, b)], axis=1) for b in range(3)], axis=0)
    got = dot(operator, operand)
    for q, cut in enumerate(cuts):
        for j in range(cols):
            at = (q * cols + j) * width
            acc_ref[:, i, j, cut] += unband(got[:, at : at + width], channels)


def rest_body(
    mid_ref, rim_ref, side_ref, middle_ref, beside_ref, deep_ref, accmid_ref, accrim_ref, *rest
):
    *deep_halos, outmid_ref, outrim_ref = rest
    channels, rows, mids, depth, width = mid_ref.shape
    cols = mids + 2

    def around(r, j, cut):
        if j in (-1, cols):
            return band(side_ref[0 if j < 0 else 1, :, r, cut])
        return column(mid_ref, rim_ref, r, j, cut)

    for i in range(rows):
        for a in range(3):
            r = i + a - 1
            if 0 <= r < rows:
                operator = middle_ref[...] if a == 1 else beside_ref[a // 2]
                add_sums(operator, lambda cut, b: [around(r, j + b - 1, cut) for j in (0, cols - 1)], outrim_ref, i)
        odd = parity("trow")
        for n, halo_ref in enumerate(deep_halos):
            side = (1 - odd) if n == 0 else odd
            cut = pl.ds(pl.multiple_of(side * (depth - BAND), BAND), BAND)
            halo = three([halo_ref[i, :, j * width : (j + 1) * width] for j in range(cols)])
            halo = jnp.concatenate(halo, axis=0)
            if n == 1:
                halo = halo * has_second("trow").astype(F32)
            got = dot(deep_ref[side], halo.astype(BF16))
            for j in range(cols):
                acc_ref, at = (outrim_ref, j // (cols - 1)) if j in (0, cols - 1) else (outmid_ref, j - 1)
                acc_ref[:, i, at, cut] += unband(got[:, j * width : (j + 1) * width], channels)


def finished(x_ref, acc_ref, owed_refs, store):
    rows, cols = x_ref.shape[1:3]
    odd = parity("srow")
    paired = has_second("srow").astype(F32)
    for n, i in enumerate([(rows - 1) * (1 - odd), (rows - 1) * odd, *range(1, rows - 1)]):
        if n < 2 and owed_refs[n] is None:
            continue
        for j in range(cols):
            total = acc_ref[:, i, j]
            if n < 2:
                owed = owed_refs[n][:, j].astype(F32)
                total = total + (owed if n == 0 else owed * paired)
            store(i, j, (x_ref[:, i, j].astype(F32) + jnp.maximum(total, 0.0)).astype(BF16))


def sent_columns(rim_ref, col_refs):
    odd = parity("scol")
    for n, ref in zip((1 - odd, odd), col_refs):
        ref[...] = rim_ref[:, :, n]


def depth_body(mid_ref, rim_ref, after_ref, *deep_refs):
    channels, rows, mids, depth, _ = mid_ref.shape
    odd = parity("trow")
    shape = (channels, channels * BAND)
    first = lax.broadcasted_iota(jnp.int32, shape, 0) * BAND
    for n, ref in enumerate(deep_refs):
        end = (1 - odd) if n == 0 else odd
        cut = pl.ds(pl.multiple_of(end * (depth - BAND), BAND), BAND)
        pick = (lax.broadcasted_iota(jnp.int32, shape, 1) == first + end * (BAND - 1)).astype(BF16)
        for i in range(rows):
            tiles = [column(mid_ref, rim_ref, i, j, cut) for j in range(mids + 2)]
            ref[i] = dot(pick, jnp.concatenate(tiles, axis=1)).astype(BF16)


def mid_body(x_ref, acc_ref, a_ref, b_ref, out_ref):
    def store(i, j, value):
        out_ref[:, i, j] = value

    finished(x_ref, acc_ref, (a_ref, b_ref), store)


def begin_body(x_ref, acc_ref, a_ref, after_ref, out_ref):
    mid_body(x_ref, acc_ref, a_ref, None, out_ref)


def next_body(x_ref, acc_ref, b_ref, begun_ref, after_ref, out_ref, cola_ref, colb_ref):
    mid_body(x_ref, acc_ref, None, b_ref, out_ref)
    sent_columns(out_ref, (cola_ref, colb_ref))


def last_body(mid_ref, rim_ref, acc_ref, a_ref, b_ref, out_ref, hold_ref, sems):
    rows, mids = mid_ref.shape[1:3]
    copies = []
    for i in range(rows):
        for j in range(mids):
            copy = pltpu.make_async_copy(mid_ref.at[:, i, j], out_ref.at[:, i, j + 1], sems.at[len(copies)])
            copy.start()
            copies.append(copy)

    def store(i, j, value):
        hold_ref[:, i, j] = value
        copy = pltpu.make_async_copy(hold_ref.at[:, i, j], out_ref.at[:, i, j * (mids + 1)], sems.at[len(copies)])
        copy.start()
        copies.append(copy)

    finished(rim_ref, acc_ref, (a_ref, b_ref), store)
    for copy in copies:
        copy.wait()


def open_body(parts, x_ref, src_w_ref, tgt_w_ref, bias_ref, *rest):
    src_ref, tgt_ref, held_ref, beside_ref, cola_ref, colb_ref, sems = rest
    last = x_ref.shape[2] - 1
    odd = parity("scol")
    pairs = (
        (src_w_ref, src_ref),
        (x_ref.at[:, :, last * (1 - odd)], cola_ref),
        (x_ref.at[:, :, last * odd], colb_ref),
        (tgt_w_ref, tgt_ref),
        (bias_ref, held_ref),
    )
    copies = [pltpu.make_async_copy(a, b, sems.at[n]) for n, (a, b) in enumerate(pairs)]
    for copy in copies:
        copy.start()
    copies[0].wait()
    operators(parts, src_ref, None, (beside_ref,))
    for copy in copies[1:]:
        copy.wait()


def swap_first(value, axis):
    return lax.ppermute(value, axis, [(n, n ^ 1) for n in range(lax.axis_size(axis))])


def swap_second(value, axis, other=None):
    count = lax.axis_size(axis)
    inside = {n: n + 1 if n % 2 else n - 1 for n in range(1, count - 1)}
    if other is None:
        return lax.ppermute(value, axis, [*inside.items(), (0, count - 1), (count - 1, 0)])
    across = lax.axis_size(other)
    pairs = []
    for n in range(count):
        for m in range(across):
            target = (inside[n], m) if n in inside else (n, m ^ 1)
            pairs.append((n * across + m, target[0] * across + target[1]))
    return lax.ppermute(value, (axis, other), pairs)


def shards(volume, src_weight, tgt_weight, bias):
    layers = src_weight.shape[0]
    channels, rows, cols, depth, width = volume.shape
    axes = ("srow", "scol", "trow")
    counts = [lax.axis_size(n) for n in axes]
    assert all(count % 2 == 0 for count in counts) and rows > 1 and cols > 2 and layers > 1
    src_w = jnp.transpose(src_weight, (0, 2, 3, 1))
    tgt_w = jnp.transpose(tgt_weight, (0, 2, 3, 1))
    deep_swaps = 1 if counts[2] == 2 else 2
    mid_shape, rim_shape = ((channels, rows, n, depth, width) for n in (cols - 2, 2))
    line = VMEM((channels, rows, depth, width), BF16)
    owed_rim = VMEM((channels, 2, depth, width), BF16)
    early = [("beside", 0)]
    src_w, tgt_w, bias, beside_0, col_a, col_b = call(
        functools.partial(open_body, early),
        [VMEM(src_w.shape, BF16), VMEM(tgt_w.shape, BF16), VMEM(bias.shape, F32)] + operator_shapes(early, channels) + [line, line],
        (volume, src_w, tgt_w, bias),
        {n: HBM for n in range(4)},
        scratch=[pltpu.SemaphoreType.DMA((5,))],
    )
    made = {early[0]: beside_0}
    kinds = ("middle", "beside", "target", "near", "deep")
    owed_inner = [VMEM((channels, cols - 2, depth, width), BF16)]
    block, sum_a = (volume,), None
    for layer in range(layers):

        def on(body, *views):
            return functools.partial(whole, body, views) if layer == 0 else body

        both, base = (middle, sides), len(block)
        mid, rim = block[0], block[-1]
        beside = swap_first(col_a, "scol"), swap_second(col_b, "scol")
        which = (0, 1) if sum_a is None else (1,)
        sums = call(on(functools.partial(inner_body, which), *both), owed_inner * len(which), (*block, made["beside", layer]))
        sum_b = sums[-1]
        inner = swap_first(sums[0], "srow") if sum_a is None else got_a, swap_second(sum_b, "srow", "scol")
        if layer == 0:
            late = [(kind, n) for n in range(layers) for kind in kinds]
            made |= build([part for part in late if part not in early], src_w, tgt_w, sum_b)
        operator = {kind: made[kind, layer] for kind in kinds}
        parts = call(
            on(part_body, *both),
            [VMEM((2, channels * BAND, depth // BAND * width), F32)] * 2,
            (*block, operator["beside"], sum_b),
            {base + 1: pl.ANY},
        )
        a, b, side = call(
            edge_body,
            [owed_rim, owed_rim, VMEM((2, *line.shape), BF16)],
            (*beside, operator["beside"], *parts, operator["middle"]),
            {5: pl.ANY},
        )
        outer = swap_first(a, "srow"), swap_second(b, "srow", "scol")
        deep = call(
            on(depth_body, *both),
            [VMEM((rows, channels, cols * width), BF16)] * deep_swaps,
            (*block, b),
            {base: pl.ANY},
        )
        deeper = [swap_first(deep[0], "trow")]
        if deep_swaps == 2:
            deeper.append(swap_second(deep[1], "trow", "scol"))
        accs = call(
            on(functools.partial(own_body, layer), *both),
            [VMEM(mid_shape, F32), VMEM(rim_shape, F32)],
            (*block, *(operator[kind] for kind in ("middle", "beside", "target", "near")), bias, b),
            {base + 5: pl.ANY},
            scratch=[VMEM((depth // BAND, 3, channels * BAND, cols * width), BF16)],
        )
        acc_mid, acc_rim = call(
            on(rest_body, *both),
            [VMEM(mid_shape, F32), VMEM(rim_shape, F32)],
            (*block, side, *(operator[kind] for kind in ("middle", "beside", "deep")), *accs, *deeper),
            aliases={base + 4: 0, base + 5: 1},
        )
        (mid,) = call(on(mid_body, middle), [VMEM(mid_shape, BF16)], (mid, acc_mid, *inner))
        if layer < layers - 1:
            whole_rim = [VMEM(rim_shape, BF16)]
            (begun,) = call(on(begin_body, sides), whole_rim, (rim, acc_rim, outer[0], mid), {3: pl.ANY})
            (sum_a,) = call(functools.partial(inner_body, (0,)), owed_inner, (mid, begun, made["beside", layer + 1]))
            got_a = swap_first(sum_a, "srow")
            rim, col_a, col_b = call(
                on(next_body, sides),
                whole_rim + [line, line],
                (rim, acc_rim, outer[1], begun, sum_a),
                {4: pl.ANY},
                aliases={3: 0},
            )
            block = (mid, rim)
        else:
            (state,) = call(
                last_body,
                [jax.ShapeDtypeStruct(volume.shape, BF16)],
                (mid, rim, acc_rim, *outer),
                out_place=HBM,
                scratch=[VMEM(rim_shape, BF16), pltpu.SemaphoreType.DMA((rows * cols,))],
            )
    return state


def solution(mesh):
    return jax.shard_map(
        shards,
        mesh=mesh,
        in_specs=(P(None, "srow", "scol", "trow", None), P(), P(), P()),
        out_specs=P(None, "srow", "scol", "trow", None),
        check_vma=False,
    )
```

```python
import functools

import jax
import jax.numpy as jnp
from jax import lax
from jax.experimental import pallas as pl
from jax.experimental.pallas import tpu as pltpu
from jax.sharding import PartitionSpec as P

BAND = 32
EDGE = 16
SCOPED = 16 * 1024 * 1024
F32 = jnp.float32
BF16 = jnp.bfloat16
VMEM, HBM = pltpu.VMEM, pltpu.HBM
def parity(axis):
    return lax.axis_index(axis) % 2


def has_second(axis):
    at = lax.axis_index(axis)
    return (at > 0) & (at < lax.axis_size(axis) - 1)


def call(body, outs, args, places=None, out_place=VMEM, scratch=(), aliases=None):
    places = places or {}
    spaces = [places.get(n, VMEM) for n in range(len(args))]
    held = [pltpu.with_memory_space_constraint(a, m) if m in (VMEM, HBM) else a for a, m in zip(args, spaces)]
    return pl.pallas_call(
        body,
        out_shape=tuple(outs),
        in_specs=[pl.BlockSpec(memory_space=m) for m in spaces],
        out_specs=tuple(pl.BlockSpec(memory_space=out_place) for _ in outs),
        scratch_shapes=list(scratch),
        input_output_aliases=aliases or {},
        compiler_params=pltpu.CompilerParams(vmem_limit_bytes=SCOPED),
        cost_estimate=pl.CostEstimate(flops=10**6, bytes_accessed=10**4, transcendentals=0),
    )(*held)


def dot(a, b):
    return jnp.dot(a, b, preferred_element_type=F32)


def operators(parts, src_w_ref, tgt_w_ref, out_refs):
    channels = src_w_ref.shape[1]
    span, small = channels * BAND, channels * EDGE

    def columns(size):
        pick_c = lax.broadcasted_iota(jnp.int32, (channels, channels * size), 1) // size
        pick_r = lax.broadcasted_iota(jnp.int32, (channels, channels * size), 0)
        return (pick_c == pick_r).astype(BF16)

    wide, narrow, single = columns(BAND), columns(EDGE), columns(1)
    row = lax.broadcasted_iota(jnp.int32, (BAND, span), 0)
    shift = row - lax.broadcasted_iota(jnp.int32, (BAND, span), 1) % BAND
    row_s = lax.broadcasted_iota(jnp.int32, (BAND, small), 0)
    col_s = lax.broadcasted_iota(jnp.int32, (BAND, small), 1) % EDGE
    near = ((row_s == 0) & (col_s == EDGE - 1), (row_s == BAND - 1) & (col_s == 0))
    row_1 = lax.broadcasted_iota(jnp.int32, (BAND, channels), 0)
    deep = (row_1 == 0, row_1 == BAND - 1)
    spread = {}

    def taps(ref, layer, o, pick, key):
        key = (key, layer, o)
        if key not in spread:
            spread[key] = lax.dot_general(ref[layer, o], pick, (((0,), (0,)), ((), ())), preferred_element_type=F32)
        return spread[key]

    for (kind, layer), out_ref in zip(parts, out_refs):
        for o in range(channels):
            rows = slice(o * BAND, (o + 1) * BAND)
            for b in range(3):
                if kind == "middle":
                    got = taps(src_w_ref, layer, o, wide, "s")
                    values = {(): jnp.where(shift == 0, got[3 + b][None, :], 0.0)}
                elif kind == "beside":
                    got = taps(src_w_ref, layer, o, wide, "s")
                    values = {(n,): jnp.where(shift == 0, got[6 * n + b][None, :], 0.0) for n in range(2)}
                elif kind == "target":
                    got = taps(tgt_w_ref, layer, o, wide, "t")
                    value = jnp.where(shift == 1, got[b][None, :], 0.0)
                    value = jnp.where(shift == 0, got[3 + b][None, :], value)
                    values = {(): jnp.where(shift == -1, got[6 + b][None, :], value)}
                else:
                    pick, at = (narrow, near) if kind == "near" else (single, deep)
                    got = taps(tgt_w_ref, layer, o, pick, kind)
                    values = {(n,): jnp.where(at[n], got[6 * n + b][None, :], 0.0) for n in range(2)}
                for index, value in values.items():
                    size = value.shape[1]
                    out_ref[(*index, rows, slice(b * size, (b + 1) * size))] = value.astype(BF16)


def operator_shapes(parts, channels):
    span = channels * BAND
    widths = dict(middle=span, beside=span, target=span, near=channels * EDGE, deep=channels)
    lead = dict(middle=(), beside=(2,), target=(), near=(2,), deep=(2,))
    return [VMEM((*lead[kind], span, 3 * widths[kind]), BF16) for kind, _ in parts]


def build_body(parts, src_w_ref, tgt_w_ref, after_ref, *out_refs):
    operators(parts, src_w_ref, tgt_w_ref, out_refs)


def build(parts, src_w, tgt_w, after):
    got = call(
        functools.partial(build_body, parts),
        operator_shapes(parts, src_w.shape[1]),
        (src_w, tgt_w, after),
        {2: pl.ANY},
    )
    return dict(zip(parts, got))


class View:
    def __init__(self, ref, count, at):
        self.ref, self.count, self.at = ref, count, at

    @property
    def shape(self):
        channels, rows, _, depth, width = self.ref.shape
        return channels, rows, self.count, depth, width

    def __getitem__(self, index):
        first, i, j, *rest = index
        return self.ref[(first, i, self.at(j), *rest)]


def middle(x_ref):
    return View(x_ref, x_ref.shape[2] - 2, lambda j: j + 1)


def sides(x_ref):
    return View(x_ref, 2, lambda j: j * (x_ref.shape[2] - 1))


def whole(body, views, x_ref, *refs):
    body(*(view(x_ref) for view in views), *refs)


def band(tile):
    channels, size, width = tile.shape
    return tile.reshape(channels * size, width)


def unband(tile, channels):
    return tile.reshape(channels, tile.shape[0] // channels, tile.shape[1])


def src_operand(tiles, cols):
    return jnp.concatenate([jnp.concatenate(tiles[b : b + cols], axis=1) for b in range(3)], axis=0)


def sent_rows(rows):
    odd = parity("srow")
    return ((rows - 1) * (1 - odd), odd), ((rows - 1) * odd, 1 - odd)


def column(mid_ref, rim_ref, i, j, cut):
    last = mid_ref.shape[2] + 1
    return band(rim_ref[:, i, j // last, cut] if j in (0, last) else mid_ref[:, i, j - 1, cut])


def bands_of(depth):
    return [slice(start, start + BAND) for start in range(0, depth, BAND)]


def owed_sums(operator, tiles, out_ref):
    channels, cols, depth, width = out_ref.shape
    cuts = bands_of(depth)
    operand = jnp.concatenate([jnp.concatenate([t for cut in cuts for t in tiles(cut, b)], axis=1) for b in range(3)], axis=0)
    got = dot(operator, operand).astype(BF16)
    for q, cut in enumerate(cuts):
        for j in range(cols):
            at = (q * cols + j) * width
            out_ref[:, j, cut] = unband(got[:, at : at + width], channels)


def inner_body(which, mid_ref, rim_ref, beside_ref, *out_refs):
    rows, cols = mid_ref.shape[1:3]
    for n, out_ref in zip(which, out_refs):
        i, side = sent_rows(rows)[n]
        owed_sums(
            beside_ref[side], lambda cut, b: [column(mid_ref, rim_ref, i, j + b, cut) for j in range(cols)], out_ref
        )


def side_of(second):
    odd = parity("scol")
    return odd if second else 1 - odd


def all_bands(read, depth):
    return jnp.concatenate([band(read(cut)) for cut in bands_of(depth)], axis=1)


def own_taps(mid_ref, rim_ref, beside_ref, i, row_side, n):
    mids, depth = mid_ref.shape[2:4]
    span = mid_ref.shape[0] * BAND
    rim = all_bands(lambda cut: rim_ref[:, i, n, cut], depth)
    mid = all_bands(lambda cut: mid_ref[:, i, n * (mids - 1), cut], depth)
    inward = pl.multiple_of((2 - 2 * n) * span, span)
    return dot(beside_ref[row_side, :, span : 2 * span], rim) + dot(beside_ref[row_side, :, pl.ds(inward, span)], mid)


def halo_tap(halo_ref, beside_ref, i, row_side, n):
    span = halo_ref.shape[0] * BAND
    outward = pl.multiple_of(2 * n * span, span)
    return dot(beside_ref[row_side, :, pl.ds(outward, span)], all_bands(lambda cut: halo_ref[:, i, cut], halo_ref.shape[2]))


def put_sums(got, out_ref):
    channels, _, depth, width = out_ref.shape
    got = got.astype(BF16)
    for q, cut in enumerate(bands_of(depth)):
        out_ref[:, 0, cut] = unband(got[:, q * width : (q + 1) * width], channels)


def near_body(mid_ref, rim_ref, cola_ref, beside_ref, after_ref, a_ref, b_ref):
    n = side_of(False)
    for (i, row_side), out_ref in zip(sent_rows(mid_ref.shape[1]), (a_ref, b_ref)):
        got = own_taps(mid_ref, rim_ref, beside_ref, i, row_side, n) + halo_tap(cola_ref, beside_ref, i, row_side, n)
        put_sums(got, out_ref)


def part_body(mid_ref, rim_ref, beside_ref, after_ref, *part_refs):
    for (i, row_side), part_ref in zip(sent_rows(mid_ref.shape[1]), part_refs):
        part_ref[...] = own_taps(mid_ref, rim_ref, beside_ref, i, row_side, side_of(True))


def far_body(cola_ref, colb_ref, beside_ref, parta_ref, partb_ref, *refs):
    a_ref, b_ref, side_ref = refs[-3:]
    rows = cola_ref.shape[1]
    n, paired = side_of(True), has_second("scol")
    side_ref[side_of(False)] = cola_ref[...]

    @pl.when(paired)
    def _():
        side_ref[n] = colb_ref[...]

    @pl.when(jnp.logical_not(paired))
    def _():
        side_ref[n] = jnp.zeros_like(colb_ref)

    for (i, row_side), part_ref, out_ref in zip(sent_rows(rows), (parta_ref, partb_ref), (a_ref, b_ref)):
        put_sums(part_ref[...] + halo_tap(side_ref.at[n], beside_ref, i, row_side, n), out_ref)


def shifted(tile, step):
    lane = lax.broadcasted_iota(jnp.int32, tile.shape, 1)
    width = tile.shape[1]
    rolled = pltpu.roll(tile.astype(F32), step % width, 1)
    gone = 0 if step == 1 else width - 1
    return jnp.where(lane == gone, 0.0, rolled)


def three(tiles):
    return [jnp.concatenate([shifted(t, step) if step else t.astype(F32) for t in tiles], axis=1) for step in (1, 0, -1)]


def own_body(
    layer, mid_ref, rim_ref, middle_ref, beside_ref, target_ref, near_ref, bias_ref, after_ref, accmid_ref, accrim_ref, lane_ref
):
    channels, rows, mids, depth, width = mid_ref.shape
    cols = mids + 2
    cuts = bands_of(depth)
    shape = (BAND, cols * width)
    bias = [jnp.broadcast_to(bias_ref[layer : layer + 1, o : o + 1], shape) for o in range(channels)]
    bias = jnp.concatenate(bias, axis=0)
    for i in range(rows):
        for q, cut in enumerate(cuts):
            tiles = [column(mid_ref, rim_ref, i, j, cut) for j in range(cols)]
            lane_ref[q, 1] = jnp.concatenate(tiles, axis=1)
            for n, step in ((0, 1), (2, -1)):
                lane_ref[q, n] = jnp.concatenate([shifted(t, step).astype(BF16) for t in tiles], axis=1)
        for q, cut in enumerate(cuts):
            total = bias + dot(target_ref[...], lane_ref[q].reshape(3 * channels * BAND, cols * width))
            for side, other, start in ((0, q - 1, BAND - EDGE), (1, q + 1, 0)):
                if 0 <= other < len(cuts):
                    parts = [unband(lane_ref[other, n], channels)[:, start : start + EDGE] for n in range(3)]
                    total = total + dot(near_ref[side], jnp.concatenate([band(p) for p in parts], axis=0))
            for n, j in enumerate((0, cols - 1)):
                accrim_ref[:, i, n, cut] = unband(total[:, j * width : (j + 1) * width], channels)
            for j in range(1, cols - 1):
                accmid_ref[:, i, j - 1, cut] = unband(total[:, j * width : (j + 1) * width], channels)
        for a in range(3):
            r = i + a - 1
            if 0 <= r < rows:
                operator = middle_ref[...] if a == 1 else beside_ref[a // 2]
                add_sums(operator, lambda cut, b: [column(mid_ref, rim_ref, r, j + b, cut) for j in range(mids)], accmid_ref, i)


def add_sums(operator, tiles, acc_ref, i):
    channels, _, cols, depth, width = acc_ref.shape
    cuts = bands_of(depth)
    operand = jnp.concatenate([jnp.concatenate([t for cut in cuts for t in tiles(cut, b)], axis=1) for b in range(3)], axis=0)
    got = dot(operator, operand)
    for q, cut in enumerate(cuts):
        for j in range(cols):
            at = (q * cols + j) * width
            acc_ref[:, i, j, cut] += unband(got[:, at : at + width], channels)


def source_body(mid_ref, rim_ref, side_ref, middle_ref, beside_ref, *refs):
    outrim_ref = refs[-1]
    rows, mids = mid_ref.shape[1:3]
    cols = mids + 2

    def around(r, j, cut):
        if j in (-1, cols):
            return band(side_ref[0 if j < 0 else 1, :, r, cut])
        return column(mid_ref, rim_ref, r, j, cut)

    for i in range(rows):
        for a in range(3):
            r = i + a - 1
            if 0 <= r < rows:
                operator = middle_ref[...] if a == 1 else beside_ref[a // 2]
                add_sums(operator, lambda cut, b: [around(r, j + b - 1, cut) for j in (0, cols - 1)], outrim_ref, i)


def deep_body(deep_ref, *refs):
    *deep_halos, _, _, outmid_ref, outrim_ref = refs
    channels, rows, mids, depth, width = outmid_ref.shape
    cols = mids + 2
    odd = parity("trow")
    for i in range(rows):
        for n, halo_ref in enumerate(deep_halos):
            side = (1 - odd) if n == 0 else odd
            cut = pl.ds(pl.multiple_of(side * (depth - BAND), BAND), BAND)
            halo = three([halo_ref[i, :, j * width : (j + 1) * width] for j in range(cols)])
            halo = jnp.concatenate(halo, axis=0)
            if n == 1:
                halo = halo * has_second("trow").astype(F32)
            got = dot(deep_ref[side], halo.astype(BF16))
            for j in range(cols):
                acc_ref, at = (outrim_ref, j // (cols - 1)) if j in (0, cols - 1) else (outmid_ref, j - 1)
                acc_ref[:, i, at, cut] += unband(got[:, j * width : (j + 1) * width], channels)


def finished(x_ref, acc_ref, swaps, owed, store):
    rows = x_ref.shape[1]
    odd = parity("srow")
    paired = has_second("srow").astype(F32)
    for n in swaps:
        i = (rows - 1) * (odd if n else 1 - odd)
        for j, brought in owed(n):
            brought = brought.astype(F32)
            total = acc_ref[:, i, j] + (brought * paired if n else brought)
            store(i, j, (x_ref[:, i, j].astype(F32) + jnp.maximum(total, 0.0)).astype(BF16))


def sent_columns(rim_ref, col_refs):
    odd = parity("scol")
    for n, ref in zip((1 - odd, odd), col_refs):
        ref[...] = rim_ref[:, :, n]


def depth_body(mid_ref, rim_ref, after_ref, *deep_refs):
    channels, rows, mids, depth, _ = mid_ref.shape
    odd = parity("trow")
    shape = (channels, channels * BAND)
    first = lax.broadcasted_iota(jnp.int32, shape, 0) * BAND
    for n, ref in enumerate(deep_refs):
        end = (1 - odd) if n == 0 else odd
        cut = pl.ds(pl.multiple_of(end * (depth - BAND), BAND), BAND)
        pick = (lax.broadcasted_iota(jnp.int32, shape, 1) == first + end * (BAND - 1)).astype(BF16)
        for i in range(rows):
            tiles = [column(mid_ref, rim_ref, i, j, cut) for j in range(mids + 2)]
            ref[i] = dot(pick, jnp.concatenate(tiles, axis=1)).astype(BF16)


def mid_body(x_ref, acc_ref, a_ref, b_ref, out_ref):
    def store(i, j, value):
        out_ref[:, i, j] = value

    finished(x_ref, acc_ref, (0, 1), lambda n: [(j, (a_ref, b_ref)[n][:, j]) for j in range(x_ref.shape[2])], store)


def side_columns(near_ref, far_ref):
    return [(side_of(False), near_ref[:, 0]), (side_of(True), far_ref[:, 0])]


def begin_body(x_ref, acc_ref, near_ref, far_ref, after_ref, out_ref):
    def store(i, j, value):
        out_ref[:, i, j] = value

    finished(x_ref, acc_ref, (0,), lambda n: side_columns(near_ref, far_ref), store)


def next_body(x_ref, acc_ref, near_ref, far_ref, begun_ref, after_ref, out_ref, cola_ref, colb_ref):
    def store(i, j, value):
        out_ref[:, i, j] = value

    finished(x_ref, acc_ref, (1,), lambda n: side_columns(near_ref, far_ref), store)
    sent_columns(out_ref, (cola_ref, colb_ref))


def last_body(mid_ref, rim_ref, acc_ref, neara_ref, nearb_ref, fara_ref, farb_ref, out_ref, hold_ref, sems):
    rows, mids = mid_ref.shape[1:3]
    copies = []

    def write(source, i, j):
        copies.append(pltpu.make_async_copy(source, out_ref.at[:, i, j], sems.at[len(copies)]))
        copies[-1].start()

    for i in range(rows):
        for j in range(mids):
            write(mid_ref.at[:, i, j], i, j + 1)

    def store(i, j, value):
        hold_ref[:, i, j] = value
        write(hold_ref.at[:, i, j], i, j * (mids + 1))

    owed = lambda n: side_columns((neara_ref, nearb_ref)[n], (fara_ref, farb_ref)[n])
    finished(rim_ref, acc_ref, (0, 1), owed, store)
    for copy in copies:
        copy.wait()


def gate_body(*refs):
    refs[-1][...] = jnp.zeros_like(refs[-1])


def pass_body(x_ref, after_ref, out_ref):
    out_ref[...] = x_ref[...]


def open_body(parts, x_ref, src_w_ref, tgt_w_ref, bias_ref, *rest):
    src_ref, tgt_ref, held_ref, beside_ref, cola_ref, colb_ref, sems = rest
    last = x_ref.shape[2] - 1
    odd = parity("scol")
    pairs = (
        (src_w_ref, src_ref),
        (x_ref.at[:, :, last * (1 - odd)], cola_ref),
        (x_ref.at[:, :, last * odd], colb_ref),
        (tgt_w_ref, tgt_ref),
        (bias_ref, held_ref),
    )
    copies = [pltpu.make_async_copy(a, b, sems.at[n]) for n, (a, b) in enumerate(pairs)]
    for copy in copies:
        copy.start()
    copies[0].wait()
    operators(parts, src_ref, None, (beside_ref,))
    for copy in copies[1:]:
        copy.wait()


def swap_first(value, axis):
    return lax.ppermute(value, axis, [(n, n ^ 1) for n in range(lax.axis_size(axis))])


def swap_second(value, axis, other):
    count, across = lax.axis_size(axis), lax.axis_size(other)
    pairs = []
    for n in range(count):
        for m in range(across):
            if 0 < n < count - 1:
                target = (n + 1 if n % 2 else n - 1, m)
            else:
                target = (n, m ^ 1)
            pairs.append((n * across + m, target[0] * across + target[1]))
    return lax.ppermute(value, (axis, other), pairs)


def shards(volume, src_weight, tgt_weight, bias):
    layers = src_weight.shape[0]
    channels, rows, cols, depth, width = volume.shape
    axes = ("srow", "scol", "trow")
    counts = [lax.axis_size(n) for n in axes]
    assert all(count % 2 == 0 for count in counts) and rows > 1 and cols > 2 and layers > 1
    src_w = jnp.transpose(src_weight, (0, 2, 3, 1))
    tgt_w = jnp.transpose(tgt_weight, (0, 2, 3, 1))
    deep_swaps = 1 if counts[2] == 2 else 2
    mid_shape, rim_shape = ((channels, rows, n, depth, width) for n in (cols - 2, 2))
    line = VMEM((channels, rows, depth, width), BF16)
    owed_side = VMEM((channels, 1, depth, width), BF16)
    early = [("beside", 0)]
    src_w, tgt_w, bias, beside_0, col_a, col_b = call(
        functools.partial(open_body, early),
        [VMEM(src_w.shape, BF16), VMEM(tgt_w.shape, BF16), VMEM(bias.shape, F32)] + operator_shapes(early, channels) + [line, line],
        (volume, src_w, tgt_w, bias),
        {n: HBM for n in range(4)},
        scratch=[pltpu.SemaphoreType.DMA((5,))],
    )
    made = {early[0]: beside_0}
    kinds = ("middle", "beside", "target", "near", "deep")
    owed_inner = [VMEM((channels, cols - 2, depth, width), BF16)]
    block, sum_a = (volume,), None
    for layer in range(layers):

        def on(body, *views):
            return functools.partial(whole, body, views) if layer == 0 else body

        both, base = (middle, sides), len(block)
        mid, rim = block[0], block[-1]
        which = (0, 1) if sum_a is None else (1,)
        sums = call(on(functools.partial(inner_body, which), *both), owed_inner * len(which), (*block, made["beside", layer]))
        sum_b = sums[-1]
        if layer == 0:
            (col_b,) = call(pass_body, [line], (col_b, sum_b), {1: pl.ANY})
        beside = swap_first(col_a, "scol"), swap_second(col_b, "scol", "trow")
        inner = swap_first(sums[0], "srow") if sum_a is None else got_a, swap_second(sum_b, "srow", "scol")
        def own(after):
            return call(
                on(functools.partial(own_body, layer), *both),
                [VMEM(mid_shape, F32), VMEM(rim_shape, F32)],
                (*block, *(operator[kind] for kind in ("middle", "beside", "target", "near")), bias, after),
                {base + 5: pl.ANY},
                scratch=[VMEM((depth // BAND, 3, channels * BAND, cols * width), BF16)],
            )

        near = call(on(near_body, *both), [owed_side] * 2, (*block, beside[0], made["beside", layer], sum_b), {base + 2: pl.ANY})
        near_got = swap_first(near[0], "srow"), swap_second(near[1], "srow", "scol")
        if layer == 0:
            made |= build([(kind, 0) for kind in kinds if kind != "beside"], src_w, tgt_w, near[1])
        operator = {kind: made[kind, layer] for kind in kinds}
        parts = call(
            on(part_body, *both),
            [VMEM((channels * BAND, depth // BAND * width), F32)] * 2,
            (*block, operator["beside"], near[1]),
            {base + 1: pl.ANY},
        )
        deep = call(
            on(depth_body, *both),
            [VMEM((rows, channels, cols * width), BF16)] * deep_swaps,
            (*block, near[1]),
            {base: pl.ANY},
        )
        deeper = [swap_first(deep[0], "trow")]
        if deep_swaps == 2:
            deeper.append(swap_second(deep[1], "trow", "scol"))
        accs = own(parts[1])
        waited = (*inner, accs[0])
        (gate,) = call(gate_body, [VMEM((8, 128), F32)], waited, {n: pl.ANY for n in range(len(waited))})
        a, b, side = call(
            far_body,
            [owed_side, owed_side, VMEM((2, *line.shape), BF16)],
            (*beside, operator["beside"], *parts, gate),
            {5: pl.ANY},
        )
        far_got = swap_first(a, "srow"), swap_second(b, "srow", "scol")
        if layer < layers - 1:
            made |= build([(kind, layer + 1) for kind in kinds], src_w, tgt_w, b)
        (acc_rim,) = call(
            on(source_body, *both),
            [VMEM(rim_shape, F32)],
            (*block, side, operator["middle"], operator["beside"], *near_got, accs[1]),
            {base + 3: pl.ANY, base + 4: pl.ANY},
            aliases={base + 5: 0},
        )
        acc_mid, acc_rim = call(
            deep_body,
            [VMEM(mid_shape, F32), VMEM(rim_shape, F32)],
            (operator["deep"], *deeper, accs[0], acc_rim),
            aliases={1 + deep_swaps: 0, 2 + deep_swaps: 1},
        )
        (mid,) = call(on(mid_body, middle), [VMEM(mid_shape, BF16)], (mid, acc_mid, *inner))
        if layer < layers - 1:
            whole_rim = [VMEM(rim_shape, BF16)]
            (begun,) = call(on(begin_body, sides), whole_rim, (rim, acc_rim, near_got[0], far_got[0], mid), {4: pl.ANY})
            (sum_a,) = call(functools.partial(inner_body, (0,)), owed_inner, (mid, begun, made["beside", layer + 1]))
            got_a = swap_first(sum_a, "srow")
            rim, col_a, col_b = call(
                on(next_body, sides),
                whole_rim + [line, line],
                (rim, acc_rim, near_got[1], far_got[1], begun, sum_a),
                {5: pl.ANY},
                aliases={4: 0},
            )
            block = (mid, rim)
        else:
            (state,) = call(
                last_body,
                [jax.ShapeDtypeStruct(volume.shape, BF16)],
                (mid, rim, acc_rim, *near_got, *far_got),
                out_place=HBM,
                scratch=[VMEM(rim_shape, BF16), pltpu.SemaphoreType.DMA((rows * cols,))],
            )
    return state


def solution(mesh):
    return jax.shard_map(
        shards,
        mesh=mesh,
        in_specs=(P(None, "srow", "scol", "trow", None), P(), P(), P()),
        out_specs=P(None, "srow", "scol", "trow", None),
        check_vma=False,
    )
```

```python
import functools

import jax
import jax.numpy as jnp
from jax import lax
from jax.experimental import pallas as pl
from jax.experimental.pallas import tpu as pltpu
from jax.sharding import PartitionSpec as P

BAND = 32
EDGE = 16
SCOPED = 16 * 1024 * 1024
F32 = jnp.float32
BF16 = jnp.bfloat16
VMEM, HBM = pltpu.VMEM, pltpu.HBM
def parity(axis):
    return lax.axis_index(axis) % 2


def has_second(axis):
    at = lax.axis_index(axis)
    return (at > 0) & (at < lax.axis_size(axis) - 1)


def call(body, outs, args, places=None, out_place=VMEM, scratch=(), aliases=None, flops=10**6):
    places = places or {}
    spaces = [places.get(n, VMEM) for n in range(len(args))]
    held = [pltpu.with_memory_space_constraint(a, m) if m in (VMEM, HBM) else a for a, m in zip(args, spaces)]
    return pl.pallas_call(
        body,
        out_shape=tuple(outs),
        in_specs=[pl.BlockSpec(memory_space=m) for m in spaces],
        out_specs=tuple(pl.BlockSpec(memory_space=out_place) for _ in outs),
        scratch_shapes=list(scratch),
        input_output_aliases=aliases or {},
        compiler_params=pltpu.CompilerParams(vmem_limit_bytes=SCOPED),
        cost_estimate=pl.CostEstimate(flops=flops, bytes_accessed=10**4, transcendentals=0),
    )(*held)


def dot(a, b):
    return jnp.dot(a, b, preferred_element_type=F32)


def operators(parts, src_w_ref, tgt_w_ref, out_refs):
    channels = src_w_ref.shape[1]
    span, small = channels * BAND, channels * EDGE

    def columns(size):
        pick_c = lax.broadcasted_iota(jnp.int32, (channels, channels * size), 1) // size
        pick_r = lax.broadcasted_iota(jnp.int32, (channels, channels * size), 0)
        return (pick_c == pick_r).astype(BF16)

    wide, narrow, single = columns(BAND), columns(EDGE), columns(1)
    row = lax.broadcasted_iota(jnp.int32, (BAND, span), 0)
    shift = row - lax.broadcasted_iota(jnp.int32, (BAND, span), 1) % BAND
    row_s = lax.broadcasted_iota(jnp.int32, (BAND, small), 0)
    col_s = lax.broadcasted_iota(jnp.int32, (BAND, small), 1) % EDGE
    near = ((row_s == 0) & (col_s == EDGE - 1), (row_s == BAND - 1) & (col_s == 0))
    row_1 = lax.broadcasted_iota(jnp.int32, (BAND, channels), 0)
    deep = (row_1 == 0, row_1 == BAND - 1)
    spread = {}

    def taps(ref, layer, o, pick, key):
        key = (key, layer, o)
        if key not in spread:
            spread[key] = lax.dot_general(ref[layer, o], pick, (((0,), (0,)), ((), ())), preferred_element_type=F32)
        return spread[key]

    for (kind, layer), out_ref in zip(parts, out_refs):
        for o in range(channels):
            rows = slice(o * BAND, (o + 1) * BAND)
            for b in range(3):
                if kind == "middle":
                    got = taps(src_w_ref, layer, o, wide, "s")
                    values = {(): jnp.where(shift == 0, got[3 + b][None, :], 0.0)}
                elif kind == "beside":
                    got = taps(src_w_ref, layer, o, wide, "s")
                    values = {(n,): jnp.where(shift == 0, got[6 * n + b][None, :], 0.0) for n in range(2)}
                elif kind == "target":
                    got = taps(tgt_w_ref, layer, o, wide, "t")
                    value = jnp.where(shift == 1, got[b][None, :], 0.0)
                    value = jnp.where(shift == 0, got[3 + b][None, :], value)
                    values = {(): jnp.where(shift == -1, got[6 + b][None, :], value)}
                else:
                    pick, at = (narrow, near) if kind == "near" else (single, deep)
                    got = taps(tgt_w_ref, layer, o, pick, kind)
                    values = {(n,): jnp.where(at[n], got[6 * n + b][None, :], 0.0) for n in range(2)}
                for index, value in values.items():
                    size = value.shape[1]
                    out_ref[(*index, rows, slice(b * size, (b + 1) * size))] = value.astype(BF16)


def operator_shapes(parts, channels):
    span = channels * BAND
    widths = dict(middle=span, beside=span, target=span, near=channels * EDGE, deep=channels)
    lead = dict(middle=(), beside=(2,), target=(), near=(2,), deep=(2,))
    return [VMEM((*lead[kind], span, 3 * widths[kind]), BF16) for kind, _ in parts]


def build_body(parts, src_w_ref, tgt_w_ref, after_ref, *out_refs):
    operators(parts, src_w_ref, tgt_w_ref, out_refs)


def build(parts, src_w, tgt_w, after):
    got = call(
        functools.partial(build_body, parts),
        operator_shapes(parts, src_w.shape[1]),
        (src_w, tgt_w, after),
        {2: pl.ANY},
    )
    return dict(zip(parts, got))


class View:
    def __init__(self, ref, count, at):
        self.ref, self.count, self.at = ref, count, at

    @property
    def shape(self):
        channels, rows, _, depth, width = self.ref.shape
        return channels, rows, self.count, depth, width

    def __getitem__(self, index):
        first, i, j, *rest = index
        return self.ref[(first, i, self.at(j), *rest)]


def middle(x_ref):
    return View(x_ref, x_ref.shape[2] - 2, lambda j: j + 1)


def sides(x_ref):
    return View(x_ref, 2, lambda j: j * (x_ref.shape[2] - 1))


def whole(body, views, x_ref, *refs):
    body(*(view(x_ref) for view in views), *refs)


def band(tile):
    channels, size, width = tile.shape
    return tile.reshape(channels * size, width)


def unband(tile, channels):
    return tile.reshape(channels, tile.shape[0] // channels, tile.shape[1])


def src_operand(tiles, cols):
    return jnp.concatenate([jnp.concatenate(tiles[b : b + cols], axis=1) for b in range(3)], axis=0)


def sent_rows(rows):
    odd = parity("srow")
    return ((rows - 1) * (1 - odd), odd), ((rows - 1) * odd, 1 - odd)


def column(mid_ref, rim_ref, i, j, cut):
    last = mid_ref.shape[2] + 1
    return band(rim_ref[:, i, j // last, cut] if j in (0, last) else mid_ref[:, i, j - 1, cut])


def bands_of(depth):
    return [slice(start, start + BAND) for start in range(0, depth, BAND)]


def owed_sums(operator, tiles, cols, out_ref):
    channels, _, depth, width = out_ref.shape
    cuts = bands_of(depth)
    operand = jnp.concatenate([jnp.concatenate([t for cut in cuts for t in tiles(cut, b)], axis=1) for b in range(3)], axis=0)
    got = dot(operator, operand).astype(BF16)
    for q, cut in enumerate(cuts):
        for j in range(cols):
            at = (q * cols + j) * width
            out_ref[:, j, cut] = unband(got[:, at : at + width], channels)


def inner_body(which, mid_ref, rim_ref, beside_ref, *out_refs):
    rows, cols = mid_ref.shape[1:3]
    for n, out_ref in zip(which, out_refs):
        i, side = sent_rows(rows)[n]
        owed_sums(
            beside_ref[side], lambda cut, b: [column(mid_ref, rim_ref, i, j + b, cut) for j in range(cols)], cols, out_ref
        )


def side_of(second):
    odd = parity("scol")
    return odd if second else 1 - odd


def all_bands(read, depth):
    return jnp.concatenate([band(read(cut)) for cut in bands_of(depth)], axis=1)


def own_taps(mid_ref, rim_ref, beside_ref, i, row_side, n):
    mids, depth = mid_ref.shape[2:4]
    span = mid_ref.shape[0] * BAND
    rim = all_bands(lambda cut: rim_ref[:, i, n, cut], depth)
    mid = all_bands(lambda cut: mid_ref[:, i, n * (mids - 1), cut], depth)
    inward = pl.multiple_of((2 - 2 * n) * span, span)
    return dot(beside_ref[row_side, :, span : 2 * span], rim) + dot(beside_ref[row_side, :, pl.ds(inward, span)], mid)


def halo_tap(halo_ref, beside_ref, i, row_side, n):
    span = halo_ref.shape[0] * BAND
    outward = pl.multiple_of(2 * n * span, span)
    return dot(beside_ref[row_side, :, pl.ds(outward, span)], all_bands(lambda cut: halo_ref[:, i, cut], halo_ref.shape[2]))


def put_sums(got, out_ref, j=0):
    channels, _, depth, width = out_ref.shape
    got = got.astype(BF16)
    for q, cut in enumerate(bands_of(depth)):
        out_ref[:, j, cut] = unband(got[:, q * width : (q + 1) * width], channels)


def near_body(mid_ref, rim_ref, cola_ref, beside_ref, *refs):
    n, mids = side_of(False), mid_ref.shape[2]
    for (i, row_side), out_ref in zip(sent_rows(mid_ref.shape[1]), refs[-2:]):
        got = own_taps(mid_ref, rim_ref, beside_ref, i, row_side, n) + halo_tap(cola_ref, beside_ref, i, row_side, n)
        put_sums(got, out_ref, mids)


def part_body(mid_ref, rim_ref, beside_ref, after_ref, *part_refs):
    for (i, row_side), part_ref in zip(sent_rows(mid_ref.shape[1]), part_refs):
        part_ref[...] = own_taps(mid_ref, rim_ref, beside_ref, i, row_side, side_of(True))


def far_body(cola_ref, colb_ref, beside_ref, parta_ref, partb_ref, *refs):
    a_ref, b_ref, side_ref = refs[-3:]
    rows = cola_ref.shape[1]
    n, paired = side_of(True), has_second("scol")
    side_ref[side_of(False)] = cola_ref[...]

    @pl.when(paired)
    def _():
        side_ref[n] = colb_ref[...]

    @pl.when(jnp.logical_not(paired))
    def _():
        side_ref[n] = jnp.zeros_like(colb_ref)

    for (i, row_side), part_ref, out_ref in zip(sent_rows(rows), (parta_ref, partb_ref), (a_ref, b_ref)):
        put_sums(part_ref[...] + halo_tap(side_ref.at[n], beside_ref, i, row_side, n), out_ref)


def shifted(tile, step):
    lane = lax.broadcasted_iota(jnp.int32, tile.shape, 1)
    width = tile.shape[1]
    rolled = pltpu.roll(tile.astype(F32), step % width, 1)
    gone = 0 if step == 1 else width - 1
    return jnp.where(lane == gone, 0.0, rolled)


def three(tiles):
    return [jnp.concatenate([shifted(t, step) if step else t.astype(F32) for t in tiles], axis=1) for step in (1, 0, -1)]


def own_body(
    layer, mid_ref, rim_ref, middle_ref, beside_ref, target_ref, near_ref, bias_ref, after_ref, accmid_ref, accrim_ref, lane_ref
):
    channels, rows, mids, depth, width = mid_ref.shape
    cols = mids + 2
    cuts = bands_of(depth)
    shape = (BAND, cols * width)
    bias = [jnp.broadcast_to(bias_ref[layer : layer + 1, o : o + 1], shape) for o in range(channels)]
    bias = jnp.concatenate(bias, axis=0)
    for i in range(rows):
        for q, cut in enumerate(cuts):
            tiles = [column(mid_ref, rim_ref, i, j, cut) for j in range(cols)]
            lane_ref[q, 1] = jnp.concatenate(tiles, axis=1)
            for n, step in ((0, 1), (2, -1)):
                lane_ref[q, n] = jnp.concatenate([shifted(t, step).astype(BF16) for t in tiles], axis=1)
        for q, cut in enumerate(cuts):
            total = bias + dot(target_ref[...], lane_ref[q].reshape(3 * channels * BAND, cols * width))
            for side, other, start in ((0, q - 1, BAND - EDGE), (1, q + 1, 0)):
                if 0 <= other < len(cuts):
                    parts = [unband(lane_ref[other, n], channels)[:, start : start + EDGE] for n in range(3)]
                    total = total + dot(near_ref[side], jnp.concatenate([band(p) for p in parts], axis=0))
            for n, j in enumerate((0, cols - 1)):
                accrim_ref[:, i, n, cut] = unband(total[:, j * width : (j + 1) * width], channels)
            for j in range(1, cols - 1):
                accmid_ref[:, i, j - 1, cut] = unband(total[:, j * width : (j + 1) * width], channels)
        for a in range(3):
            r = i + a - 1
            if 0 <= r < rows:
                operator = middle_ref[...] if a == 1 else beside_ref[a // 2]
                add_sums(operator, lambda cut, b: [column(mid_ref, rim_ref, r, j + b, cut) for j in range(mids)], accmid_ref, i)


def add_sums(operator, tiles, acc_ref, i):
    channels, _, cols, depth, width = acc_ref.shape
    cuts = bands_of(depth)
    operand = jnp.concatenate([jnp.concatenate([t for cut in cuts for t in tiles(cut, b)], axis=1) for b in range(3)], axis=0)
    got = dot(operator, operand)
    for q, cut in enumerate(cuts):
        for j in range(cols):
            at = (q * cols + j) * width
            acc_ref[:, i, j, cut] += unband(got[:, at : at + width], channels)


def source_body(mid_ref, rim_ref, side_ref, middle_ref, beside_ref, *refs):
    outrim_ref = refs[-1]
    rows, mids = mid_ref.shape[1:3]
    cols = mids + 2

    def around(r, j, cut):
        if j in (-1, cols):
            return band(side_ref[0 if j < 0 else 1, :, r, cut])
        return column(mid_ref, rim_ref, r, j, cut)

    for i in range(rows):
        for a in range(3):
            r = i + a - 1
            if 0 <= r < rows:
                operator = middle_ref[...] if a == 1 else beside_ref[a // 2]
                add_sums(operator, lambda cut, b: [around(r, j + b - 1, cut) for j in (0, cols - 1)], outrim_ref, i)


def deep_body(deep_ref, *refs):
    *deep_halos, _, _, outmid_ref, outrim_ref = refs
    channels, rows, mids, depth, width = outmid_ref.shape
    cols = mids + 2
    odd = parity("trow")
    for i in range(rows):
        for n, halo_ref in enumerate(deep_halos):
            side = (1 - odd) if n == 0 else odd
            cut = pl.ds(pl.multiple_of(side * (depth - BAND), BAND), BAND)
            halo = three([halo_ref[i, :, j * width : (j + 1) * width] for j in range(cols)])
            halo = jnp.concatenate(halo, axis=0)
            if n == 1:
                halo = halo * has_second("trow").astype(F32)
            got = dot(deep_ref[side], halo.astype(BF16))
            for j in range(cols):
                acc_ref, at = (outrim_ref, j // (cols - 1)) if j in (0, cols - 1) else (outmid_ref, j - 1)
                acc_ref[:, i, at, cut] += unband(got[:, j * width : (j + 1) * width], channels)


def finished(x_ref, acc_ref, swaps, owed, store):
    rows = x_ref.shape[1]
    odd = parity("srow")
    paired = has_second("srow").astype(F32)
    for n in swaps:
        i = (rows - 1) * (odd if n else 1 - odd)
        for j, brought in owed(n):
            brought = brought.astype(F32)
            total = acc_ref[:, i, j] + (brought * paired if n else brought)
            store(i, j, (x_ref[:, i, j].astype(F32) + jnp.maximum(total, 0.0)).astype(BF16))


def sent_columns(rim_ref, col_refs):
    odd = parity("scol")
    for n, ref in zip((1 - odd, odd), col_refs):
        ref[...] = rim_ref[:, :, n]


def depth_body(mid_ref, rim_ref, after_ref, *deep_refs):
    channels, rows, mids, depth, _ = mid_ref.shape
    odd = parity("trow")
    shape = (channels, channels * BAND)
    first = lax.broadcasted_iota(jnp.int32, shape, 0) * BAND
    for n, ref in enumerate(deep_refs):
        end = (1 - odd) if n == 0 else odd
        cut = pl.ds(pl.multiple_of(end * (depth - BAND), BAND), BAND)
        pick = (lax.broadcasted_iota(jnp.int32, shape, 1) == first + end * (BAND - 1)).astype(BF16)
        for i in range(rows):
            tiles = [column(mid_ref, rim_ref, i, j, cut) for j in range(mids + 2)]
            ref[i] = dot(pick, jnp.concatenate(tiles, axis=1)).astype(BF16)


def mid_body(x_ref, acc_ref, a_ref, b_ref, out_ref):
    def store(i, j, value):
        out_ref[:, i, j] = value

    finished(x_ref, acc_ref, (0, 1), lambda n: [(j, (a_ref, b_ref)[n][:, j]) for j in range(x_ref.shape[2])], store)


def side_columns(near_ref, far_ref):
    return [(side_of(False), near_ref[:, near_ref.shape[1] - 1]), (side_of(True), far_ref[:, 0])]


def begin_body(x_ref, acc_ref, near_ref, far_ref, after_ref, out_ref):
    def store(i, j, value):
        out_ref[:, i, j] = value

    finished(x_ref, acc_ref, (0,), lambda n: side_columns(near_ref, far_ref), store)


def next_body(x_ref, acc_ref, near_ref, far_ref, begun_ref, after_ref, out_ref, cola_ref, colb_ref):
    def store(i, j, value):
        out_ref[:, i, j] = value

    finished(x_ref, acc_ref, (1,), lambda n: side_columns(near_ref, far_ref), store)
    sent_columns(out_ref, (cola_ref, colb_ref))


def last_body(mid_ref, rim_ref, acc_ref, neara_ref, nearb_ref, fara_ref, farb_ref, out_ref, hold_ref, sems):
    rows, mids = mid_ref.shape[1:3]
    copies = []

    def write(source, i, j):
        copies.append(pltpu.make_async_copy(source, out_ref.at[:, i, j], sems.at[len(copies)]))
        copies[-1].start()

    for i in range(rows):
        for j in range(mids):
            write(mid_ref.at[:, i, j], i, j + 1)

    def store(i, j, value):
        hold_ref[:, i, j] = value
        write(hold_ref.at[:, i, j], i, j * (mids + 1))

    owed = lambda n: side_columns((neara_ref, nearb_ref)[n], (fara_ref, farb_ref)[n])
    finished(rim_ref, acc_ref, (0, 1), owed, store)
    for copy in copies:
        copy.wait()


def pass_body(x_ref, after_ref, also_ref, out_ref):
    out_ref[...] = x_ref[...]


def open_body(parts, x_ref, src_w_ref, tgt_w_ref, bias_ref, *rest):
    src_ref, tgt_ref, held_ref, beside_ref, cola_ref, colb_ref, sems = rest
    last = x_ref.shape[2] - 1
    odd = parity("scol")
    pairs = (
        (src_w_ref, src_ref),
        (x_ref.at[:, :, last * (1 - odd)], cola_ref),
        (x_ref.at[:, :, last * odd], colb_ref),
        (tgt_w_ref, tgt_ref),
        (bias_ref, held_ref),
    )
    copies = [pltpu.make_async_copy(a, b, sems.at[n]) for n, (a, b) in enumerate(pairs)]
    for copy in copies:
        copy.start()
    copies[0].wait()
    operators(parts, src_ref, None, (beside_ref,))
    for copy in copies[1:]:
        copy.wait()


def swap_first(value, axis):
    return lax.ppermute(value, axis, [(n, n ^ 1) for n in range(lax.axis_size(axis))])


def swap_second(value, axis, other):
    count, across = lax.axis_size(axis), lax.axis_size(other)
    pairs = []
    for n in range(count):
        for m in range(across):
            if 0 < n < count - 1:
                target = (n + 1 if n % 2 else n - 1, m)
            else:
                target = (n, m ^ 1)
            pairs.append((n * across + m, target[0] * across + target[1]))
    return lax.ppermute(value, (axis, other), pairs)


def shards(volume, src_weight, tgt_weight, bias):
    layers = src_weight.shape[0]
    channels, rows, cols, depth, width = volume.shape
    axes = ("srow", "scol", "trow")
    counts = [lax.axis_size(n) for n in axes]
    assert all(count % 2 == 0 for count in counts) and rows > 1 and cols > 2 and layers > 1
    src_w = jnp.transpose(src_weight, (0, 2, 3, 1))
    tgt_w = jnp.transpose(tgt_weight, (0, 2, 3, 1))
    deep_swaps = 1 if counts[2] == 2 else 2
    mid_shape, rim_shape = ((channels, rows, n, depth, width) for n in (cols - 2, 2))
    line = VMEM((channels, rows, depth, width), BF16)
    owed_side = VMEM((channels, 1, depth, width), BF16)
    early = [("beside", 0)]
    src_w, tgt_w, bias, beside_0, col_a, col_b = call(
        functools.partial(open_body, early),
        [VMEM(src_w.shape, BF16), VMEM(tgt_w.shape, BF16), VMEM(bias.shape, F32)] + operator_shapes(early, channels) + [line, line],
        (volume, src_w, tgt_w, bias),
        {n: HBM for n in range(4)},
        scratch=[pltpu.SemaphoreType.DMA((5,))],
    )
    made = {early[0]: beside_0}
    kinds = ("middle", "beside", "target", "near", "deep")
    owed_inner = [VMEM((channels, cols - 1, depth, width), BF16)]
    block, sum_a = (volume,), None
    for layer in range(layers):

        def on(body, *views):
            return functools.partial(whole, body, views) if layer == 0 else body

        both, base = (middle, sides), len(block)
        mid, rim = block[0], block[-1]
        which = (0, 1) if sum_a is None else (1,)
        sums = call(on(functools.partial(inner_body, which), *both), owed_inner * len(which), (*block, made["beside", layer]))
        sum_a, sum_b = sums if sum_a is None else (sum_a, *sums)
        got_col_a = swap_first(col_a, "scol")
        near = call(
            on(near_body, *both),
            owed_inner * 2,
            (*block, got_col_a, made["beside", layer], sum_a, sum_b),
            aliases={base + 2: 0, base + 3: 1},
        )
        near_got = swap_first(near[0], "srow"), swap_second(near[1], "srow", "scol")
        (col_b,) = call(pass_body, [line], (col_b, *near), {1: pl.ANY, 2: pl.ANY})
        beside = got_col_a, swap_second(col_b, "scol", "trow")
        if layer == 0:
            made |= build([(kind, 0) for kind in kinds if kind != "beside"], src_w, tgt_w, sum_b)
        operator = {kind: made[kind, layer] for kind in kinds}
        parts = call(
            on(part_body, *both),
            [VMEM((channels * BAND, depth // BAND * width), F32)] * 2,
            (*block, operator["beside"], sum_b),
            {base + 1: pl.ANY},
        )
        deep = call(
            on(depth_body, *both),
            [VMEM((rows, channels, cols * width), BF16)] * deep_swaps,
            (*block, near[1]),
            {base: pl.ANY},
        )
        deeper = [swap_first(deep[0], "trow")]
        if deep_swaps == 2:
            deeper.append(swap_second(deep[1], "trow", "scol"))
        accs = call(
            on(functools.partial(own_body, layer), *both),
            [VMEM(mid_shape, F32), VMEM(rim_shape, F32)],
            (*block, *(operator[kind] for kind in ("middle", "beside", "target", "near")), bias, parts[1]),
            {base + 5: pl.ANY},
            scratch=[VMEM((depth // BAND, 3, channels * BAND, cols * width), BF16)],
            flops=10**10,
        )
        a, b, side = call(
            far_body,
            [owed_side, owed_side, VMEM((2, *line.shape), BF16)],
            (*beside, operator["beside"], *parts, accs[0]),
            {5: pl.ANY},
        )
        far_got = swap_first(a, "srow"), swap_second(b, "srow", "scol")
        if layer < layers - 1:
            made |= build([(kind, layer + 1) for kind in kinds], src_w, tgt_w, b)
        (acc_rim,) = call(
            on(source_body, *both),
            [VMEM(rim_shape, F32)],
            (*block, side, operator["middle"], operator["beside"], accs[1]),
            aliases={base + 3: 0},
        )
        acc_mid, acc_rim = call(
            deep_body,
            [VMEM(mid_shape, F32), VMEM(rim_shape, F32)],
            (operator["deep"], *deeper, accs[0], acc_rim),
            aliases={1 + deep_swaps: 0, 2 + deep_swaps: 1},
        )
        (mid,) = call(on(mid_body, middle), [VMEM(mid_shape, BF16)], (mid, acc_mid, *near_got))
        if layer < layers - 1:
            whole_rim = [VMEM(rim_shape, BF16)]
            (begun,) = call(on(begin_body, sides), whole_rim, (rim, acc_rim, near_got[0], far_got[0], mid), {4: pl.ANY})
            (sum_a,) = call(functools.partial(inner_body, (0,)), owed_inner, (mid, begun, made["beside", layer + 1]))
            rim, col_a, col_b = call(
                on(next_body, sides),
                whole_rim + [line, line],
                (rim, acc_rim, near_got[1], far_got[1], begun, sum_a),
                {5: pl.ANY},
                aliases={4: 0},
            )
            block = (mid, rim)
        else:
            (state,) = call(
                last_body,
                [jax.ShapeDtypeStruct(volume.shape, BF16)],
                (mid, rim, acc_rim, *near_got, *far_got),
                out_place=HBM,
                scratch=[VMEM(rim_shape, BF16), pltpu.SemaphoreType.DMA((rows * cols,))],
            )
    return state


def solution(mesh):
    return jax.shard_map(
        shards,
        mesh=mesh,
        in_specs=(P(None, "srow", "scol", "trow", None), P(), P(), P()),
        out_specs=P(None, "srow", "scol", "trow", None),
        check_vma=False,
    )
```

```python
import functools

import jax
import jax.numpy as jnp
from jax import lax
from jax.experimental import pallas as pl
from jax.experimental.pallas import tpu as pltpu
from jax.sharding import PartitionSpec as P

BAND = 32
EDGE = 16
SCOPED = 16 * 1024 * 1024
F32 = jnp.float32
BF16 = jnp.bfloat16
VMEM, HBM = pltpu.VMEM, pltpu.HBM
def parity(axis):
    return lax.axis_index(axis) % 2


def has_second(axis):
    at = lax.axis_index(axis)
    return (at > 0) & (at < lax.axis_size(axis) - 1)


def call(body, outs, args, places=None, out_place=VMEM, scratch=(), aliases=None, flops=10**6):
    places = places or {}
    spaces = [places.get(n, VMEM) for n in range(len(args))]
    held = [pltpu.with_memory_space_constraint(a, m) if m in (VMEM, HBM) else a for a, m in zip(args, spaces)]
    return pl.pallas_call(
        body,
        out_shape=tuple(outs),
        in_specs=[pl.BlockSpec(memory_space=m) for m in spaces],
        out_specs=tuple(pl.BlockSpec(memory_space=out_place) for _ in outs),
        scratch_shapes=list(scratch),
        input_output_aliases=aliases or {},
        compiler_params=pltpu.CompilerParams(vmem_limit_bytes=SCOPED),
        cost_estimate=pl.CostEstimate(flops=flops, bytes_accessed=10**4, transcendentals=0),
    )(*held)


def dot(a, b):
    return jnp.dot(a, b, preferred_element_type=F32)


def operators(parts, src_w_ref, tgt_w_ref, out_refs):
    channels = src_w_ref.shape[1]
    span, small = channels * BAND, channels * EDGE

    def columns(size):
        pick_c = lax.broadcasted_iota(jnp.int32, (channels, channels * size), 1) // size
        pick_r = lax.broadcasted_iota(jnp.int32, (channels, channels * size), 0)
        return (pick_c == pick_r).astype(BF16)

    wide, narrow, single = columns(BAND), columns(EDGE), columns(1)
    row = lax.broadcasted_iota(jnp.int32, (BAND, span), 0)
    shift = row - lax.broadcasted_iota(jnp.int32, (BAND, span), 1) % BAND
    row_s = lax.broadcasted_iota(jnp.int32, (BAND, small), 0)
    col_s = lax.broadcasted_iota(jnp.int32, (BAND, small), 1) % EDGE
    near = ((row_s == 0) & (col_s == EDGE - 1), (row_s == BAND - 1) & (col_s == 0))
    row_1 = lax.broadcasted_iota(jnp.int32, (BAND, channels), 0)
    deep = (row_1 == 0, row_1 == BAND - 1)
    spread = {}

    def taps(ref, layer, o, pick, key):
        key = (key, layer, o)
        if key not in spread:
            spread[key] = lax.dot_general(ref[layer, o], pick, (((0,), (0,)), ((), ())), preferred_element_type=F32)
        return spread[key]

    for (kind, layer), out_ref in zip(parts, out_refs):
        for o in range(channels):
            rows = slice(o * BAND, (o + 1) * BAND)
            for b in range(3):
                if kind == "middle":
                    got = taps(src_w_ref, layer, o, wide, "s")
                    values = {(): jnp.where(shift == 0, got[3 + b][None, :], 0.0)}
                elif kind == "beside":
                    got = taps(src_w_ref, layer, o, wide, "s")
                    values = {(n,): jnp.where(shift == 0, got[6 * n + b][None, :], 0.0) for n in range(2)}
                elif kind == "target":
                    got = taps(tgt_w_ref, layer, o, wide, "t")
                    value = jnp.where(shift == 1, got[b][None, :], 0.0)
                    value = jnp.where(shift == 0, got[3 + b][None, :], value)
                    values = {(): jnp.where(shift == -1, got[6 + b][None, :], value)}
                else:
                    pick, at = (narrow, near) if kind == "near" else (single, deep)
                    got = taps(tgt_w_ref, layer, o, pick, kind)
                    values = {(n,): jnp.where(at[n], got[6 * n + b][None, :], 0.0) for n in range(2)}
                for index, value in values.items():
                    size = value.shape[1]
                    out_ref[(*index, rows, slice(b * size, (b + 1) * size))] = value.astype(BF16)


def operator_shapes(parts, channels):
    span = channels * BAND
    widths = dict(middle=span, beside=span, target=span, near=channels * EDGE, deep=channels)
    lead = dict(middle=(), beside=(2,), target=(), near=(2,), deep=(2,))
    return [VMEM((*lead[kind], span, 3 * widths[kind]), BF16) for kind, _ in parts]


def build_body(parts, src_w_ref, tgt_w_ref, after_ref, *out_refs):
    operators(parts, src_w_ref, tgt_w_ref, out_refs)


def build(parts, src_w, tgt_w, after):
    got = call(
        functools.partial(build_body, parts),
        operator_shapes(parts, src_w.shape[1]),
        (src_w, tgt_w, after),
        {2: pl.ANY},
    )
    return dict(zip(parts, got))


class View:
    def __init__(self, ref, count, at):
        self.ref, self.count, self.at = ref, count, at

    @property
    def shape(self):
        channels, rows, _, depth, width = self.ref.shape
        return channels, rows, self.count, depth, width

    def __getitem__(self, index):
        first, i, j, *rest = index
        return self.ref[(first, i, self.at(j), *rest)]


def middle(x_ref):
    return View(x_ref, x_ref.shape[2] - 2, lambda j: j + 1)


def sides(x_ref):
    return View(x_ref, 2, lambda j: j * (x_ref.shape[2] - 1))


def whole(body, views, x_ref, *refs):
    body(*(view(x_ref) for view in views), *refs)


def band(tile):
    channels, size, width = tile.shape
    return tile.reshape(channels * size, width)


def unband(tile, channels):
    return tile.reshape(channels, tile.shape[0] // channels, tile.shape[1])


def src_operand(tiles, cols):
    return jnp.concatenate([jnp.concatenate(tiles[b : b + cols], axis=1) for b in range(3)], axis=0)


def sent_rows(rows):
    odd = parity("srow")
    return ((rows - 1) * (1 - odd), odd), ((rows - 1) * odd, 1 - odd)


def column(mid_ref, rim_ref, i, j, cut):
    last = mid_ref.shape[2] + 1
    return band(rim_ref[:, i, j // last, cut] if j in (0, last) else mid_ref[:, i, j - 1, cut])


def bands_of(depth):
    return [slice(start, start + BAND) for start in range(0, depth, BAND)]


def owed_sums(operator, tiles, cols, out_ref):
    channels, _, depth, width = out_ref.shape
    cuts = bands_of(depth)
    operand = jnp.concatenate([jnp.concatenate([t for cut in cuts for t in tiles(cut, b)], axis=1) for b in range(3)], axis=0)
    got = dot(operator, operand).astype(BF16)
    for q, cut in enumerate(cuts):
        for j in range(cols):
            at = (q * cols + j) * width
            out_ref[:, j, cut] = unband(got[:, at : at + width], channels)


def inner_body(which, mid_ref, rim_ref, beside_ref, *out_refs):
    rows, cols = mid_ref.shape[1:3]
    for n, out_ref in zip(which, out_refs):
        i, side = sent_rows(rows)[n]
        owed_sums(
            beside_ref[side], lambda cut, b: [column(mid_ref, rim_ref, i, j + b, cut) for j in range(cols)], cols, out_ref
        )


def side_of(second):
    odd = parity("scol")
    return odd if second else 1 - odd


def all_bands(read, depth):
    return jnp.concatenate([band(read(cut)) for cut in bands_of(depth)], axis=1)


def own_taps(mid_ref, rim_ref, beside_ref, i, row_side, n):
    mids, depth = mid_ref.shape[2:4]
    span = mid_ref.shape[0] * BAND
    rim = all_bands(lambda cut: rim_ref[:, i, n, cut], depth)
    mid = all_bands(lambda cut: mid_ref[:, i, n * (mids - 1), cut], depth)
    inward = pl.multiple_of((2 - 2 * n) * span, span)
    return dot(beside_ref[row_side, :, span : 2 * span], rim) + dot(beside_ref[row_side, :, pl.ds(inward, span)], mid)


def halo_tap(halo_ref, beside_ref, i, row_side, n):
    span = halo_ref.shape[0] * BAND
    outward = pl.multiple_of(2 * n * span, span)
    return dot(beside_ref[row_side, :, pl.ds(outward, span)], all_bands(lambda cut: halo_ref[:, i, cut], halo_ref.shape[2]))


def put_sums(got, out_ref, j=0):
    channels, _, depth, width = out_ref.shape
    got = got.astype(BF16)
    for q, cut in enumerate(bands_of(depth)):
        out_ref[:, j, cut] = unband(got[:, q * width : (q + 1) * width], channels)


def near_body(mid_ref, rim_ref, cola_ref, beside_ref, *refs):
    n, mids = side_of(False), mid_ref.shape[2]
    for (i, row_side), out_ref in zip(sent_rows(mid_ref.shape[1]), refs[-2:]):
        got = own_taps(mid_ref, rim_ref, beside_ref, i, row_side, n) + halo_tap(cola_ref, beside_ref, i, row_side, n)
        put_sums(got, out_ref, mids)


def part_body(mid_ref, rim_ref, beside_ref, after_ref, *part_refs):
    for (i, row_side), part_ref in zip(sent_rows(mid_ref.shape[1]), part_refs):
        part_ref[...] = own_taps(mid_ref, rim_ref, beside_ref, i, row_side, side_of(True))


def far_body(cola_ref, colb_ref, beside_ref, parta_ref, partb_ref, *refs):
    a_ref, b_ref, side_ref = refs[-3:]
    rows = cola_ref.shape[1]
    n, paired = side_of(True), has_second("scol")
    side_ref[side_of(False)] = cola_ref[...]

    @pl.when(paired)
    def _():
        side_ref[n] = colb_ref[...]

    @pl.when(jnp.logical_not(paired))
    def _():
        side_ref[n] = jnp.zeros_like(colb_ref)

    for (i, row_side), part_ref, out_ref in zip(sent_rows(rows), (parta_ref, partb_ref), (a_ref, b_ref)):
        put_sums(part_ref[...] + halo_tap(side_ref.at[n], beside_ref, i, row_side, n), out_ref)


def shifted(tile, step):
    lane = lax.broadcasted_iota(jnp.int32, tile.shape, 1)
    width = tile.shape[1]
    rolled = pltpu.roll(tile.astype(F32), step % width, 1)
    gone = 0 if step == 1 else width - 1
    return jnp.where(lane == gone, 0.0, rolled)


def three(tiles):
    return [jnp.concatenate([shifted(t, step) if step else t.astype(F32) for t in tiles], axis=1) for step in (1, 0, -1)]


def own_body(
    layer, mid_ref, rim_ref, middle_ref, beside_ref, target_ref, near_ref, bias_ref, after_ref, accmid_ref, accrim_ref, lane_ref
):
    channels, rows, mids, depth, width = mid_ref.shape
    cols = mids + 2
    cuts = bands_of(depth)
    shape = (BAND, cols * width)
    bias = [jnp.broadcast_to(bias_ref[layer : layer + 1, o : o + 1], shape) for o in range(channels)]
    bias = jnp.concatenate(bias, axis=0)
    for i in range(rows):
        for q, cut in enumerate(cuts):
            tiles = [column(mid_ref, rim_ref, i, j, cut) for j in range(cols)]
            lane_ref[q, 1] = jnp.concatenate(tiles, axis=1)
            for n, step in ((0, 1), (2, -1)):
                lane_ref[q, n] = jnp.concatenate([shifted(t, step).astype(BF16) for t in tiles], axis=1)
        for q, cut in enumerate(cuts):
            total = bias + dot(target_ref[...], lane_ref[q].reshape(3 * channels * BAND, cols * width))
            for side, other, start in ((0, q - 1, BAND - EDGE), (1, q + 1, 0)):
                if 0 <= other < len(cuts):
                    parts = [unband(lane_ref[other, n], channels)[:, start : start + EDGE] for n in range(3)]
                    total = total + dot(near_ref[side], jnp.concatenate([band(p) for p in parts], axis=0))
            for n, j in enumerate((0, cols - 1)):
                accrim_ref[:, i, n, cut] = unband(total[:, j * width : (j + 1) * width], channels)
            for j in range(1, cols - 1):
                accmid_ref[:, i, j - 1, cut] = unband(total[:, j * width : (j + 1) * width], channels)
        for a in range(3):
            r = i + a - 1
            if 0 <= r < rows:
                operator = middle_ref[...] if a == 1 else beside_ref[a // 2]
                add_sums(operator, lambda cut, b: [column(mid_ref, rim_ref, r, j + b, cut) for j in range(mids)], accmid_ref, i)


def add_sums(operator, tiles, acc_ref, i):
    channels, _, cols, depth, width = acc_ref.shape
    cuts = bands_of(depth)
    operand = jnp.concatenate([jnp.concatenate([t for cut in cuts for t in tiles(cut, b)], axis=1) for b in range(3)], axis=0)
    got = dot(operator, operand)
    for q, cut in enumerate(cuts):
        for j in range(cols):
            at = (q * cols + j) * width
            acc_ref[:, i, j, cut] += unband(got[:, at : at + width], channels)


def source_body(mid_ref, rim_ref, side_ref, middle_ref, beside_ref, *refs):
    outrim_ref = refs[-1]
    rows, mids = mid_ref.shape[1:3]
    cols = mids + 2

    def around(r, j, cut):
        if j in (-1, cols):
            return band(side_ref[0 if j < 0 else 1, :, r, cut])
        return column(mid_ref, rim_ref, r, j, cut)

    for i in range(rows):
        for a in range(3):
            r = i + a - 1
            if 0 <= r < rows:
                operator = middle_ref[...] if a == 1 else beside_ref[a // 2]
                add_sums(operator, lambda cut, b: [around(r, j + b - 1, cut) for j in (0, cols - 1)], outrim_ref, i)


def deep_body(deep_ref, *refs):
    *deep_halos, _, _, outmid_ref, outrim_ref = refs
    channels, rows, mids, depth, width = outmid_ref.shape
    cols = mids + 2
    odd = parity("trow")
    for i in range(rows):
        for n, halo_ref in enumerate(deep_halos):
            side = (1 - odd) if n == 0 else odd
            cut = pl.ds(pl.multiple_of(side * (depth - BAND), BAND), BAND)
            halo = three([halo_ref[i, :, j * width : (j + 1) * width] for j in range(cols)])
            halo = jnp.concatenate(halo, axis=0)
            if n == 1:
                halo = halo * has_second("trow").astype(F32)
            got = dot(deep_ref[side], halo.astype(BF16))
            for j in range(cols):
                acc_ref, at = (outrim_ref, j // (cols - 1)) if j in (0, cols - 1) else (outmid_ref, j - 1)
                acc_ref[:, i, at, cut] += unband(got[:, j * width : (j + 1) * width], channels)


def finished(x_ref, acc_ref, swaps, owed, store):
    rows = x_ref.shape[1]
    odd = parity("srow")
    paired = has_second("srow").astype(F32)
    for n in swaps:
        i = (rows - 1) * (odd if n else 1 - odd)
        for j, brought in owed(n):
            brought = brought.astype(F32)
            total = acc_ref[:, i, j] + (brought * paired if n else brought)
            store(i, j, (x_ref[:, i, j].astype(F32) + jnp.maximum(total, 0.0)).astype(BF16))


def sent_columns(rim_ref, col_refs):
    odd = parity("scol")
    for n, ref in zip((1 - odd, odd), col_refs):
        ref[...] = rim_ref[:, :, n]


def depth_body(mid_ref, rim_ref, after_ref, *deep_refs):
    channels, rows, mids, depth, _ = mid_ref.shape
    odd = parity("trow")
    shape = (channels, channels * BAND)
    first = lax.broadcasted_iota(jnp.int32, shape, 0) * BAND
    for n, ref in enumerate(deep_refs):
        end = (1 - odd) if n == 0 else odd
        cut = pl.ds(pl.multiple_of(end * (depth - BAND), BAND), BAND)
        pick = (lax.broadcasted_iota(jnp.int32, shape, 1) == first + end * (BAND - 1)).astype(BF16)
        for i in range(rows):
            tiles = [column(mid_ref, rim_ref, i, j, cut) for j in range(mids + 2)]
            ref[i] = dot(pick, jnp.concatenate(tiles, axis=1)).astype(BF16)


def mid_body(x_ref, acc_ref, a_ref, b_ref, out_ref):
    def store(i, j, value):
        out_ref[:, i, j] = value

    finished(x_ref, acc_ref, (0, 1), lambda n: [(j, (a_ref, b_ref)[n][:, j]) for j in range(x_ref.shape[2])], store)


def side_columns(near_ref, far_ref):
    return [(side_of(False), near_ref[:, near_ref.shape[1] - 1]), (side_of(True), far_ref[:, 0])]


def begin_body(x_ref, acc_ref, near_ref, far_ref, after_ref, out_ref):
    def store(i, j, value):
        out_ref[:, i, j] = value

    finished(x_ref, acc_ref, (0,), lambda n: side_columns(near_ref, far_ref), store)


def next_body(x_ref, acc_ref, near_ref, far_ref, begun_ref, after_ref, out_ref, cola_ref, colb_ref):
    def store(i, j, value):
        out_ref[:, i, j] = value

    finished(x_ref, acc_ref, (1,), lambda n: side_columns(near_ref, far_ref), store)
    sent_columns(out_ref, (cola_ref, colb_ref))


def last_body(mid_ref, rim_ref, acc_ref, neara_ref, nearb_ref, fara_ref, farb_ref, out_ref, hold_ref, sems):
    rows, mids = mid_ref.shape[1:3]
    copies = []

    def write(source, i, j):
        copies.append(pltpu.make_async_copy(source, out_ref.at[:, i, j], sems.at[len(copies)]))
        copies[-1].start()

    for i in range(rows):
        for j in range(mids):
            write(mid_ref.at[:, i, j], i, j + 1)

    def store(i, j, value):
        hold_ref[:, i, j] = value
        write(hold_ref.at[:, i, j], i, j * (mids + 1))

    owed = lambda n: side_columns((neara_ref, nearb_ref)[n], (fara_ref, farb_ref)[n])
    finished(rim_ref, acc_ref, (0, 1), owed, store)
    for copy in copies:
        copy.wait()


def pass_body(x_ref, after_ref, also_ref, out_ref):
    out_ref[...] = x_ref[...]


def open_body(parts, x_ref, src_w_ref, tgt_w_ref, bias_ref, *rest):
    src_ref, tgt_ref, held_ref, beside_ref, cola_ref, colb_ref, sems = rest
    last = x_ref.shape[2] - 1
    odd = parity("scol")
    pairs = (
        (src_w_ref, src_ref),
        (x_ref.at[:, :, last * (1 - odd)], cola_ref),
        (x_ref.at[:, :, last * odd], colb_ref),
        (tgt_w_ref, tgt_ref),
        (bias_ref, held_ref),
    )
    copies = [pltpu.make_async_copy(a, b, sems.at[n]) for n, (a, b) in enumerate(pairs)]
    for copy in copies:
        copy.start()
    copies[0].wait()
    operators(parts, src_ref, None, (beside_ref,))
    for copy in copies[1:]:
        copy.wait()


def swap_first(value, axis):
    return lax.ppermute(value, axis, [(n, n ^ 1) for n in range(lax.axis_size(axis))])


def swap_second(value, axis, other):
    count, across = lax.axis_size(axis), lax.axis_size(other)
    pairs = []
    for n in range(count):
        for m in range(across):
            if 0 < n < count - 1:
                target = (n + 1 if n % 2 else n - 1, m)
            else:
                target = (n, m ^ 1)
            pairs.append((n * across + m, target[0] * across + target[1]))
    return lax.ppermute(value, (axis, other), pairs)


def shards(volume, src_weight, tgt_weight, bias):
    layers = src_weight.shape[0]
    channels, rows, cols, depth, width = volume.shape
    axes = ("srow", "scol", "trow")
    counts = [lax.axis_size(n) for n in axes]
    assert all(count % 2 == 0 for count in counts) and rows > 1 and cols > 2 and layers > 1
    src_w = jnp.transpose(src_weight, (0, 2, 3, 1))
    tgt_w = jnp.transpose(tgt_weight, (0, 2, 3, 1))
    deep_swaps = 1 if counts[2] == 2 else 2
    mid_shape, rim_shape = ((channels, rows, n, depth, width) for n in (cols - 2, 2))
    line = VMEM((channels, rows, depth, width), BF16)
    owed_side = VMEM((channels, 1, depth, width), BF16)
    early = [("beside", 0)]
    src_w, tgt_w, bias, beside_0, col_a, col_b = call(
        functools.partial(open_body, early),
        [VMEM(src_w.shape, BF16), VMEM(tgt_w.shape, BF16), VMEM(bias.shape, F32)] + operator_shapes(early, channels) + [line, line],
        (volume, src_w, tgt_w, bias),
        {n: HBM for n in range(4)},
        scratch=[pltpu.SemaphoreType.DMA((5,))],
    )
    made = {early[0]: beside_0}
    kinds = ("middle", "beside", "target", "near", "deep")
    owed_inner = [VMEM((channels, cols - 1, depth, width), BF16)]
    block, sum_a = (volume,), None
    for layer in range(layers):

        def on(body, *views):
            return functools.partial(whole, body, views) if layer == 0 else body

        both, base = (middle, sides), len(block)
        mid, rim = block[0], block[-1]
        which = (0, 1) if sum_a is None else (1,)
        sums = call(on(functools.partial(inner_body, which), *both), owed_inner * len(which), (*block, made["beside", layer]))
        sum_a, sum_b = sums if sum_a is None else (sum_a, *sums)
        got_col_a = swap_first(col_a, "scol")
        near = call(
            on(near_body, *both),
            owed_inner * 2,
            (*block, got_col_a, made["beside", layer], sum_a, sum_b),
            aliases={base + 2: 0, base + 3: 1},
        )
        near_got = swap_first(near[0], "srow"), swap_second(near[1], "srow", "scol")
        (col_b,) = call(pass_body, [line], (col_b, *near), {1: pl.ANY, 2: pl.ANY})
        beside = got_col_a, swap_second(col_b, "scol", "trow")
        if layer == 0:
            made |= build([(kind, 0) for kind in kinds if kind != "beside"], src_w, tgt_w, sum_b)
        operator = {kind: made[kind, layer] for kind in kinds}
        parts = call(
            on(part_body, *both),
            [VMEM((channels * BAND, depth // BAND * width), F32)] * 2,
            (*block, operator["beside"], sum_b),
            {base + 1: pl.ANY},
        )
        deep = call(
            on(depth_body, *both),
            [VMEM((rows, channels, cols * width), BF16)] * deep_swaps,
            (*block, near[0]),
            {base: pl.ANY},
        )
        deeper = [swap_first(deep[0], "trow")]
        if deep_swaps == 2:
            deeper.append(swap_second(deep[1], "trow", "scol"))
        accs = call(
            on(functools.partial(own_body, layer), *both),
            [VMEM(mid_shape, F32), VMEM(rim_shape, F32)],
            (*block, *(operator[kind] for kind in ("middle", "beside", "target", "near")), bias, parts[1]),
            {base + 5: pl.ANY},
            scratch=[VMEM((depth // BAND, 3, channels * BAND, cols * width), BF16)],
            flops=10**10,
        )
        a, b, side = call(
            far_body,
            [owed_side, owed_side, VMEM((2, *line.shape), BF16)],
            (*beside, operator["beside"], *parts, accs[0], *deeper),
            {5 + n: pl.ANY for n in range(1 + deep_swaps)},
        )
        far_got = swap_first(a, "srow"), swap_second(b, "srow", "scol")
        if layer < layers - 1:
            made |= build([(kind, layer + 1) for kind in kinds], src_w, tgt_w, b)
        (acc_rim,) = call(
            on(source_body, *both),
            [VMEM(rim_shape, F32)],
            (*block, side, operator["middle"], operator["beside"], accs[1]),
            aliases={base + 3: 0},
        )
        acc_mid, acc_rim = call(
            deep_body,
            [VMEM(mid_shape, F32), VMEM(rim_shape, F32)],
            (operator["deep"], *deeper, accs[0], acc_rim),
            aliases={1 + deep_swaps: 0, 2 + deep_swaps: 1},
        )
        (mid,) = call(on(mid_body, middle), [VMEM(mid_shape, BF16)], (mid, acc_mid, *near_got))
        if layer < layers - 1:
            whole_rim = [VMEM(rim_shape, BF16)]
            (begun,) = call(on(begin_body, sides), whole_rim, (rim, acc_rim, near_got[0], far_got[0], mid), {4: pl.ANY})
            (sum_a,) = call(functools.partial(inner_body, (0,)), owed_inner, (mid, begun, made["beside", layer + 1]))
            rim, col_a, col_b = call(
                on(next_body, sides),
                whole_rim + [line, line],
                (rim, acc_rim, near_got[1], far_got[1], begun, sum_a),
                {5: pl.ANY},
                aliases={4: 0},
            )
            block = (mid, rim)
        else:
            (state,) = call(
                last_body,
                [jax.ShapeDtypeStruct(volume.shape, BF16)],
                (mid, rim, acc_rim, *near_got, *far_got),
                out_place=HBM,
                scratch=[VMEM(rim_shape, BF16), pltpu.SemaphoreType.DMA((rows * cols,))],
            )
    return state


def solution(mesh):
    return jax.shard_map(
        shards,
        mesh=mesh,
        in_specs=(P(None, "srow", "scol", "trow", None), P(), P(), P()),
        out_specs=P(None, "srow", "scol", "trow", None),
        check_vma=False,
    )
```

```python
import functools

import jax
import jax.numpy as jnp
from jax import lax
from jax.experimental import pallas as pl
from jax.experimental.pallas import tpu as pltpu
from jax.sharding import PartitionSpec as P

BAND = 32
EDGE = 16
SCOPED = 16 * 1024 * 1024
F32 = jnp.float32
BF16 = jnp.bfloat16
VMEM, HBM = pltpu.VMEM, pltpu.HBM
def parity(axis):
    return lax.axis_index(axis) % 2


def has_second(axis):
    at = lax.axis_index(axis)
    return (at > 0) & (at < lax.axis_size(axis) - 1)


def call(body, outs, args, places=None, out_place=VMEM, scratch=(), aliases=None):
    places = places or {}
    spaces = [places.get(n, VMEM) for n in range(len(args))]
    held = [pltpu.with_memory_space_constraint(a, m) if m in (VMEM, HBM) else a for a, m in zip(args, spaces)]
    return pl.pallas_call(
        body,
        out_shape=tuple(outs),
        in_specs=[pl.BlockSpec(memory_space=m) for m in spaces],
        out_specs=tuple(pl.BlockSpec(memory_space=out_place) for _ in outs),
        scratch_shapes=list(scratch),
        input_output_aliases=aliases or {},
        compiler_params=pltpu.CompilerParams(vmem_limit_bytes=SCOPED),
        cost_estimate=pl.CostEstimate(flops=10**6, bytes_accessed=10**4, transcendentals=0),
    )(*held)


def dot(a, b):
    return jnp.dot(a, b, preferred_element_type=F32)


def operators(parts, src_w_ref, tgt_w_ref, out_refs):
    channels = src_w_ref.shape[1]
    span, small = channels * BAND, channels * EDGE

    def columns(size):
        pick_c = lax.broadcasted_iota(jnp.int32, (channels, channels * size), 1) // size
        pick_r = lax.broadcasted_iota(jnp.int32, (channels, channels * size), 0)
        return (pick_c == pick_r).astype(BF16)

    wide, narrow, single = columns(BAND), columns(EDGE), columns(1)
    row = lax.broadcasted_iota(jnp.int32, (BAND, span), 0)
    shift = row - lax.broadcasted_iota(jnp.int32, (BAND, span), 1) % BAND
    row_s = lax.broadcasted_iota(jnp.int32, (BAND, small), 0)
    col_s = lax.broadcasted_iota(jnp.int32, (BAND, small), 1) % EDGE
    near = ((row_s == 0) & (col_s == EDGE - 1), (row_s == BAND - 1) & (col_s == 0))
    row_1 = lax.broadcasted_iota(jnp.int32, (BAND, channels), 0)
    deep = (row_1 == 0, row_1 == BAND - 1)
    spread = {}

    def taps(ref, layer, o, pick, key):
        key = (key, layer, o)
        if key not in spread:
            spread[key] = lax.dot_general(ref[layer, o], pick, (((0,), (0,)), ((), ())), preferred_element_type=F32)
        return spread[key]

    for (kind, layer), out_ref in zip(parts, out_refs):
        for o in range(channels):
            rows = slice(o * BAND, (o + 1) * BAND)
            for b in range(3):
                if kind == "middle":
                    got = taps(src_w_ref, layer, o, wide, "s")
                    values = {(): jnp.where(shift == 0, got[3 + b][None, :], 0.0)}
                elif kind == "beside":
                    got = taps(src_w_ref, layer, o, wide, "s")
                    values = {(n,): jnp.where(shift == 0, got[6 * n + b][None, :], 0.0) for n in range(2)}
                elif kind == "target":
                    got = taps(tgt_w_ref, layer, o, wide, "t")
                    value = jnp.where(shift == 1, got[b][None, :], 0.0)
                    value = jnp.where(shift == 0, got[3 + b][None, :], value)
                    values = {(): jnp.where(shift == -1, got[6 + b][None, :], value)}
                else:
                    pick, at = (narrow, near) if kind == "near" else (single, deep)
                    got = taps(tgt_w_ref, layer, o, pick, kind)
                    values = {(n,): jnp.where(at[n], got[6 * n + b][None, :], 0.0) for n in range(2)}
                for index, value in values.items():
                    size = value.shape[1]
                    out_ref[(*index, rows, slice(b * size, (b + 1) * size))] = value.astype(BF16)


def operator_shapes(parts, channels):
    span = channels * BAND
    widths = dict(middle=span, beside=span, target=span, near=channels * EDGE, deep=channels)
    lead = dict(middle=(), beside=(2,), target=(), near=(2,), deep=(2,))
    return [VMEM((*lead[kind], span, 3 * widths[kind]), BF16) for kind, _ in parts]


def build_body(parts, src_w_ref, tgt_w_ref, after_ref, *out_refs):
    operators(parts, src_w_ref, tgt_w_ref, out_refs)


def build(parts, src_w, tgt_w, after):
    got = call(
        functools.partial(build_body, parts),
        operator_shapes(parts, src_w.shape[1]),
        (src_w, tgt_w, after),
        {2: pl.ANY},
    )
    return dict(zip(parts, got))


class View:
    def __init__(self, ref, columns):
        self.ref, self.columns = ref, columns

    @property
    def shape(self):
        channels, rows, _, depth, width = self.ref.shape
        return channels, rows, len(self.columns), depth, width

    def __getitem__(self, index):
        first, i, j, *rest = index
        return self.ref[(first, i, self.columns[j], *rest)]


def middle(x_ref):
    return View(x_ref, tuple(range(1, x_ref.shape[2] - 1)))


def sides(x_ref):
    return View(x_ref, (0, x_ref.shape[2] - 1))


def whole(body, views, x_ref, *refs):
    body(*(view(x_ref) for view in views), *refs)


def band(tile):
    channels, size, width = tile.shape
    return tile.reshape(channels * size, width)


def unband(tile, channels):
    return tile.reshape(channels, tile.shape[0] // channels, tile.shape[1])


def src_operand(tiles, cols):
    return jnp.concatenate([jnp.concatenate(tiles[b : b + cols], axis=1) for b in range(3)], axis=0)


def sent_rows(rows):
    odd = parity("srow")
    return ((rows - 1) * (1 - odd), odd), ((rows - 1) * odd, 1 - odd)


def column(mid_ref, rim_ref, i, j, cut):
    last = mid_ref.shape[2] + 1
    return band(rim_ref[:, i, j // last, cut] if j in (0, last) else mid_ref[:, i, j - 1, cut])


def bands_of(depth):
    return [slice(start, start + BAND) for start in range(0, depth, BAND)]


def owed_sums(operator, tiles, out_ref):
    channels, cols, depth, width = out_ref.shape
    cuts = bands_of(depth)
    operand = jnp.concatenate([jnp.concatenate([t for cut in cuts for t in tiles(cut, b)], axis=1) for b in range(3)], axis=0)
    got = dot(operator, operand).astype(BF16)
    for q, cut in enumerate(cuts):
        for j in range(cols):
            at = (q * cols + j) * width
            out_ref[:, j, cut] = unband(got[:, at : at + width], channels)


def inner_body(which, mid_ref, rim_ref, beside_ref, *out_refs):
    rows, cols = mid_ref.shape[1:3]
    for n, out_ref in zip(which, out_refs):
        i, side = sent_rows(rows)[n]
        owed_sums(
            beside_ref[side], lambda cut, b: [column(mid_ref, rim_ref, i, j + b, cut) for j in range(cols)], out_ref
        )


def part_body(mid_ref, rim_ref, beside_ref, after_ref, *part_refs):
    rows, cols = mid_ref.shape[1], mid_ref.shape[2] + 2
    cuts = bands_of(mid_ref.shape[3])
    for (i, side), part_ref in zip(sent_rows(rows), part_refs):
        span = part_ref.shape[1]
        for n, (first, j) in enumerate(((1, 0), (0, cols - 2))):
            tiles = [jnp.concatenate([column(mid_ref, rim_ref, i, j + b, cut) for cut in cuts], axis=1) for b in range(2)]
            operator = beside_ref[side, :, first * span : (first + 2) * span]
            part_ref[n] = dot(operator, jnp.concatenate(tiles, axis=0))


def edge_body(cola_ref, colb_ref, beside_ref, parta_ref, partb_ref, after_ref, a_ref, b_ref, side_ref):
    channels, rows, depth, width = cola_ref.shape
    odd, paired = parity("scol"), has_second("scol")
    side_ref[1 - odd] = cola_ref[...]

    @pl.when(paired)
    def _():
        side_ref[odd] = colb_ref[...]

    @pl.when(jnp.logical_not(paired))
    def _():
        side_ref[odd] = jnp.zeros_like(colb_ref)

    cuts = bands_of(depth)
    for (i, side), part_ref, out_ref in zip(sent_rows(rows), (parta_ref, partb_ref), (a_ref, b_ref)):
        span = part_ref.shape[1]
        for n, tap in enumerate((0, 2)):
            halo = jnp.concatenate([band(side_ref[n, :, i, cut]) for cut in cuts], axis=1)
            got = (part_ref[n] + dot(beside_ref[side, :, tap * span : (tap + 1) * span], halo)).astype(BF16)
            for q, cut in enumerate(cuts):
                out_ref[:, n, cut] = unband(got[:, q * width : (q + 1) * width], channels)


def shifted(tile, step):
    lane = lax.broadcasted_iota(jnp.int32, tile.shape, 1)
    width = tile.shape[1]
    rolled = pltpu.roll(tile.astype(F32), step % width, 1)
    gone = 0 if step == 1 else width - 1
    return jnp.where(lane == gone, 0.0, rolled)


def three(tiles):
    return [jnp.concatenate([shifted(t, step) if step else t.astype(F32) for t in tiles], axis=1) for step in (1, 0, -1)]


def own_body(
    layer, mid_ref, rim_ref, middle_ref, beside_ref, target_ref, near_ref, bias_ref, after_ref, accmid_ref, accrim_ref, lane_ref
):
    channels, rows, mids, depth, width = mid_ref.shape
    cols = mids + 2
    cuts = bands_of(depth)
    shape = (BAND, cols * width)
    bias = [jnp.broadcast_to(bias_ref[layer : layer + 1, o : o + 1], shape) for o in range(channels)]
    bias = jnp.concatenate(bias, axis=0)
    for i in range(rows):
        for q, cut in enumerate(cuts):
            tiles = [column(mid_ref, rim_ref, i, j, cut) for j in range(cols)]
            lane_ref[q, 1] = jnp.concatenate(tiles, axis=1)
            for n, step in ((0, 1), (2, -1)):
                lane_ref[q, n] = jnp.concatenate([shifted(t, step).astype(BF16) for t in tiles], axis=1)
        for q, cut in enumerate(cuts):
            total = bias + dot(target_ref[...], lane_ref[q].reshape(3 * channels * BAND, cols * width))
            for side, other, start in ((0, q - 1, BAND - EDGE), (1, q + 1, 0)):
                if 0 <= other < len(cuts):
                    parts = [unband(lane_ref[other, n], channels)[:, start : start + EDGE] for n in range(3)]
                    total = total + dot(near_ref[side], jnp.concatenate([band(p) for p in parts], axis=0))
            for n, j in enumerate((0, cols - 1)):
                accrim_ref[:, i, n, cut] = unband(total[:, j * width : (j + 1) * width], channels)
            for j in range(1, cols - 1):
                accmid_ref[:, i, j - 1, cut] = unband(total[:, j * width : (j + 1) * width], channels)
        for a in range(3):
            r = i + a - 1
            if 0 <= r < rows:
                operator = middle_ref[...] if a == 1 else beside_ref[a // 2]
                add_sums(operator, lambda cut, b: [column(mid_ref, rim_ref, r, j + b, cut) for j in range(mids)], accmid_ref, i)


def add_sums(operator, tiles, acc_ref, i):
    channels, _, cols, depth, width = acc_ref.shape
    cuts = bands_of(depth)
    operand = jnp.concatenate([jnp.concatenate([t for cut in cuts for t in tiles(cut, b)], axis=1) for b in range(3)], axis=0)
    got = dot(operator, operand)
    for q, cut in enumerate(cuts):
        for j in range(cols):
            at = (q * cols + j) * width
            acc_ref[:, i, j, cut] += unband(got[:, at : at + width], channels)


def rest_body(
    mid_ref, rim_ref, side_ref, middle_ref, beside_ref, deep_ref, accmid_ref, accrim_ref, *rest
):
    *deep_halos, outmid_ref, outrim_ref = rest
    channels, rows, mids, depth, width = mid_ref.shape
    cols = mids + 2

    def around(r, j, cut):
        if j in (-1, cols):
            return band(side_ref[0 if j < 0 else 1, :, r, cut])
        return column(mid_ref, rim_ref, r, j, cut)

    for i in range(rows):
        for a in range(3):
            r = i + a - 1
            if 0 <= r < rows:
                operator = middle_ref[...] if a == 1 else beside_ref[a // 2]
                add_sums(operator, lambda cut, b: [around(r, j + b - 1, cut) for j in (0, cols - 1)], outrim_ref, i)
        odd = parity("trow")
        for n, halo_ref in enumerate(deep_halos):
            side = (1 - odd) if n == 0 else odd
            cut = pl.ds(pl.multiple_of(side * (depth - BAND), BAND), BAND)
            halo = three([halo_ref[i, :, j * width : (j + 1) * width] for j in range(cols)])
            halo = jnp.concatenate(halo, axis=0)
            if n == 1:
                halo = halo * has_second("trow").astype(F32)
            got = dot(deep_ref[side], halo.astype(BF16))
            for j in range(cols):
                acc_ref, at = (outrim_ref, j // (cols - 1)) if j in (0, cols - 1) else (outmid_ref, j - 1)
                acc_ref[:, i, at, cut] += unband(got[:, j * width : (j + 1) * width], channels)


def finished(x_ref, acc_ref, owed_refs, store):
    rows, cols = x_ref.shape[1:3]
    odd = parity("srow")
    paired = has_second("srow").astype(F32)
    for n, i in enumerate([(rows - 1) * (1 - odd), (rows - 1) * odd, *range(1, rows - 1)]):
        if n < 2 and owed_refs[n] is None:
            continue
        for j in range(cols):
            total = acc_ref[:, i, j]
            if n < 2:
                owed = owed_refs[n][:, j].astype(F32)
                total = total + (owed if n == 0 else owed * paired)
            store(i, j, (x_ref[:, i, j].astype(F32) + jnp.maximum(total, 0.0)).astype(BF16))


def sent_columns(rim_ref, col_refs):
    odd = parity("scol")
    for n, ref in zip((1 - odd, odd), col_refs):
        ref[...] = rim_ref[:, :, n]


def depth_body(mid_ref, rim_ref, after_ref, *deep_refs):
    channels, rows, mids, depth, _ = mid_ref.shape
    odd = parity("trow")
    shape = (channels, channels * BAND)
    first = lax.broadcasted_iota(jnp.int32, shape, 0) * BAND
    for n, ref in enumerate(deep_refs):
        end = (1 - odd) if n == 0 else odd
        cut = pl.ds(pl.multiple_of(end * (depth - BAND), BAND), BAND)
        pick = (lax.broadcasted_iota(jnp.int32, shape, 1) == first + end * (BAND - 1)).astype(BF16)
        for i in range(rows):
            tiles = [column(mid_ref, rim_ref, i, j, cut) for j in range(mids + 2)]
            ref[i] = dot(pick, jnp.concatenate(tiles, axis=1)).astype(BF16)


def mid_body(x_ref, acc_ref, a_ref, b_ref, out_ref):
    def store(i, j, value):
        out_ref[:, i, j] = value

    finished(x_ref, acc_ref, (a_ref, b_ref), store)


def begin_body(x_ref, acc_ref, a_ref, after_ref, out_ref):
    mid_body(x_ref, acc_ref, a_ref, None, out_ref)


def next_body(x_ref, acc_ref, b_ref, begun_ref, after_ref, out_ref, cola_ref, colb_ref):
    mid_body(x_ref, acc_ref, None, b_ref, out_ref)
    sent_columns(out_ref, (cola_ref, colb_ref))


def write_body(first, step, x_ref, acc_ref, a_ref, b_ref, *refs):
    out_ref, hold_ref, sems = refs[-3:]
    copies = []

    def store(i, j, value):
        hold_ref[:, i, j] = value
        copies.append(pltpu.make_async_copy(hold_ref.at[:, i, j], out_ref.at[:, i, first + step * j], sems.at[len(copies)]))
        copies[-1].start()

    finished(x_ref, acc_ref, (a_ref, b_ref), store)
    for copy in copies:
        copy.wait()


def open_body(parts, x_ref, src_w_ref, tgt_w_ref, bias_ref, *rest):
    src_ref, tgt_ref, held_ref, beside_ref, cola_ref, colb_ref, sems = rest
    last = x_ref.shape[2] - 1
    odd = parity("scol")
    pairs = (
        (src_w_ref, src_ref),
        (x_ref.at[:, :, last * (1 - odd)], cola_ref),
        (x_ref.at[:, :, last * odd], colb_ref),
        (tgt_w_ref, tgt_ref),
        (bias_ref, held_ref),
    )
    copies = [pltpu.make_async_copy(a, b, sems.at[n]) for n, (a, b) in enumerate(pairs)]
    for copy in copies:
        copy.start()
    copies[0].wait()
    operators(parts, src_ref, None, (beside_ref,))
    for copy in copies[1:]:
        copy.wait()


def swap_first(value, axis):
    return lax.ppermute(value, axis, [(n, n ^ 1) for n in range(lax.axis_size(axis))])


def swap_second(value, axis, other):
    count, across = lax.axis_size(axis), lax.axis_size(other)
    pairs = []
    for n in range(count):
        for m in range(across):
            if 0 < n < count - 1:
                target = (n + 1 if n % 2 else n - 1, m)
            else:
                target = (n, m ^ 1)
            pairs.append((n * across + m, target[0] * across + target[1]))
    return lax.ppermute(value, (axis, other), pairs)


def shards(volume, src_weight, tgt_weight, bias):
    layers = src_weight.shape[0]
    channels, rows, cols, depth, width = volume.shape
    axes = ("srow", "scol", "trow")
    counts = [lax.axis_size(n) for n in axes]
    assert all(count % 2 == 0 for count in counts) and rows > 1 and cols > 2 and layers > 1
    src_w = jnp.transpose(src_weight, (0, 2, 3, 1))
    tgt_w = jnp.transpose(tgt_weight, (0, 2, 3, 1))
    deep_swaps = 1 if counts[2] == 2 else 2
    mid_shape, rim_shape = ((channels, rows, n, depth, width) for n in (cols - 2, 2))
    line = VMEM((channels, rows, depth, width), BF16)
    owed_rim = VMEM((channels, 2, depth, width), BF16)
    early = [("beside", 0)]
    src_w, tgt_w, bias, beside_0, col_a, col_b = call(
        functools.partial(open_body, early),
        [VMEM(src_w.shape, BF16), VMEM(tgt_w.shape, BF16), VMEM(bias.shape, F32)] + operator_shapes(early, channels) + [line, line],
        (volume, src_w, tgt_w, bias),
        {n: HBM for n in range(4)},
        scratch=[pltpu.SemaphoreType.DMA((5,))],
    )
    made = {early[0]: beside_0}
    kinds = ("middle", "beside", "target", "near", "deep")
    owed_inner = [VMEM((channels, cols - 2, depth, width), BF16)]
    block, sum_a = (volume,), None
    for layer in range(layers):

        def on(body, *views):
            return functools.partial(whole, body, views) if layer == 0 else body

        both, base = (middle, sides), len(block)
        mid, rim = block[0], block[-1]
        beside = swap_first(col_a, "scol"), swap_second(col_b, "scol", "trow")
        which = (0, 1) if sum_a is None else (1,)
        sums = call(on(functools.partial(inner_body, which), *both), owed_inner * len(which), (*block, made["beside", layer]))
        sum_b = sums[-1]
        inner = swap_first(sums[0], "srow") if sum_a is None else got_a, swap_second(sum_b, "srow", "scol")
        if layer == 0:
            late = [(kind, n) for n in range(layers) for kind in kinds]
            made |= build([part for part in late if part not in early], src_w, tgt_w, sum_b)
        operator = {kind: made[kind, layer] for kind in kinds}
        parts = call(
            on(part_body, *both),
            [VMEM((2, channels * BAND, depth // BAND * width), F32)] * 2,
            (*block, operator["beside"], sum_b),
            {base + 1: pl.ANY},
        )
        a, b, side = call(
            edge_body,
            [owed_rim, owed_rim, VMEM((2, *line.shape), BF16)],
            (*beside, operator["beside"], *parts, operator["middle"]),
            {5: pl.ANY},
        )
        outer = swap_first(a, "srow"), swap_second(b, "srow", "scol")
        deep = call(
            on(depth_body, *both),
            [VMEM((rows, channels, cols * width), BF16)] * deep_swaps,
            (*block, b),
            {base: pl.ANY},
        )
        deeper = [swap_first(deep[0], "trow")]
        if deep_swaps == 2:
            deeper.append(swap_second(deep[1], "trow", "scol"))
        accs = call(
            on(functools.partial(own_body, layer), *both),
            [VMEM(mid_shape, F32), VMEM(rim_shape, F32)],
            (*block, *(operator[kind] for kind in ("middle", "beside", "target", "near")), bias, b),
            {base + 5: pl.ANY},
            scratch=[VMEM((depth // BAND, 3, channels * BAND, cols * width), BF16)],
        )
        acc_mid, acc_rim = call(
            on(rest_body, *both),
            [VMEM(mid_shape, F32), VMEM(rim_shape, F32)],
            (*block, side, *(operator[kind] for kind in ("middle", "beside", "deep")), *accs, *deeper),
            aliases={base + 4: 0, base + 5: 1},
        )
        if layer < layers - 1:
            (mid,) = call(on(mid_body, middle), [VMEM(mid_shape, BF16)], (mid, acc_mid, *inner))
            whole_rim = [VMEM(rim_shape, BF16)]
            (begun,) = call(on(begin_body, sides), whole_rim, (rim, acc_rim, outer[0], mid), {3: pl.ANY})
            (sum_a,) = call(functools.partial(inner_body, (0,)), owed_inner, (mid, begun, made["beside", layer + 1]))
            got_a = swap_first(sum_a, "srow")
            rim, col_a, col_b = call(
                on(next_body, sides),
                whole_rim + [line, line],
                (rim, acc_rim, outer[1], begun, sum_a),
                {4: pl.ANY},
                aliases={3: 0},
            )
            block = (mid, rim)
        else:
            result, state = [jax.ShapeDtypeStruct(volume.shape, BF16)], ()
            for first, step, shape, operands in (
                (1, 1, mid_shape, (mid, acc_mid, *inner)),
                (0, cols - 1, rim_shape, (rim, acc_rim, *outer)),
            ):
                state = call(
                    functools.partial(write_body, first, step),
                    result,
                    (*operands, *state),
                    {4: HBM},
                    out_place=HBM,
                    scratch=[VMEM(shape, BF16), pltpu.SemaphoreType.DMA((shape[1] * shape[2],))],
                    aliases={4: 0} if state else None,
                )
    return state[0]


def solution(mesh):
    return jax.shard_map(
        shards,
        mesh=mesh,
        in_specs=(P(None, "srow", "scol", "trow", None), P(), P(), P()),
        out_specs=P(None, "srow", "scol", "trow", None),
        check_vma=False,
    )
```

```python
import functools

import jax
import jax.numpy as jnp
from jax import lax
from jax.experimental import pallas as pl
from jax.experimental.pallas import tpu as pltpu
from jax.sharding import PartitionSpec as P

BAND = 32
EDGE = 16
SCOPED = 16 * 1024 * 1024
F32 = jnp.float32
BF16 = jnp.bfloat16
VMEM, HBM = pltpu.VMEM, pltpu.HBM
def parity(axis):
    return lax.axis_index(axis) % 2


def has_second(axis):
    at = lax.axis_index(axis)
    return (at > 0) & (at < lax.axis_size(axis) - 1)


def call(body, outs, args, places=None, out_place=VMEM, scratch=(), aliases=None, flops=10**6):
    places = places or {}
    spaces = [places.get(n, VMEM) for n in range(len(args))]
    held = [pltpu.with_memory_space_constraint(a, m) if m in (VMEM, HBM) else a for a, m in zip(args, spaces)]
    return pl.pallas_call(
        body,
        out_shape=tuple(outs),
        in_specs=[pl.BlockSpec(memory_space=m) for m in spaces],
        out_specs=tuple(pl.BlockSpec(memory_space=out_place) for _ in outs),
        scratch_shapes=list(scratch),
        input_output_aliases=aliases or {},
        compiler_params=pltpu.CompilerParams(vmem_limit_bytes=SCOPED),
        cost_estimate=pl.CostEstimate(flops=flops, bytes_accessed=10**4, transcendentals=0),
    )(*held)


def dot(a, b):
    return jnp.dot(a, b, preferred_element_type=F32)


def operators(parts, src_w_ref, tgt_w_ref, out_refs):
    channels = src_w_ref.shape[1]
    span, small = channels * BAND, channels * EDGE

    def columns(size):
        pick_c = lax.broadcasted_iota(jnp.int32, (channels, channels * size), 1) // size
        pick_r = lax.broadcasted_iota(jnp.int32, (channels, channels * size), 0)
        return (pick_c == pick_r).astype(BF16)

    wide, narrow, single = columns(BAND), columns(EDGE), columns(1)
    row = lax.broadcasted_iota(jnp.int32, (BAND, span), 0)
    shift = row - lax.broadcasted_iota(jnp.int32, (BAND, span), 1) % BAND
    row_s = lax.broadcasted_iota(jnp.int32, (BAND, small), 0)
    col_s = lax.broadcasted_iota(jnp.int32, (BAND, small), 1) % EDGE
    near = ((row_s == 0) & (col_s == EDGE - 1), (row_s == BAND - 1) & (col_s == 0))
    row_1 = lax.broadcasted_iota(jnp.int32, (BAND, channels), 0)
    deep = (row_1 == 0, row_1 == BAND - 1)
    spread = {}

    def taps(ref, layer, o, pick, key):
        key = (key, layer, o)
        if key not in spread:
            spread[key] = lax.dot_general(ref[layer, o], pick, (((0,), (0,)), ((), ())), preferred_element_type=F32)
        return spread[key]

    for (kind, layer), out_ref in zip(parts, out_refs):
        for o in range(channels):
            rows = slice(o * BAND, (o + 1) * BAND)
            for b in range(3):
                if kind == "middle":
                    got = taps(src_w_ref, layer, o, wide, "s")
                    values = {(): jnp.where(shift == 0, got[3 + b][None, :], 0.0)}
                elif kind == "beside":
                    got = taps(src_w_ref, layer, o, wide, "s")
                    values = {(n,): jnp.where(shift == 0, got[6 * n + b][None, :], 0.0) for n in range(2)}
                elif kind == "target":
                    got = taps(tgt_w_ref, layer, o, wide, "t")
                    value = jnp.where(shift == 1, got[b][None, :], 0.0)
                    value = jnp.where(shift == 0, got[3 + b][None, :], value)
                    values = {(): jnp.where(shift == -1, got[6 + b][None, :], value)}
                else:
                    pick, at = (narrow, near) if kind == "near" else (single, deep)
                    got = taps(tgt_w_ref, layer, o, pick, kind)
                    values = {(n,): jnp.where(at[n], got[6 * n + b][None, :], 0.0) for n in range(2)}
                for index, value in values.items():
                    size = value.shape[1]
                    out_ref[(*index, rows, slice(b * size, (b + 1) * size))] = value.astype(BF16)


def operator_shapes(parts, channels):
    span = channels * BAND
    widths = dict(middle=span, beside=span, target=span, near=channels * EDGE, deep=channels)
    lead = dict(middle=(), beside=(2,), target=(), near=(2,), deep=(2,))
    return [VMEM((*lead[kind], span, 3 * widths[kind]), BF16) for kind, _ in parts]


def build_body(parts, src_w_ref, tgt_w_ref, after_ref, *out_refs):
    operators(parts, src_w_ref, tgt_w_ref, out_refs)


def build(parts, src_w, tgt_w, after):
    got = call(
        functools.partial(build_body, parts),
        operator_shapes(parts, src_w.shape[1]),
        (src_w, tgt_w, after),
        {2: pl.ANY},
    )
    return dict(zip(parts, got))


class View:
    def __init__(self, ref, columns):
        self.ref, self.columns = ref, columns

    @property
    def shape(self):
        channels, rows, _, depth, width = self.ref.shape
        return channels, rows, len(self.columns), depth, width

    def __getitem__(self, index):
        first, i, j, *rest = index
        return self.ref[(first, i, self.columns[j], *rest)]


def middle(x_ref):
    return View(x_ref, tuple(range(1, x_ref.shape[2] - 1)))


def sides(x_ref):
    return View(x_ref, (0, x_ref.shape[2] - 1))


def whole(body, views, x_ref, *refs):
    body(*(view(x_ref) for view in views), *refs)


def band(tile):
    channels, size, width = tile.shape
    return tile.reshape(channels * size, width)


def unband(tile, channels):
    return tile.reshape(channels, tile.shape[0] // channels, tile.shape[1])


def src_operand(tiles, cols):
    return jnp.concatenate([jnp.concatenate(tiles[b : b + cols], axis=1) for b in range(3)], axis=0)


def sent_rows(rows):
    odd = parity("srow")
    return ((rows - 1) * (1 - odd), odd), ((rows - 1) * odd, 1 - odd)


def column(mid_ref, rim_ref, i, j, cut):
    last = mid_ref.shape[2] + 1
    return band(rim_ref[:, i, j // last, cut] if j in (0, last) else mid_ref[:, i, j - 1, cut])


def bands_of(depth):
    return [slice(start, start + BAND) for start in range(0, depth, BAND)]


def owed_sums(operator, tiles, out_ref):
    channels, cols, depth, width = out_ref.shape
    cuts = bands_of(depth)
    operand = jnp.concatenate([jnp.concatenate([t for cut in cuts for t in tiles(cut, b)], axis=1) for b in range(3)], axis=0)
    got = dot(operator, operand).astype(BF16)
    for q, cut in enumerate(cuts):
        for j in range(cols):
            at = (q * cols + j) * width
            out_ref[:, j, cut] = unband(got[:, at : at + width], channels)


def inner_body(which, mid_ref, rim_ref, beside_ref, *out_refs):
    rows, cols = mid_ref.shape[1:3]
    for n, out_ref in zip(which, out_refs):
        i, side = sent_rows(rows)[n]
        owed_sums(
            beside_ref[side], lambda cut, b: [column(mid_ref, rim_ref, i, j + b, cut) for j in range(cols)], out_ref
        )


def part_body(mid_ref, rim_ref, beside_ref, after_ref, *part_refs):
    rows, cols = mid_ref.shape[1], mid_ref.shape[2] + 2
    cuts = bands_of(mid_ref.shape[3])
    for (i, side), part_ref in zip(sent_rows(rows), part_refs):
        span = part_ref.shape[1]
        for n, (first, j) in enumerate(((1, 0), (0, cols - 2))):
            tiles = [jnp.concatenate([column(mid_ref, rim_ref, i, j + b, cut) for cut in cuts], axis=1) for b in range(2)]
            operator = beside_ref[side, :, first * span : (first + 2) * span]
            part_ref[n] = dot(operator, jnp.concatenate(tiles, axis=0))


def edge_body(cola_ref, colb_ref, beside_ref, parta_ref, partb_ref, after_ref, a_ref, b_ref, side_ref):
    channels, rows, depth, width = cola_ref.shape
    odd, paired = parity("scol"), has_second("scol")
    side_ref[1 - odd] = cola_ref[...]

    @pl.when(paired)
    def _():
        side_ref[odd] = colb_ref[...]

    @pl.when(jnp.logical_not(paired))
    def _():
        side_ref[odd] = jnp.zeros_like(colb_ref)

    cuts = bands_of(depth)
    for (i, side), part_ref, out_ref in zip(sent_rows(rows), (parta_ref, partb_ref), (a_ref, b_ref)):
        span = part_ref.shape[1]
        for n, tap in enumerate((0, 2)):
            halo = jnp.concatenate([band(side_ref[n, :, i, cut]) for cut in cuts], axis=1)
            got = (part_ref[n] + dot(beside_ref[side, :, tap * span : (tap + 1) * span], halo)).astype(BF16)
            for q, cut in enumerate(cuts):
                out_ref[:, n, cut] = unband(got[:, q * width : (q + 1) * width], channels)


def shifted(tile, step):
    lane = lax.broadcasted_iota(jnp.int32, tile.shape, 1)
    width = tile.shape[1]
    rolled = pltpu.roll(tile.astype(F32), step % width, 1)
    gone = 0 if step == 1 else width - 1
    return jnp.where(lane == gone, 0.0, rolled)


def three(tiles):
    return [jnp.concatenate([shifted(t, step) if step else t.astype(F32) for t in tiles], axis=1) for step in (1, 0, -1)]


def own_body(
    layer, mid_ref, rim_ref, middle_ref, beside_ref, target_ref, near_ref, bias_ref, after_ref, accmid_ref, accrim_ref, lane_ref
):
    channels, rows, mids, depth, width = mid_ref.shape
    cols = mids + 2
    cuts = bands_of(depth)
    shape = (BAND, cols * width)
    bias = [jnp.broadcast_to(bias_ref[layer : layer + 1, o : o + 1], shape) for o in range(channels)]
    bias = jnp.concatenate(bias, axis=0)
    for i in range(rows):
        for q, cut in enumerate(cuts):
            tiles = [column(mid_ref, rim_ref, i, j, cut) for j in range(cols)]
            lane_ref[q, 1] = jnp.concatenate(tiles, axis=1)
            for n, step in ((0, 1), (2, -1)):
                lane_ref[q, n] = jnp.concatenate([shifted(t, step).astype(BF16) for t in tiles], axis=1)
        for q, cut in enumerate(cuts):
            total = bias + dot(target_ref[...], lane_ref[q].reshape(3 * channels * BAND, cols * width))
            for side, other, start in ((0, q - 1, BAND - EDGE), (1, q + 1, 0)):
                if 0 <= other < len(cuts):
                    parts = [unband(lane_ref[other, n], channels)[:, start : start + EDGE] for n in range(3)]
                    total = total + dot(near_ref[side], jnp.concatenate([band(p) for p in parts], axis=0))
            for n, j in enumerate((0, cols - 1)):
                accrim_ref[:, i, n, cut] = unband(total[:, j * width : (j + 1) * width], channels)
            for j in range(1, cols - 1):
                accmid_ref[:, i, j - 1, cut] = unband(total[:, j * width : (j + 1) * width], channels)
        for a in range(3):
            r = i + a - 1
            if 0 <= r < rows:
                operator = middle_ref[...] if a == 1 else beside_ref[a // 2]
                add_sums(operator, lambda cut, b: [column(mid_ref, rim_ref, r, j + b, cut) for j in range(mids)], accmid_ref, i)


def add_sums(operator, tiles, acc_ref, i):
    channels, _, cols, depth, width = acc_ref.shape
    cuts = bands_of(depth)
    operand = jnp.concatenate([jnp.concatenate([t for cut in cuts for t in tiles(cut, b)], axis=1) for b in range(3)], axis=0)
    got = dot(operator, operand)
    for q, cut in enumerate(cuts):
        for j in range(cols):
            at = (q * cols + j) * width
            acc_ref[:, i, j, cut] += unband(got[:, at : at + width], channels)


def rest_body(
    mid_ref, rim_ref, side_ref, middle_ref, beside_ref, deep_ref, accmid_ref, accrim_ref, *rest
):
    *deep_halos, outmid_ref, outrim_ref = rest
    channels, rows, mids, depth, width = mid_ref.shape
    cols = mids + 2

    def around(r, j, cut):
        if j in (-1, cols):
            return band(side_ref[0 if j < 0 else 1, :, r, cut])
        return column(mid_ref, rim_ref, r, j, cut)

    for i in range(rows):
        for a in range(3):
            r = i + a - 1
            if 0 <= r < rows:
                operator = middle_ref[...] if a == 1 else beside_ref[a // 2]
                add_sums(operator, lambda cut, b: [around(r, j + b - 1, cut) for j in (0, cols - 1)], outrim_ref, i)
        odd = parity("trow")
        for n, halo_ref in enumerate(deep_halos):
            side = (1 - odd) if n == 0 else odd
            cut = pl.ds(pl.multiple_of(side * (depth - BAND), BAND), BAND)
            halo = three([halo_ref[i, :, j * width : (j + 1) * width] for j in range(cols)])
            halo = jnp.concatenate(halo, axis=0)
            if n == 1:
                halo = halo * has_second("trow").astype(F32)
            got = dot(deep_ref[side], halo.astype(BF16))
            for j in range(cols):
                acc_ref, at = (outrim_ref, j // (cols - 1)) if j in (0, cols - 1) else (outmid_ref, j - 1)
                acc_ref[:, i, at, cut] += unband(got[:, j * width : (j + 1) * width], channels)


def finished(x_ref, acc_ref, owed_refs, store):
    rows, cols = x_ref.shape[1:3]
    odd = parity("srow")
    paired = has_second("srow").astype(F32)
    for n, i in enumerate([(rows - 1) * (1 - odd), (rows - 1) * odd, *range(1, rows - 1)]):
        if n < 2 and owed_refs[n] is None:
            continue
        for j in range(cols):
            total = acc_ref[:, i, j]
            if n < 2:
                owed = owed_refs[n][:, j].astype(F32)
                total = total + (owed if n == 0 else owed * paired)
            store(i, j, (x_ref[:, i, j].astype(F32) + jnp.maximum(total, 0.0)).astype(BF16))


def sent_columns(rim_ref, col_refs):
    odd = parity("scol")
    for n, ref in zip((1 - odd, odd), col_refs):
        ref[...] = rim_ref[:, :, n]


def depth_body(mid_ref, rim_ref, after_ref, *deep_refs):
    channels, rows, mids, depth, _ = mid_ref.shape
    odd = parity("trow")
    shape = (channels, channels * BAND)
    first = lax.broadcasted_iota(jnp.int32, shape, 0) * BAND
    for n, ref in enumerate(deep_refs):
        end = (1 - odd) if n == 0 else odd
        cut = pl.ds(pl.multiple_of(end * (depth - BAND), BAND), BAND)
        pick = (lax.broadcasted_iota(jnp.int32, shape, 1) == first + end * (BAND - 1)).astype(BF16)
        for i in range(rows):
            tiles = [column(mid_ref, rim_ref, i, j, cut) for j in range(mids + 2)]
            ref[i] = dot(pick, jnp.concatenate(tiles, axis=1)).astype(BF16)


def mid_body(x_ref, acc_ref, a_ref, b_ref, out_ref):
    def store(i, j, value):
        out_ref[:, i, j] = value

    finished(x_ref, acc_ref, (a_ref, b_ref), store)


def begin_body(x_ref, acc_ref, a_ref, after_ref, out_ref):
    mid_body(x_ref, acc_ref, a_ref, None, out_ref)


def next_body(x_ref, acc_ref, b_ref, begun_ref, after_ref, out_ref, cola_ref, colb_ref):
    mid_body(x_ref, acc_ref, None, b_ref, out_ref)
    sent_columns(out_ref, (cola_ref, colb_ref))


def write_body(first, step, x_ref, acc_ref, a_ref, b_ref, *refs):
    out_ref, hold_ref, sems = refs[-3:]
    copies = []

    def store(i, j, value):
        hold_ref[:, i, j] = value
        copies.append(pltpu.make_async_copy(hold_ref.at[:, i, j], out_ref.at[:, i, first + step * j], sems.at[len(copies)]))
        copies[-1].start()

    finished(x_ref, acc_ref, (a_ref, b_ref), store)
    for copy in copies:
        copy.wait()


def open_body(parts, x_ref, src_w_ref, tgt_w_ref, bias_ref, *rest):
    src_ref, tgt_ref, held_ref, beside_ref, cola_ref, colb_ref, sems = rest
    last = x_ref.shape[2] - 1
    odd = parity("scol")
    pairs = (
        (src_w_ref, src_ref),
        (x_ref.at[:, :, last * (1 - odd)], cola_ref),
        (x_ref.at[:, :, last * odd], colb_ref),
        (tgt_w_ref, tgt_ref),
        (bias_ref, held_ref),
    )
    copies = [pltpu.make_async_copy(a, b, sems.at[n]) for n, (a, b) in enumerate(pairs)]
    for copy in copies:
        copy.start()
    copies[0].wait()
    operators(parts, src_ref, None, (beside_ref,))
    for copy in copies[1:]:
        copy.wait()


def swap_first(value, axis):
    return lax.ppermute(value, axis, [(n, n ^ 1) for n in range(lax.axis_size(axis))])


def swap_second(value, axis, other):
    count, across = lax.axis_size(axis), lax.axis_size(other)
    pairs = []
    for n in range(count):
        for m in range(across):
            if 0 < n < count - 1:
                target = (n + 1 if n % 2 else n - 1, m)
            else:
                target = (n, m ^ 1)
            pairs.append((n * across + m, target[0] * across + target[1]))
    return lax.ppermute(value, (axis, other), pairs)


def shards(volume, src_weight, tgt_weight, bias):
    layers = src_weight.shape[0]
    channels, rows, cols, depth, width = volume.shape
    axes = ("srow", "scol", "trow")
    counts = [lax.axis_size(n) for n in axes]
    assert all(count % 2 == 0 for count in counts) and rows > 1 and cols > 2 and layers > 1
    src_w = jnp.transpose(src_weight, (0, 2, 3, 1))
    tgt_w = jnp.transpose(tgt_weight, (0, 2, 3, 1))
    deep_swaps = 1 if counts[2] == 2 else 2
    mid_shape, rim_shape = ((channels, rows, n, depth, width) for n in (cols - 2, 2))
    line = VMEM((channels, rows, depth, width), BF16)
    owed_rim = VMEM((channels, 2, depth, width), BF16)
    early = [("beside", 0)]
    src_w, tgt_w, bias, beside_0, col_a, col_b = call(
        functools.partial(open_body, early),
        [VMEM(src_w.shape, BF16), VMEM(tgt_w.shape, BF16), VMEM(bias.shape, F32)] + operator_shapes(early, channels) + [line, line],
        (volume, src_w, tgt_w, bias),
        {n: HBM for n in range(4)},
        scratch=[pltpu.SemaphoreType.DMA((5,))],
    )
    made = {early[0]: beside_0}
    kinds = ("middle", "beside", "target", "near", "deep")
    owed_inner = [VMEM((channels, cols - 2, depth, width), BF16)]
    block, sum_a = (volume,), None
    for layer in range(layers):

        def on(body, *views):
            return functools.partial(whole, body, views) if layer == 0 else body

        both, base = (middle, sides), len(block)
        mid, rim = block[0], block[-1]
        beside = swap_first(col_a, "scol"), swap_second(col_b, "scol", "trow")
        which = (0, 1) if sum_a is None else (1,)
        sums = call(on(functools.partial(inner_body, which), *both), owed_inner * len(which), (*block, made["beside", layer]))
        sum_b = sums[-1]
        inner = swap_first(sums[0], "srow") if sum_a is None else got_a, swap_second(sum_b, "srow", "scol")
        if layer == 0:
            late = [(kind, n) for n in range(layers) for kind in kinds]
            made |= build([part for part in late if part not in early], src_w, tgt_w, sum_b)
        operator = {kind: made[kind, layer] for kind in kinds}
        parts = call(
            on(part_body, *both),
            [VMEM((2, channels * BAND, depth // BAND * width), F32)] * 2,
            (*block, operator["beside"], sum_b),
            {base + 1: pl.ANY},
            flops=10**10 if layer else 10**6,
        )
        a, b, side = call(
            edge_body,
            [owed_rim, owed_rim, VMEM((2, *line.shape), BF16)],
            (*beside, operator["beside"], *parts, operator["middle"]),
            {5: pl.ANY},
        )
        outer = swap_first(a, "srow"), swap_second(b, "srow", "scol")
        deep = call(
            on(depth_body, *both),
            [VMEM((rows, channels, cols * width), BF16)] * deep_swaps,
            (*block, b),
            {base: pl.ANY},
        )
        deeper = [swap_first(deep[0], "trow")]
        if deep_swaps == 2:
            deeper.append(swap_second(deep[1], "trow", "scol"))
        accs = call(
            on(functools.partial(own_body, layer), *both),
            [VMEM(mid_shape, F32), VMEM(rim_shape, F32)],
            (*block, *(operator[kind] for kind in ("middle", "beside", "target", "near")), bias, b),
            {base + 5: pl.ANY},
            scratch=[VMEM((depth // BAND, 3, channels * BAND, cols * width), BF16)],
        )
        acc_mid, acc_rim = call(
            on(rest_body, *both),
            [VMEM(mid_shape, F32), VMEM(rim_shape, F32)],
            (*block, side, *(operator[kind] for kind in ("middle", "beside", "deep")), *accs, *deeper),
            aliases={base + 4: 0, base + 5: 1},
        )
        if layer < layers - 1:
            (mid,) = call(on(mid_body, middle), [VMEM(mid_shape, BF16)], (mid, acc_mid, *inner))
            whole_rim = [VMEM(rim_shape, BF16)]
            (begun,) = call(on(begin_body, sides), whole_rim, (rim, acc_rim, outer[0], mid), {3: pl.ANY})
            (sum_a,) = call(functools.partial(inner_body, (0,)), owed_inner, (mid, begun, made["beside", layer + 1]))
            got_a = swap_first(sum_a, "srow")
            rim, col_a, col_b = call(
                on(next_body, sides),
                whole_rim + [line, line],
                (rim, acc_rim, outer[1], begun, sum_a),
                {4: pl.ANY},
                aliases={3: 0},
            )
            block = (mid, rim)
        else:
            result, state = [jax.ShapeDtypeStruct(volume.shape, BF16)], ()
            for first, step, shape, operands in (
                (1, 1, mid_shape, (mid, acc_mid, *inner)),
                (0, cols - 1, rim_shape, (rim, acc_rim, *outer)),
            ):
                state = call(
                    functools.partial(write_body, first, step),
                    result,
                    (*operands, *state),
                    {4: HBM},
                    out_place=HBM,
                    scratch=[VMEM(shape, BF16), pltpu.SemaphoreType.DMA((shape[1] * shape[2],))],
                    aliases={4: 0} if state else None,
                )
    return state[0]


def solution(mesh):
    return jax.shard_map(
        shards,
        mesh=mesh,
        in_specs=(P(None, "srow", "scol", "trow", None), P(), P(), P()),
        out_specs=P(None, "srow", "scol", "trow", None),
        check_vma=False,
    )
```

```python
import functools

import jax
import jax.numpy as jnp
from jax import lax
from jax.experimental import pallas as pl
from jax.experimental.pallas import tpu as pltpu
from jax.sharding import PartitionSpec as P

BAND = 32
EDGE = 16
SCOPED = 16 * 1024 * 1024
F32 = jnp.float32
BF16 = jnp.bfloat16
VMEM, HBM = pltpu.VMEM, pltpu.HBM
def parity(axis):
    return lax.axis_index(axis) % 2


def has_second(axis):
    at = lax.axis_index(axis)
    return (at > 0) & (at < lax.axis_size(axis) - 1)


def call(body, outs, args, places=None, out_place=VMEM, scratch=(), aliases=None):
    places = places or {}
    spaces = [places.get(n, VMEM) for n in range(len(args))]
    held = [pltpu.with_memory_space_constraint(a, m) if m in (VMEM, HBM) else a for a, m in zip(args, spaces)]
    return pl.pallas_call(
        body,
        out_shape=tuple(outs),
        in_specs=[pl.BlockSpec(memory_space=m) for m in spaces],
        out_specs=tuple(pl.BlockSpec(memory_space=out_place) for _ in outs),
        scratch_shapes=list(scratch),
        input_output_aliases=aliases or {},
        compiler_params=pltpu.CompilerParams(vmem_limit_bytes=SCOPED),
        cost_estimate=pl.CostEstimate(flops=10**6, bytes_accessed=10**4, transcendentals=0),
    )(*held)


def dot(a, b):
    return jnp.dot(a, b, preferred_element_type=F32)


def operators(parts, src_w_ref, tgt_w_ref, out_refs):
    channels = src_w_ref.shape[1]
    span, small = channels * BAND, channels * EDGE

    def columns(size):
        pick_c = lax.broadcasted_iota(jnp.int32, (channels, channels * size), 1) // size
        pick_r = lax.broadcasted_iota(jnp.int32, (channels, channels * size), 0)
        return (pick_c == pick_r).astype(BF16)

    wide, narrow, single = columns(BAND), columns(EDGE), columns(1)
    row = lax.broadcasted_iota(jnp.int32, (BAND, span), 0)
    shift = row - lax.broadcasted_iota(jnp.int32, (BAND, span), 1) % BAND
    row_s = lax.broadcasted_iota(jnp.int32, (BAND, small), 0)
    col_s = lax.broadcasted_iota(jnp.int32, (BAND, small), 1) % EDGE
    near = ((row_s == 0) & (col_s == EDGE - 1), (row_s == BAND - 1) & (col_s == 0))
    row_1 = lax.broadcasted_iota(jnp.int32, (BAND, channels), 0)
    deep = (row_1 == 0, row_1 == BAND - 1)
    spread = {}

    def taps(ref, layer, o, pick, key):
        key = (key, layer, o)
        if key not in spread:
            spread[key] = lax.dot_general(ref[layer, o], pick, (((0,), (0,)), ((), ())), preferred_element_type=F32)
        return spread[key]

    for (kind, layer), out_ref in zip(parts, out_refs):
        for o in range(channels):
            rows = slice(o * BAND, (o + 1) * BAND)
            for b in range(3):
                if kind == "middle":
                    got = taps(src_w_ref, layer, o, wide, "s")
                    values = {(): jnp.where(shift == 0, got[3 + b][None, :], 0.0)}
                elif kind == "beside":
                    got = taps(src_w_ref, layer, o, wide, "s")
                    values = {(n,): jnp.where(shift == 0, got[6 * n + b][None, :], 0.0) for n in range(2)}
                elif kind == "target":
                    got = taps(tgt_w_ref, layer, o, wide, "t")
                    value = jnp.where(shift == 1, got[b][None, :], 0.0)
                    value = jnp.where(shift == 0, got[3 + b][None, :], value)
                    values = {(): jnp.where(shift == -1, got[6 + b][None, :], value)}
                else:
                    pick, at = (narrow, near) if kind == "near" else (single, deep)
                    got = taps(tgt_w_ref, layer, o, pick, kind)
                    values = {(n,): jnp.where(at[n], got[6 * n + b][None, :], 0.0) for n in range(2)}
                for index, value in values.items():
                    size = value.shape[1]
                    out_ref[(*index, rows, slice(b * size, (b + 1) * size))] = value.astype(BF16)


def operator_shapes(parts, channels):
    span = channels * BAND
    widths = dict(middle=span, beside=span, target=span, near=channels * EDGE, deep=channels)
    lead = dict(middle=(), beside=(2,), target=(), near=(2,), deep=(2,))
    return [VMEM((*lead[kind], span, 3 * widths[kind]), BF16) for kind, _ in parts]


def build_body(parts, src_w_ref, tgt_w_ref, after_ref, *out_refs):
    operators(parts, src_w_ref, tgt_w_ref, out_refs)


def build(parts, src_w, tgt_w, after):
    got = call(
        functools.partial(build_body, parts),
        operator_shapes(parts, src_w.shape[1]),
        (src_w, tgt_w, after),
        {2: pl.ANY},
    )
    return dict(zip(parts, got))


class View:
    def __init__(self, ref, columns):
        self.ref, self.columns = ref, columns

    @property
    def shape(self):
        channels, rows, _, depth, width = self.ref.shape
        return channels, rows, len(self.columns), depth, width

    def __getitem__(self, index):
        first, i, j, *rest = index
        return self.ref[(first, i, self.columns[j], *rest)]


def middle(x_ref):
    return View(x_ref, tuple(range(1, x_ref.shape[2] - 1)))


def sides(x_ref):
    return View(x_ref, (0, x_ref.shape[2] - 1))


def whole(body, views, x_ref, *refs):
    body(*(view(x_ref) for view in views), *refs)


def band(tile):
    channels, size, width = tile.shape
    return tile.reshape(channels * size, width)


def unband(tile, channels):
    return tile.reshape(channels, tile.shape[0] // channels, tile.shape[1])


def src_operand(tiles, cols):
    return jnp.concatenate([jnp.concatenate(tiles[b : b + cols], axis=1) for b in range(3)], axis=0)


def sent_rows(rows):
    odd = parity("srow")
    return ((rows - 1) * (1 - odd), odd), ((rows - 1) * odd, 1 - odd)


def column(mid_ref, rim_ref, i, j, cut):
    last = mid_ref.shape[2] + 1
    return band(rim_ref[:, i, j // last, cut] if j in (0, last) else mid_ref[:, i, j - 1, cut])


def bands_of(depth):
    return [slice(start, start + BAND) for start in range(0, depth, BAND)]


def owed_sums(operator, tiles, out_ref):
    channels, cols, depth, width = out_ref.shape
    cuts = bands_of(depth)
    operand = jnp.concatenate([jnp.concatenate([t for cut in cuts for t in tiles(cut, b)], axis=1) for b in range(3)], axis=0)
    got = dot(operator, operand).astype(BF16)
    for q, cut in enumerate(cuts):
        for j in range(cols):
            at = (q * cols + j) * width
            out_ref[:, j, cut] = unband(got[:, at : at + width], channels)


def inner_body(which, mid_ref, rim_ref, beside_ref, *out_refs):
    rows, cols = mid_ref.shape[1:3]
    for n, out_ref in zip(which, out_refs):
        i, side = sent_rows(rows)[n]
        owed_sums(
            beside_ref[side], lambda cut, b: [column(mid_ref, rim_ref, i, j + b, cut) for j in range(cols)], out_ref
        )


def part_body(mid_ref, rim_ref, beside_ref, after_ref, *part_refs):
    rows, cols = mid_ref.shape[1], mid_ref.shape[2] + 2
    cuts = bands_of(mid_ref.shape[3])
    for (i, side), part_ref in zip(sent_rows(rows), part_refs):
        span = part_ref.shape[1]
        for n, (first, j) in enumerate(((1, 0), (0, cols - 2))):
            tiles = [jnp.concatenate([column(mid_ref, rim_ref, i, j + b, cut) for cut in cuts], axis=1) for b in range(2)]
            operator = beside_ref[side, :, first * span : (first + 2) * span]
            part_ref[n] = dot(operator, jnp.concatenate(tiles, axis=0))


def edge_body(cola_ref, colb_ref, beside_ref, parta_ref, partb_ref, after_ref, a_ref, b_ref, side_ref):
    channels, rows, depth, width = cola_ref.shape
    odd, paired = parity("scol"), has_second("scol")
    side_ref[1 - odd] = cola_ref[...]

    @pl.when(paired)
    def _():
        side_ref[odd] = colb_ref[...]

    @pl.when(jnp.logical_not(paired))
    def _():
        side_ref[odd] = jnp.zeros_like(colb_ref)

    cuts = bands_of(depth)
    for (i, side), part_ref, out_ref in zip(sent_rows(rows), (parta_ref, partb_ref), (a_ref, b_ref)):
        span = part_ref.shape[1]
        for n, tap in enumerate((0, 2)):
            halo = jnp.concatenate([band(side_ref[n, :, i, cut]) for cut in cuts], axis=1)
            got = (part_ref[n] + dot(beside_ref[side, :, tap * span : (tap + 1) * span], halo)).astype(BF16)
            for q, cut in enumerate(cuts):
                out_ref[:, n, cut] = unband(got[:, q * width : (q + 1) * width], channels)


def shifted(tile, step):
    lane = lax.broadcasted_iota(jnp.int32, tile.shape, 1)
    width = tile.shape[1]
    rolled = pltpu.roll(tile.astype(F32), step % width, 1)
    gone = 0 if step == 1 else width - 1
    return jnp.where(lane == gone, 0.0, rolled)


def three(tiles):
    return [jnp.concatenate([shifted(t, step) if step else t.astype(F32) for t in tiles], axis=1) for step in (1, 0, -1)]


def own_body(
    layer, mid_ref, rim_ref, middle_ref, beside_ref, target_ref, near_ref, bias_ref, after_ref, accmid_ref, accrim_ref, lane_ref
):
    channels, rows, mids, depth, width = mid_ref.shape
    cols = mids + 2
    cuts = bands_of(depth)
    shape = (BAND, cols * width)
    bias = [jnp.broadcast_to(bias_ref[layer : layer + 1, o : o + 1], shape) for o in range(channels)]
    bias = jnp.concatenate(bias, axis=0)
    for i in range(rows):
        for q, cut in enumerate(cuts):
            tiles = [column(mid_ref, rim_ref, i, j, cut) for j in range(cols)]
            lane_ref[q, 1] = jnp.concatenate(tiles, axis=1)
            for n, step in ((0, 1), (2, -1)):
                lane_ref[q, n] = jnp.concatenate([shifted(t, step).astype(BF16) for t in tiles], axis=1)
        for q, cut in enumerate(cuts):
            total = bias + dot(target_ref[...], lane_ref[q].reshape(3 * channels * BAND, cols * width))
            for side, other, start in ((0, q - 1, BAND - EDGE), (1, q + 1, 0)):
                if 0 <= other < len(cuts):
                    parts = [unband(lane_ref[other, n], channels)[:, start : start + EDGE] for n in range(3)]
                    total = total + dot(near_ref[side], jnp.concatenate([band(p) for p in parts], axis=0))
            for n, j in enumerate((0, cols - 1)):
                accrim_ref[:, i, n, cut] = unband(total[:, j * width : (j + 1) * width], channels)
            for j in range(1, cols - 1):
                accmid_ref[:, i, j - 1, cut] = unband(total[:, j * width : (j + 1) * width], channels)
        for a in range(3):
            r = i + a - 1
            if 0 <= r < rows:
                operator = middle_ref[...] if a == 1 else beside_ref[a // 2]
                add_sums(operator, lambda cut, b: [column(mid_ref, rim_ref, r, j + b, cut) for j in range(mids)], accmid_ref, i)


def add_sums(operator, tiles, acc_ref, i):
    channels, _, cols, depth, width = acc_ref.shape
    cuts = bands_of(depth)
    operand = jnp.concatenate([jnp.concatenate([t for cut in cuts for t in tiles(cut, b)], axis=1) for b in range(3)], axis=0)
    got = dot(operator, operand)
    for q, cut in enumerate(cuts):
        for j in range(cols):
            at = (q * cols + j) * width
            acc_ref[:, i, j, cut] += unband(got[:, at : at + width], channels)


def rest_body(
    mid_ref, rim_ref, side_ref, middle_ref, beside_ref, deep_ref, accmid_ref, accrim_ref, *rest
):
    *deep_halos, outmid_ref, outrim_ref = rest
    channels, rows, mids, depth, width = mid_ref.shape
    cols = mids + 2

    def around(r, j, cut):
        if j in (-1, cols):
            return band(side_ref[0 if j < 0 else 1, :, r, cut])
        return column(mid_ref, rim_ref, r, j, cut)

    for i in range(rows):
        for a in range(3):
            r = i + a - 1
            if 0 <= r < rows:
                operator = middle_ref[...] if a == 1 else beside_ref[a // 2]
                add_sums(operator, lambda cut, b: [around(r, j + b - 1, cut) for j in (0, cols - 1)], outrim_ref, i)
        odd = parity("trow")
        for n, halo_ref in enumerate(deep_halos):
            side = (1 - odd) if n == 0 else odd
            cut = pl.ds(pl.multiple_of(side * (depth - BAND), BAND), BAND)
            halo = three([halo_ref[i, :, j * width : (j + 1) * width] for j in range(cols)])
            halo = jnp.concatenate(halo, axis=0)
            if n == 1:
                halo = halo * has_second("trow").astype(F32)
            got = dot(deep_ref[side], halo.astype(BF16))
            for j in range(cols):
                acc_ref, at = (outrim_ref, j // (cols - 1)) if j in (0, cols - 1) else (outmid_ref, j - 1)
                acc_ref[:, i, at, cut] += unband(got[:, j * width : (j + 1) * width], channels)


def finished(x_ref, acc_ref, owed_refs, store):
    rows, cols = x_ref.shape[1:3]
    odd = parity("srow")
    paired = has_second("srow").astype(F32)
    for n, i in enumerate([(rows - 1) * (1 - odd), (rows - 1) * odd, *range(1, rows - 1)]):
        if n < 2 and owed_refs[n] is None:
            continue
        for j in range(cols):
            total = acc_ref[:, i, j]
            if n < 2:
                owed = owed_refs[n][:, j].astype(F32)
                total = total + (owed if n == 0 else owed * paired)
            store(i, j, (x_ref[:, i, j].astype(F32) + jnp.maximum(total, 0.0)).astype(BF16))


def sent_columns(rim_ref, col_refs):
    odd = parity("scol")
    for n, ref in zip((1 - odd, odd), col_refs):
        ref[...] = rim_ref[:, :, n]


def depth_body(mid_ref, rim_ref, after_ref, *deep_refs):
    channels, rows, mids, depth, _ = mid_ref.shape
    odd = parity("trow")
    shape = (channels, channels * BAND)
    first = lax.broadcasted_iota(jnp.int32, shape, 0) * BAND
    for n, ref in enumerate(deep_refs):
        end = (1 - odd) if n == 0 else odd
        cut = pl.ds(pl.multiple_of(end * (depth - BAND), BAND), BAND)
        pick = (lax.broadcasted_iota(jnp.int32, shape, 1) == first + end * (BAND - 1)).astype(BF16)
        for i in range(rows):
            tiles = [column(mid_ref, rim_ref, i, j, cut) for j in range(mids + 2)]
            ref[i] = dot(pick, jnp.concatenate(tiles, axis=1)).astype(BF16)


def mid_body(x_ref, acc_ref, a_ref, b_ref, out_ref):
    def store(i, j, value):
        out_ref[:, i, j] = value

    finished(x_ref, acc_ref, (a_ref, b_ref), store)


def begin_body(x_ref, acc_ref, a_ref, after_ref, out_ref):
    mid_body(x_ref, acc_ref, a_ref, None, out_ref)


def next_body(x_ref, acc_ref, b_ref, begun_ref, after_ref, out_ref, cola_ref, colb_ref):
    mid_body(x_ref, acc_ref, None, b_ref, out_ref)
    sent_columns(out_ref, (cola_ref, colb_ref))


def write_body(first, step, x_ref, acc_ref, a_ref, b_ref, *refs):
    out_ref, hold_ref, sems = refs[-3:]
    copies = []

    def store(i, j, value):
        hold_ref[:, i, j] = value
        copies.append(pltpu.make_async_copy(hold_ref.at[:, i, j], out_ref.at[:, i, first + step * j], sems.at[len(copies)]))
        copies[-1].start()

    finished(x_ref, acc_ref, (a_ref, b_ref), store)
    for copy in copies:
        copy.wait()


def open_body(parts, x_ref, src_w_ref, tgt_w_ref, bias_ref, *rest):
    src_ref, tgt_ref, held_ref, beside_ref, cola_ref, colb_ref, sems = rest
    last = x_ref.shape[2] - 1
    odd = parity("scol")
    pairs = (
        (src_w_ref, src_ref),
        (x_ref.at[:, :, last * (1 - odd)], cola_ref),
        (x_ref.at[:, :, last * odd], colb_ref),
        (tgt_w_ref, tgt_ref),
        (bias_ref, held_ref),
    )
    copies = [pltpu.make_async_copy(a, b, sems.at[n]) for n, (a, b) in enumerate(pairs)]
    for copy in copies:
        copy.start()
    copies[0].wait()
    operators(parts, src_ref, None, (beside_ref,))
    for copy in copies[1:]:
        copy.wait()


def swap_first(value, axis):
    return lax.ppermute(value, axis, [(n, n ^ 1) for n in range(lax.axis_size(axis))])


def swap_second(value, axis, other):
    count, across = lax.axis_size(axis), lax.axis_size(other)
    pairs = []
    for n in range(count):
        for m in range(across):
            if 0 < n < count - 1:
                target = (n + 1 if n % 2 else n - 1, m)
            else:
                target = (n, m ^ 1)
            pairs.append((n * across + m, target[0] * across + target[1]))
    return lax.ppermute(value, (axis, other), pairs)


def swap_inside(value, axis):
    pairs = [(n, n + 1 if n % 2 else n - 1) for n in range(1, lax.axis_size(axis) - 1)]
    return lax.ppermute(value, axis, pairs)


def shards(volume, src_weight, tgt_weight, bias):
    layers = src_weight.shape[0]
    channels, rows, cols, depth, width = volume.shape
    axes = ("srow", "scol", "trow")
    counts = [lax.axis_size(n) for n in axes]
    assert all(count % 2 == 0 for count in counts) and rows > 1 and cols > 2 and layers > 1
    src_w = jnp.transpose(src_weight, (0, 2, 3, 1))
    tgt_w = jnp.transpose(tgt_weight, (0, 2, 3, 1))
    deep_swaps = 1 if counts[2] == 2 else 2
    mid_shape, rim_shape = ((channels, rows, n, depth, width) for n in (cols - 2, 2))
    line = VMEM((channels, rows, depth, width), BF16)
    owed_rim = VMEM((channels, 2, depth, width), BF16)
    early = [("beside", 0)]
    src_w, tgt_w, bias, beside_0, col_a, col_b = call(
        functools.partial(open_body, early),
        [VMEM(src_w.shape, BF16), VMEM(tgt_w.shape, BF16), VMEM(bias.shape, F32)] + operator_shapes(early, channels) + [line, line],
        (volume, src_w, tgt_w, bias),
        {n: HBM for n in range(4)},
        scratch=[pltpu.SemaphoreType.DMA((5,))],
    )
    made = {early[0]: beside_0}
    kinds = ("middle", "beside", "target", "near", "deep")
    owed_inner = [VMEM((channels, cols - 2, depth, width), BF16)]
    block, sum_a = (volume,), None
    for layer in range(layers):

        def on(body, *views):
            return functools.partial(whole, body, views) if layer == 0 else body

        both, base = (middle, sides), len(block)
        mid, rim = block[0], block[-1]
        beside = swap_first(col_a, "scol"), swap_inside(col_b, "scol")
        which = (0, 1) if sum_a is None else (1,)
        sums = call(on(functools.partial(inner_body, which), *both), owed_inner * len(which), (*block, made["beside", layer]))
        sum_b = sums[-1]
        inner = swap_first(sums[0], "srow") if sum_a is None else got_a, swap_second(sum_b, "srow", "scol")
        if layer == 0:
            late = [(kind, n) for n in range(layers) for kind in kinds]
            made |= build([part for part in late if part not in early], src_w, tgt_w, sum_b)
        operator = {kind: made[kind, layer] for kind in kinds}
        parts = call(
            on(part_body, *both),
            [VMEM((2, channels * BAND, depth // BAND * width), F32)] * 2,
            (*block, operator["beside"], sum_b),
            {base + 1: pl.ANY},
        )
        a, b, side = call(
            edge_body,
            [owed_rim, owed_rim, VMEM((2, *line.shape), BF16)],
            (*beside, operator["beside"], *parts, operator["middle"]),
            {5: pl.ANY},
        )
        outer = swap_first(a, "srow"), swap_second(b, "srow", "scol")
        deep = call(
            on(depth_body, *both),
            [VMEM((rows, channels, cols * width), BF16)] * deep_swaps,
            (*block, b),
            {base: pl.ANY},
        )
        deeper = [swap_first(deep[0], "trow")]
        if deep_swaps == 2:
            deeper.append(swap_second(deep[1], "trow", "scol"))
        accs = call(
            on(functools.partial(own_body, layer), *both),
            [VMEM(mid_shape, F32), VMEM(rim_shape, F32)],
            (*block, *(operator[kind] for kind in ("middle", "beside", "target", "near")), bias, b),
            {base + 5: pl.ANY},
            scratch=[VMEM((depth // BAND, 3, channels * BAND, cols * width), BF16)],
        )
        acc_mid, acc_rim = call(
            on(rest_body, *both),
            [VMEM(mid_shape, F32), VMEM(rim_shape, F32)],
            (*block, side, *(operator[kind] for kind in ("middle", "beside", "deep")), *accs, *deeper),
            aliases={base + 4: 0, base + 5: 1},
        )
        if layer < layers - 1:
            (mid,) = call(on(mid_body, middle), [VMEM(mid_shape, BF16)], (mid, acc_mid, *inner))
            whole_rim = [VMEM(rim_shape, BF16)]
            (begun,) = call(on(begin_body, sides), whole_rim, (rim, acc_rim, outer[0], mid), {3: pl.ANY})
            (sum_a,) = call(functools.partial(inner_body, (0,)), owed_inner, (mid, begun, made["beside", layer + 1]))
            got_a = swap_first(sum_a, "srow")
            rim, col_a, col_b = call(
                on(next_body, sides),
                whole_rim + [line, line],
                (rim, acc_rim, outer[1], begun, sum_a),
                {4: pl.ANY},
                aliases={3: 0},
            )
            block = (mid, rim)
        else:
            result, state = [jax.ShapeDtypeStruct(volume.shape, BF16)], ()
            for first, step, shape, operands in (
                (1, 1, mid_shape, (mid, acc_mid, *inner)),
                (0, cols - 1, rim_shape, (rim, acc_rim, *outer)),
            ):
                state = call(
                    functools.partial(write_body, first, step),
                    result,
                    (*operands, *state),
                    {4: HBM},
                    out_place=HBM,
                    scratch=[VMEM(shape, BF16), pltpu.SemaphoreType.DMA((shape[1] * shape[2],))],
                    aliases={4: 0} if state else None,
                )
    return state[0]


def solution(mesh):
    return jax.shard_map(
        shards,
        mesh=mesh,
        in_specs=(P(None, "srow", "scol", "trow", None), P(), P(), P()),
        out_specs=P(None, "srow", "scol", "trow", None),
        check_vma=False,
    )
```

```python
import functools

import jax
import jax.numpy as jnp
from jax import lax
from jax.experimental import pallas as pl
from jax.experimental.pallas import tpu as pltpu
from jax.sharding import PartitionSpec as P

BAND = 32
EDGE = 16
SCOPED = 16 * 1024 * 1024
F32 = jnp.float32
BF16 = jnp.bfloat16
VMEM, HBM = pltpu.VMEM, pltpu.HBM
def parity(axis):
    return lax.axis_index(axis) % 2


def has_second(axis):
    at = lax.axis_index(axis)
    return (at > 0) & (at < lax.axis_size(axis) - 1)


def call(body, outs, args, places=None, out_place=VMEM, scratch=(), aliases=None):
    places = places or {}
    spaces = [places.get(n, VMEM) for n in range(len(args))]
    held = [pltpu.with_memory_space_constraint(a, m) if m in (VMEM, HBM) else a for a, m in zip(args, spaces)]
    return pl.pallas_call(
        body,
        out_shape=tuple(outs),
        in_specs=[pl.BlockSpec(memory_space=m) for m in spaces],
        out_specs=tuple(pl.BlockSpec(memory_space=out_place) for _ in outs),
        scratch_shapes=list(scratch),
        input_output_aliases=aliases or {},
        compiler_params=pltpu.CompilerParams(vmem_limit_bytes=SCOPED),
        cost_estimate=pl.CostEstimate(flops=10**6, bytes_accessed=10**4, transcendentals=0),
    )(*held)


def dot(a, b):
    return jnp.dot(a, b, preferred_element_type=F32)


def operators(parts, src_w_ref, tgt_w_ref, out_refs):
    channels = src_w_ref.shape[1]
    span, small = channels * BAND, channels * EDGE

    def columns(size):
        pick_c = lax.broadcasted_iota(jnp.int32, (channels, channels * size), 1) // size
        pick_r = lax.broadcasted_iota(jnp.int32, (channels, channels * size), 0)
        return (pick_c == pick_r).astype(BF16)

    wide, narrow, single = columns(BAND), columns(EDGE), columns(1)
    row = lax.broadcasted_iota(jnp.int32, (BAND, span), 0)
    shift = row - lax.broadcasted_iota(jnp.int32, (BAND, span), 1) % BAND
    row_s = lax.broadcasted_iota(jnp.int32, (BAND, small), 0)
    col_s = lax.broadcasted_iota(jnp.int32, (BAND, small), 1) % EDGE
    near = ((row_s == 0) & (col_s == EDGE - 1), (row_s == BAND - 1) & (col_s == 0))
    row_1 = lax.broadcasted_iota(jnp.int32, (BAND, channels), 0)
    deep = (row_1 == 0, row_1 == BAND - 1)
    spread = {}

    def taps(ref, layer, o, pick, key):
        key = (key, layer, o)
        if key not in spread:
            spread[key] = lax.dot_general(ref[layer, o], pick, (((0,), (0,)), ((), ())), preferred_element_type=F32)
        return spread[key]

    for (kind, layer), out_ref in zip(parts, out_refs):
        for o in range(channels):
            rows = slice(o * BAND, (o + 1) * BAND)
            for b in range(3):
                if kind == "middle":
                    got = taps(src_w_ref, layer, o, wide, "s")
                    values = {(): jnp.where(shift == 0, got[3 + b][None, :], 0.0)}
                elif kind == "beside":
                    got = taps(src_w_ref, layer, o, wide, "s")
                    values = {(n,): jnp.where(shift == 0, got[6 * n + b][None, :], 0.0) for n in range(2)}
                elif kind == "target":
                    got = taps(tgt_w_ref, layer, o, wide, "t")
                    value = jnp.where(shift == 1, got[b][None, :], 0.0)
                    value = jnp.where(shift == 0, got[3 + b][None, :], value)
                    values = {(): jnp.where(shift == -1, got[6 + b][None, :], value)}
                else:
                    pick, at = (narrow, near) if kind == "near" else (single, deep)
                    got = taps(tgt_w_ref, layer, o, pick, kind)
                    values = {(n,): jnp.where(at[n], got[6 * n + b][None, :], 0.0) for n in range(2)}
                for index, value in values.items():
                    size = value.shape[1]
                    out_ref[(*index, rows, slice(b * size, (b + 1) * size))] = value.astype(BF16)


def operator_shapes(parts, channels):
    span = channels * BAND
    widths = dict(middle=span, beside=span, target=span, near=channels * EDGE, deep=channels)
    lead = dict(middle=(), beside=(2,), target=(), near=(2,), deep=(2,))
    return [VMEM((*lead[kind], span, 3 * widths[kind]), BF16) for kind, _ in parts]


def build_body(parts, src_w_ref, tgt_w_ref, after_ref, *out_refs):
    operators(parts, src_w_ref, tgt_w_ref, out_refs)


def build(parts, src_w, tgt_w, after):
    got = call(
        functools.partial(build_body, parts),
        operator_shapes(parts, src_w.shape[1]),
        (src_w, tgt_w, after),
        {2: pl.ANY},
    )
    return dict(zip(parts, got))


class View:
    def __init__(self, ref, columns):
        self.ref, self.columns = ref, columns

    @property
    def shape(self):
        channels, rows, _, depth, width = self.ref.shape
        return channels, rows, len(self.columns), depth, width

    def __getitem__(self, index):
        first, i, j, *rest = index
        return self.ref[(first, i, self.columns[j], *rest)]


def middle(x_ref):
    return View(x_ref, tuple(range(1, x_ref.shape[2] - 1)))


def sides(x_ref):
    return View(x_ref, (0, x_ref.shape[2] - 1))


def whole(body, views, x_ref, *refs):
    body(*(view(x_ref) for view in views), *refs)


def band(tile):
    channels, size, width = tile.shape
    return tile.reshape(channels * size, width)


def unband(tile, channels):
    return tile.reshape(channels, tile.shape[0] // channels, tile.shape[1])


def src_operand(tiles, cols):
    return jnp.concatenate([jnp.concatenate(tiles[b : b + cols], axis=1) for b in range(3)], axis=0)


def sent_rows(rows):
    odd = parity("srow")
    return ((rows - 1) * (1 - odd), odd), ((rows - 1) * odd, 1 - odd)


def column(mid_ref, rim_ref, i, j, cut):
    last = mid_ref.shape[2] + 1
    return band(rim_ref[:, i, j // last, cut] if j in (0, last) else mid_ref[:, i, j - 1, cut])


def bands_of(depth):
    return [slice(start, start + BAND) for start in range(0, depth, BAND)]


def owed_sums(operator, tiles, out_ref):
    channels, cols, depth, width = out_ref.shape
    cuts = bands_of(depth)
    operand = jnp.concatenate([jnp.concatenate([t for cut in cuts for t in tiles(cut, b)], axis=1) for b in range(3)], axis=0)
    got = dot(operator, operand).astype(BF16)
    for q, cut in enumerate(cuts):
        for j in range(cols):
            at = (q * cols + j) * width
            out_ref[:, j, cut] = unband(got[:, at : at + width], channels)


def inner_body(which, mid_ref, rim_ref, beside_ref, *out_refs):
    rows, cols = mid_ref.shape[1:3]
    for n, out_ref in zip(which, out_refs):
        i, side = sent_rows(rows)[n]
        owed_sums(
            beside_ref[side], lambda cut, b: [column(mid_ref, rim_ref, i, j + b, cut) for j in range(cols)], out_ref
        )


def part_body(mid_ref, rim_ref, beside_ref, after_ref, *part_refs):
    rows, cols = mid_ref.shape[1], mid_ref.shape[2] + 2
    cuts = bands_of(mid_ref.shape[3])
    for (i, side), part_ref in zip(sent_rows(rows), part_refs):
        span = part_ref.shape[1]
        for n, (first, j) in enumerate(((1, 0), (0, cols - 2))):
            tiles = [jnp.concatenate([column(mid_ref, rim_ref, i, j + b, cut) for cut in cuts], axis=1) for b in range(2)]
            operator = beside_ref[side, :, first * span : (first + 2) * span]
            part_ref[n] = dot(operator, jnp.concatenate(tiles, axis=0))


def edge_body(cola_ref, colb_ref, beside_ref, parta_ref, partb_ref, after_ref, a_ref, b_ref, side_ref):
    channels, rows, depth, width = cola_ref.shape
    odd, paired = parity("scol"), has_second("scol")
    side_ref[1 - odd] = cola_ref[...]

    @pl.when(paired)
    def _():
        side_ref[odd] = colb_ref[...]

    @pl.when(jnp.logical_not(paired))
    def _():
        side_ref[odd] = jnp.zeros_like(colb_ref)

    cuts = bands_of(depth)
    for (i, side), part_ref, out_ref in zip(sent_rows(rows), (parta_ref, partb_ref), (a_ref, b_ref)):
        span = part_ref.shape[1]
        for n, tap in enumerate((0, 2)):
            halo = jnp.concatenate([band(side_ref[n, :, i, cut]) for cut in cuts], axis=1)
            got = (part_ref[n] + dot(beside_ref[side, :, tap * span : (tap + 1) * span], halo)).astype(BF16)
            for q, cut in enumerate(cuts):
                out_ref[:, n, cut] = unband(got[:, q * width : (q + 1) * width], channels)


def shifted(tile, step):
    lane = lax.broadcasted_iota(jnp.int32, tile.shape, 1)
    width = tile.shape[1]
    rolled = pltpu.roll(tile.astype(F32), step % width, 1)
    gone = 0 if step == 1 else width - 1
    return jnp.where(lane == gone, 0.0, rolled)


def three(tiles):
    return [jnp.concatenate([shifted(t, step) if step else t.astype(F32) for t in tiles], axis=1) for step in (1, 0, -1)]


def own_body(
    layer, mid_ref, rim_ref, middle_ref, beside_ref, target_ref, near_ref, bias_ref, after_ref, accmid_ref, accrim_ref, lane_ref
):
    channels, rows, mids, depth, width = mid_ref.shape
    cols = mids + 2
    cuts = bands_of(depth)
    shape = (BAND, cols * width)
    bias = [jnp.broadcast_to(bias_ref[layer : layer + 1, o : o + 1], shape) for o in range(channels)]
    bias = jnp.concatenate(bias, axis=0)
    for i in range(rows):
        for q, cut in enumerate(cuts):
            tiles = [column(mid_ref, rim_ref, i, j, cut) for j in range(cols)]
            lane_ref[q, 1] = jnp.concatenate(tiles, axis=1)
            for n, step in ((0, 1), (2, -1)):
                lane_ref[q, n] = jnp.concatenate([shifted(t, step).astype(BF16) for t in tiles], axis=1)
        for q, cut in enumerate(cuts):
            total = bias + dot(target_ref[...], lane_ref[q].reshape(3 * channels * BAND, cols * width))
            for side, other, start in ((0, q - 1, BAND - EDGE), (1, q + 1, 0)):
                if 0 <= other < len(cuts):
                    parts = [unband(lane_ref[other, n], channels)[:, start : start + EDGE] for n in range(3)]
                    total = total + dot(near_ref[side], jnp.concatenate([band(p) for p in parts], axis=0))
            for n, j in enumerate((0, cols - 1)):
                accrim_ref[:, i, n, cut] = unband(total[:, j * width : (j + 1) * width], channels)
            for j in range(1, cols - 1):
                accmid_ref[:, i, j - 1, cut] = unband(total[:, j * width : (j + 1) * width], channels)
        for a in range(3):
            r = i + a - 1
            if 0 <= r < rows:
                operator = middle_ref[...] if a == 1 else beside_ref[a // 2]
                add_sums(operator, lambda cut, b: [column(mid_ref, rim_ref, r, j + b, cut) for j in range(mids)], accmid_ref, i)


def add_sums(operator, tiles, acc_ref, i):
    channels, _, cols, depth, width = acc_ref.shape
    cuts = bands_of(depth)
    operand = jnp.concatenate([jnp.concatenate([t for cut in cuts for t in tiles(cut, b)], axis=1) for b in range(3)], axis=0)
    got = dot(operator, operand)
    for q, cut in enumerate(cuts):
        for j in range(cols):
            at = (q * cols + j) * width
            acc_ref[:, i, j, cut] += unband(got[:, at : at + width], channels)


def rest_body(
    mid_ref, rim_ref, side_ref, middle_ref, beside_ref, deep_ref, accmid_ref, accrim_ref, *rest
):
    *deep_halos, outmid_ref, outrim_ref = rest
    channels, rows, mids, depth, width = mid_ref.shape
    cols = mids + 2

    def around(r, j, cut):
        if j in (-1, cols):
            return band(side_ref[0 if j < 0 else 1, :, r, cut])
        return column(mid_ref, rim_ref, r, j, cut)

    for i in range(rows):
        for a in range(3):
            r = i + a - 1
            if 0 <= r < rows:
                operator = middle_ref[...] if a == 1 else beside_ref[a // 2]
                add_sums(operator, lambda cut, b: [around(r, j + b - 1, cut) for j in (0, cols - 1)], outrim_ref, i)
        odd = parity("trow")
        for n, halo_ref in enumerate(deep_halos):
            side = (1 - odd) if n == 0 else odd
            cut = pl.ds(pl.multiple_of(side * (depth - BAND), BAND), BAND)
            halo = three([halo_ref[i, :, j * width : (j + 1) * width] for j in range(cols)])
            halo = jnp.concatenate(halo, axis=0)
            if n == 1:
                halo = halo * has_second("trow").astype(F32)
            got = dot(deep_ref[side], halo.astype(BF16))
            for j in range(cols):
                acc_ref, at = (outrim_ref, j // (cols - 1)) if j in (0, cols - 1) else (outmid_ref, j - 1)
                acc_ref[:, i, at, cut] += unband(got[:, j * width : (j + 1) * width], channels)


def finished(x_ref, acc_ref, owed_refs, store):
    rows, cols = x_ref.shape[1:3]
    odd = parity("srow")
    paired = has_second("srow").astype(F32)
    for n, i in enumerate([(rows - 1) * (1 - odd), (rows - 1) * odd, *range(1, rows - 1)]):
        if n < 2 and owed_refs[n] is None:
            continue
        for j in range(cols):
            total = acc_ref[:, i, j]
            if n < 2:
                owed = owed_refs[n][:, j].astype(F32)
                total = total + (owed if n == 0 else owed * paired)
            store(i, j, (x_ref[:, i, j].astype(F32) + jnp.maximum(total, 0.0)).astype(BF16))


def sent_columns(rim_ref, col_refs):
    odd = parity("scol")
    for n, ref in zip((1 - odd, odd), col_refs):
        ref[...] = rim_ref[:, :, n]


def depth_body(mid_ref, rim_ref, after_ref, *deep_refs):
    channels, rows, mids, depth, _ = mid_ref.shape
    odd = parity("trow")
    shape = (channels, channels * BAND)
    first = lax.broadcasted_iota(jnp.int32, shape, 0) * BAND
    for n, ref in enumerate(deep_refs):
        end = (1 - odd) if n == 0 else odd
        cut = pl.ds(pl.multiple_of(end * (depth - BAND), BAND), BAND)
        pick = (lax.broadcasted_iota(jnp.int32, shape, 1) == first + end * (BAND - 1)).astype(BF16)
        for i in range(rows):
            tiles = [column(mid_ref, rim_ref, i, j, cut) for j in range(mids + 2)]
            ref[i] = dot(pick, jnp.concatenate(tiles, axis=1)).astype(BF16)


def mid_body(x_ref, acc_ref, a_ref, b_ref, out_ref):
    def store(i, j, value):
        out_ref[:, i, j] = value

    finished(x_ref, acc_ref, (a_ref, b_ref), store)


def begin_body(x_ref, acc_ref, a_ref, after_ref, out_ref):
    mid_body(x_ref, acc_ref, a_ref, None, out_ref)


def next_body(x_ref, acc_ref, b_ref, begun_ref, after_ref, out_ref, cola_ref, colb_ref):
    mid_body(x_ref, acc_ref, None, b_ref, out_ref)
    sent_columns(out_ref, (cola_ref, colb_ref))


def write_body(first, step, x_ref, acc_ref, a_ref, b_ref, *refs):
    out_ref, hold_ref, sems = refs[-3:]
    copies = []

    def store(i, j, value):
        hold_ref[:, i, j] = value
        copies.append(pltpu.make_async_copy(hold_ref.at[:, i, j], out_ref.at[:, i, first + step * j], sems.at[len(copies)]))
        copies[-1].start()

    finished(x_ref, acc_ref, (a_ref, b_ref), store)
    for copy in copies:
        copy.wait()


def open_body(parts, x_ref, src_w_ref, tgt_w_ref, bias_ref, *rest):
    src_ref, tgt_ref, held_ref, beside_ref, cola_ref, colb_ref, sems = rest
    last = x_ref.shape[2] - 1
    odd = parity("scol")
    pairs = (
        (src_w_ref, src_ref),
        (x_ref.at[:, :, last * (1 - odd)], cola_ref),
        (x_ref.at[:, :, last * odd], colb_ref),
        (tgt_w_ref, tgt_ref),
        (bias_ref, held_ref),
    )
    copies = [pltpu.make_async_copy(a, b, sems.at[n]) for n, (a, b) in enumerate(pairs)]
    for copy in copies:
        copy.start()
    copies[0].wait()
    operators(parts, src_ref, None, (beside_ref,))
    for copy in copies[1:]:
        copy.wait()


def swap_first(value, axis):
    return lax.ppermute(value, axis, [(n, n ^ 1) for n in range(lax.axis_size(axis))])


def swap_second(value, axis, other):
    count, across = lax.axis_size(axis), lax.axis_size(other)
    pairs = []
    for n in range(count):
        for m in range(across):
            if 0 < n < count - 1:
                target = (n + 1 if n % 2 else n - 1, m)
            else:
                target = (n, m ^ 1)
            pairs.append((n * across + m, target[0] * across + target[1]))
    return lax.ppermute(value, (axis, other), pairs)


def shards(volume, src_weight, tgt_weight, bias):
    layers = src_weight.shape[0]
    channels, rows, cols, depth, width = volume.shape
    axes = ("srow", "scol", "trow")
    counts = [lax.axis_size(n) for n in axes]
    assert all(count % 2 == 0 for count in counts) and rows > 1 and cols > 2 and layers > 1
    src_w = jnp.transpose(src_weight, (0, 2, 3, 1))
    tgt_w = jnp.transpose(tgt_weight, (0, 2, 3, 1))
    deep_swaps = 1 if counts[2] == 2 else 2
    mid_shape, rim_shape = ((channels, rows, n, depth, width) for n in (cols - 2, 2))
    line = VMEM((channels, rows, depth, width), BF16)
    owed_rim = VMEM((channels, 2, depth, width), BF16)
    early = [("beside", 0)]
    src_w, tgt_w, bias, beside_0, col_a, col_b = call(
        functools.partial(open_body, early),
        [VMEM(src_w.shape, BF16), VMEM(tgt_w.shape, BF16), VMEM(bias.shape, F32)] + operator_shapes(early, channels) + [line, line],
        (volume, src_w, tgt_w, bias),
        {n: HBM for n in range(4)},
        scratch=[pltpu.SemaphoreType.DMA((5,))],
    )
    made = {early[0]: beside_0}
    kinds = ("middle", "beside", "target", "near", "deep")
    owed_inner = [VMEM((channels, cols - 2, depth, width), BF16)]
    block, sum_a = (volume,), None
    for layer in range(layers):

        def on(body, *views):
            return functools.partial(whole, body, views) if layer == 0 else body

        both, base = (middle, sides), len(block)
        mid, rim = block[0], block[-1]
        beside = swap_first(col_a, "scol"), swap_second(col_b, "scol", "trow")
        which = (0, 1) if sum_a is None else (1,)
        sums = call(on(functools.partial(inner_body, which), *both), owed_inner * len(which), (*block, made["beside", layer]))
        sum_b = sums[-1]
        inner = swap_first(sums[0], "srow") if sum_a is None else got_a, swap_second(sum_b, "srow", "scol")
        late = [(kind, layer) for kind in kinds] + [("beside", n) for n in range(layer + 1, min(layer + 2, layers))]
        made |= build([part for part in late if part not in made], src_w, tgt_w, sum_b)
        operator = {kind: made[kind, layer] for kind in kinds}
        parts = call(
            on(part_body, *both),
            [VMEM((2, channels * BAND, depth // BAND * width), F32)] * 2,
            (*block, operator["beside"], sum_b),
            {base + 1: pl.ANY},
        )
        a, b, side = call(
            edge_body,
            [owed_rim, owed_rim, VMEM((2, *line.shape), BF16)],
            (*beside, operator["beside"], *parts, operator["middle"]),
            {5: pl.ANY},
        )
        outer = swap_first(a, "srow"), swap_second(b, "srow", "scol")
        deep = call(
            on(depth_body, *both),
            [VMEM((rows, channels, cols * width), BF16)] * deep_swaps,
            (*block, b),
            {base: pl.ANY},
        )
        deeper = [swap_first(deep[0], "trow")]
        if deep_swaps == 2:
            deeper.append(swap_second(deep[1], "trow", "scol"))
        accs = call(
            on(functools.partial(own_body, layer), *both),
            [VMEM(mid_shape, F32), VMEM(rim_shape, F32)],
            (*block, *(operator[kind] for kind in ("middle", "beside", "target", "near")), bias, b),
            {base + 5: pl.ANY},
            scratch=[VMEM((depth // BAND, 3, channels * BAND, cols * width), BF16)],
        )
        acc_mid, acc_rim = call(
            on(rest_body, *both),
            [VMEM(mid_shape, F32), VMEM(rim_shape, F32)],
            (*block, side, *(operator[kind] for kind in ("middle", "beside", "deep")), *accs, *deeper),
            aliases={base + 4: 0, base + 5: 1},
        )
        if layer < layers - 1:
            (mid,) = call(on(mid_body, middle), [VMEM(mid_shape, BF16)], (mid, acc_mid, *inner))
            whole_rim = [VMEM(rim_shape, BF16)]
            (begun,) = call(on(begin_body, sides), whole_rim, (rim, acc_rim, outer[0], mid), {3: pl.ANY})
            (sum_a,) = call(functools.partial(inner_body, (0,)), owed_inner, (mid, begun, made["beside", layer + 1]))
            got_a = swap_first(sum_a, "srow")
            rim, col_a, col_b = call(
                on(next_body, sides),
                whole_rim + [line, line],
                (rim, acc_rim, outer[1], begun, sum_a),
                {4: pl.ANY},
                aliases={3: 0},
            )
            block = (mid, rim)
        else:
            result, state = [jax.ShapeDtypeStruct(volume.shape, BF16)], ()
            for first, step, shape, operands in (
                (1, 1, mid_shape, (mid, acc_mid, *inner)),
                (0, cols - 1, rim_shape, (rim, acc_rim, *outer)),
            ):
                state = call(
                    functools.partial(write_body, first, step),
                    result,
                    (*operands, *state),
                    {4: HBM},
                    out_place=HBM,
                    scratch=[VMEM(shape, BF16), pltpu.SemaphoreType.DMA((shape[1] * shape[2],))],
                    aliases={4: 0} if state else None,
                )
    return state[0]


def solution(mesh):
    return jax.shard_map(
        shards,
        mesh=mesh,
        in_specs=(P(None, "srow", "scol", "trow", None), P(), P(), P()),
        out_specs=P(None, "srow", "scol", "trow", None),
        check_vma=False,
    )
```

```python
import functools

import jax
import jax.numpy as jnp
from jax import lax
from jax.experimental import pallas as pl
from jax.experimental.pallas import tpu as pltpu
from jax.sharding import PartitionSpec as P

BAND = 32
EDGE = 16
SCOPED = 16 * 1024 * 1024
F32 = jnp.float32
BF16 = jnp.bfloat16
VMEM, HBM = pltpu.VMEM, pltpu.HBM
def parity(axis):
    return lax.axis_index(axis) % 2


def has_second(axis):
    at = lax.axis_index(axis)
    return (at > 0) & (at < lax.axis_size(axis) - 1)


def call(body, outs, args, places=None, out_place=VMEM, scratch=(), aliases=None):
    places = places or {}
    spaces = [places.get(n, VMEM) for n in range(len(args))]
    held = [pltpu.with_memory_space_constraint(a, m) if m in (VMEM, HBM) else a for a, m in zip(args, spaces)]
    return pl.pallas_call(
        body,
        out_shape=tuple(outs),
        in_specs=[pl.BlockSpec(memory_space=m) for m in spaces],
        out_specs=tuple(pl.BlockSpec(memory_space=out_place) for _ in outs),
        scratch_shapes=list(scratch),
        input_output_aliases=aliases or {},
        compiler_params=pltpu.CompilerParams(vmem_limit_bytes=SCOPED),
        cost_estimate=pl.CostEstimate(flops=10**6, bytes_accessed=10**4, transcendentals=0),
    )(*held)


def dot(a, b):
    return jnp.dot(a, b, preferred_element_type=F32)


def operators(parts, src_w_ref, tgt_w_ref, out_refs):
    channels = src_w_ref.shape[1]
    span, small = channels * BAND, channels * EDGE

    def columns(size):
        pick_c = lax.broadcasted_iota(jnp.int32, (channels, channels * size), 1) // size
        pick_r = lax.broadcasted_iota(jnp.int32, (channels, channels * size), 0)
        return (pick_c == pick_r).astype(BF16)

    wide, narrow, single = columns(BAND), columns(EDGE), columns(1)
    row = lax.broadcasted_iota(jnp.int32, (BAND, span), 0)
    shift = row - lax.broadcasted_iota(jnp.int32, (BAND, span), 1) % BAND
    row_s = lax.broadcasted_iota(jnp.int32, (BAND, small), 0)
    col_s = lax.broadcasted_iota(jnp.int32, (BAND, small), 1) % EDGE
    near = ((row_s == 0) & (col_s == EDGE - 1), (row_s == BAND - 1) & (col_s == 0))
    row_1 = lax.broadcasted_iota(jnp.int32, (BAND, channels), 0)
    deep = (row_1 == 0, row_1 == BAND - 1)
    spread = {}

    def taps(ref, layer, o, pick, key):
        key = (key, layer, o)
        if key not in spread:
            spread[key] = lax.dot_general(ref[layer, o], pick, (((0,), (0,)), ((), ())), preferred_element_type=F32)
        return spread[key]

    for (kind, layer), out_ref in zip(parts, out_refs):
        for o in range(channels):
            rows = slice(o * BAND, (o + 1) * BAND)
            for b in range(3):
                if kind == "middle":
                    got = taps(src_w_ref, layer, o, wide, "s")
                    values = {(): jnp.where(shift == 0, got[3 + b][None, :], 0.0)}
                elif kind == "beside":
                    got = taps(src_w_ref, layer, o, wide, "s")
                    values = {(n,): jnp.where(shift == 0, got[6 * n + b][None, :], 0.0) for n in range(2)}
                elif kind == "target":
                    got = taps(tgt_w_ref, layer, o, wide, "t")
                    value = jnp.where(shift == 1, got[b][None, :], 0.0)
                    value = jnp.where(shift == 0, got[3 + b][None, :], value)
                    values = {(): jnp.where(shift == -1, got[6 + b][None, :], value)}
                else:
                    pick, at = (narrow, near) if kind == "near" else (single, deep)
                    got = taps(tgt_w_ref, layer, o, pick, kind)
                    values = {(n,): jnp.where(at[n], got[6 * n + b][None, :], 0.0) for n in range(2)}
                for index, value in values.items():
                    size = value.shape[1]
                    out_ref[(*index, rows, slice(b * size, (b + 1) * size))] = value.astype(BF16)


def operator_shapes(parts, channels):
    span = channels * BAND
    widths = dict(middle=span, beside=span, target=span, near=channels * EDGE, deep=channels)
    lead = dict(middle=(), beside=(2,), target=(), near=(2,), deep=(2,))
    return [VMEM((*lead[kind], span, 3 * widths[kind]), BF16) for kind, _ in parts]


def build_body(parts, src_w_ref, tgt_w_ref, after_ref, *out_refs):
    operators(parts, src_w_ref, tgt_w_ref, out_refs)


def build(parts, src_w, tgt_w, after):
    got = call(
        functools.partial(build_body, parts),
        operator_shapes(parts, src_w.shape[1]),
        (src_w, tgt_w, after),
        {2: pl.ANY},
    )
    return dict(zip(parts, got))


class View:
    def __init__(self, ref, columns):
        self.ref, self.columns = ref, columns

    @property
    def shape(self):
        channels, rows, _, depth, width = self.ref.shape
        return channels, rows, len(self.columns), depth, width

    def __getitem__(self, index):
        first, i, j, *rest = index
        return self.ref[(first, i, self.columns[j], *rest)]


def middle(x_ref):
    return View(x_ref, tuple(range(1, x_ref.shape[2] - 1)))


def sides(x_ref):
    return View(x_ref, (0, x_ref.shape[2] - 1))


def whole(body, views, x_ref, *refs):
    body(*(view(x_ref) for view in views), *refs)


def band(tile):
    channels, size, width = tile.shape
    return tile.reshape(channels * size, width)


def unband(tile, channels):
    return tile.reshape(channels, tile.shape[0] // channels, tile.shape[1])


def src_operand(tiles, cols):
    return jnp.concatenate([jnp.concatenate(tiles[b : b + cols], axis=1) for b in range(3)], axis=0)


def sent_rows(rows):
    odd = parity("srow")
    return ((rows - 1) * (1 - odd), odd), ((rows - 1) * odd, 1 - odd)


def column(mid_ref, rim_ref, i, j, cut):
    last = mid_ref.shape[2] + 1
    return band(rim_ref[:, i, j // last, cut] if j in (0, last) else mid_ref[:, i, j - 1, cut])


def bands_of(depth):
    return [slice(start, start + BAND) for start in range(0, depth, BAND)]


def owed_sums(operator, tiles, out_ref):
    channels, cols, depth, width = out_ref.shape
    cuts = bands_of(depth)
    operand = jnp.concatenate([jnp.concatenate([t for cut in cuts for t in tiles(cut, b)], axis=1) for b in range(3)], axis=0)
    got = dot(operator, operand).astype(BF16)
    for q, cut in enumerate(cuts):
        for j in range(cols):
            at = (q * cols + j) * width
            out_ref[:, j, cut] = unband(got[:, at : at + width], channels)


def inner_body(which, mid_ref, rim_ref, beside_ref, *out_refs):
    rows, cols = mid_ref.shape[1:3]
    for n, out_ref in zip(which, out_refs):
        i, side = sent_rows(rows)[n]
        owed_sums(
            beside_ref[side], lambda cut, b: [column(mid_ref, rim_ref, i, j + b, cut) for j in range(cols)], out_ref
        )


def part_body(mid_ref, rim_ref, beside_ref, after_ref, *part_refs):
    rows, cols = mid_ref.shape[1], mid_ref.shape[2] + 2
    cuts = bands_of(mid_ref.shape[3])
    for (i, side), part_ref in zip(sent_rows(rows), part_refs):
        span = part_ref.shape[1]
        for n, (first, j) in enumerate(((1, 0), (0, cols - 2))):
            tiles = [jnp.concatenate([column(mid_ref, rim_ref, i, j + b, cut) for cut in cuts], axis=1) for b in range(2)]
            operator = beside_ref[side, :, first * span : (first + 2) * span]
            part_ref[n] = dot(operator, jnp.concatenate(tiles, axis=0))


def edge_body(cola_ref, colb_ref, beside_ref, parta_ref, partb_ref, after_ref, a_ref, b_ref, side_ref):
    channels, rows, depth, width = cola_ref.shape
    odd, paired = parity("scol"), has_second("scol")
    side_ref[1 - odd] = cola_ref[...]

    @pl.when(paired)
    def _():
        side_ref[odd] = colb_ref[...]

    @pl.when(jnp.logical_not(paired))
    def _():
        side_ref[odd] = jnp.zeros_like(colb_ref)

    cuts = bands_of(depth)
    for (i, side), part_ref, out_ref in zip(sent_rows(rows), (parta_ref, partb_ref), (a_ref, b_ref)):
        span = part_ref.shape[1]
        for n, tap in enumerate((0, 2)):
            halo = jnp.concatenate([band(side_ref[n, :, i, cut]) for cut in cuts], axis=1)
            got = (part_ref[n] + dot(beside_ref[side, :, tap * span : (tap + 1) * span], halo)).astype(BF16)
            for q, cut in enumerate(cuts):
                out_ref[:, n, cut] = unband(got[:, q * width : (q + 1) * width], channels)


def shifted(tile, step):
    lane = lax.broadcasted_iota(jnp.int32, tile.shape, 1)
    width = tile.shape[1]
    rolled = pltpu.roll(tile.astype(F32), step % width, 1)
    gone = 0 if step == 1 else width - 1
    return jnp.where(lane == gone, 0.0, rolled)


def three(tiles):
    return [jnp.concatenate([shifted(t, step) if step else t.astype(F32) for t in tiles], axis=1) for step in (1, 0, -1)]


def own_body(
    layer, mid_ref, rim_ref, middle_ref, beside_ref, target_ref, near_ref, bias_ref, after_ref, accmid_ref, accrim_ref, lane_ref
):
    channels, rows, mids, depth, width = mid_ref.shape
    cols = mids + 2
    cuts = bands_of(depth)
    shape = (BAND, cols * width)
    bias = [jnp.broadcast_to(bias_ref[layer : layer + 1, o : o + 1], shape) for o in range(channels)]
    bias = jnp.concatenate(bias, axis=0)
    for i in range(rows):
        for q, cut in enumerate(cuts):
            tiles = [column(mid_ref, rim_ref, i, j, cut) for j in range(cols)]
            lane_ref[q, 1] = jnp.concatenate(tiles, axis=1)
            for n, step in ((0, 1), (2, -1)):
                lane_ref[q, n] = jnp.concatenate([shifted(t, step).astype(BF16) for t in tiles], axis=1)
        for q, cut in enumerate(cuts):
            total = bias + dot(target_ref[...], lane_ref[q].reshape(3 * channels * BAND, cols * width))
            for side, other, start in ((0, q - 1, BAND - EDGE), (1, q + 1, 0)):
                if 0 <= other < len(cuts):
                    parts = [unband(lane_ref[other, n], channels)[:, start : start + EDGE] for n in range(3)]
                    total = total + dot(near_ref[side], jnp.concatenate([band(p) for p in parts], axis=0))
            for n, j in enumerate((0, cols - 1)):
                accrim_ref[:, i, n, cut] = unband(total[:, j * width : (j + 1) * width], channels)
            for j in range(1, cols - 1):
                accmid_ref[:, i, j - 1, cut] = unband(total[:, j * width : (j + 1) * width], channels)
        for a in range(3):
            r = i + a - 1
            if 0 <= r < rows:
                operator = middle_ref[...] if a == 1 else beside_ref[a // 2]
                add_sums(operator, lambda cut, b: [column(mid_ref, rim_ref, r, j + b, cut) for j in range(mids)], accmid_ref, i)


def add_sums(operator, tiles, acc_ref, i):
    channels, _, cols, depth, width = acc_ref.shape
    cuts = bands_of(depth)
    operand = jnp.concatenate([jnp.concatenate([t for cut in cuts for t in tiles(cut, b)], axis=1) for b in range(3)], axis=0)
    got = dot(operator, operand)
    for q, cut in enumerate(cuts):
        for j in range(cols):
            at = (q * cols + j) * width
            acc_ref[:, i, j, cut] += unband(got[:, at : at + width], channels)


def rest_body(
    mid_ref, rim_ref, side_ref, middle_ref, beside_ref, deep_ref, accmid_ref, accrim_ref, *rest
):
    *deep_halos, outmid_ref, outrim_ref = rest
    channels, rows, mids, depth, width = mid_ref.shape
    cols = mids + 2

    def around(r, j, cut):
        if j in (-1, cols):
            return band(side_ref[0 if j < 0 else 1, :, r, cut])
        return column(mid_ref, rim_ref, r, j, cut)

    for i in range(rows):
        for a in range(3):
            r = i + a - 1
            if 0 <= r < rows:
                operator = middle_ref[...] if a == 1 else beside_ref[a // 2]
                add_sums(operator, lambda cut, b: [around(r, j + b - 1, cut) for j in (0, cols - 1)], outrim_ref, i)
        odd = parity("trow")
        for n, halo_ref in enumerate(deep_halos):
            side = (1 - odd) if n == 0 else odd
            cut = pl.ds(pl.multiple_of(side * (depth - BAND), BAND), BAND)
            halo = three([halo_ref[i, :, j * width : (j + 1) * width] for j in range(cols)])
            halo = jnp.concatenate(halo, axis=0)
            if n == 1:
                halo = halo * has_second("trow").astype(F32)
            got = dot(deep_ref[side], halo.astype(BF16))
            for j in range(cols):
                acc_ref, at = (outrim_ref, j // (cols - 1)) if j in (0, cols - 1) else (outmid_ref, j - 1)
                acc_ref[:, i, at, cut] += unband(got[:, j * width : (j + 1) * width], channels)


def finished(x_ref, acc_ref, owed_refs, store):
    rows, cols = x_ref.shape[1:3]
    odd = parity("srow")
    paired = has_second("srow").astype(F32)
    for n, i in enumerate([(rows - 1) * (1 - odd), (rows - 1) * odd, *range(1, rows - 1)]):
        if n < 2 and owed_refs[n] is None:
            continue
        for j in range(cols):
            total = acc_ref[:, i, j]
            if n < 2:
                owed = owed_refs[n][:, j].astype(F32)
                total = total + (owed if n == 0 else owed * paired)
            store(i, j, (x_ref[:, i, j].astype(F32) + jnp.maximum(total, 0.0)).astype(BF16))


def sent_columns(rim_ref, col_refs):
    odd = parity("scol")
    for n, ref in zip((1 - odd, odd), col_refs):
        ref[...] = rim_ref[:, :, n]


def depth_body(mid_ref, rim_ref, after_ref, *deep_refs):
    channels, rows, mids, depth, _ = mid_ref.shape
    odd = parity("trow")
    shape = (channels, channels * BAND)
    first = lax.broadcasted_iota(jnp.int32, shape, 0) * BAND
    for n, ref in enumerate(deep_refs):
        end = (1 - odd) if n == 0 else odd
        cut = pl.ds(pl.multiple_of(end * (depth - BAND), BAND), BAND)
        pick = (lax.broadcasted_iota(jnp.int32, shape, 1) == first + end * (BAND - 1)).astype(BF16)
        for i in range(rows):
            tiles = [column(mid_ref, rim_ref, i, j, cut) for j in range(mids + 2)]
            ref[i] = dot(pick, jnp.concatenate(tiles, axis=1)).astype(BF16)


def mid_body(x_ref, acc_ref, a_ref, b_ref, out_ref):
    def store(i, j, value):
        out_ref[:, i, j] = value

    finished(x_ref, acc_ref, (a_ref, b_ref), store)


def begin_body(x_ref, acc_ref, a_ref, after_ref, out_ref):
    mid_body(x_ref, acc_ref, a_ref, None, out_ref)


def next_body(x_ref, acc_ref, b_ref, begun_ref, after_ref, out_ref, cola_ref, colb_ref):
    mid_body(x_ref, acc_ref, None, b_ref, out_ref)
    sent_columns(out_ref, (cola_ref, colb_ref))


def write_body(first, step, x_ref, acc_ref, a_ref, b_ref, *refs):
    out_ref, hold_ref, sems = refs[-3:]
    copies = []

    def store(i, j, value):
        hold_ref[:, i, j] = value
        copies.append(pltpu.make_async_copy(hold_ref.at[:, i, j], out_ref.at[:, i, first + step * j], sems.at[len(copies)]))
        copies[-1].start()

    finished(x_ref, acc_ref, (a_ref, b_ref), store)
    for copy in copies:
        copy.wait()


def open_body(parts, x_ref, src_w_ref, tgt_w_ref, bias_ref, *rest):
    src_ref, tgt_ref, held_ref, beside_ref, cola_ref, colb_ref, sems = rest
    last = x_ref.shape[2] - 1
    odd = parity("scol")
    pairs = (
        (src_w_ref, src_ref),
        (x_ref.at[:, :, last * (1 - odd)], cola_ref),
        (x_ref.at[:, :, last * odd], colb_ref),
        (tgt_w_ref, tgt_ref),
        (bias_ref, held_ref),
    )
    copies = [pltpu.make_async_copy(a, b, sems.at[n]) for n, (a, b) in enumerate(pairs)]
    for copy in copies:
        copy.start()
    copies[0].wait()
    operators(parts, src_ref, None, (beside_ref,))
    for copy in copies[1:]:
        copy.wait()


def swap_first(value, axis):
    return lax.ppermute(value, axis, [(n, n ^ 1) for n in range(lax.axis_size(axis))])


def swap_second(value, axis, other):
    count, across = lax.axis_size(axis), lax.axis_size(other)
    pairs = []
    for n in range(count):
        for m in range(across):
            if 0 < n < count - 1:
                target = (n + 1 if n % 2 else n - 1, m)
            else:
                target = (n, m ^ 1)
            pairs.append((n * across + m, target[0] * across + target[1]))
    return lax.ppermute(value, (axis, other), pairs)


def shards(volume, src_weight, tgt_weight, bias):
    layers = src_weight.shape[0]
    channels, rows, cols, depth, width = volume.shape
    axes = ("srow", "scol", "trow")
    counts = [lax.axis_size(n) for n in axes]
    assert all(count % 2 == 0 for count in counts) and rows > 1 and cols > 2 and layers > 1
    src_w = jnp.transpose(src_weight, (0, 2, 3, 1))
    tgt_w = jnp.transpose(tgt_weight, (0, 2, 3, 1))
    deep_swaps = 1 if counts[2] == 2 else 2
    mid_shape, rim_shape = ((channels, rows, n, depth, width) for n in (cols - 2, 2))
    line = VMEM((channels, rows, depth, width), BF16)
    owed_rim = VMEM((channels, 2, depth, width), BF16)
    early = [("beside", 0)]
    src_w, tgt_w, bias, beside_0, col_a, col_b = call(
        functools.partial(open_body, early),
        [VMEM(src_w.shape, BF16), VMEM(tgt_w.shape, BF16), VMEM(bias.shape, F32)] + operator_shapes(early, channels) + [line, line],
        (volume, src_w, tgt_w, bias),
        {n: HBM for n in range(4)},
        scratch=[pltpu.SemaphoreType.DMA((5,))],
    )
    made = {early[0]: beside_0}
    kinds = ("middle", "beside", "target", "near", "deep")
    owed_inner = [VMEM((channels, cols - 2, depth, width), BF16)]
    block, sum_a = (volume,), None
    for layer in range(layers):

        def on(body, *views):
            return functools.partial(whole, body, views) if layer == 0 else body

        both, base = (middle, sides), len(block)
        mid, rim = block[0], block[-1]
        beside = swap_first(col_a, "scol"), swap_second(col_b, "scol", "trow")
        if sum_a is None:
            (sum_a,) = call(on(functools.partial(inner_body, (0,)), *both), owed_inner, (*block, made["beside", layer]))
            got_a = swap_first(sum_a, "srow")
        (sum_b,) = call(on(functools.partial(inner_body, (1,)), *both), owed_inner, (*block, made["beside", layer]))
        inner = got_a, swap_second(sum_b, "srow", "scol")
        if layer == 0:
            late = [(kind, n) for n in range(layers) for kind in kinds]
            made |= build([part for part in late if part not in early], src_w, tgt_w, sum_b)
        operator = {kind: made[kind, layer] for kind in kinds}
        parts = call(
            on(part_body, *both),
            [VMEM((2, channels * BAND, depth // BAND * width), F32)] * 2,
            (*block, operator["beside"], sum_b),
            {base + 1: pl.ANY},
        )
        a, b, side = call(
            edge_body,
            [owed_rim, owed_rim, VMEM((2, *line.shape), BF16)],
            (*beside, operator["beside"], *parts, operator["middle"]),
            {5: pl.ANY},
        )
        outer = swap_first(a, "srow"), swap_second(b, "srow", "scol")
        deep = call(
            on(depth_body, *both),
            [VMEM((rows, channels, cols * width), BF16)] * deep_swaps,
            (*block, b),
            {base: pl.ANY},
        )
        deeper = [swap_first(deep[0], "trow")]
        if deep_swaps == 2:
            deeper.append(swap_second(deep[1], "trow", "scol"))
        accs = call(
            on(functools.partial(own_body, layer), *both),
            [VMEM(mid_shape, F32), VMEM(rim_shape, F32)],
            (*block, *(operator[kind] for kind in ("middle", "beside", "target", "near")), bias, b),
            {base + 5: pl.ANY},
            scratch=[VMEM((depth // BAND, 3, channels * BAND, cols * width), BF16)],
        )
        acc_mid, acc_rim = call(
            on(rest_body, *both),
            [VMEM(mid_shape, F32), VMEM(rim_shape, F32)],
            (*block, side, *(operator[kind] for kind in ("middle", "beside", "deep")), *accs, *deeper),
            aliases={base + 4: 0, base + 5: 1},
        )
        if layer < layers - 1:
            (mid,) = call(on(mid_body, middle), [VMEM(mid_shape, BF16)], (mid, acc_mid, *inner))
            whole_rim = [VMEM(rim_shape, BF16)]
            (begun,) = call(on(begin_body, sides), whole_rim, (rim, acc_rim, outer[0], mid), {3: pl.ANY})
            (sum_a,) = call(functools.partial(inner_body, (0,)), owed_inner, (mid, begun, made["beside", layer + 1]))
            got_a = swap_first(sum_a, "srow")
            rim, col_a, col_b = call(
                on(next_body, sides),
                whole_rim + [line, line],
                (rim, acc_rim, outer[1], begun, sum_a),
                {4: pl.ANY},
                aliases={3: 0},
            )
            block = (mid, rim)
        else:
            result, state = [jax.ShapeDtypeStruct(volume.shape, BF16)], ()
            for first, step, shape, operands in (
                (1, 1, mid_shape, (mid, acc_mid, *inner)),
                (0, cols - 1, rim_shape, (rim, acc_rim, *outer)),
            ):
                state = call(
                    functools.partial(write_body, first, step),
                    result,
                    (*operands, *state),
                    {4: HBM},
                    out_place=HBM,
                    scratch=[VMEM(shape, BF16), pltpu.SemaphoreType.DMA((shape[1] * shape[2],))],
                    aliases={4: 0} if state else None,
                )
    return state[0]


def solution(mesh):
    return jax.shard_map(
        shards,
        mesh=mesh,
        in_specs=(P(None, "srow", "scol", "trow", None), P(), P(), P()),
        out_specs=P(None, "srow", "scol", "trow", None),
        check_vma=False,
    )
```

```python
import functools

import jax
import jax.numpy as jnp
from jax import lax
from jax.experimental import pallas as pl
from jax.experimental.pallas import tpu as pltpu
from jax.sharding import PartitionSpec as P

BAND = 32
EDGE = 16
SCOPED = 16 * 1024 * 1024
F32 = jnp.float32
BF16 = jnp.bfloat16
VMEM, HBM = pltpu.VMEM, pltpu.HBM
def parity(axis):
    return lax.axis_index(axis) % 2


def has_second(axis):
    at = lax.axis_index(axis)
    return (at > 0) & (at < lax.axis_size(axis) - 1)


def call(body, outs, args, places=None, out_place=VMEM, scratch=(), aliases=None):
    places = places or {}
    spaces = [places.get(n, VMEM) for n in range(len(args))]
    held = [pltpu.with_memory_space_constraint(a, m) if m in (VMEM, HBM) else a for a, m in zip(args, spaces)]
    return pl.pallas_call(
        body,
        out_shape=tuple(outs),
        in_specs=[pl.BlockSpec(memory_space=m) for m in spaces],
        out_specs=tuple(pl.BlockSpec(memory_space=out_place) for _ in outs),
        scratch_shapes=list(scratch),
        input_output_aliases=aliases or {},
        compiler_params=pltpu.CompilerParams(vmem_limit_bytes=SCOPED),
        cost_estimate=pl.CostEstimate(flops=10**6, bytes_accessed=10**4, transcendentals=0),
    )(*held)


def dot(a, b):
    return jnp.dot(a, b, preferred_element_type=F32)


def operators(parts, src_w_ref, tgt_w_ref, out_refs):
    channels = src_w_ref.shape[1]
    span, small = channels * BAND, channels * EDGE

    def columns(size):
        pick_c = lax.broadcasted_iota(jnp.int32, (channels, channels * size), 1) // size
        pick_r = lax.broadcasted_iota(jnp.int32, (channels, channels * size), 0)
        return (pick_c == pick_r).astype(BF16)

    wide, narrow, single = columns(BAND), columns(EDGE), columns(1)
    row = lax.broadcasted_iota(jnp.int32, (BAND, span), 0)
    shift = row - lax.broadcasted_iota(jnp.int32, (BAND, span), 1) % BAND
    row_s = lax.broadcasted_iota(jnp.int32, (BAND, small), 0)
    col_s = lax.broadcasted_iota(jnp.int32, (BAND, small), 1) % EDGE
    near = ((row_s == 0) & (col_s == EDGE - 1), (row_s == BAND - 1) & (col_s == 0))
    row_1 = lax.broadcasted_iota(jnp.int32, (BAND, channels), 0)
    deep = (row_1 == 0, row_1 == BAND - 1)
    spread = {}

    def taps(ref, layer, o, pick, key):
        key = (key, layer, o)
        if key not in spread:
            spread[key] = lax.dot_general(ref[layer, o], pick, (((0,), (0,)), ((), ())), preferred_element_type=F32)
        return spread[key]

    for (kind, layer), out_ref in zip(parts, out_refs):
        for o in range(channels):
            rows = slice(o * BAND, (o + 1) * BAND)
            for b in range(3):
                if kind == "middle":
                    got = taps(src_w_ref, layer, o, wide, "s")
                    values = {(): jnp.where(shift == 0, got[3 + b][None, :], 0.0)}
                elif kind == "beside":
                    got = taps(src_w_ref, layer, o, wide, "s")
                    values = {(n,): jnp.where(shift == 0, got[6 * n + b][None, :], 0.0) for n in range(2)}
                elif kind == "target":
                    got = taps(tgt_w_ref, layer, o, wide, "t")
                    value = jnp.where(shift == 1, got[b][None, :], 0.0)
                    value = jnp.where(shift == 0, got[3 + b][None, :], value)
                    values = {(): jnp.where(shift == -1, got[6 + b][None, :], value)}
                else:
                    pick, at = (narrow, near) if kind == "near" else (single, deep)
                    got = taps(tgt_w_ref, layer, o, pick, kind)
                    values = {(n,): jnp.where(at[n], got[6 * n + b][None, :], 0.0) for n in range(2)}
                for index, value in values.items():
                    size = value.shape[1]
                    out_ref[(*index, rows, slice(b * size, (b + 1) * size))] = value.astype(BF16)


def operator_shapes(parts, channels):
    span = channels * BAND
    widths = dict(middle=span, beside=span, target=span, near=channels * EDGE, deep=channels)
    lead = dict(middle=(), beside=(2,), target=(), near=(2,), deep=(2,))
    return [VMEM((*lead[kind], span, 3 * widths[kind]), BF16) for kind, _ in parts]


def build_body(parts, src_w_ref, tgt_w_ref, after_ref, *out_refs):
    operators(parts, src_w_ref, tgt_w_ref, out_refs)


def build(parts, src_w, tgt_w, after):
    got = call(
        functools.partial(build_body, parts),
        operator_shapes(parts, src_w.shape[1]),
        (src_w, tgt_w, after),
        {2: pl.ANY},
    )
    return dict(zip(parts, got))


class View:
    def __init__(self, ref, columns):
        self.ref, self.columns = ref, columns

    @property
    def shape(self):
        channels, rows, _, depth, width = self.ref.shape
        return channels, rows, len(self.columns), depth, width

    def __getitem__(self, index):
        first, i, j, *rest = index
        return self.ref[(first, i, self.columns[j], *rest)]


def middle(x_ref):
    return View(x_ref, tuple(range(1, x_ref.shape[2] - 1)))


def sides(x_ref):
    return View(x_ref, (0, x_ref.shape[2] - 1))


def whole(body, views, x_ref, *refs):
    body(*(view(x_ref) for view in views), *refs)


def band(tile):
    channels, size, width = tile.shape
    return tile.reshape(channels * size, width)


def unband(tile, channels):
    return tile.reshape(channels, tile.shape[0] // channels, tile.shape[1])


def src_operand(tiles, cols):
    return jnp.concatenate([jnp.concatenate(tiles[b : b + cols], axis=1) for b in range(3)], axis=0)


def sent_rows(rows):
    odd = parity("srow")
    return ((rows - 1) * (1 - odd), odd), ((rows - 1) * odd, 1 - odd)


def column(mid_ref, rim_ref, i, j, cut):
    last = mid_ref.shape[2] + 1
    return band(rim_ref[:, i, j // last, cut] if j in (0, last) else mid_ref[:, i, j - 1, cut])


def bands_of(depth):
    return [slice(start, start + BAND) for start in range(0, depth, BAND)]


def owed_sums(operator, tiles, out_ref):
    channels, cols, depth, width = out_ref.shape
    cuts = bands_of(depth)
    operand = jnp.concatenate([jnp.concatenate([t for cut in cuts for t in tiles(cut, b)], axis=1) for b in range(3)], axis=0)
    got = dot(operator, operand).astype(BF16)
    for q, cut in enumerate(cuts):
        for j in range(cols):
            at = (q * cols + j) * width
            out_ref[:, j, cut] = unband(got[:, at : at + width], channels)


def inner_body(which, mid_ref, rim_ref, beside_ref, *out_refs):
    rows, cols = mid_ref.shape[1:3]
    for n, out_ref in zip(which, out_refs[-len(which) :]):
        i, side = sent_rows(rows)[n]
        owed_sums(
            beside_ref[side], lambda cut, b: [column(mid_ref, rim_ref, i, j + b, cut) for j in range(cols)], out_ref
        )


def part_body(mid_ref, rim_ref, beside_ref, after_ref, *part_refs):
    rows, cols = mid_ref.shape[1], mid_ref.shape[2] + 2
    cuts = bands_of(mid_ref.shape[3])
    for (i, side), part_ref in zip(sent_rows(rows), part_refs):
        span = part_ref.shape[1]
        for n, (first, j) in enumerate(((1, 0), (0, cols - 2))):
            tiles = [jnp.concatenate([column(mid_ref, rim_ref, i, j + b, cut) for cut in cuts], axis=1) for b in range(2)]
            operator = beside_ref[side, :, first * span : (first + 2) * span]
            part_ref[n] = dot(operator, jnp.concatenate(tiles, axis=0))


def edge_body(cola_ref, colb_ref, beside_ref, parta_ref, partb_ref, after_ref, a_ref, b_ref, side_ref):
    channels, rows, depth, width = cola_ref.shape
    odd, paired = parity("scol"), has_second("scol")
    side_ref[1 - odd] = cola_ref[...]

    @pl.when(paired)
    def _():
        side_ref[odd] = colb_ref[...]

    @pl.when(jnp.logical_not(paired))
    def _():
        side_ref[odd] = jnp.zeros_like(colb_ref)

    cuts = bands_of(depth)
    for (i, side), part_ref, out_ref in zip(sent_rows(rows), (parta_ref, partb_ref), (a_ref, b_ref)):
        span = part_ref.shape[1]
        for n, tap in enumerate((0, 2)):
            halo = jnp.concatenate([band(side_ref[n, :, i, cut]) for cut in cuts], axis=1)
            got = (part_ref[n] + dot(beside_ref[side, :, tap * span : (tap + 1) * span], halo)).astype(BF16)
            for q, cut in enumerate(cuts):
                out_ref[:, n, cut] = unband(got[:, q * width : (q + 1) * width], channels)


def shifted(tile, step):
    lane = lax.broadcasted_iota(jnp.int32, tile.shape, 1)
    width = tile.shape[1]
    rolled = pltpu.roll(tile.astype(F32), step % width, 1)
    gone = 0 if step == 1 else width - 1
    return jnp.where(lane == gone, 0.0, rolled)


def three(tiles):
    return [jnp.concatenate([shifted(t, step) if step else t.astype(F32) for t in tiles], axis=1) for step in (1, 0, -1)]


def own_body(
    layer, mid_ref, rim_ref, middle_ref, beside_ref, target_ref, near_ref, bias_ref, after_ref, accmid_ref, accrim_ref, lane_ref
):
    channels, rows, mids, depth, width = mid_ref.shape
    cols = mids + 2
    cuts = bands_of(depth)
    shape = (BAND, cols * width)
    bias = [jnp.broadcast_to(bias_ref[layer : layer + 1, o : o + 1], shape) for o in range(channels)]
    bias = jnp.concatenate(bias, axis=0)
    for i in range(rows):
        for q, cut in enumerate(cuts):
            tiles = [column(mid_ref, rim_ref, i, j, cut) for j in range(cols)]
            lane_ref[q, 1] = jnp.concatenate(tiles, axis=1)
            for n, step in ((0, 1), (2, -1)):
                lane_ref[q, n] = jnp.concatenate([shifted(t, step).astype(BF16) for t in tiles], axis=1)
        for q, cut in enumerate(cuts):
            total = bias + dot(target_ref[...], lane_ref[q].reshape(3 * channels * BAND, cols * width))
            for side, other, start in ((0, q - 1, BAND - EDGE), (1, q + 1, 0)):
                if 0 <= other < len(cuts):
                    parts = [unband(lane_ref[other, n], channels)[:, start : start + EDGE] for n in range(3)]
                    total = total + dot(near_ref[side], jnp.concatenate([band(p) for p in parts], axis=0))
            for n, j in enumerate((0, cols - 1)):
                accrim_ref[:, i, n, cut] = unband(total[:, j * width : (j + 1) * width], channels)
            for j in range(1, cols - 1):
                accmid_ref[:, i, j - 1, cut] = unband(total[:, j * width : (j + 1) * width], channels)
        for a in range(3):
            r = i + a - 1
            if 0 <= r < rows:
                operator = middle_ref[...] if a == 1 else beside_ref[a // 2]
                add_sums(operator, lambda cut, b: [column(mid_ref, rim_ref, r, j + b, cut) for j in range(mids)], accmid_ref, i)


def add_sums(operator, tiles, acc_ref, i):
    channels, _, cols, depth, width = acc_ref.shape
    cuts = bands_of(depth)
    operand = jnp.concatenate([jnp.concatenate([t for cut in cuts for t in tiles(cut, b)], axis=1) for b in range(3)], axis=0)
    got = dot(operator, operand)
    for q, cut in enumerate(cuts):
        for j in range(cols):
            at = (q * cols + j) * width
            acc_ref[:, i, j, cut] += unband(got[:, at : at + width], channels)


def rest_body(
    mid_ref, rim_ref, side_ref, middle_ref, beside_ref, deep_ref, accmid_ref, accrim_ref, *rest
):
    *deep_halos, outmid_ref, outrim_ref = rest
    channels, rows, mids, depth, width = mid_ref.shape
    cols = mids + 2

    def around(r, j, cut):
        if j in (-1, cols):
            return band(side_ref[0 if j < 0 else 1, :, r, cut])
        return column(mid_ref, rim_ref, r, j, cut)

    for i in range(rows):
        for a in range(3):
            r = i + a - 1
            if 0 <= r < rows:
                operator = middle_ref[...] if a == 1 else beside_ref[a // 2]
                add_sums(operator, lambda cut, b: [around(r, j + b - 1, cut) for j in (0, cols - 1)], outrim_ref, i)
        odd = parity("trow")
        for n, halo_ref in enumerate(deep_halos):
            side = (1 - odd) if n == 0 else odd
            cut = pl.ds(pl.multiple_of(side * (depth - BAND), BAND), BAND)
            halo = three([halo_ref[i, :, j * width : (j + 1) * width] for j in range(cols)])
            halo = jnp.concatenate(halo, axis=0)
            if n == 1:
                halo = halo * has_second("trow").astype(F32)
            got = dot(deep_ref[side], halo.astype(BF16))
            for j in range(cols):
                acc_ref, at = (outrim_ref, j // (cols - 1)) if j in (0, cols - 1) else (outmid_ref, j - 1)
                acc_ref[:, i, at, cut] += unband(got[:, j * width : (j + 1) * width], channels)


def finished(x_ref, acc_ref, owed_refs, store):
    rows, cols = x_ref.shape[1:3]
    odd = parity("srow")
    paired = has_second("srow").astype(F32)
    for n, i in enumerate([(rows - 1) * (1 - odd), (rows - 1) * odd, *range(1, rows - 1)]):
        if n < 2 and owed_refs[n] is None:
            continue
        for j in range(cols):
            total = acc_ref[:, i, j]
            if n < 2:
                owed = owed_refs[n][:, j].astype(F32)
                total = total + (owed if n == 0 else owed * paired)
            store(i, j, (x_ref[:, i, j].astype(F32) + jnp.maximum(total, 0.0)).astype(BF16))


def sent_columns(rim_ref, col_refs):
    odd = parity("scol")
    for n, ref in zip((1 - odd, odd), col_refs):
        ref[...] = rim_ref[:, :, n]


def depth_body(mid_ref, rim_ref, after_ref, *deep_refs):
    channels, rows, mids, depth, _ = mid_ref.shape
    odd = parity("trow")
    shape = (channels, channels * BAND)
    first = lax.broadcasted_iota(jnp.int32, shape, 0) * BAND
    for n, ref in enumerate(deep_refs):
        end = (1 - odd) if n == 0 else odd
        cut = pl.ds(pl.multiple_of(end * (depth - BAND), BAND), BAND)
        pick = (lax.broadcasted_iota(jnp.int32, shape, 1) == first + end * (BAND - 1)).astype(BF16)
        for i in range(rows):
            tiles = [column(mid_ref, rim_ref, i, j, cut) for j in range(mids + 2)]
            ref[i] = dot(pick, jnp.concatenate(tiles, axis=1)).astype(BF16)


def mid_body(x_ref, acc_ref, a_ref, b_ref, out_ref):
    def store(i, j, value):
        out_ref[:, i, j] = value

    finished(x_ref, acc_ref, (a_ref, b_ref), store)


def begin_body(x_ref, acc_ref, a_ref, after_ref, out_ref):
    mid_body(x_ref, acc_ref, a_ref, None, out_ref)


def next_body(x_ref, acc_ref, b_ref, begun_ref, after_ref, out_ref, cola_ref, colb_ref):
    mid_body(x_ref, acc_ref, None, b_ref, out_ref)
    sent_columns(out_ref, (cola_ref, colb_ref))


def write_body(first, step, x_ref, acc_ref, a_ref, b_ref, *refs):
    out_ref, hold_ref, sems = refs[-3:]
    copies = []

    def store(i, j, value):
        hold_ref[:, i, j] = value
        copies.append(pltpu.make_async_copy(hold_ref.at[:, i, j], out_ref.at[:, i, first + step * j], sems.at[len(copies)]))
        copies[-1].start()

    finished(x_ref, acc_ref, (a_ref, b_ref), store)
    for copy in copies:
        copy.wait()


def open_body(parts, x_ref, src_w_ref, tgt_w_ref, bias_ref, *rest):
    src_ref, tgt_ref, held_ref, beside_ref, cola_ref, colb_ref, sems = rest
    last = x_ref.shape[2] - 1
    odd = parity("scol")
    pairs = (
        (src_w_ref, src_ref),
        (x_ref.at[:, :, last * (1 - odd)], cola_ref),
        (x_ref.at[:, :, last * odd], colb_ref),
        (tgt_w_ref, tgt_ref),
        (bias_ref, held_ref),
    )
    copies = [pltpu.make_async_copy(a, b, sems.at[n]) for n, (a, b) in enumerate(pairs)]
    for copy in copies:
        copy.start()
    copies[0].wait()
    operators(parts, src_ref, None, (beside_ref,))
    for copy in copies[1:]:
        copy.wait()


def swap_first(value, axis):
    return lax.ppermute(value, axis, [(n, n ^ 1) for n in range(lax.axis_size(axis))])


def swap_second(value, axis, other):
    count, across = lax.axis_size(axis), lax.axis_size(other)
    pairs = []
    for n in range(count):
        for m in range(across):
            if 0 < n < count - 1:
                target = (n + 1 if n % 2 else n - 1, m)
            else:
                target = (n, m ^ 1)
            pairs.append((n * across + m, target[0] * across + target[1]))
    return lax.ppermute(value, (axis, other), pairs)


def shards(volume, src_weight, tgt_weight, bias):
    layers = src_weight.shape[0]
    channels, rows, cols, depth, width = volume.shape
    axes = ("srow", "scol", "trow")
    counts = [lax.axis_size(n) for n in axes]
    assert all(count % 2 == 0 for count in counts) and rows > 1 and cols > 2 and layers > 1
    src_w = jnp.transpose(src_weight, (0, 2, 3, 1))
    tgt_w = jnp.transpose(tgt_weight, (0, 2, 3, 1))
    deep_swaps = 1 if counts[2] == 2 else 2
    mid_shape, rim_shape = ((channels, rows, n, depth, width) for n in (cols - 2, 2))
    line = VMEM((channels, rows, depth, width), BF16)
    owed_rim = VMEM((channels, 2, depth, width), BF16)
    early = [("beside", 0)]
    src_w, tgt_w, bias, beside_0, col_a, col_b = call(
        functools.partial(open_body, early),
        [VMEM(src_w.shape, BF16), VMEM(tgt_w.shape, BF16), VMEM(bias.shape, F32)] + operator_shapes(early, channels) + [line, line],
        (volume, src_w, tgt_w, bias),
        {n: HBM for n in range(4)},
        scratch=[pltpu.SemaphoreType.DMA((5,))],
    )
    made = {early[0]: beside_0}
    kinds = ("middle", "beside", "target", "near", "deep")
    owed_inner = [VMEM((channels, cols - 2, depth, width), BF16)]
    block, sum_a = (volume,), None
    for layer in range(layers):

        def on(body, *views):
            return functools.partial(whole, body, views) if layer == 0 else body

        both, base = (middle, sides), len(block)
        mid, rim = block[0], block[-1]
        beside = swap_first(col_a, "scol"), swap_second(col_b, "scol", "trow")
        if sum_a is None:
            (sum_a,) = call(on(functools.partial(inner_body, (0,)), *both), owed_inner, (*block, made["beside", layer]))
            got_a = swap_first(sum_a, "srow")
        (sum_b,) = call(
            on(functools.partial(inner_body, (1,)), *both),
            owed_inner,
            (*block, made["beside", layer], sum_a),
            {base + 1: pl.ANY},
        )
        inner = got_a, swap_second(sum_b, "srow", "scol")
        if layer == 0:
            late = [(kind, n) for n in range(layers) for kind in kinds]
            made |= build([part for part in late if part not in early], src_w, tgt_w, sum_b)
        operator = {kind: made[kind, layer] for kind in kinds}
        parts = call(
            on(part_body, *both),
            [VMEM((2, channels * BAND, depth // BAND * width), F32)] * 2,
            (*block, operator["beside"], sum_b),
            {base + 1: pl.ANY},
        )
        a, b, side = call(
            edge_body,
            [owed_rim, owed_rim, VMEM((2, *line.shape), BF16)],
            (*beside, operator["beside"], *parts, operator["middle"]),
            {5: pl.ANY},
        )
        outer = swap_first(a, "srow"), swap_second(b, "srow", "scol")
        deep = call(
            on(depth_body, *both),
            [VMEM((rows, channels, cols * width), BF16)] * deep_swaps,
            (*block, b),
            {base: pl.ANY},
        )
        deeper = [swap_first(deep[0], "trow")]
        if deep_swaps == 2:
            deeper.append(swap_second(deep[1], "trow", "scol"))
        accs = call(
            on(functools.partial(own_body, layer), *both),
            [VMEM(mid_shape, F32), VMEM(rim_shape, F32)],
            (*block, *(operator[kind] for kind in ("middle", "beside", "target", "near")), bias, b),
            {base + 5: pl.ANY},
            scratch=[VMEM((depth // BAND, 3, channels * BAND, cols * width), BF16)],
        )
        acc_mid, acc_rim = call(
            on(rest_body, *both),
            [VMEM(mid_shape, F32), VMEM(rim_shape, F32)],
            (*block, side, *(operator[kind] for kind in ("middle", "beside", "deep")), *accs, *deeper),
            aliases={base + 4: 0, base + 5: 1},
        )
        if layer < layers - 1:
            (mid,) = call(on(mid_body, middle), [VMEM(mid_shape, BF16)], (mid, acc_mid, *inner))
            whole_rim = [VMEM(rim_shape, BF16)]
            (begun,) = call(on(begin_body, sides), whole_rim, (rim, acc_rim, outer[0], mid), {3: pl.ANY})
            (sum_a,) = call(functools.partial(inner_body, (0,)), owed_inner, (mid, begun, made["beside", layer + 1]))
            got_a = swap_first(sum_a, "srow")
            rim, col_a, col_b = call(
                on(next_body, sides),
                whole_rim + [line, line],
                (rim, acc_rim, outer[1], begun, sum_a),
                {4: pl.ANY},
                aliases={3: 0},
            )
            block = (mid, rim)
        else:
            result, state = [jax.ShapeDtypeStruct(volume.shape, BF16)], ()
            for first, step, shape, operands in (
                (1, 1, mid_shape, (mid, acc_mid, *inner)),
                (0, cols - 1, rim_shape, (rim, acc_rim, *outer)),
            ):
                state = call(
                    functools.partial(write_body, first, step),
                    result,
                    (*operands, *state),
                    {4: HBM},
                    out_place=HBM,
                    scratch=[VMEM(shape, BF16), pltpu.SemaphoreType.DMA((shape[1] * shape[2],))],
                    aliases={4: 0} if state else None,
                )
    return state[0]


def solution(mesh):
    return jax.shard_map(
        shards,
        mesh=mesh,
        in_specs=(P(None, "srow", "scol", "trow", None), P(), P(), P()),
        out_specs=P(None, "srow", "scol", "trow", None),
        check_vma=False,
    )
```
